32 devices in a mesh: dp: 8 (over y, x, core), blk: 4 (over z).
Axes of the slice: x: 2, y: 2, z: 4, core: 2. Of those that a mesh axis runs over, the one named last changes fastest.
Arguments:
- hidden_in: bfloat16 [2, 8, 1024, 768], P(None, 'dp', 'blk'), may hold values from -6 to 6
- segment_ids: int32 [2, 8, 1024], P(None, 'dp', 'blk'), may hold values from 0 to 15, as said below
- queries: bfloat16 [2, 128, 768], P(None, 'dp'), may hold values from -0.5390625 to 0.5390625
- targets: int32 [2, 128], P(None, 'dp'), may hold values from 0 to 127, each once within a row
- cotangent: bfloat16 [2, 8, 1024, 768], P(None, 'dp', 'blk'), may hold values from -3 to 3
- query_weight: bfloat16 [768, 768], P('dp'), may hold values from -0.21875 to 0.21875
- key_weight: bfloat16 [768, 768], P('dp'), may hold values from -0.21875 to 0.21875
- value_weight: bfloat16 [768, 768], P('dp'), may hold values from -0.21875 to 0.21875
- output_weight: bfloat16 [768, 768], P('dp'), may hold values from -1.75 to 1.75
- query_bias: bfloat16 [768], P('dp'), may hold values from -3 to 3
- value_bias: bfloat16 [768], P('dp'), may hold values from -0.29882812 to 0.29882812
- output_bias: bfloat16 [768], P('dp'), may hold values from -1.1953125 to 1.1953125
- first_gain: bfloat16 [768], P('dp'), may hold values from 0.5 to 1.5
- first_shift: bfloat16 [768], P('dp'), may hold values from -1.1953125 to 1.1953125
- inner_weight: bfloat16 [768, 3072], P('dp'), may hold values from -0.21875 to 0.21875
- inner_bias: bfloat16 [3072], P('dp'), may hold values from -1.796875 to 1.796875
- outer_weight: bfloat16 [3072, 768], P('dp'), may hold values from -0.109375 to 0.109375
- outer_bias: bfloat16 [768], P('dp'), may hold values from -1.1953125 to 1.1953125
- second_gain: bfloat16 [768], P('dp'), may hold values from 0.5 to 1.5
- second_shift: bfloat16 [768], P('dp'), may hold values from -1.1953125 to 1.1953125
Outputs:
- hidden_out: bfloat16 [2, 8, 1024, 768], P(None, 'dp', 'blk')
- embeddings: bfloat16 [2, 128, 768], P(None, 'dp')
- query_loss: float32 [2, 128], P(None, 'dp')
- query_grad: float32 [2, 128, 768], P(None, 'dp')
- hidden_grad: bfloat16 [2, 8, 1024, 768], P(None, 'dp', 'blk')
- query_weight_grad: float32 [768, 768], P('dp')
- key_weight_grad: float32 [768, 768], P('dp')
- value_weight_grad: float32 [768, 768], P('dp')
- output_weight_grad: float32 [768, 768], P('dp')
- query_bias_grad: float32 [768], P('dp')
- value_bias_grad: float32 [768], P('dp')
- output_bias_grad: float32 [768], P('dp')
- first_gain_grad: float32 [768], P('dp')
- first_shift_grad: float32 [768], P('dp')
- inner_weight_grad: float32 [768, 3072], P('dp')
- inner_bias_grad: float32 [3072], P('dp')
- outer_weight_grad: float32 [3072, 768], P('dp')
- outer_bias_grad: float32 [768], P('dp')
- second_gain_grad: float32 [768], P('dp')
- second_shift_grad: float32 [768], P('dp')
The draws below stay inside these ranges and needn't reach their ends.
Inputs may be any that keep to these rules, and one draw needn't show every extreme that they name: `segment_ids`: in each row the segment numbers never fall along the row and every number occurs; the first position of a segment is its CLS token. For each index of dp, one of its rows in one of the micro-batches holds a segment that begins within the first 256 positions and ends within the last 256; in every other row each block of 256 positions holds the first positions of exactly 4 segments. Each micro-batch's targets name every passage of it once.
All inputs are finite; a program needn't handle non-finite values.
Results may differ from the reference program's by a relative error of at most 0.023.
Values may be sent and summed in bfloat16 or wider, within the bound.
A program may use at most 80 MiB of HBM per device.

```python
import math
import jax
import jax.numpy as jnp
from jax import lax

D = 768
HEADS = 12
HEAD_DIM = 64
FF = 3072
TOK_BLK = 256
ROWS = 1
MICRO = 2
SEG_DEV = 4
ROW_LEN = 1024
SEGS = 16
ALL_ROWS = 8
PASS = 128
N_DP = 8
N_BLK = 4


def spread_cuts(row_key):

    def block_offsets(block_number):
        picked = jax.random.permutation(jax.random.fold_in(row_key, 10 + block_number), TOK_BLK)[:SEG_DEV]
        return jnp.sort(picked)
    offsets = jax.vmap(block_offsets)(jnp.arange(N_BLK))
    offsets = offsets.at[0, 0].set(0)
    starts = (jnp.arange(N_BLK)[:, None] * TOK_BLK + offsets).reshape(N_BLK * SEG_DEV)
    return starts[1:]


def draw_row_segments(row_key, spanning):
    segment_count = SEG_DEV * N_BLK
    cut_count = segment_count - 1
    early_cuts = jnp.sort(jax.random.permutation(jax.random.fold_in(row_key, 1), TOK_BLK - 1)[:cut_count] + 1)
    late_cuts = jnp.sort(jax.random.permutation(jax.random.fold_in(row_key, 2), TOK_BLK - 1)[:cut_count] + (ROW_LEN - TOK_BLK + 1))
    long_index = jax.random.randint(jax.random.fold_in(row_key, 3), (), 0, segment_count)
    order = jnp.arange(cut_count)
    framed = jnp.where(order < long_index, early_cuts, late_cuts)
    chosen = jnp.where(spanning, framed, spread_cuts(row_key))
    position = jnp.arange(ROW_LEN)
    return jnp.sum((position[:, None] >= chosen[None, :]).astype(jnp.int32), axis=1).astype(jnp.int32)


def draw_segment_ids(key, part):
    key = jax.random.fold_in(key, 11)
    total_rows = ROWS * N_DP
    chosen_row = jax.random.randint(jax.random.fold_in(key, 1), (N_DP,), 0, ROWS)
    chosen_micro = jax.random.randint(jax.random.fold_in(key, 4), (N_DP,), 0, MICRO)
    row_index = jnp.arange(total_rows)
    micro_index = jnp.arange(MICRO)
    row_hit = row_index % ROWS == chosen_row[row_index // ROWS]
    micro_hit = micro_index[:, None] == chosen_micro[row_index // ROWS][None, :]
    spanning = row_hit[None, :] & micro_hit
    base_key = jax.random.fold_in(key, 2)
    row_keys = jax.vmap(lambda number: jax.random.fold_in(base_key, number))(jnp.arange(MICRO * total_rows))
    segments = jax.vmap(draw_row_segments)(row_keys, spanning.reshape(MICRO * total_rows))
    return segments.reshape(MICRO, total_rows, ROW_LEN).astype(jnp.int32)


def raised(entries, own_key, source, target, blocks, factor):
    owner, partner = [(jnp.arange(entries.shape[axis_at]) // (entries.shape[axis_at] // blocks)).reshape([-1 if axis == axis_at else 1 for axis in range(entries.ndim)]) for axis_at in (source, target)]
    chosen = jax.random.permutation(own_key, blocks)[partner]
    strong = (owner == chosen) | (owner == (partner + blocks // 2) % blocks)
    return jnp.where(strong, factor * entries, entries)


def block_levels(rng, shape, shards, least, high):
    loudness, own = 1.0, jax.random.fold_in(rng, 6)
    for dim, parts in shards:
        steps = jnp.exp(jax.random.uniform(jax.random.fold_in(own, dim), (parts,), jnp.float32, least / len(shards), high / len(shards)))
        loudness = loudness * jnp.repeat(steps, shape[dim] // parts).reshape([-1 if axis == dim else 1 for axis in range(len(shape))])
    return loudness


def gaussian(own_key, extent, width, bound, shards=(), held_as=jnp.bfloat16):
    level = block_levels(own_key, extent, shards, -0.22, 0.18) if shards else 1.0
    array = jax.random.normal(own_key, extent, jnp.float32) * width * level
    return jnp.minimum(jnp.maximum(array, -bound), bound).astype(held_as)


def heavy_noise(own_key, shape, spread, limit, split, heavy, held_as=jnp.bfloat16):
    array = spread * jax.random.normal(own_key, shape, jnp.float32)
    if split:
        array = array * block_levels(own_key, shape, split, -0.22, 0.18)
    return jnp.clip(raised(array, jax.random.fold_in(own_key, 3), *heavy), -limit, limit).astype(held_as)


def setup_inputs(seed: int = 0) -> dict:
    streams_of = jax.random.split(jax.random.key(seed), 21)
    return {
        "hidden_in": gaussian(streams_of[0], (MICRO, ALL_ROWS, ROW_LEN, D), 1.0, 6.0, ((1, 8), (2, 4))),
        "segment_ids": draw_segment_ids(jax.random.fold_in(streams_of[20], 71), 0),
        "queries": gaussian(streams_of[2], (MICRO, PASS, D), (3.0 / D ** 0.5), 0.5390625, ((1, 8),)),
        "targets": jax.vmap(lambda own: jax.random.permutation(own, PASS))(jax.random.split(streams_of[3], MICRO)).reshape((MICRO, PASS)).astype(jnp.int32),
        "cotangent": heavy_noise(streams_of[4], (MICRO, ALL_ROWS, ROW_LEN, D), 0.5, 3.0, ((1, 8), (2, 4)), (1, 3, 8, 2.0)),
        "query_weight": gaussian(streams_of[5], (D, D), D ** -0.5, 0.21875, ((0, 8),)),
        "key_weight": gaussian(streams_of[6], (D, D), D ** -0.5, 0.21875, ((0, 8),)),
        "value_weight": gaussian(streams_of[7], (D, D), D ** -0.5, 0.21875, ((0, 8),)),
        "output_weight": gaussian(streams_of[8], (D, D), (D // 64) ** -0.5, 1.75, ((0, 8),)),
        "query_bias": gaussian(streams_of[9], (D,), 0.5, 3.0, ((0, 8),)),
        "value_bias": gaussian(streams_of[10], (D,), 0.05, 0.29882812, ((0, 8),)),
        "output_bias": gaussian(streams_of[11], (D,), 0.2, 1.1953125, ((0, 8),)),
        "first_gain": jnp.clip(1.0 + 0.1 * jax.random.normal(streams_of[12], (D,), jnp.float32), 0.5, 1.5).astype(jnp.bfloat16),
        "first_shift": gaussian(streams_of[13], (D,), 0.2, 1.1953125, ((0, 8),)),
        "inner_weight": gaussian(streams_of[14], (D, FF), D ** -0.5, 0.21875, ((0, 8),)),
        "inner_bias": gaussian(streams_of[15], (FF,), 0.3, 1.796875, ((0, 8),)),
        "outer_weight": gaussian(streams_of[16], (FF, D), FF ** -0.5, 0.109375, ((0, 8),)),
        "outer_bias": gaussian(streams_of[17], (D,), 0.2, 1.1953125, ((0, 8),)),
        "second_gain": jnp.clip(1.0 + 0.1 * jax.random.normal(streams_of[18], (D,), jnp.float32), 0.5, 1.5).astype(jnp.bfloat16),
        "second_shift": gaussian(streams_of[19], (D,), 0.2, 1.1953125, ((0, 8),)),
    }


@jax.custom_vjp
def low(v):
    return lax.optimization_barrier(v.astype(jnp.bfloat16)).astype(jnp.float32)

@jax.custom_vjp
def low_back(v):
    return v

def low_keep(v):
    return (low(v), None)

def low_pass(kept, grad):
    return (grad,)

def back_keep(v):
    return (v, None)

def back_low(kept, grad):
    return (low(grad),)
low.defvjp(low_keep, low_pass)
low_back.defvjp(back_keep, back_low)
EPSILON = 1e-12
NEGATIVE = -1000000000.0
PRECISE = lax.Precision.HIGHEST

def round_both(values):
    return low(low_back(values))

def layer_norm(values, norm_gain, norm_shift):
    center = values - lax.optimization_barrier(jnp.mean(values, axis=-1, keepdims=True))
    factor = lax.rsqrt(lax.optimization_barrier(jnp.mean(center * center, axis=-1, keepdims=True)) + EPSILON)
    return center * factor * norm_gain + norm_shift

def attend_block(query_rows, query_segment, key_rows, value_rows, key_segment):
    score_scale = 1.0 / math.sqrt(HEAD_DIM)
    raw_scores = low_back(jnp.einsum('qhd,khd->hqk', query_rows, key_rows, precision=PRECISE))
    same_doc = (query_segment[:, None] == key_segment[None, :])[None]
    scores = jnp.where(same_doc, score_scale * raw_scores, NEGATIVE)
    row_peak = lax.optimization_barrier(jnp.max(scores, axis=-1, keepdims=True))
    weights = jnp.exp(scores - row_peak)
    row_total = lax.optimization_barrier(jnp.sum(weights, axis=-1))
    summed = low_back(jnp.einsum('hqk,khd->qhd', low(weights), value_rows, precision=PRECISE))
    return summed / jnp.transpose(row_total)[:, :, None]

def attention(query_rows, key_rows, value_rows, segment):
    row_count = query_rows.shape[0]
    block_size = min(512, ROW_LEN)
    block_count = ROW_LEN // block_size
    query_blocks = query_rows.reshape(row_count * block_count, block_size, HEADS, HEAD_DIM)
    segment_blocks = segment.reshape(row_count * block_count, block_size)
    owners = jnp.arange(row_count * block_count, dtype=jnp.int32) // block_count

    def one_block(item):
        block_query, block_segment, owner = item
        return attend_block(block_query, block_segment, key_rows[owner], value_rows[owner], segment[owner])
    context = lax.map(jax.checkpoint(one_block), (query_blocks, segment_blocks, owners))
    return context.reshape(row_count * ROW_LEN, HEADS * HEAD_DIM)

def micro_batch(params, hidden, segment, query_vectors, target_index):
    wq_full, wk_full, wv_full, wo_full, bq_full, bv_full, bo_full, gain_one, shift_one, w_inner, b_inner, w_outer, b_outer, gain_two, shift_two = params
    row_count = hidden.shape[0]
    flat_rows = hidden.reshape(row_count * ROW_LEN, D)
    query_rows = round_both(jnp.dot(flat_rows, wq_full, precision=PRECISE) + bq_full)
    key_rows = round_both(jnp.dot(flat_rows, wk_full, precision=PRECISE))
    value_rows = round_both(jnp.dot(flat_rows, wv_full, precision=PRECISE) + bv_full)
    shape_heads = (row_count, ROW_LEN, HEADS, HEAD_DIM)
    context = attention(query_rows.reshape(shape_heads), key_rows.reshape(shape_heads), value_rows.reshape(shape_heads), segment)
    attended = low_back(jnp.dot(round_both(context), wo_full, precision=PRECISE) + bo_full)
    first_out = layer_norm(flat_rows + attended, gain_one, shift_one)
    inner_pre = low_back(jnp.dot(low(first_out), w_inner, precision=PRECISE) + b_inner)
    active = low(jax.nn.gelu(inner_pre, approximate=False))
    outer_out = low_back(jnp.dot(active, w_outer, precision=PRECISE) + b_outer)
    output = layer_norm(first_out + outer_out, gain_two, shift_two)
    rows_out = output.reshape(row_count, ROW_LEN, D)
    numbers = jnp.arange(SEGS, dtype=jnp.int32)
    starts = lax.optimization_barrier(jnp.sum((segment[:, :, None] < numbers[None, None, :]).astype(jnp.int32), axis=1)).astype(jnp.int32)
    embeds = low(jnp.take_along_axis(rows_out, starts[:, :, None], axis=1)).reshape(row_count * SEGS, D)
    scores = jnp.dot(query_vectors, embeds.T, precision=PRECISE)
    picked = jnp.take_along_axis(scores, target_index[:, None], axis=1)[:, 0]
    losses = jax.nn.logsumexp(scores, axis=-1) - picked
    return (rows_out, losses, embeds)

def reference(hidden_in, segment_ids, queries, targets, cotangent, query_weight, key_weight, value_weight, output_weight, query_bias, value_bias, output_bias, first_gain, first_shift, inner_weight, inner_bias, outer_weight, outer_bias, second_gain, second_shift):
    raw_params = (query_weight, key_weight, value_weight, output_weight, query_bias, value_bias, output_bias, first_gain, first_shift, inner_weight, inner_bias, outer_weight, outer_bias, second_gain, second_shift)
    params = tuple((param.astype(jnp.float32) for param in raw_params))

    def forward(params_in, hidden_all, query_all):
        outs_list, loss_list, embed_list = ([], [], [])
        for micro_index in range(MICRO):
            rows_out, losses, embeds = micro_batch(params_in, hidden_all[micro_index], segment_ids[micro_index], query_all[micro_index], targets[micro_index])
            outs_list.append(rows_out)
            loss_list.append(losses)
            embed_list.append(embeds)
        return (jnp.stack(outs_list), jnp.stack(loss_list), jnp.stack(embed_list))
    primal, pullback = jax.vjp(forward, params, hidden_in.astype(jnp.float32), queries.astype(jnp.float32))
    output, losses, embeds = primal
    grads, hidden_grad, query_grad = pullback((cotangent.astype(jnp.float32), jnp.ones_like(losses), jnp.zeros_like(embeds)))
    return (output.astype(jnp.bfloat16), embeds.astype(jnp.bfloat16), losses, query_grad, hidden_grad.astype(jnp.bfloat16), grads[0], grads[1], grads[2], grads[3], grads[4], grads[5], grads[6], grads[7], grads[8], grads[9], grads[10], grads[11], grads[12], grads[13], grads[14])
```

```python
import functools
import math

import jax
import jax.numpy as jnp
from jax import lax
from jax.experimental import pallas as pl
from jax.experimental.pallas import tpu as pltpu
from jax.sharding import PartitionSpec as P

HEADS = 12


EPSILON = 1e-12
NEGATIVE = -1000000000.0
PRECISE = lax.Precision.HIGHEST


def passed_along(x, axis, by):
    size = lax.axis_size(axis)
    return lax.ppermute(x, axis, [(i, (i + by) % size) for i in range(size)])


def as_sent(x):
    return jax.tree.map(lambda a: a.astype(jnp.bfloat16) if a.dtype == jnp.float32 else a, x)


def layer_norm(values, norm_gain, norm_shift):
    center = values - jnp.mean(values, axis=-1, keepdims=True)
    factor = lax.rsqrt(jnp.mean(center * center, axis=-1, keepdims=True) + EPSILON)
    normed = center * factor
    return (normed * norm_gain + norm_shift, normed, factor)


def norm_back(gradient, normed, factor, norm_gain):
    scaled = gradient * norm_gain
    inner_term = (
        scaled
        - jnp.mean(scaled, axis=-1, keepdims=True)
        - normed * jnp.mean(scaled * normed, axis=-1, keepdims=True)
    )
    return inner_term * factor


def gelu_slope(values):
    normal_cdf = 0.5 * (1.0 + lax.erf(values * (1.0 / math.sqrt(2.0))))
    return normal_cdf + values * jnp.exp(-0.5 * values * values) * (1.0 / math.sqrt(2.0 * math.pi))


def scores_of(query_rows, key_rows, query_segment, key_segment, score_scale):
    raw_scores = jnp.einsum(
        "rqhd,rkhd->rhqk", query_rows, key_rows, preferred_element_type=jnp.float32
    )
    same_doc = (query_segment[:, :, None] == key_segment[:, None, :])[:, None]
    return jnp.where(same_doc, score_scale * raw_scores, NEGATIVE)


def contribute(
    query_rows,
    push_grad,
    delta_term,
    peak_term,
    query_segment,
    key_rows,
    value_rows,
    key_segment,
    score_scale,
):
    scores = scores_of(query_rows, key_rows, query_segment, key_segment, score_scale)
    weights = jnp.exp(scores - peak_term[..., None])
    pushed = jnp.einsum(
        "rqhd,rkhd->rhqk", push_grad, value_rows, preferred_element_type=jnp.float32
    )
    dscore = (weights * (pushed - delta_term[..., None]) * score_scale).astype(jnp.bfloat16)
    query_part = jnp.einsum("rhqk,rkhd->rqhd", dscore, key_rows, preferred_element_type=jnp.float32)
    key_part = jnp.einsum("rhqk,rqhd->rkhd", dscore, query_rows, preferred_element_type=jnp.float32)
    value_part = jnp.einsum(
        "rhqk,rqhd->rkhd",
        weights.astype(jnp.bfloat16),
        push_grad,
        preferred_element_type=jnp.float32,
    )
    return (query_part, key_part, value_part)


def ring_body(
    hidden_in,
    segment_ids,
    queries,
    targets,
    cotangent,
    query_weight,
    key_weight,
    value_weight,
    output_weight,
    query_bias,
    value_bias,
    output_bias,
    first_gain,
    first_shift,
    inner_weight,
    inner_bias,
    outer_weight,
    outer_bias,
    second_gain,
    second_shift,
):
    shards = (
        query_weight,
        key_weight,
        value_weight,
        output_weight,
        query_bias,
        value_bias,
        output_bias,
        first_gain,
        first_shift,
        inner_weight,
        inner_bias,
        outer_weight,
        outer_bias,
        second_gain,
        second_shift,
    )
    cycle_size = lax.axis_size("blk")
    cycle_place = lax.axis_index("blk")
    micro_count, row_count, block_tokens, model_width = hidden_in.shape
    segment_count = queries.shape[1] // row_count
    head_count = HEADS
    head_dim = model_width // head_count
    score_scale = 1.0 / math.sqrt(head_dim)
    token_count = row_count * block_tokens
    head_shape = (row_count, block_tokens, head_count, head_dim)
    grad_totals = tuple((jnp.zeros(shard_piece.shape, jnp.float32) for shard_piece in shards))
    local_sum = None
    gathered = None
    out_list, embed_list, loss_list, qgrad_list, hgrad_list = ([], [], [], [], [])
    for micro_index in range(micro_count):
        gathered = (
            lax.all_gather(shards[0], "dp", axis=0, tiled=True),
            lax.all_gather(shards[1], "dp", axis=0, tiled=True),
            lax.all_gather(shards[2], "dp", axis=0, tiled=True),
            lax.all_gather(shards[3], "dp", axis=0, tiled=True),
            lax.all_gather(shards[4], "dp", axis=0, tiled=True),
            lax.all_gather(shards[5], "dp", axis=0, tiled=True),
            lax.all_gather(shards[6], "dp", axis=0, tiled=True),
            lax.all_gather(shards[7], "dp", axis=0, tiled=True),
            lax.all_gather(shards[8], "dp", axis=0, tiled=True),
            lax.all_gather(shards[9], "dp", axis=0, tiled=True),
            lax.all_gather(shards[10], "dp", axis=0, tiled=True),
            lax.all_gather(shards[11], "dp", axis=0, tiled=True),
            lax.all_gather(shards[12], "dp", axis=0, tiled=True),
            lax.all_gather(shards[13], "dp", axis=0, tiled=True),
            lax.all_gather(shards[14], "dp", axis=0, tiled=True),
        )
        (
            wq_full,
            wk_full,
            wv_full,
            wo_full,
            bq_full,
            bv_full,
            bo_full,
            gain_one,
            shift_one,
            w_inner,
            b_inner,
            w_outer,
            b_outer,
            gain_two,
            shift_two,
        ) = gathered
        gain_one = gain_one.astype(jnp.float32)
        gain_two = gain_two.astype(jnp.float32)
        segment = segment_ids[micro_index]
        flat_rows = hidden_in[micro_index].reshape(token_count, model_width)
        query_rows = (
            (
                jnp.dot(flat_rows, wq_full, preferred_element_type=jnp.float32)
                + bq_full.astype(jnp.float32)
            )
            .astype(jnp.bfloat16)
            .reshape(head_shape)
        )
        key_rows = (
            jnp.dot(flat_rows, wk_full, preferred_element_type=jnp.float32)
            .astype(jnp.bfloat16)
            .reshape(head_shape)
        )
        value_rows = (
            (
                jnp.dot(flat_rows, wv_full, preferred_element_type=jnp.float32)
                + bv_full.astype(jnp.float32)
            )
            .astype(jnp.bfloat16)
            .reshape(head_shape)
        )

        def absorb(softmax_state, visit_keys, visit_values, visit_segment):
            running_peak, running_total, running_sum = softmax_state
            scores = scores_of(query_rows, visit_keys, segment, visit_segment, score_scale)
            new_peak = jnp.maximum(running_peak, jnp.max(scores, axis=-1))
            decay_factor = jnp.exp(running_peak - new_peak)
            weights = jnp.exp(scores - new_peak[..., None])
            running_total = running_total * decay_factor + jnp.sum(weights, axis=-1)
            update = jnp.einsum(
                "rhqk,rkhd->rqhd",
                weights.astype(jnp.bfloat16),
                visit_values,
                preferred_element_type=jnp.float32,
            )
            running_sum = running_sum * jnp.transpose(decay_factor, (0, 2, 1))[..., None] + update
            return (new_peak, running_total, running_sum)

        start_state = (
            jnp.full((row_count, head_count, block_tokens), -1e30, jnp.float32),
            jnp.zeros((row_count, head_count, block_tokens), jnp.float32),
            jnp.zeros(head_shape, jnp.float32),
        )
        first_state = absorb(start_state, key_rows, value_rows, segment)

        def forward_step(cycle_step, cycle_carry):
            visit_keys, visit_values, visit_segment, prior_segment, softmax_state = cycle_carry
            visit_keys, visit_values, visit_segment = passed_along(
                (visit_keys, visit_values, visit_segment), "blk", 1
            )
            prior_segment = jnp.where(cycle_step == 1, visit_segment[:, -1], prior_segment)
            return (
                visit_keys,
                visit_values,
                visit_segment,
                prior_segment,
                absorb(softmax_state, visit_keys, visit_values, visit_segment),
            )

        cycle_carry = lax.fori_loop(
            1, cycle_size, forward_step, (key_rows, value_rows, segment, segment[:, 0], first_state)
        )
        prior_segment = cycle_carry[3]
        row_peak, row_total, running_sum = cycle_carry[4]
        total_heads = jnp.transpose(row_total, (0, 2, 1))[..., None]
        context = running_sum / total_heads
        context_low = context.reshape(token_count, model_width).astype(jnp.bfloat16)
        attended = jnp.dot(
            context_low, wo_full, preferred_element_type=jnp.float32
        ) + bo_full.astype(jnp.float32)
        first_out, first_normed, first_factor = layer_norm(
            flat_rows.astype(jnp.float32) + attended, gain_one, shift_one.astype(jnp.float32)
        )
        first_low = first_out.astype(jnp.bfloat16)
        inner_pre = jnp.dot(
            first_low, w_inner, preferred_element_type=jnp.float32
        ) + b_inner.astype(jnp.float32)
        active = jax.nn.gelu(inner_pre, approximate=False).astype(jnp.bfloat16)
        outer_out = jnp.dot(active, w_outer, preferred_element_type=jnp.float32) + b_outer.astype(
            jnp.float32
        )
        output, second_normed, second_factor = layer_norm(
            first_out + outer_out, gain_two, shift_two.astype(jnp.float32)
        )
        output_low = output.astype(jnp.bfloat16)
        out_list.append(output_low.reshape(row_count, block_tokens, model_width))
        position = cycle_place * block_tokens + jnp.arange(block_tokens, dtype=jnp.int32)
        before = jnp.concatenate([prior_segment[:, None], segment[:, :-1]], axis=1)
        leading = (position[None, :] == 0) | (segment != before)
        numbers = jnp.arange(segment_count, dtype=jnp.int32)
        select = (leading[:, None, :] & (segment[:, None, :] == numbers[None, :, None])).astype(
            jnp.float32
        )
        cls_table = jnp.einsum(
            "rsi,rid->rsd",
            select.astype(jnp.bfloat16),
            output_low.reshape(row_count, block_tokens, model_width),
            preferred_element_type=jnp.float32,
        )
        own_table = lax.psum(cls_table.astype(jnp.bfloat16), "blk").reshape(
            row_count * segment_count, model_width
        )
        embed_list.append(own_table)
        everyone = lax.all_gather(own_table, "dp", axis=0, tiled=True)
        query_vectors = queries[micro_index]
        query_scores = jnp.dot(query_vectors, everyone.T, preferred_element_type=jnp.float32)
        score_peak = jnp.max(query_scores, axis=1, keepdims=True)
        log_total = score_peak[:, 0] + jnp.log(jnp.sum(jnp.exp(query_scores - score_peak), axis=1))
        target_hot = (
            jnp.arange(query_scores.shape[1], dtype=jnp.int32)[None, :]
            == targets[micro_index][:, None]
        ).astype(jnp.float32)
        loss_list.append(log_total - jnp.sum(query_scores * target_hot, axis=1))
        dscore_query = jnp.exp(query_scores - log_total[:, None]) - target_hot
        qgrad_list.append(jnp.dot(dscore_query, everyone.astype(jnp.float32), precision=PRECISE))
        embed_part = jnp.dot(dscore_query.T, query_vectors.astype(jnp.float32), precision=PRECISE)
        embed_grad = (
            lax.psum_scatter(embed_part.astype(jnp.bfloat16), "dp", scatter_dimension=0, tiled=True)
            .astype(jnp.float32)
            .reshape(row_count, segment_count, model_width)
        )
        cls_grad = jnp.einsum("rsi,rsd->rid", select, embed_grad, precision=PRECISE)
        dout = cotangent[micro_index].reshape(token_count, model_width).astype(
            jnp.float32
        ) + cls_grad.reshape(token_count, model_width)
        gain_two_grad = jnp.sum(dout * second_normed, axis=0)
        shift_two_grad = jnp.sum(dout, axis=0)
        dsecond = norm_back(dout, second_normed, second_factor, gain_two)
        douter = dsecond.astype(jnp.bfloat16)
        outer_bias_grad = jnp.sum(douter.astype(jnp.float32), axis=0)
        outer_weight_grad = jnp.einsum(
            "nf,nd->fd", active, douter, preferred_element_type=jnp.float32
        )
        dactive = jnp.einsum("nd,fd->nf", douter, w_outer, preferred_element_type=jnp.float32)
        dinner = (dactive * gelu_slope(inner_pre)).astype(jnp.bfloat16)
        inner_bias_grad = jnp.sum(dinner.astype(jnp.float32), axis=0)
        inner_weight_grad = jnp.einsum(
            "nd,nf->df", first_low, dinner, preferred_element_type=jnp.float32
        )
        dfirst = dsecond + jnp.einsum(
            "nf,df->nd", dinner, w_inner, preferred_element_type=jnp.float32
        )
        gain_one_grad = jnp.sum(dfirst * first_normed, axis=0)
        shift_one_grad = jnp.sum(dfirst, axis=0)
        dresidual = norm_back(dfirst, first_normed, first_factor, gain_one)
        dattended = dresidual.astype(jnp.bfloat16)
        output_bias_grad = jnp.sum(dattended.astype(jnp.float32), axis=0)
        output_weight_grad = jnp.einsum(
            "nd,ne->de", context_low, dattended, preferred_element_type=jnp.float32
        )
        dcontext = jnp.einsum(
            "ne,de->nd", dattended, wo_full, preferred_element_type=jnp.float32
        ).astype(jnp.bfloat16)
        dcontext_wide = dcontext.astype(jnp.float32).reshape(head_shape)
        push_grad = (dcontext_wide / total_heads).astype(jnp.bfloat16)
        delta_term = jnp.transpose(
            jnp.sum(dcontext_wide * context, axis=-1) / total_heads[..., 0], (0, 2, 1)
        )
        own_query, own_key, own_value = contribute(
            query_rows,
            push_grad,
            delta_term,
            row_peak,
            segment,
            key_rows,
            value_rows,
            segment,
            score_scale,
        )

        def key_step(cycle_step, cycle_carry):
            visit_keys, visit_values, visit_segment, query_sum, key_sum, value_sum = cycle_carry
            visit_keys, visit_values, visit_segment = passed_along(
                (visit_keys, visit_values, visit_segment), "blk", 1
            )
            key_sum, value_sum = (
                passed_along(key_sum.astype(jnp.bfloat16), "blk", 1).astype(key_sum.dtype),
                passed_along(value_sum.astype(jnp.bfloat16), "blk", 1).astype(value_sum.dtype),
            )
            query_part, key_part, value_part = contribute(
                query_rows,
                push_grad,
                delta_term,
                row_peak,
                segment,
                visit_keys,
                visit_values,
                visit_segment,
                score_scale,
            )
            return (
                visit_keys,
                visit_values,
                visit_segment,
                query_sum + query_part,
                key_sum + key_part,
                value_sum + value_part,
            )

        back_carry = lax.fori_loop(
            1, cycle_size, key_step, (key_rows, value_rows, segment, own_query, own_key, own_value)
        )
        query_sum = back_carry[3]
        key_sum, value_sum = (
            passed_along(back_carry[4].astype(jnp.bfloat16), "blk", 1).astype(jnp.float32),
            passed_along(back_carry[5].astype(jnp.bfloat16), "blk", 1).astype(jnp.float32),
        )
        dquery = query_sum.astype(jnp.bfloat16).reshape(token_count, model_width)
        dkey = key_sum.astype(jnp.bfloat16).reshape(token_count, model_width)
        dvalue = value_sum.astype(jnp.bfloat16).reshape(token_count, model_width)
        dhidden = dresidual + jnp.einsum(
            "ne,de->nd", dquery, wq_full, preferred_element_type=jnp.float32
        )
        dhidden = dhidden + jnp.einsum(
            "ne,de->nd", dkey, wk_full, preferred_element_type=jnp.float32
        )
        dhidden = dhidden + jnp.einsum(
            "ne,de->nd", dvalue, wv_full, preferred_element_type=jnp.float32
        )
        hgrad_list.append(
            dhidden.astype(jnp.bfloat16).reshape(row_count, block_tokens, model_width)
        )
        local_grads = (
            jnp.einsum("nd,ne->de", flat_rows, dquery, preferred_element_type=jnp.float32),
            jnp.einsum("nd,ne->de", flat_rows, dkey, preferred_element_type=jnp.float32),
            jnp.einsum("nd,ne->de", flat_rows, dvalue, preferred_element_type=jnp.float32),
            output_weight_grad,
            jnp.sum(dquery.astype(jnp.float32), axis=0),
            jnp.sum(dvalue.astype(jnp.float32), axis=0),
            output_bias_grad,
            gain_one_grad,
            shift_one_grad,
            inner_weight_grad,
            inner_bias_grad,
            outer_weight_grad,
            outer_bias_grad,
            gain_two_grad,
            shift_two_grad,
        )
        local_sum = local_grads
        reduced = jax.tree.map(
            lambda part: part.astype(jnp.float32),
            lax.psum_scatter(as_sent(local_sum), "dp", scatter_dimension=0, tiled=True),
        )
        reduced = jax.tree.map(
            lambda part: part.astype(jnp.float32), lax.psum(as_sent(reduced), "blk")
        )
        grad_totals = tuple(
            (total_piece + new_piece for total_piece, new_piece in zip(grad_totals, reduced))
        )
        local_sum = None
    return (
        jnp.stack(out_list),
        jnp.stack(embed_list),
        jnp.stack(loss_list),
        jnp.stack(qgrad_list),
        jnp.stack(hgrad_list),
        grad_totals[0],
        grad_totals[1],
        grad_totals[2],
        grad_totals[3],
        grad_totals[4],
        grad_totals[5],
        grad_totals[6],
        grad_totals[7],
        grad_totals[8],
        grad_totals[9],
        grad_totals[10],
        grad_totals[11],
        grad_totals[12],
        grad_totals[13],
        grad_totals[14],
    )


MESH = pl.DeviceIdType.MESH
VMEM_LIMIT = 60 * 1024 * 1024
SIDE = {"c": 1, "x": 2, "y": 4}


def place():
    dp, blk = lax.axis_index("dp"), lax.axis_index("blk")
    bits = {"c": lax.rem(dp, 2), "x": lax.rem(dp // 2, 2), "y": dp // 4}
    return dp, blk, bits


def across(dp, blk, bits, *axes):
    other = dp
    for axis in axes:
        other = other + SIDE[axis] * (1 - 2 * bits[axis])
    return (other, blk)


def greet(peers):
    barrier = pltpu.get_barrier_semaphore()
    for peer in peers:
        pl.semaphore_signal(barrier, inc=1, device_id=peer, device_id_type=MESH)
    pl.semaphore_wait(barrier, len(peers))


def remote(source, target, send_sem, recv_sem, peer):
    return pltpu.make_async_remote_copy(
        src_ref=source,
        dst_ref=target,
        send_sem=send_sem,
        recv_sem=recv_sem,
        device_id=peer,
        device_id_type=MESH,
    )


def comm_params(collective):
    return pltpu.CompilerParams(
        collective_id=collective, has_side_effects=True, vmem_limit_bytes=VMEM_LIMIT
    )


ANY = pl.BlockSpec(memory_space=pl.ANY)
IN_VMEM = pl.BlockSpec(memory_space=pltpu.VMEM)


def gather_kernel(routes, ring_size, *refs):
    count = len(routes)
    shards, seg_shard = refs[:count], refs[count]
    fulls, seg_full = refs[count + 1 : 2 * count + 1], refs[2 * count + 1]
    send_sem, recv_sem, seg_send, seg_recv, local_sem = refs[2 * count + 2 :]
    dp, blk, bits = place()
    sibling = across(dp, blk, bits, "c")
    ring = [(dp, lax.rem(blk + step, ring_size)) for step in range(1, ring_size)]
    greet([sibling, across(dp, blk, bits, "x"), across(dp, blk, bits, "y")] + ring)
    seg_rows = seg_shard.shape[0]
    started = []
    locals_started = []
    for step, peer in enumerate(ring):
        copy = remote(
            seg_shard,
            seg_full.at[pl.ds(blk * seg_rows, seg_rows)],
            seg_send.at[step],
            seg_recv.at[step],
            peer,
        )
        copy.start()
        started.append(copy)
    copy = pltpu.make_async_copy(
        seg_shard, seg_full.at[pl.ds(blk * seg_rows, seg_rows)], local_sem.at[count]
    )
    copy.start()
    locals_started.append(copy)

    def block(item, owner):
        rows = shards[item].shape[0]
        return fulls[item].at[pl.ds(owner * rows, rows)]

    inbound = {}
    for item, (first, second) in enumerate(routes):
        for slot, peer in enumerate(
            (across(dp, blk, bits, first), across(dp, blk, bits, second), sibling)
        ):
            copy = remote(
                shards[item],
                block(item, dp),
                send_sem.at[item, slot],
                recv_sem.at[item, slot],
                peer,
            )
            copy.start()
            inbound[item, slot] = copy
        copy = pltpu.make_async_copy(shards[item], block(item, dp), local_sem.at[item])
        copy.start()
        locals_started.append(copy)
    for item, (first, second) in enumerate(routes):
        inbound[item, 0].wait_recv()
        held = block(item, across(dp, blk, bits, first)[0])
        for slot, peer in ((3, across(dp, blk, bits, second)), (4, sibling)):
            copy = remote(held, held, send_sem.at[item, slot], recv_sem.at[item, slot], peer)
            copy.start()
            inbound[item, slot] = copy
    for item, (first, second) in enumerate(routes):
        inbound[item, 1].wait_recv()
        held = block(item, across(dp, blk, bits, second)[0])
        copy = remote(held, held, send_sem.at[item, 5], recv_sem.at[item, 5], sibling)
        copy.start()
        inbound[item, 5] = copy
    for item, (first, second) in enumerate(routes):
        inbound[item, 3].wait_recv()
        held = block(item, across(dp, blk, bits, first, second)[0])
        copy = remote(held, held, send_sem.at[item, 6], recv_sem.at[item, 6], sibling)
        copy.start()
        inbound[item, 6] = copy
    for item in range(count):
        for slot in (2, 4, 5, 6):
            inbound[item, slot].wait_recv()
        for slot in range(7):
            inbound[item, slot].wait_send()
    for copy in started:
        copy.wait()
    for copy in locals_started:
        copy.wait()


def gather_all(shards, routes, segments, dp_size, ring_size):
    count = len(shards)
    return pl.pallas_call(
        functools.partial(gather_kernel, routes, ring_size),
        out_shape=tuple(
            jax.ShapeDtypeStruct((dp_size * s.shape[0], s.shape[1]), s.dtype) for s in shards
        )
        + (
            jax.ShapeDtypeStruct((ring_size * segments.shape[0], segments.shape[1]), jnp.int32),
        ),
        in_specs=[ANY] * (count + 1),
        out_specs=(ANY,) * (count + 1),
        scratch_shapes=[
            pltpu.SemaphoreType.DMA((count, 7)),
            pltpu.SemaphoreType.DMA((count, 7)),
            pltpu.SemaphoreType.DMA((ring_size,)),
            pltpu.SemaphoreType.DMA((ring_size,)),
            pltpu.SemaphoreType.DMA((count + 1,)),
        ],
        compiler_params=comm_params(1),
    )(*shards, segments)


def to_heads_kernel(ring_size, *refs):
    count = (len(refs) - 4) // 1
    parts, (out, send_sem, recv_sem, local_sem) = refs[:count], refs[count:]
    dp, blk, _ = place()
    greet([(dp, lax.rem(blk + step, ring_size)) for step in range(1, ring_size)])
    micro, rows, tokens = parts[0].shape
    group = rows // ring_size
    copies = []
    for m in range(micro):
        for index, part in enumerate(parts):
            for step in range(ring_size):
                owner = lax.rem(blk + step, ring_size)
                source = part.at[m, pl.ds(owner * group, group)]
                target = out.at[m, index, :, pl.ds(pl.multiple_of(blk * tokens, tokens), tokens)]
                if step == 0:
                    copy = pltpu.make_async_copy(source, target, local_sem.at[m, index])
                else:
                    copy = remote(
                        source,
                        target,
                        send_sem.at[m, index, step],
                        recv_sem.at[m, index, step],
                        (dp, owner),
                    )
                copy.start()
                copies.append(copy)
    for copy in copies:
        copy.wait()


def to_heads(parts, ring_size, collective):
    micro, rows, tokens = parts[0].shape
    count = len(parts)
    return pl.pallas_call(
        functools.partial(to_heads_kernel, ring_size),
        out_shape=jax.ShapeDtypeStruct(
            (micro, count, rows // ring_size, tokens * ring_size), parts[0].dtype
        ),
        in_specs=[ANY] * count,
        out_specs=ANY,
        scratch_shapes=[
            pltpu.SemaphoreType.DMA((micro, count, ring_size)),
            pltpu.SemaphoreType.DMA((micro, count, ring_size)),
            pltpu.SemaphoreType.DMA((micro, count)),
        ],
        compiler_params=comm_params(collective),
    )(*parts)


def to_tokens_kernel(ring_size, *refs):
    count = (len(refs) - 3) // 2
    parts, outs = refs[:count], refs[count : 2 * count]
    send_sem, recv_sem, local_sem = refs[2 * count :]
    dp, blk, _ = place()
    greet([(dp, lax.rem(blk + step, ring_size)) for step in range(1, ring_size)])
    micro, group, length = parts[0].shape
    tokens = length // ring_size
    copies = []
    for m in range(micro):
        for index, (part, out) in enumerate(zip(parts, outs)):
            for step in range(ring_size):
                owner = lax.rem(blk + step, ring_size)
                source = part.at[m, :, pl.ds(pl.multiple_of(owner * tokens, tokens), tokens)]
                target = out.at[m, pl.ds(blk * group, group)]
                if step == 0:
                    copy = pltpu.make_async_copy(source, target, local_sem.at[m, index])
                else:
                    copy = remote(
                        source,
                        target,
                        send_sem.at[m, index, step],
                        recv_sem.at[m, index, step],
                        (dp, owner),
                    )
                copy.start()
                copies.append(copy)
    for copy in copies:
        copy.wait()


def to_tokens(parts, ring_size, collective):
    micro, group, length = parts[0].shape
    count = len(parts)
    out = pl.pallas_call(
        functools.partial(to_tokens_kernel, ring_size),
        out_shape=tuple(
            jax.ShapeDtypeStruct((micro, group * ring_size, length // ring_size), p.dtype)
            for p in parts
        ),
        in_specs=[ANY] * count,
        out_specs=(ANY,) * count,
        scratch_shapes=[
            pltpu.SemaphoreType.DMA((micro, count, ring_size)),
            pltpu.SemaphoreType.DMA((micro, count, ring_size)),
            pltpu.SemaphoreType.DMA((micro, count)),
        ],
        compiler_params=comm_params(collective),
    )(*parts)
    return out


def tables_kernel(ring_size, dp_size, own, out, arrived, send_sem, recv_sem, ring_send, ring_recv):
    dp, blk, _ = place()
    ring = [(dp, lax.rem(blk + step, ring_size)) for step in range(1, ring_size)]
    group = [(lax.rem(dp + step, dp_size), blk) for step in range(1, dp_size)]
    greet(ring + group)
    copies = []
    for step, peer in enumerate(ring):
        copy = remote(own, arrived.at[step], ring_send.at[step], ring_recv.at[step], peer)
        copy.start()
        copies.append(copy)
    for copy in copies:
        copy.wait()
    total = own[...].astype(jnp.float32)
    for step in range(ring_size - 1):
        total = total + arrived[step].astype(jnp.float32)
    out[dp] = total.astype(out.dtype)
    copies = []
    for step, peer in enumerate(group):
        copy = remote(out.at[dp], out.at[dp], send_sem.at[step], recv_sem.at[step], peer)
        copy.start()
        copies.append(copy)
    for copy in copies:
        copy.wait()


def gather_tables(own, ring_size, dp_size):
    return pl.pallas_call(
        functools.partial(tables_kernel, ring_size, dp_size),
        out_shape=jax.ShapeDtypeStruct((dp_size,) + own.shape, own.dtype),
        in_specs=[IN_VMEM],
        out_specs=IN_VMEM,
        scratch_shapes=[
            pltpu.VMEM((ring_size - 1,) + own.shape, own.dtype),
            pltpu.SemaphoreType.DMA((dp_size,)),
            pltpu.SemaphoreType.DMA((dp_size,)),
            pltpu.SemaphoreType.DMA((ring_size,)),
            pltpu.SemaphoreType.DMA((ring_size,)),
        ],
        compiler_params=comm_params(4),
    )(own)


def reduce_kernel(routes, *refs):
    count = len(routes)
    grads, outs = refs[:count], refs[count : 2 * count]
    buffers = refs[2 * count : 2 * count + 7 * count]
    own = buffers[:count]
    from_core = buffers[count : 2 * count]
    from_first = buffers[2 * count : 3 * count]
    from_second = buffers[3 * count : 4 * count]
    ring_one = buffers[4 * count : 5 * count]
    ring_two = buffers[5 * count : 6 * count]
    ring_three = buffers[6 * count : 7 * count]
    send_sem, recv_sem, local_sem = refs[9 * count :]
    dp, blk, bits = place()
    sibling = across(dp, blk, bits, "c")
    is_end = (blk == 0) | (blk == 3)
    is_middle = (blk == 1) | (blk == 2)
    partner = (dp, blk + 1 - 2 * lax.rem(blk, 2))
    facing = (dp, 3 - blk)
    greet(
        [
            sibling,
            across(dp, blk, bits, "x"),
            across(dp, blk, bits, "y"),
            partner,
            facing,
        ]
    )
    sent = []

    def owner(core, axes, first_bit, second_bit):
        return core + SIDE[axes[0]] * first_bit + SIDE[axes[1]] * second_bit

    def block(item, which):
        rows = grads[item].shape[0] // 8
        return grads[item].at[pl.ds(which * rows, rows)]

    def go(source, target, item, slot, peer):
        copy = remote(source, target, send_sem.at[item, slot], recv_sem.at[item, slot], peer)
        copy.start()
        return copy

    flying = {}

    def start_core(item):
        axes = routes[item]
        for f in range(2):
            for s in range(2):
                copy = go(
                    block(item, owner(1 - bits["c"], axes, f, s)),
                    from_core[item].at[f, s],
                    item,
                    2 * f + s,
                    sibling,
                )
                flying[item, 2 * f + s] = copy
                mine = pltpu.make_async_copy(
                    block(item, owner(bits["c"], axes, f, s)),
                    own[item].at[f, s],
                    local_sem.at[item, 2 * f + s],
                )
                mine.start()
                flying[item, "own", 2 * f + s] = mine

    def added(left, right):
        return (left.astype(jnp.float32) + right.astype(jnp.float32)).astype(jnp.bfloat16)

    def after_core(item):
        axes = routes[item]
        mine = bits[axes[0]]
        for slot in range(4):
            flying[item, slot].wait_recv()
            flying[item, "own", slot].wait()
        for f in (1 - mine, mine):
            for s in range(2):
                own[item][f, s] = added(own[item][f, s], from_core[item][f, s])
                if f is not mine:
                    flying[item, 4 + s] = go(
                        own[item].at[f, s],
                        from_first[item].at[s],
                        item,
                        4 + s,
                        across(dp, blk, bits, axes[0]),
                    )

    def after_first(item):
        axes = routes[item]
        f, mine = bits[axes[0]], bits[axes[1]]
        for s in range(2):
            flying[item, 4 + s].wait_recv()
        own[item][f, 1 - mine] = added(own[item][f, 1 - mine], from_first[item][1 - mine])
        flying[item, 6] = go(
            own[item].at[f, 1 - mine],
            from_second[item],
            item,
            6,
            across(dp, blk, bits, axes[1]),
        )
        own[item][f, mine] = added(own[item][f, mine], from_first[item][mine])

    def after_second(item):
        axes = routes[item]
        f, s = bits[axes[0]], bits[axes[1]]
        flying[item, 6].wait_recv()
        ring_one[item][0] = added(own[item][f, s], from_second[item][...])

        def ring_copy(source, target, slot, peer):
            return remote(source, target, send_sem.at[item, slot], recv_sem.at[item, slot], peer)

        flying[item, 7] = ring_copy(ring_one[item].at[0], ring_one[item].at[1], 7, partner)
        flying[item, 8] = ring_copy(ring_two[item].at[0], ring_two[item].at[1], 8, facing)
        flying[item, 9] = ring_copy(ring_three[item].at[0], ring_three[item].at[1], 9, partner)

        @pl.when(is_end)
        def _():
            flying[item, 7].start()

    def at_middle(item):
        @pl.when(is_middle)
        def _():
            flying[item, 7].wait_recv()
            ring_two[item][0] = added(ring_one[item][0], ring_one[item][1])
            flying[item, 8].start()

    def across_middle(item):
        @pl.when(is_middle)
        def _():
            flying[item, 8].wait_recv()
            ring_three[item][0] = added(ring_two[item][0], ring_two[item][1])
            flying[item, 9].start()
            outs[item][...] = ring_three[item][0].astype(jnp.float32)

    def at_end(item):
        @pl.when(is_end)
        def _():
            flying[item, 9].wait_recv()
            outs[item][...] = ring_three[item][1].astype(jnp.float32)

    stages = (after_core, after_first, after_second, at_middle, across_middle, at_end)
    for item in range(count):
        start_core(item)
    for tick in range(count + len(stages) - 1):
        for depth in reversed(range(len(stages))):
            item = tick - depth
            if 0 <= item < count:
                stages[depth](item)
    for item in range(count):
        for slot in range(7):
            flying[item, slot].wait_send()

    @pl.when(is_end)
    def _():
        for item in range(count):
            flying[item, 7].wait_send()

    @pl.when(is_middle)
    def _():
        for item in range(count):
            flying[item, 8].wait_send()
            flying[item, 9].wait_send()


def reduce_all(grads, routes, collective):
    count = len(grads)
    shards = [(g.shape[0] // 8, g.shape[1]) for g in grads]
    scratch = []
    for lead in ((2, 2), (2, 2), (2,), (), (2,), (2,), (2,)):
        scratch += [pltpu.VMEM(lead + shard, jnp.bfloat16) for shard in shards]
    return pl.pallas_call(
        functools.partial(reduce_kernel, routes),
        out_shape=tuple(jax.ShapeDtypeStruct(shard, jnp.float32) for shard in shards),
        in_specs=[ANY] * count,
        out_specs=(IN_VMEM,) * count,
        scratch_shapes=scratch
        + [
            pltpu.SemaphoreType.DMA((count, 10)),
            pltpu.SemaphoreType.DMA((count, 10)),
            pltpu.SemaphoreType.DMA((count, 4)),
        ],
        compiler_params=comm_params(collective),
    )(*grads)


def contract(left, right, left_dim, right_dim):
    return lax.dot_general(
        left, right, (((left_dim,), (right_dim,)), ((), ())), preferred_element_type=jnp.float32
    )


def attend_kernel(score_scale, block, qkv, seg_col, seg_row, context, low, stats):
    queries_t, keys_t, values_t = qkv[0, 0, 0], qkv[0, 1, 0], qkv[0, 2, 0]
    length = keys_t.shape[1]
    keys = keys_t.T
    for start in range(0, length, block):
        span = slice(start, start + block)
        raw = contract(keys, queries_t[:, span], 1, 0)
        same = seg_col[0] == seg_row[0, :, span]
        scores = jnp.where(same, raw * score_scale, NEGATIVE)
        peak = jnp.max(scores, axis=0, keepdims=True)
        weights = jnp.exp(scores - peak)
        total = jnp.sum(weights, axis=0, keepdims=True)
        gathered = contract(values_t, weights.astype(jnp.bfloat16), 1, 0)
        ctx = gathered / total
        context[0, 0, :, span] = ctx
        low[0, 0, :, span] = ctx.astype(jnp.bfloat16)
        stats[0, 0, 0:1, span] = peak
        stats[0, 0, 1:2, span] = total


def attend(qkv, seg_col, seg_row, score_scale):
    micro, _, heads, depth, length = qkv.shape
    block = min(256, length)
    return pl.pallas_call(
        functools.partial(attend_kernel, score_scale, block),
        grid=(micro, heads),
        out_shape=(
            jax.ShapeDtypeStruct((micro, heads, depth, length), jnp.float32),
            jax.ShapeDtypeStruct((micro, heads, depth, length), jnp.bfloat16),
            jax.ShapeDtypeStruct((micro, heads, 2, length), jnp.float32),
        ),
        in_specs=[
            pl.BlockSpec((1, 3, 1, depth, length), lambda m, h: (m, 0, h, 0, 0)),
            pl.BlockSpec((1, length, 1), lambda m, h: (m, 0, 0)),
            pl.BlockSpec((1, 1, length), lambda m, h: (m, 0, 0)),
        ],
        out_specs=(
            pl.BlockSpec((1, 1, depth, length), lambda m, h: (m, h, 0, 0)),
            pl.BlockSpec((1, 1, depth, length), lambda m, h: (m, h, 0, 0)),
            pl.BlockSpec((1, 1, 2, length), lambda m, h: (m, h, 0, 0)),
        ),
        compiler_params=pltpu.CompilerParams(vmem_limit_bytes=VMEM_LIMIT),
    )(qkv, seg_col, seg_row)


def attend_back_kernel(
    score_scale, block, qkv, seg_col, seg_row, context, stats, dcontext, dqueries, dkeys, dvalues
):
    queries_t, keys_t, values_t = qkv[0, 0, 0], qkv[0, 1, 0], qkv[0, 2, 0]
    depth, length = keys_t.shape
    keys, values = keys_t.T, values_t.T
    dkey_sum = jnp.zeros((depth, length), jnp.float32)
    dvalue_sum = jnp.zeros((depth, length), jnp.float32)
    for start in range(0, length, block):
        span = slice(start, start + block)
        peak, total = stats[0, 0, 0:1, span], stats[0, 0, 1:2, span]
        dctx = dcontext[0, 0, :, span].astype(jnp.float32)
        push = (dctx / total).astype(jnp.bfloat16)
        delta = jnp.sum(dctx * context[0, 0, :, span], axis=0, keepdims=True) / total
        raw = contract(keys, queries_t[:, span], 1, 0)
        same = seg_col[0] == seg_row[0, :, span]
        weights = jnp.exp(jnp.where(same, raw * score_scale, NEGATIVE) - peak)
        pushed = contract(values, push, 1, 0)
        dscore = (weights * (pushed - delta) * score_scale).astype(jnp.bfloat16)
        dqueries[0, 0, :, span] = contract(keys_t, dscore, 1, 0).astype(jnp.bfloat16)
        dkey_sum = dkey_sum + contract(queries_t[:, span], dscore, 1, 1)
        dvalue_sum = dvalue_sum + contract(push, weights.astype(jnp.bfloat16), 1, 1)
    dkeys[0, 0] = dkey_sum.astype(jnp.bfloat16)
    dvalues[0, 0] = dvalue_sum.astype(jnp.bfloat16)


def attend_back(qkv, seg_col, seg_row, context, stats, dcontext, score_scale):
    micro, _, heads, depth, length = qkv.shape
    block = min(256, length)
    head_block = pl.BlockSpec((1, 1, depth, length), lambda m, h: (m, h, 0, 0))
    return pl.pallas_call(
        functools.partial(attend_back_kernel, score_scale, block),
        grid=(micro, heads),
        out_shape=(jax.ShapeDtypeStruct((micro, heads, depth, length), jnp.bfloat16),) * 3,
        in_specs=[
            pl.BlockSpec((1, 3, 1, depth, length), lambda m, h: (m, 0, h, 0, 0)),
            pl.BlockSpec((1, length, 1), lambda m, h: (m, 0, 0)),
            pl.BlockSpec((1, 1, length), lambda m, h: (m, 0, 0)),
            head_block,
            pl.BlockSpec((1, 1, 2, length), lambda m, h: (m, h, 0, 0)),
            head_block,
        ],
        out_specs=(head_block,) * 3,
        compiler_params=pltpu.CompilerParams(vmem_limit_bytes=VMEM_LIMIT),
    )(qkv, seg_col, seg_row, context, stats, dcontext)


def fast_body(
    hidden_in,
    segment_ids,
    queries,
    targets,
    cotangent,
    query_weight,
    key_weight,
    value_weight,
    output_weight,
    query_bias,
    value_bias,
    output_bias,
    first_gain,
    first_shift,
    inner_weight,
    inner_bias,
    outer_weight,
    outer_bias,
    second_gain,
    second_shift,
):
    dp_size, ring_size = lax.axis_size("dp"), lax.axis_size("blk")
    dp, blk = lax.axis_index("dp"), lax.axis_index("blk")
    micro, row_count, block_tokens, width = hidden_in.shape
    row_queries = queries.shape[1]
    length = block_tokens * ring_size
    head_dim = width // HEADS
    own_heads = HEADS // ring_size
    score_scale = 1.0 / math.sqrt(head_dim)
    tokens = micro * block_tokens
    wide = jnp.float32
    narrow = jnp.bfloat16

    vectors = (
        query_bias,
        value_bias,
        output_bias,
        first_gain,
        first_shift,
        outer_bias,
        second_gain,
        second_shift,
        inner_bias,
    )
    vector_size = sum(v.shape[0] for v in vectors)
    piece = vectors[0].shape[0]
    pack_size = -(-vector_size // 2048) * 2048
    pack = jnp.pad(jnp.concatenate(vectors), (0, pack_size - vector_size)).reshape(-1, 128)
    target_pack = jnp.pad(targets, ((0, 8 - micro), (0, 128 - row_queries)))
    seg_pack = jnp.pad(segment_ids.reshape(micro, block_tokens), ((0, 8 - micro), (0, 0)))
    shards = (
        pack,
        target_pack,
        queries.reshape(micro * row_queries, width),
        query_weight,
        key_weight,
        value_weight,
        output_weight,
        inner_weight,
        outer_weight,
    )
    routes = (("x", "y"), ("y", "x"), ("x", "y")) + (("x", "y"), ("y", "x")) * 3
    (
        pack_all,
        targets_all,
        queries_all,
        wq_full,
        wk_full,
        wv_full,
        wo_full,
        w_inner,
        w_outer,
        seg_all,
    ) = gather_all(shards, routes, seg_pack, dp_size, ring_size)
    pack_rows = pack_all.reshape(dp_size, pack_size)
    eight = (
        pack_rows[:, : 8 * piece].reshape(dp_size, 8, piece).transpose(1, 0, 2).reshape(8, width)
    )
    bq_full, bv_full, bo_full, gain_one, shift_one, b_outer, gain_two, shift_two = eight.astype(
        wide
    )
    b_inner = pack_rows[:, 8 * piece : vector_size].reshape(-1).astype(wide)
    targets_all = (
        targets_all.reshape(dp_size, 8, 128)[:, :micro, :row_queries]
        .transpose(1, 0, 2)
        .reshape(micro, dp_size * row_queries)
    )
    queries_all = (
        queries_all.reshape(dp_size, micro, row_queries, width)
        .transpose(1, 0, 2, 3)
        .reshape(micro, dp_size * row_queries, width)
    )
    seg_row = (
        seg_all.reshape(ring_size, 8, block_tokens)[:, :micro]
        .transpose(1, 0, 2)
        .reshape(micro, 1, length)
    )
    seg_col = seg_row.reshape(micro, length, 1)

    flat_rows = hidden_in.reshape(tokens, width)
    rows_of = hidden_in.reshape(micro, block_tokens, width)

    def projected(weight, bias=None):
        out = jnp.einsum("mtd,de->met", rows_of, weight, preferred_element_type=wide)
        if bias is not None:
            out = out + bias[None, :, None]
        return out.astype(narrow)

    qkv = to_heads(
        (projected(wq_full, bq_full), projected(wk_full), projected(wv_full, bv_full)),
        ring_size,
        2,
    ).reshape(micro, 3, own_heads, head_dim, length)
    context, context_low, stats = attend(qkv, seg_col, seg_row, score_scale)
    (context_t,) = to_tokens(
        (context_low.reshape(micro, own_heads * head_dim, length),), ring_size, 3
    )
    attended = (
        jnp.einsum("met,ed->mtd", context_t, wo_full, preferred_element_type=wide).reshape(
            tokens, width
        )
        + bo_full
    )
    first_out, first_normed, first_factor = layer_norm(
        flat_rows.astype(wide) + attended, gain_one, shift_one
    )
    first_low = first_out.astype(narrow)
    inner_pre = jnp.dot(first_low, w_inner, preferred_element_type=wide) + b_inner
    active = jax.nn.gelu(inner_pre, approximate=False).astype(narrow)
    outer_out = jnp.dot(active, w_outer, preferred_element_type=wide) + b_outer
    output, second_normed, second_factor = layer_norm(first_out + outer_out, gain_two, shift_two)
    output_low = output.astype(narrow)
    output_rows = output_low.reshape(micro, block_tokens, width)

    segment = segment_ids.reshape(micro, block_tokens)
    padded = jnp.pad(seg_row.reshape(micro, length), ((0, 0), (1, 0)), constant_values=-1)
    before = lax.dynamic_slice(padded, (0, blk * block_tokens), (micro, block_tokens))
    numbers = jnp.arange(row_queries, dtype=jnp.int32)
    select = (
        (segment != before)[:, None, :] & (segment[:, None, :] == numbers[None, :, None])
    ).astype(wide)
    own_table = jnp.einsum(
        "msi,mid->msd", select.astype(narrow), output_rows, preferred_element_type=wide
    ).astype(narrow)
    tables = gather_tables(own_table.reshape(micro * row_queries, width), ring_size, dp_size)
    tables = tables.reshape(dp_size, micro, row_queries, width)
    everyone = tables.transpose(1, 0, 2, 3).reshape(micro, dp_size * row_queries, width)
    embeddings = lax.dynamic_index_in_dim(tables, dp, 0, keepdims=False)
    query_scores = jnp.einsum("mqd,mpd->mqp", queries_all, everyone, preferred_element_type=wide)
    score_peak = jnp.max(query_scores, axis=2, keepdims=True)
    log_total = score_peak[..., 0] + jnp.log(jnp.sum(jnp.exp(query_scores - score_peak), axis=2))
    target_hot = (
        jnp.arange(query_scores.shape[2], dtype=jnp.int32)[None, None, :]
        == targets_all[:, :, None]
    ).astype(wide)
    losses = log_total - jnp.sum(query_scores * target_hot, axis=2)
    query_loss = lax.dynamic_slice(losses, (0, dp * row_queries), (micro, row_queries))
    dscore_query = jnp.exp(query_scores - log_total[..., None]) - target_hot
    own_dscore = lax.dynamic_slice(
        dscore_query, (0, dp * row_queries, 0), (micro, row_queries, dp_size * row_queries)
    )
    query_grad = jnp.einsum("mqp,mpd->mqd", own_dscore, everyone.astype(wide), precision=PRECISE)
    own_columns = lax.dynamic_slice(
        dscore_query, (0, 0, dp * row_queries), (micro, dp_size * row_queries, row_queries)
    )
    embed_grad = jnp.einsum(
        "mqs,mqd->msd", own_columns, queries_all.astype(wide), precision=PRECISE
    )
    cls_grad = jnp.einsum("msi,msd->mid", select, embed_grad, precision=PRECISE)
    dout = cotangent.reshape(tokens, width).astype(wide) + cls_grad.reshape(tokens, width)
    gain_two_grad = jnp.sum(dout * second_normed, axis=0)
    shift_two_grad = jnp.sum(dout, axis=0)
    dsecond = norm_back(dout, second_normed, second_factor, gain_two)
    douter = dsecond.astype(narrow)
    outer_bias_grad = jnp.sum(douter.astype(wide), axis=0)
    outer_weight_grad = jnp.einsum(
        "nf,nd->fd", active, douter, preferred_element_type=wide
    ).astype(narrow)
    dactive = jnp.einsum("nd,fd->nf", douter, w_outer, preferred_element_type=wide)
    dinner = (dactive * gelu_slope(inner_pre)).astype(narrow)
    inner_bias_grad = jnp.sum(dinner.astype(wide), axis=0)
    inner_weight_grad = jnp.einsum(
        "nd,nf->df", first_low, dinner, preferred_element_type=wide
    ).astype(narrow)
    dfirst = dsecond + jnp.einsum("nf,df->nd", dinner, w_inner, preferred_element_type=wide)
    gain_one_grad = jnp.sum(dfirst * first_normed, axis=0)
    shift_one_grad = jnp.sum(dfirst, axis=0)
    dresidual = norm_back(dfirst, first_normed, first_factor, gain_one)
    dattended = dresidual.astype(narrow)
    output_bias_grad = jnp.sum(dattended.astype(wide), axis=0)
    datt_rows = dattended.reshape(micro, block_tokens, width)
    output_weight_grad = jnp.einsum(
        "met,mtd->ed", context_t, datt_rows, preferred_element_type=wide
    ).astype(narrow)
    dcontext_t = jnp.einsum(
        "mtd,ed->met", datt_rows, wo_full, preferred_element_type=wide
    ).astype(narrow)
    dcontext = to_heads((dcontext_t,), ring_size, 5).reshape(
        micro, own_heads, head_dim, length
    )
    dparts = attend_back(qkv, seg_col, seg_row, context, stats, dcontext, score_scale)
    dquery_t, dkey_t, dvalue_t = to_tokens(
        tuple(part.reshape(micro, own_heads * head_dim, length) for part in dparts), ring_size, 6
    )
    dhidden = dresidual.reshape(micro, block_tokens, width)
    for part, weight in ((dquery_t, wq_full), (dkey_t, wk_full), (dvalue_t, wv_full)):
        dhidden = dhidden + jnp.einsum("met,de->mtd", part, weight, preferred_element_type=wide)
    weight_grads = tuple(
        jnp.einsum("mtd,met->de", rows_of, part, preferred_element_type=wide).astype(narrow)
        for part in (dquery_t, dkey_t, dvalue_t)
    )
    query_bias_grad = jnp.sum(dquery_t.astype(wide), axis=(0, 2))
    value_bias_grad = jnp.sum(dvalue_t.astype(wide), axis=(0, 2))
    vector_grads = jnp.stack(
        (
            query_bias_grad,
            value_bias_grad,
            output_bias_grad,
            gain_one_grad,
            shift_one_grad,
            outer_bias_grad,
            gain_two_grad,
            shift_two_grad,
        )
    )
    grad_pack = jnp.concatenate(
        (
            vector_grads.reshape(8, dp_size, piece).transpose(1, 0, 2).reshape(dp_size, -1),
            inner_bias_grad.reshape(dp_size, -1),
            jnp.zeros((dp_size, pack_size - vector_size), wide),
        ),
        axis=1,
    )
    grad_pack = grad_pack.astype(narrow).reshape(-1, 128)
    reduced = reduce_all(
        (outer_weight_grad, inner_weight_grad, output_weight_grad) + weight_grads + (grad_pack,),
        (("x", "y"), ("y", "x")) * 3 + (("x", "y"),),
        7,
    )
    d_outer, d_inner, d_wo, d_wq, d_wk, d_wv, d_pack = reduced
    d_pack = d_pack.reshape(-1)
    small = [d_pack[i * piece : (i + 1) * piece] for i in range(8)]
    d_bq, d_bv, d_bo, d_g1, d_s1, d_bu, d_g2, d_s2 = small
    d_bi = d_pack[8 * piece : vector_size]
    shape = (micro, row_count, block_tokens, width)
    return (
        output_low.reshape(shape),
        embeddings,
        query_loss,
        query_grad,
        dhidden.astype(narrow).reshape(shape),
        d_wq,
        d_wk,
        d_wv,
        d_wo,
        d_bq,
        d_bv,
        d_bo,
        d_g1,
        d_s1,
        d_inner,
        d_bi,
        d_outer,
        d_bu,
        d_g2,
        d_s2,
    )


def solution(mesh):
    in_specs = (
        P(None, "dp", "blk", None),
        P(None, "dp", "blk"),
        P(None, "dp", None),
        P(None, "dp"),
        P(None, "dp", "blk", None),
        P("dp", None),
        P("dp", None),
        P("dp", None),
        P("dp", None),
        P("dp"),
        P("dp"),
        P("dp"),
        P("dp"),
        P("dp"),
        P("dp", None),
        P("dp"),
        P("dp", None),
        P("dp"),
        P("dp"),
        P("dp"),
    )
    out_specs = (
        P(None, "dp", "blk", None),
        P(None, "dp", None),
        P(None, "dp"),
        P(None, "dp", None),
        P(None, "dp", "blk", None),
        P("dp", None),
        P("dp", None),
        P("dp", None),
        P("dp", None),
        P("dp"),
        P("dp"),
        P("dp"),
        P("dp"),
        P("dp"),
        P("dp", None),
        P("dp"),
        P("dp", None),
        P("dp"),
        P("dp"),
        P("dp"),
    )
    fast = mesh.shape["dp"] == 8 and mesh.shape["blk"] == 4
    body = fast_body if fast else ring_body
    return jax.shard_map(body, mesh=mesh, in_specs=in_specs, out_specs=out_specs, check_vma=False)
```

```python
import functools
import math

import jax
import jax.numpy as jnp
from jax import lax
from jax.experimental import pallas as pl
from jax.experimental.pallas import tpu as pltpu
from jax.sharding import PartitionSpec as P

HEADS = 12


EPSILON = 1e-12
NEGATIVE = -1000000000.0
PRECISE = lax.Precision.HIGHEST


def passed_along(x, axis, by):
    size = lax.axis_size(axis)
    return lax.ppermute(x, axis, [(i, (i + by) % size) for i in range(size)])


def as_sent(x):
    return jax.tree.map(lambda a: a.astype(jnp.bfloat16) if a.dtype == jnp.float32 else a, x)


def layer_norm(values, norm_gain, norm_shift):
    center = values - jnp.mean(values, axis=-1, keepdims=True)
    factor = lax.rsqrt(jnp.mean(center * center, axis=-1, keepdims=True) + EPSILON)
    normed = center * factor
    return (normed * norm_gain + norm_shift, normed, factor)


def norm_back(gradient, normed, factor, norm_gain):
    scaled = gradient * norm_gain
    inner_term = (
        scaled
        - jnp.mean(scaled, axis=-1, keepdims=True)
        - normed * jnp.mean(scaled * normed, axis=-1, keepdims=True)
    )
    return inner_term * factor


def gelu_slope(values):
    normal_cdf = 0.5 * (1.0 + lax.erf(values * (1.0 / math.sqrt(2.0))))
    return normal_cdf + values * jnp.exp(-0.5 * values * values) * (1.0 / math.sqrt(2.0 * math.pi))


def scores_of(query_rows, key_rows, query_segment, key_segment, score_scale):
    raw_scores = jnp.einsum(
        "rqhd,rkhd->rhqk", query_rows, key_rows, preferred_element_type=jnp.float32
    )
    same_doc = (query_segment[:, :, None] == key_segment[:, None, :])[:, None]
    return jnp.where(same_doc, score_scale * raw_scores, NEGATIVE)


def contribute(
    query_rows,
    push_grad,
    delta_term,
    peak_term,
    query_segment,
    key_rows,
    value_rows,
    key_segment,
    score_scale,
):
    scores = scores_of(query_rows, key_rows, query_segment, key_segment, score_scale)
    weights = jnp.exp(scores - peak_term[..., None])
    pushed = jnp.einsum(
        "rqhd,rkhd->rhqk", push_grad, value_rows, preferred_element_type=jnp.float32
    )
    dscore = (weights * (pushed - delta_term[..., None]) * score_scale).astype(jnp.bfloat16)
    query_part = jnp.einsum("rhqk,rkhd->rqhd", dscore, key_rows, preferred_element_type=jnp.float32)
    key_part = jnp.einsum("rhqk,rqhd->rkhd", dscore, query_rows, preferred_element_type=jnp.float32)
    value_part = jnp.einsum(
        "rhqk,rqhd->rkhd",
        weights.astype(jnp.bfloat16),
        push_grad,
        preferred_element_type=jnp.float32,
    )
    return (query_part, key_part, value_part)


def ring_body(
    hidden_in,
    segment_ids,
    queries,
    targets,
    cotangent,
    query_weight,
    key_weight,
    value_weight,
    output_weight,
    query_bias,
    value_bias,
    output_bias,
    first_gain,
    first_shift,
    inner_weight,
    inner_bias,
    outer_weight,
    outer_bias,
    second_gain,
    second_shift,
):
    shards = (
        query_weight,
        key_weight,
        value_weight,
        output_weight,
        query_bias,
        value_bias,
        output_bias,
        first_gain,
        first_shift,
        inner_weight,
        inner_bias,
        outer_weight,
        outer_bias,
        second_gain,
        second_shift,
    )
    cycle_size = lax.axis_size("blk")
    cycle_place = lax.axis_index("blk")
    micro_count, row_count, block_tokens, model_width = hidden_in.shape
    segment_count = queries.shape[1] // row_count
    head_count = HEADS
    head_dim = model_width // head_count
    score_scale = 1.0 / math.sqrt(head_dim)
    token_count = row_count * block_tokens
    head_shape = (row_count, block_tokens, head_count, head_dim)
    grad_totals = tuple((jnp.zeros(shard_piece.shape, jnp.float32) for shard_piece in shards))
    local_sum = None
    gathered = None
    out_list, embed_list, loss_list, qgrad_list, hgrad_list = ([], [], [], [], [])
    for micro_index in range(micro_count):
        gathered = (
            lax.all_gather(shards[0], "dp", axis=0, tiled=True),
            lax.all_gather(shards[1], "dp", axis=0, tiled=True),
            lax.all_gather(shards[2], "dp", axis=0, tiled=True),
            lax.all_gather(shards[3], "dp", axis=0, tiled=True),
            lax.all_gather(shards[4], "dp", axis=0, tiled=True),
            lax.all_gather(shards[5], "dp", axis=0, tiled=True),
            lax.all_gather(shards[6], "dp", axis=0, tiled=True),
            lax.all_gather(shards[7], "dp", axis=0, tiled=True),
            lax.all_gather(shards[8], "dp", axis=0, tiled=True),
            lax.all_gather(shards[9], "dp", axis=0, tiled=True),
            lax.all_gather(shards[10], "dp", axis=0, tiled=True),
            lax.all_gather(shards[11], "dp", axis=0, tiled=True),
            lax.all_gather(shards[12], "dp", axis=0, tiled=True),
            lax.all_gather(shards[13], "dp", axis=0, tiled=True),
            lax.all_gather(shards[14], "dp", axis=0, tiled=True),
        )
        (
            wq_full,
            wk_full,
            wv_full,
            wo_full,
            bq_full,
            bv_full,
            bo_full,
            gain_one,
            shift_one,
            w_inner,
            b_inner,
            w_outer,
            b_outer,
            gain_two,
            shift_two,
        ) = gathered
        gain_one = gain_one.astype(jnp.float32)
        gain_two = gain_two.astype(jnp.float32)
        segment = segment_ids[micro_index]
        flat_rows = hidden_in[micro_index].reshape(token_count, model_width)
        query_rows = (
            (
                jnp.dot(flat_rows, wq_full, preferred_element_type=jnp.float32)
                + bq_full.astype(jnp.float32)
            )
            .astype(jnp.bfloat16)
            .reshape(head_shape)
        )
        key_rows = (
            jnp.dot(flat_rows, wk_full, preferred_element_type=jnp.float32)
            .astype(jnp.bfloat16)
            .reshape(head_shape)
        )
        value_rows = (
            (
                jnp.dot(flat_rows, wv_full, preferred_element_type=jnp.float32)
                + bv_full.astype(jnp.float32)
            )
            .astype(jnp.bfloat16)
            .reshape(head_shape)
        )

        def absorb(softmax_state, visit_keys, visit_values, visit_segment):
            running_peak, running_total, running_sum = softmax_state
            scores = scores_of(query_rows, visit_keys, segment, visit_segment, score_scale)
            new_peak = jnp.maximum(running_peak, jnp.max(scores, axis=-1))
            decay_factor = jnp.exp(running_peak - new_peak)
            weights = jnp.exp(scores - new_peak[..., None])
            running_total = running_total * decay_factor + jnp.sum(weights, axis=-1)
            update = jnp.einsum(
                "rhqk,rkhd->rqhd",
                weights.astype(jnp.bfloat16),
                visit_values,
                preferred_element_type=jnp.float32,
            )
            running_sum = running_sum * jnp.transpose(decay_factor, (0, 2, 1))[..., None] + update
            return (new_peak, running_total, running_sum)

        start_state = (
            jnp.full((row_count, head_count, block_tokens), -1e30, jnp.float32),
            jnp.zeros((row_count, head_count, block_tokens), jnp.float32),
            jnp.zeros(head_shape, jnp.float32),
        )
        first_state = absorb(start_state, key_rows, value_rows, segment)

        def forward_step(cycle_step, cycle_carry):
            visit_keys, visit_values, visit_segment, prior_segment, softmax_state = cycle_carry
            visit_keys, visit_values, visit_segment = passed_along(
                (visit_keys, visit_values, visit_segment), "blk", 1
            )
            prior_segment = jnp.where(cycle_step == 1, visit_segment[:, -1], prior_segment)
            return (
                visit_keys,
                visit_values,
                visit_segment,
                prior_segment,
                absorb(softmax_state, visit_keys, visit_values, visit_segment),
            )

        cycle_carry = lax.fori_loop(
            1, cycle_size, forward_step, (key_rows, value_rows, segment, segment[:, 0], first_state)
        )
        prior_segment = cycle_carry[3]
        row_peak, row_total, running_sum = cycle_carry[4]
        total_heads = jnp.transpose(row_total, (0, 2, 1))[..., None]
        context = running_sum / total_heads
        context_low = context.reshape(token_count, model_width).astype(jnp.bfloat16)
        attended = jnp.dot(
            context_low, wo_full, preferred_element_type=jnp.float32
        ) + bo_full.astype(jnp.float32)
        first_out, first_normed, first_factor = layer_norm(
            flat_rows.astype(jnp.float32) + attended, gain_one, shift_one.astype(jnp.float32)
        )
        first_low = first_out.astype(jnp.bfloat16)
        inner_pre = jnp.dot(
            first_low, w_inner, preferred_element_type=jnp.float32
        ) + b_inner.astype(jnp.float32)
        active = jax.nn.gelu(inner_pre, approximate=False).astype(jnp.bfloat16)
        outer_out = jnp.dot(active, w_outer, preferred_element_type=jnp.float32) + b_outer.astype(
            jnp.float32
        )
        output, second_normed, second_factor = layer_norm(
            first_out + outer_out, gain_two, shift_two.astype(jnp.float32)
        )
        output_low = output.astype(jnp.bfloat16)
        out_list.append(output_low.reshape(row_count, block_tokens, model_width))
        position = cycle_place * block_tokens + jnp.arange(block_tokens, dtype=jnp.int32)
        before = jnp.concatenate([prior_segment[:, None], segment[:, :-1]], axis=1)
        leading = (position[None, :] == 0) | (segment != before)
        numbers = jnp.arange(segment_count, dtype=jnp.int32)
        select = (leading[:, None, :] & (segment[:, None, :] == numbers[None, :, None])).astype(
            jnp.float32
        )
        cls_table = jnp.einsum(
            "rsi,rid->rsd",
            select.astype(jnp.bfloat16),
            output_low.reshape(row_count, block_tokens, model_width),
            preferred_element_type=jnp.float32,
        )
        own_table = lax.psum(cls_table.astype(jnp.bfloat16), "blk").reshape(
            row_count * segment_count, model_width
        )
        embed_list.append(own_table)
        everyone = lax.all_gather(own_table, "dp", axis=0, tiled=True)
        query_vectors = queries[micro_index]
        query_scores = jnp.dot(query_vectors, everyone.T, preferred_element_type=jnp.float32)
        score_peak = jnp.max(query_scores, axis=1, keepdims=True)
        log_total = score_peak[:, 0] + jnp.log(jnp.sum(jnp.exp(query_scores - score_peak), axis=1))
        target_hot = (
            jnp.arange(query_scores.shape[1], dtype=jnp.int32)[None, :]
            == targets[micro_index][:, None]
        ).astype(jnp.float32)
        loss_list.append(log_total - jnp.sum(query_scores * target_hot, axis=1))
        dscore_query = jnp.exp(query_scores - log_total[:, None]) - target_hot
        qgrad_list.append(jnp.dot(dscore_query, everyone.astype(jnp.float32), precision=PRECISE))
        embed_part = jnp.dot(dscore_query.T, query_vectors.astype(jnp.float32), precision=PRECISE)
        embed_grad = (
            lax.psum_scatter(embed_part.astype(jnp.bfloat16), "dp", scatter_dimension=0, tiled=True)
            .astype(jnp.float32)
            .reshape(row_count, segment_count, model_width)
        )
        cls_grad = jnp.einsum("rsi,rsd->rid", select, embed_grad, precision=PRECISE)
        dout = cotangent[micro_index].reshape(token_count, model_width).astype(
            jnp.float32
        ) + cls_grad.reshape(token_count, model_width)
        gain_two_grad = jnp.sum(dout * second_normed, axis=0)
        shift_two_grad = jnp.sum(dout, axis=0)
        dsecond = norm_back(dout, second_normed, second_factor, gain_two)
        douter = dsecond.astype(jnp.bfloat16)
        outer_bias_grad = jnp.sum(douter.astype(jnp.float32), axis=0)
        outer_weight_grad = jnp.einsum(
            "nf,nd->fd", active, douter, preferred_element_type=jnp.float32
        )
        dactive = jnp.einsum("nd,fd->nf", douter, w_outer, preferred_element_type=jnp.float32)
        dinner = (dactive * gelu_slope(inner_pre)).astype(jnp.bfloat16)
        inner_bias_grad = jnp.sum(dinner.astype(jnp.float32), axis=0)
        inner_weight_grad = jnp.einsum(
            "nd,nf->df", first_low, dinner, preferred_element_type=jnp.float32
        )
        dfirst = dsecond + jnp.einsum(
            "nf,df->nd", dinner, w_inner, preferred_element_type=jnp.float32
        )
        gain_one_grad = jnp.sum(dfirst * first_normed, axis=0)
        shift_one_grad = jnp.sum(dfirst, axis=0)
        dresidual = norm_back(dfirst, first_normed, first_factor, gain_one)
        dattended = dresidual.astype(jnp.bfloat16)
        output_bias_grad = jnp.sum(dattended.astype(jnp.float32), axis=0)
        output_weight_grad = jnp.einsum(
            "nd,ne->de", context_low, dattended, preferred_element_type=jnp.float32
        )
        dcontext = jnp.einsum(
            "ne,de->nd", dattended, wo_full, preferred_element_type=jnp.float32
        ).astype(jnp.bfloat16)
        dcontext_wide = dcontext.astype(jnp.float32).reshape(head_shape)
        push_grad = (dcontext_wide / total_heads).astype(jnp.bfloat16)
        delta_term = jnp.transpose(
            jnp.sum(dcontext_wide * context, axis=-1) / total_heads[..., 0], (0, 2, 1)
        )
        own_query, own_key, own_value = contribute(
            query_rows,
            push_grad,
            delta_term,
            row_peak,
            segment,
            key_rows,
            value_rows,
            segment,
            score_scale,
        )

        def key_step(cycle_step, cycle_carry):
            visit_keys, visit_values, visit_segment, query_sum, key_sum, value_sum = cycle_carry
            visit_keys, visit_values, visit_segment = passed_along(
                (visit_keys, visit_values, visit_segment), "blk", 1
            )
            key_sum, value_sum = (
                passed_along(key_sum.astype(jnp.bfloat16), "blk", 1).astype(key_sum.dtype),
                passed_along(value_sum.astype(jnp.bfloat16), "blk", 1).astype(value_sum.dtype),
            )
            query_part, key_part, value_part = contribute(
                query_rows,
                push_grad,
                delta_term,
                row_peak,
                segment,
                visit_keys,
                visit_values,
                visit_segment,
                score_scale,
            )
            return (
                visit_keys,
                visit_values,
                visit_segment,
                query_sum + query_part,
                key_sum + key_part,
                value_sum + value_part,
            )

        back_carry = lax.fori_loop(
            1, cycle_size, key_step, (key_rows, value_rows, segment, own_query, own_key, own_value)
        )
        query_sum = back_carry[3]
        key_sum, value_sum = (
            passed_along(back_carry[4].astype(jnp.bfloat16), "blk", 1).astype(jnp.float32),
            passed_along(back_carry[5].astype(jnp.bfloat16), "blk", 1).astype(jnp.float32),
        )
        dquery = query_sum.astype(jnp.bfloat16).reshape(token_count, model_width)
        dkey = key_sum.astype(jnp.bfloat16).reshape(token_count, model_width)
        dvalue = value_sum.astype(jnp.bfloat16).reshape(token_count, model_width)
        dhidden = dresidual + jnp.einsum(
            "ne,de->nd", dquery, wq_full, preferred_element_type=jnp.float32
        )
        dhidden = dhidden + jnp.einsum(
            "ne,de->nd", dkey, wk_full, preferred_element_type=jnp.float32
        )
        dhidden = dhidden + jnp.einsum(
            "ne,de->nd", dvalue, wv_full, preferred_element_type=jnp.float32
        )
        hgrad_list.append(
            dhidden.astype(jnp.bfloat16).reshape(row_count, block_tokens, model_width)
        )
        local_grads = (
            jnp.einsum("nd,ne->de", flat_rows, dquery, preferred_element_type=jnp.float32),
            jnp.einsum("nd,ne->de", flat_rows, dkey, preferred_element_type=jnp.float32),
            jnp.einsum("nd,ne->de", flat_rows, dvalue, preferred_element_type=jnp.float32),
            output_weight_grad,
            jnp.sum(dquery.astype(jnp.float32), axis=0),
            jnp.sum(dvalue.astype(jnp.float32), axis=0),
            output_bias_grad,
            gain_one_grad,
            shift_one_grad,
            inner_weight_grad,
            inner_bias_grad,
            outer_weight_grad,
            outer_bias_grad,
            gain_two_grad,
            shift_two_grad,
        )
        local_sum = local_grads
        reduced = jax.tree.map(
            lambda part: part.astype(jnp.float32),
            lax.psum_scatter(as_sent(local_sum), "dp", scatter_dimension=0, tiled=True),
        )
        reduced = jax.tree.map(
            lambda part: part.astype(jnp.float32), lax.psum(as_sent(reduced), "blk")
        )
        grad_totals = tuple(
            (total_piece + new_piece for total_piece, new_piece in zip(grad_totals, reduced))
        )
        local_sum = None
    return (
        jnp.stack(out_list),
        jnp.stack(embed_list),
        jnp.stack(loss_list),
        jnp.stack(qgrad_list),
        jnp.stack(hgrad_list),
        grad_totals[0],
        grad_totals[1],
        grad_totals[2],
        grad_totals[3],
        grad_totals[4],
        grad_totals[5],
        grad_totals[6],
        grad_totals[7],
        grad_totals[8],
        grad_totals[9],
        grad_totals[10],
        grad_totals[11],
        grad_totals[12],
        grad_totals[13],
        grad_totals[14],
    )


MESH = pl.DeviceIdType.MESH
VMEM_LIMIT = 60 * 1024 * 1024
SIDE = {"c": 1, "x": 2, "y": 4}


def place():
    dp, blk = lax.axis_index("dp"), lax.axis_index("blk")
    bits = {"c": lax.rem(dp, 2), "x": lax.rem(dp // 2, 2), "y": dp // 4}
    return dp, blk, bits


def across(dp, blk, bits, *axes):
    other = dp
    for axis in axes:
        other = other + SIDE[axis] * (1 - 2 * bits[axis])
    return (other, blk)


def greet(peers):
    barrier = pltpu.get_barrier_semaphore()
    for peer in peers:
        pl.semaphore_signal(barrier, inc=1, device_id=peer, device_id_type=MESH)
    pl.semaphore_wait(barrier, len(peers))


def remote(source, target, send_sem, recv_sem, peer):
    return pltpu.make_async_remote_copy(
        src_ref=source,
        dst_ref=target,
        send_sem=send_sem,
        recv_sem=recv_sem,
        device_id=peer,
        device_id_type=MESH,
    )


def comm_params(collective):
    return pltpu.CompilerParams(
        collective_id=collective, has_side_effects=True, vmem_limit_bytes=VMEM_LIMIT
    )


ANY = pl.BlockSpec(memory_space=pl.ANY)
IN_VMEM = pl.BlockSpec(memory_space=pltpu.VMEM)


def window_start(blk, group, window):
    return pl.multiple_of((blk * group) // 128 * 128, 128)


def gather_kernel(items, ring_size, *refs):
    count = 1 + max(item["source"] for item in items)
    places = 1 + max(item["target"] for item in items)
    shards, seg_shard, hidden = refs[:count], refs[count], refs[count + 1]
    fulls = refs[count + 2 : count + 2 + places]
    seg_full, hidden_full = refs[count + 2 + places : count + 4 + places]
    (
        send_sem,
        recv_sem,
        seg_send,
        seg_recv,
        line_send,
        line_recv,
        local_sem,
        line_local,
    ) = refs[count + 4 + places :]
    dp, blk, bits = place()
    sibling = across(dp, blk, bits, "c")
    ring = [(dp, lax.rem(blk + step, ring_size)) for step in range(1, ring_size)]
    greet([sibling, across(dp, blk, bits, "x"), across(dp, blk, bits, "y")] + ring)
    seg_rows = seg_shard.shape[0]
    micro, tokens, _ = hidden.shape
    waiting = []
    sending = []

    def line_copy(m, side, distance):
        away = 1 - 2 * side
        owner = blk + away * distance
        view = hidden_full.at[m, pl.ds(pl.multiple_of(owner * tokens, tokens), tokens)]
        return remote(
            hidden.at[m] if distance == 0 else view,
            view,
            line_send.at[m, side, distance],
            line_recv.at[m, side, distance + 1],
            (dp, blk - away),
        )

    def arrival(m, side, distance):
        away = 1 - 2 * side
        owner = blk + away * distance
        view = hidden_full.at[m, pl.ds(pl.multiple_of(owner * tokens, tokens), tokens)]
        return remote(
            view,
            view,
            line_send.at[m, side, distance],
            line_recv.at[m, side, distance],
            (dp, blk - away),
        )

    def can_send(side):
        return blk > 0 if side == 0 else blk < ring_size - 1

    def exists(side, distance):
        return blk + distance < ring_size if side == 0 else blk >= distance

    for m in range(micro):
        for side in range(2):

            @pl.when(can_send(side))
            def _():
                line_copy(m, side, 0).start()

    for step, peer in enumerate(ring):
        copy = remote(
            seg_shard,
            seg_full.at[pl.ds(blk * seg_rows, seg_rows)],
            seg_send.at[step],
            seg_recv.at[step],
            peer,
        )
        copy.start()
        waiting.append(copy)
    copy = pltpu.make_async_copy(
        seg_shard, seg_full.at[pl.ds(blk * seg_rows, seg_rows)], local_sem.at[len(items)]
    )
    copy.start()
    waiting.append(copy)
    for m in range(micro):
        copy = pltpu.make_async_copy(
            hidden.at[m],
            hidden_full.at[m, pl.ds(pl.multiple_of(blk * tokens, tokens), tokens)],
            line_local.at[m],
        )
        copy.start()
        waiting.append(copy)

    def own_part(item):
        spec = items[item]
        column = spec["from_column"]
        if column is None:
            column = window_start(blk, spec["group"], spec["columns"])
        return shards[spec["source"]].at[
            pl.ds(spec["row"], spec["rows"]), pl.ds(column, spec["columns"])
        ]

    def block(item, owner):
        spec = items[item]
        first = owner * spec["stride"] + spec["row"]
        return fulls[spec["target"]].at[
            pl.ds(first, spec["rows"]), pl.ds(spec["to_column"], spec["columns"])
        ]

    inbound = {}
    for item, spec in enumerate(items):
        first, second = spec["route"]
        for slot, peer in enumerate(
            (across(dp, blk, bits, first), across(dp, blk, bits, second), sibling)
        ):
            copy = remote(
                own_part(item),
                block(item, dp),
                send_sem.at[item, slot],
                recv_sem.at[item, slot],
                peer,
            )
            copy.start()
            inbound[item, slot] = copy
        copy = pltpu.make_async_copy(own_part(item), block(item, dp), local_sem.at[item])
        copy.start()
        waiting.append(copy)

    def line_step(m, distance):
        for side in range(2):

            @pl.when(exists(side, distance))
            def _():
                arrival(m, side, distance).wait_recv()

            if distance < ring_size - 1:

                @pl.when(exists(side, distance) & can_send(side))
                def _():
                    line_copy(m, side, distance).start()

    def relay_first(item):
        first, second = items[item]["route"]
        inbound[item, 0].wait_recv()
        held = block(item, across(dp, blk, bits, first)[0])
        for slot, peer in ((3, across(dp, blk, bits, second)), (4, sibling)):
            copy = remote(held, held, send_sem.at[item, slot], recv_sem.at[item, slot], peer)
            copy.start()
            inbound[item, slot] = copy

    def relay_second(item):
        first, second = items[item]["route"]
        inbound[item, 1].wait_recv()
        held = block(item, across(dp, blk, bits, second)[0])
        copy = remote(held, held, send_sem.at[item, 5], recv_sem.at[item, 5], sibling)
        copy.start()
        inbound[item, 5] = copy

    def relay_third(item):
        first, second = items[item]["route"]
        inbound[item, 3].wait_recv()
        held = block(item, across(dp, blk, bits, first, second)[0])
        copy = remote(held, held, send_sem.at[item, 6], recv_sem.at[item, 6], sibling)
        copy.start()
        inbound[item, 6] = copy

    steps = [(m, distance) for m in range(micro) for distance in range(1, ring_size)]
    total = len(items) + 3
    done = 0
    for tick in range(total):
        if tick < len(items):
            relay_first(tick)
            relay_second(tick)
        if 0 <= tick - 3 < len(items):
            relay_third(tick - 3)
        while done < len(steps) and done * total < len(steps) * (tick + 1):
            line_step(*steps[done])
            done += 1
    for item in range(len(items)):
        for slot in (2, 4, 5, 6):
            inbound[item, slot].wait_recv()
        for slot in range(7):
            inbound[item, slot].wait_send()
    for m in range(micro):
        for side in range(2):
            for distance in range(ring_size - 1):

                @pl.when(exists(side, distance) & can_send(side))
                def _():
                    line_copy(m, side, distance).wait_send()

    for copy in waiting:
        copy.wait()


def gather_all(shards, items, targets, segments, hidden, ring_size):
    micro, tokens, width = hidden.shape
    count = len(shards)
    return pl.pallas_call(
        functools.partial(gather_kernel, items, ring_size),
        out_shape=tuple(targets)
        + (
            jax.ShapeDtypeStruct((ring_size * segments.shape[0], segments.shape[1]), jnp.int32),
            jax.ShapeDtypeStruct((micro, ring_size * tokens, width), hidden.dtype),
        ),
        in_specs=[ANY] * (count + 2),
        out_specs=(ANY,) * (len(targets) + 2),
        scratch_shapes=[
            pltpu.SemaphoreType.DMA((len(items), 7)),
            pltpu.SemaphoreType.DMA((len(items), 7)),
            pltpu.SemaphoreType.DMA((ring_size,)),
            pltpu.SemaphoreType.DMA((ring_size,)),
            pltpu.SemaphoreType.DMA((micro, 2, ring_size)),
            pltpu.SemaphoreType.DMA((micro, 2, ring_size)),
            pltpu.SemaphoreType.DMA((len(items) + 1,)),
            pltpu.SemaphoreType.DMA((micro,)),
        ],
        compiler_params=comm_params(1),
    )(*shards, segments, hidden)


def to_heads_kernel(ring_size, *refs):
    count = (len(refs) - 4) // 1
    parts, (out, send_sem, recv_sem, local_sem) = refs[:count], refs[count:]
    dp, blk, _ = place()
    greet([(dp, lax.rem(blk + step, ring_size)) for step in range(1, ring_size)])
    micro, rows, tokens = parts[0].shape
    group = rows // ring_size
    copies = []
    for m in range(micro):
        for index, part in enumerate(parts):
            for step in range(ring_size):
                owner = lax.rem(blk + step, ring_size)
                source = part.at[m, pl.ds(owner * group, group)]
                target = out.at[m, index, :, pl.ds(pl.multiple_of(blk * tokens, tokens), tokens)]
                if step == 0:
                    copy = pltpu.make_async_copy(source, target, local_sem.at[m, index])
                else:
                    copy = remote(
                        source,
                        target,
                        send_sem.at[m, index, step],
                        recv_sem.at[m, index, step],
                        (dp, owner),
                    )
                copy.start()
                copies.append(copy)
    for copy in copies:
        copy.wait()


def to_heads(parts, ring_size, collective):
    micro, rows, tokens = parts[0].shape
    count = len(parts)
    return pl.pallas_call(
        functools.partial(to_heads_kernel, ring_size),
        out_shape=jax.ShapeDtypeStruct(
            (micro, count, rows // ring_size, tokens * ring_size), parts[0].dtype
        ),
        in_specs=[ANY] * count,
        out_specs=ANY,
        scratch_shapes=[
            pltpu.SemaphoreType.DMA((micro, count, ring_size)),
            pltpu.SemaphoreType.DMA((micro, count, ring_size)),
            pltpu.SemaphoreType.DMA((micro, count)),
        ],
        compiler_params=comm_params(collective),
    )(*parts)


def to_tokens_kernel(ring_size, *refs):
    count = (len(refs) - 3) // 2
    parts, outs = refs[:count], refs[count : 2 * count]
    send_sem, recv_sem, local_sem = refs[2 * count :]
    dp, blk, _ = place()
    greet([(dp, lax.rem(blk + step, ring_size)) for step in range(1, ring_size)])
    micro, group, length = parts[0].shape
    tokens = length // ring_size
    copies = []
    for m in range(micro):
        for index, (part, out) in enumerate(zip(parts, outs)):
            for step in range(ring_size):
                owner = lax.rem(blk + step, ring_size)
                source = part.at[m, :, pl.ds(pl.multiple_of(owner * tokens, tokens), tokens)]
                target = out.at[m, pl.ds(blk * group, group)]
                if step == 0:
                    copy = pltpu.make_async_copy(source, target, local_sem.at[m, index])
                else:
                    copy = remote(
                        source,
                        target,
                        send_sem.at[m, index, step],
                        recv_sem.at[m, index, step],
                        (dp, owner),
                    )
                copy.start()
                copies.append(copy)
    for copy in copies:
        copy.wait()


def to_tokens(parts, ring_size, collective):
    micro, group, length = parts[0].shape
    count = len(parts)
    out = pl.pallas_call(
        functools.partial(to_tokens_kernel, ring_size),
        out_shape=tuple(
            jax.ShapeDtypeStruct((micro, group * ring_size, length // ring_size), p.dtype)
            for p in parts
        ),
        in_specs=[ANY] * count,
        out_specs=(ANY,) * count,
        scratch_shapes=[
            pltpu.SemaphoreType.DMA((micro, count, ring_size)),
            pltpu.SemaphoreType.DMA((micro, count, ring_size)),
            pltpu.SemaphoreType.DMA((micro, count)),
        ],
        compiler_params=comm_params(collective),
    )(*parts)
    return out


def tables_kernel(ring_size, dp_size, own, out, arrived, send_sem, recv_sem, ring_send, ring_recv):
    dp, blk, _ = place()
    ring = [(dp, lax.rem(blk + step, ring_size)) for step in range(1, ring_size)]
    group = [(lax.rem(dp + step, dp_size), blk) for step in range(1, dp_size)]
    greet(ring + group)
    copies = []
    for step, peer in enumerate(ring):
        copy = remote(own, arrived.at[step], ring_send.at[step], ring_recv.at[step], peer)
        copy.start()
        copies.append(copy)
    for copy in copies:
        copy.wait()
    total = own[...].astype(jnp.float32)
    for step in range(ring_size - 1):
        total = total + arrived[step].astype(jnp.float32)
    out[dp] = total.astype(out.dtype)
    copies = []
    for step, peer in enumerate(group):
        copy = remote(out.at[dp], out.at[dp], send_sem.at[step], recv_sem.at[step], peer)
        copy.start()
        copies.append(copy)
    for copy in copies:
        copy.wait()


def gather_tables(own, ring_size, dp_size):
    return pl.pallas_call(
        functools.partial(tables_kernel, ring_size, dp_size),
        out_shape=jax.ShapeDtypeStruct((dp_size,) + own.shape, own.dtype),
        in_specs=[IN_VMEM],
        out_specs=IN_VMEM,
        scratch_shapes=[
            pltpu.VMEM((ring_size - 1,) + own.shape, own.dtype),
            pltpu.SemaphoreType.DMA((dp_size,)),
            pltpu.SemaphoreType.DMA((dp_size,)),
            pltpu.SemaphoreType.DMA((ring_size,)),
            pltpu.SemaphoreType.DMA((ring_size,)),
        ],
        compiler_params=comm_params(4),
    )(own)


def added(left, right):
    return (left.astype(jnp.float32) + right.astype(jnp.float32)).astype(jnp.bfloat16)


def reduce_kernel(items, ring_size, *refs):
    count = len(items)
    inputs = 1 + max(item["source"] for item in items)
    grads, outs = refs[:inputs], refs[inputs : 2 * inputs]
    own, from_core, from_first, from_second, ring_one, ring_two, ring_three = refs[
        2 * inputs : 2 * inputs + 7
    ]
    send_sem, recv_sem, local_sem = refs[2 * inputs + 7 :]
    dp, blk, bits = place()
    sibling = across(dp, blk, bits, "c")
    is_end = (blk == 0) | (blk == 3)
    is_middle = (blk == 1) | (blk == 2)
    partner = (dp, blk + 1 - 2 * lax.rem(blk, 2))
    facing = (dp, 3 - blk)
    ring = [(dp, lax.rem(blk + step, ring_size)) for step in range(1, ring_size)]
    greet([sibling, across(dp, blk, bits, "x"), across(dp, blk, bits, "y")] + ring)

    def owner(core, axes, first_bit, second_bit):
        return core + SIDE[axes[0]] * first_bit + SIDE[axes[1]] * second_bit

    def block(item, which):
        spec = items[item]
        return grads[spec["source"]].at[
            pl.ds(which * spec["stride"] + spec["row"], spec["rows"]),
            pl.ds(spec["column"], spec["columns"]),
        ]

    def cut(buffer, item, *index):
        spec = items[item]
        return buffer.at[(item,) + index + (pl.ds(0, spec["rows"]), pl.ds(0, spec["columns"]))]

    def result(item):
        spec = items[item]
        return outs[spec["source"]].at[
            pl.ds(spec["row"], spec["rows"]), pl.ds(spec["column"], spec["columns"])
        ]

    def copier(source, target, item, slot, peer):
        return remote(source, target, send_sem.at[item, slot], recv_sem.at[item, slot], peer)

    def go(source, target, item, slot, peer):
        copy = copier(source, target, item, slot, peer)
        copy.start()
        return copy

    flying = {}

    def start_core(item):
        axes = items[item]["route"]
        for f in range(2):
            for s in range(2):
                slot = 2 * f + s
                flying[item, slot] = go(
                    block(item, owner(1 - bits["c"], axes, f, s)),
                    cut(from_core, item, f, s),
                    item,
                    slot,
                    sibling,
                )
                mine = pltpu.make_async_copy(
                    block(item, owner(bits["c"], axes, f, s)),
                    cut(own, item, f, s),
                    local_sem.at[item, slot],
                )
                mine.start()
                flying[item, "own", slot] = mine

    def after_core(item):
        axes = items[item]["route"]
        mine = bits[axes[0]]
        for slot in range(4):
            flying[item, slot].wait_recv()
            flying[item, "own", slot].wait()
        for f in (1 - mine, mine):
            for s in range(2):
                part = cut(own, item, f, s)
                part[...] = added(part[...], cut(from_core, item, f, s)[...])
                if f is not mine:
                    flying[item, 4 + s] = go(
                        part,
                        cut(from_first, item, s),
                        item,
                        4 + s,
                        across(dp, blk, bits, axes[0]),
                    )

    def after_first(item):
        axes = items[item]["route"]
        f, mine = bits[axes[0]], bits[axes[1]]
        for s in range(2):
            flying[item, 4 + s].wait_recv()
        part = cut(own, item, f, 1 - mine)
        part[...] = added(part[...], cut(from_first, item, 1 - mine)[...])
        flying[item, 6] = go(
            part, cut(from_second, item), item, 6, across(dp, blk, bits, axes[1])
        )
        part = cut(own, item, f, mine)
        part[...] = added(part[...], cut(from_first, item, mine)[...])

    def after_second(item):
        axes = items[item]["route"]
        f, s = bits[axes[0]], bits[axes[1]]
        flying[item, 6].wait_recv()
        total = added(cut(own, item, f, s)[...], cut(from_second, item)[...])
        if items[item]["gathered"]:
            out = outs[items[item]["source"]]
            out[blk] = total
            for step, peer in enumerate(ring):
                flying[item, 7 + step] = go(out.at[blk], out.at[blk], item, 7 + step, peer)
            return
        cut(ring_one, item, 0)[...] = total
        flying[item, 7] = copier(
            cut(ring_one, item, 0), cut(ring_one, item, 1), item, 7, partner
        )
        flying[item, 8] = copier(cut(ring_two, item, 0), cut(ring_two, item, 1), item, 8, facing)
        flying[item, 9] = copier(result(item), result(item), item, 9, partner)

        @pl.when(is_end)
        def _():
            flying[item, 7].start()

    def at_middle(item):
        if items[item]["gathered"]:
            return

        @pl.when(is_middle)
        def _():
            flying[item, 7].wait_recv()
            part = cut(ring_two, item, 0)
            part[...] = added(cut(ring_one, item, 0)[...], cut(ring_one, item, 1)[...])
            flying[item, 8].start()

    def across_middle(item):
        if items[item]["gathered"]:
            return

        @pl.when(is_middle)
        def _():
            flying[item, 8].wait_recv()
            result(item)[...] = added(cut(ring_two, item, 0)[...], cut(ring_two, item, 1)[...])
            flying[item, 9].start()

    def at_end(item):
        if items[item]["gathered"]:
            for step in range(ring_size - 1):
                flying[item, 7 + step].wait_recv()
            return

        @pl.when(is_end)
        def _():
            flying[item, 9].wait_recv()

    stages = (after_core, after_first, after_second, at_middle, across_middle, at_end)
    for item in range(count):
        start_core(item)
    for tick in range(count + len(stages) - 1):
        for depth in reversed(range(len(stages))):
            item = tick - depth
            if 0 <= item < count:
                stages[depth](item)
    for item in range(count):
        for slot in range(7):
            flying[item, slot].wait_send()
        if items[item]["gathered"]:
            for step in range(ring_size - 1):
                flying[item, 7 + step].wait_send()

    @pl.when(is_end)
    def _():
        for item in range(count):
            if not items[item]["gathered"]:
                flying[item, 7].wait_send()

    @pl.when(is_middle)
    def _():
        for item in range(count):
            if not items[item]["gathered"]:
                flying[item, 8].wait_send()
                flying[item, 9].wait_send()


def reduce_all(grads, items, dp_size, ring_size, collective):
    count = len(items)
    inputs = len(grads)
    rows = max(item["rows"] for item in items)
    columns = max(item["columns"] for item in items)
    piece = (rows, columns)
    outs = []
    for index, grad in enumerate(grads):
        shard = (grad.shape[0] // dp_size, grad.shape[1])
        if any(item["gathered"] for item in items if item["source"] == index):
            shard = (ring_size,) + shard
        outs.append(jax.ShapeDtypeStruct(shard, jnp.bfloat16))
    scratch = [
        pltpu.VMEM((count,) + lead + piece, jnp.bfloat16)
        for lead in ((2, 2), (2, 2), (2,), (), (2,), (2,), (2,))
    ]
    return pl.pallas_call(
        functools.partial(reduce_kernel, items, ring_size),
        out_shape=tuple(outs),
        in_specs=[ANY] * inputs,
        out_specs=(IN_VMEM,) * inputs,
        scratch_shapes=scratch
        + [
            pltpu.SemaphoreType.DMA((count, 10)),
            pltpu.SemaphoreType.DMA((count, 10)),
            pltpu.SemaphoreType.DMA((count, 4)),
        ],
        compiler_params=comm_params(collective),
    )(*grads)


def scatter_line_kernel(ring_size, parts, out, passed, arrived, send_sem, recv_sem):
    dp, blk, _ = place()
    greet_line(dp, blk, ring_size)
    micro, _, tokens, _ = parts.shape

    def can_receive(side):
        return blk < ring_size - 1 if side == 0 else blk > 0

    def has_target(side, distance):
        return blk >= distance if side == 0 else blk + distance < ring_size

    def hop(source, m, side, distance):
        return remote(
            source,
            arrived.at[m, side, distance - 1],
            send_sem.at[m, side, distance],
            recv_sem.at[m, side, distance - 1],
            (dp, blk - 1 + 2 * side),
        )

    def arrival(m, side, distance):
        view = arrived.at[m, side, distance]
        return remote(
            view,
            view,
            send_sem.at[m, side, distance],
            recv_sem.at[m, side, distance],
            (dp, blk - 1 + 2 * side),
        )

    for distance in reversed(range(1, ring_size)):
        for m in range(micro):
            for side in range(2):
                target = blk - distance * (1 - 2 * side)
                if distance < ring_size - 1:

                    @pl.when(has_target(side, distance) & can_receive(side))
                    def _():
                        arrival(m, side, distance).wait_recv()
                        passed[m, side, distance] = added(
                            parts[m, target], arrived[m, side, distance]
                        )
                        hop(passed.at[m, side, distance], m, side, distance).start()

                @pl.when(has_target(side, distance) & jnp.logical_not(can_receive(side)))
                def _():
                    hop(parts.at[m, target], m, side, distance).start()

    for m in range(micro):
        out[m] = parts[m, blk].astype(jnp.float32)
        for side in range(2):

            @pl.when(can_receive(side))
            def _():
                arrival(m, side, 0).wait_recv()
                out[m] += arrived[m, side, 0].astype(jnp.float32)

    for distance in range(1, ring_size):
        for m in range(micro):
            for side in range(2):

                @pl.when(has_target(side, distance))
                def _():
                    hop(passed.at[m, side, distance], m, side, distance).wait_send()


def greet_line(dp, blk, ring_size):
    barrier = pltpu.get_barrier_semaphore()

    @pl.when(blk > 0)
    def _():
        pl.semaphore_signal(barrier, inc=1, device_id=(dp, blk - 1), device_id_type=MESH)

    @pl.when(blk < ring_size - 1)
    def _():
        pl.semaphore_signal(barrier, inc=1, device_id=(dp, blk + 1), device_id_type=MESH)

    @pl.when((blk > 0) & (blk < ring_size - 1))
    def _():
        pl.semaphore_wait(barrier, 2)

    @pl.when((blk == 0) | (blk == ring_size - 1))
    def _():
        pl.semaphore_wait(barrier, 1)


def scatter_line(parts, ring_size, collective):
    micro, _, tokens, width = parts.shape
    return pl.pallas_call(
        functools.partial(scatter_line_kernel, ring_size),
        out_shape=jax.ShapeDtypeStruct((micro, tokens, width), jnp.float32),
        in_specs=[IN_VMEM],
        out_specs=IN_VMEM,
        scratch_shapes=[
            pltpu.VMEM((micro, 2, ring_size, tokens, width), jnp.bfloat16),
            pltpu.VMEM((micro, 2, ring_size, tokens, width), jnp.bfloat16),
            pltpu.SemaphoreType.DMA((micro, 2, ring_size)),
            pltpu.SemaphoreType.DMA((micro, 2, ring_size)),
        ],
        compiler_params=comm_params(collective),
    )(parts)


def contract(left, right, left_dim, right_dim):
    return lax.dot_general(
        left, right, (((left_dim,), (right_dim,)), ((), ())), preferred_element_type=jnp.float32
    )


def attend_kernel(score_scale, block, qkv, seg_col, seg_row, context, low, stats):
    queries_t, keys_t, values_t = qkv[0, 0, 0], qkv[0, 1, 0], qkv[0, 2, 0]
    length = keys_t.shape[1]
    keys = keys_t.T
    for start in range(0, length, block):
        span = slice(start, start + block)
        raw = contract(keys, queries_t[:, span], 1, 0)
        same = seg_col[0] == seg_row[0, :, span]
        scores = jnp.where(same, raw * score_scale, NEGATIVE)
        peak = jnp.max(scores, axis=0, keepdims=True)
        weights = jnp.exp(scores - peak)
        total = jnp.sum(weights, axis=0, keepdims=True)
        gathered = contract(values_t, weights.astype(jnp.bfloat16), 1, 0)
        ctx = gathered / total
        context[0, 0, :, span] = ctx
        low[0, 0, :, span] = ctx.astype(jnp.bfloat16)
        stats[0, 0, 0:1, span] = peak
        stats[0, 0, 1:2, span] = total


def attend(qkv, seg_col, seg_row, score_scale):
    micro, _, heads, depth, length = qkv.shape
    block = min(256, length)
    return pl.pallas_call(
        functools.partial(attend_kernel, score_scale, block),
        grid=(micro, heads),
        out_shape=(
            jax.ShapeDtypeStruct((micro, heads, depth, length), jnp.float32),
            jax.ShapeDtypeStruct((micro, heads, depth, length), jnp.bfloat16),
            jax.ShapeDtypeStruct((micro, heads, 2, length), jnp.float32),
        ),
        in_specs=[
            pl.BlockSpec((1, 3, 1, depth, length), lambda m, h: (m, 0, h, 0, 0)),
            pl.BlockSpec((1, length, 1), lambda m, h: (m, 0, 0)),
            pl.BlockSpec((1, 1, length), lambda m, h: (m, 0, 0)),
        ],
        out_specs=(
            pl.BlockSpec((1, 1, depth, length), lambda m, h: (m, h, 0, 0)),
            pl.BlockSpec((1, 1, depth, length), lambda m, h: (m, h, 0, 0)),
            pl.BlockSpec((1, 1, 2, length), lambda m, h: (m, h, 0, 0)),
        ),
        compiler_params=pltpu.CompilerParams(vmem_limit_bytes=VMEM_LIMIT),
    )(qkv, seg_col, seg_row)


def attend_back_kernel(
    score_scale, block, qkv, seg_col, seg_row, context, stats, dcontext, dqueries, dkeys, dvalues
):
    queries_t, keys_t, values_t = qkv[0, 0, 0], qkv[0, 1, 0], qkv[0, 2, 0]
    depth, length = keys_t.shape
    keys, values = keys_t.T, values_t.T
    dkey_sum = jnp.zeros((depth, length), jnp.float32)
    dvalue_sum = jnp.zeros((depth, length), jnp.float32)
    for start in range(0, length, block):
        span = slice(start, start + block)
        peak, total = stats[0, 0, 0:1, span], stats[0, 0, 1:2, span]
        dctx = dcontext[0, 0, :, span].astype(jnp.float32)
        push = (dctx / total).astype(jnp.bfloat16)
        delta = jnp.sum(dctx * context[0, 0, :, span], axis=0, keepdims=True) / total
        raw = contract(keys, queries_t[:, span], 1, 0)
        same = seg_col[0] == seg_row[0, :, span]
        weights = jnp.exp(jnp.where(same, raw * score_scale, NEGATIVE) - peak)
        pushed = contract(values, push, 1, 0)
        dscore = (weights * (pushed - delta) * score_scale).astype(jnp.bfloat16)
        dqueries[0, 0, :, span] = contract(keys_t, dscore, 1, 0).astype(jnp.bfloat16)
        dkey_sum = dkey_sum + contract(queries_t[:, span], dscore, 1, 1)
        dvalue_sum = dvalue_sum + contract(push, weights.astype(jnp.bfloat16), 1, 1)
    dkeys[0, 0] = dkey_sum.astype(jnp.bfloat16)
    dvalues[0, 0] = dvalue_sum.astype(jnp.bfloat16)


def attend_back(qkv, seg_col, seg_row, context, stats, dcontext, score_scale):
    micro, _, heads, depth, length = qkv.shape
    block = min(256, length)
    head_block = pl.BlockSpec((1, 1, depth, length), lambda m, h: (m, h, 0, 0))
    return pl.pallas_call(
        functools.partial(attend_back_kernel, score_scale, block),
        grid=(micro, heads),
        out_shape=(jax.ShapeDtypeStruct((micro, heads, depth, length), jnp.bfloat16),) * 3,
        in_specs=[
            pl.BlockSpec((1, 3, 1, depth, length), lambda m, h: (m, 0, h, 0, 0)),
            pl.BlockSpec((1, length, 1), lambda m, h: (m, 0, 0)),
            pl.BlockSpec((1, 1, length), lambda m, h: (m, 0, 0)),
            head_block,
            pl.BlockSpec((1, 1, 2, length), lambda m, h: (m, h, 0, 0)),
            head_block,
        ],
        out_specs=(head_block,) * 3,
        compiler_params=pltpu.CompilerParams(vmem_limit_bytes=VMEM_LIMIT),
    )(qkv, seg_col, seg_row, context, stats, dcontext)


def fast_body(
    hidden_in,
    segment_ids,
    queries,
    targets,
    cotangent,
    query_weight,
    key_weight,
    value_weight,
    output_weight,
    query_bias,
    value_bias,
    output_bias,
    first_gain,
    first_shift,
    inner_weight,
    inner_bias,
    outer_weight,
    outer_bias,
    second_gain,
    second_shift,
):
    dp_size, ring_size = lax.axis_size("dp"), lax.axis_size("blk")
    dp, blk = lax.axis_index("dp"), lax.axis_index("blk")
    micro, row_count, block_tokens, width = hidden_in.shape
    row_queries = queries.shape[1]
    length = block_tokens * ring_size
    head_dim = width // HEADS
    own_heads = HEADS // ring_size
    score_scale = 1.0 / math.sqrt(head_dim)
    tokens = micro * block_tokens
    wide = jnp.float32
    narrow = jnp.bfloat16

    vectors = (
        query_bias,
        value_bias,
        output_bias,
        first_gain,
        first_shift,
        outer_bias,
        second_gain,
        second_shift,
        inner_bias,
    )
    piece = vectors[0].shape[0]
    inner_piece = inner_bias.shape[0]
    group = own_heads * head_dim
    window = -(-group // 128) * 128
    window_heads = window // head_dim
    hidden_rows = hidden_in.reshape(micro, block_tokens, width)
    pack = jnp.concatenate(
        (
            jnp.pad(jnp.stack(vectors[:8]), ((0, 0), (0, inner_piece - piece))),
            jnp.pad(inner_bias[None], ((0, 7), (0, 0))),
        )
    )
    target_pack = jnp.pad(targets, ((0, 8 - micro), (0, 128 - row_queries)))
    seg_pack = jnp.pad(segment_ids.reshape(micro, block_tokens), ((0, 8 - micro), (0, 0)))
    shards = (
        query_weight,
        key_weight,
        value_weight,
        pack,
        target_pack,
        queries.reshape(micro * row_queries, width),
        output_weight,
        inner_weight,
        outer_weight,
    )
    ways = (("x", "y"), ("y", "x"))
    items = []

    def add_item(source, target, row=0, rows=None, from_column=0, columns=None, to_column=0):
        shape = shards[source].shape
        items.append(
            {
                "source": source,
                "target": target,
                "row": row,
                "rows": rows or shape[0],
                "stride": shape[0],
                "from_column": from_column,
                "columns": columns or shape[1],
                "to_column": to_column,
                "group": group,
                "route": ways[len(items) % 2],
            }
        )

    for index in range(3):
        add_item(index, 0, from_column=None, columns=window, to_column=index * window)
    for index in range(3, 7):
        add_item(index, index - 2)
    for part in range(4):
        add_item(
            7, 5, from_column=part * width, columns=width, to_column=part * width
        )
        add_item(8, 6, row=part * piece, rows=piece)
    targets_out = [jax.ShapeDtypeStruct((width, 3 * window), narrow)] + [
        jax.ShapeDtypeStruct((dp_size * s.shape[0], s.shape[1]), s.dtype) for s in shards[3:]
    ]
    (
        w_window,
        pack_all,
        targets_all,
        queries_all,
        wo_full,
        w_inner,
        w_outer,
        seg_all,
        hidden_all,
    ) = gather_all(shards, items, targets_out, seg_pack, hidden_rows, ring_size)
    pack_rows = pack_all.reshape(dp_size, 16, inner_piece)
    eight = pack_rows[:, :8, :piece].transpose(1, 0, 2).reshape(8, width).astype(wide)
    bq_full, bv_full, bo_full, gain_one, shift_one, b_outer, gain_two, shift_two = eight
    b_inner = pack_rows[:, 8].reshape(-1).astype(wide)
    targets_all = (
        targets_all.reshape(dp_size, 8, 128)[:, :micro, :row_queries]
        .transpose(1, 0, 2)
        .reshape(micro, dp_size * row_queries)
    )
    queries_all = (
        queries_all.reshape(dp_size, micro, row_queries, width)
        .transpose(1, 0, 2, 3)
        .reshape(micro, dp_size * row_queries, width)
    )
    seg_row = (
        seg_all.reshape(ring_size, 8, block_tokens)[:, :micro]
        .transpose(1, 0, 2)
        .reshape(micro, 1, length)
    )
    seg_col = seg_row.reshape(micro, length, 1)

    flat_rows = hidden_in.reshape(tokens, width)
    window_at = (blk * group) // 128 * 128
    head_at = (blk * group - window_at) // head_dim
    bias_window = jnp.concatenate(
        (
            lax.dynamic_slice(bq_full, (window_at,), (window,)),
            jnp.zeros((window,), wide),
            lax.dynamic_slice(bv_full, (window_at,), (window,)),
        )
    )
    qkv_window = (
        jnp.einsum("mtd,de->met", hidden_all, w_window, preferred_element_type=wide)
        + bias_window[None, :, None]
    ).astype(narrow)
    qkv = lax.dynamic_slice(
        qkv_window.reshape(micro, 3, window_heads, head_dim, length),
        (0, 0, head_at, 0, 0),
        (micro, 3, own_heads, head_dim, length),
    )
    context, context_low, stats = attend(qkv, seg_col, seg_row, score_scale)
    (context_t,) = to_tokens(
        (context_low.reshape(micro, own_heads * head_dim, length),), ring_size, 3
    )
    attended = (
        jnp.einsum("met,ed->mtd", context_t, wo_full, preferred_element_type=wide).reshape(
            tokens, width
        )
        + bo_full
    )
    first_out, first_normed, first_factor = layer_norm(
        flat_rows.astype(wide) + attended, gain_one, shift_one
    )
    first_low = first_out.astype(narrow)
    inner_pre = jnp.dot(first_low, w_inner, preferred_element_type=wide) + b_inner
    active = jax.nn.gelu(inner_pre, approximate=False).astype(narrow)
    outer_out = jnp.dot(active, w_outer, preferred_element_type=wide) + b_outer
    output, second_normed, second_factor = layer_norm(first_out + outer_out, gain_two, shift_two)
    output_low = output.astype(narrow)
    output_rows = output_low.reshape(micro, block_tokens, width)

    segment = segment_ids.reshape(micro, block_tokens)
    padded = jnp.pad(seg_row.reshape(micro, length), ((0, 0), (1, 0)), constant_values=-1)
    before = lax.dynamic_slice(padded, (0, blk * block_tokens), (micro, block_tokens))
    numbers = jnp.arange(row_queries, dtype=jnp.int32)
    select = (
        (segment != before)[:, None, :] & (segment[:, None, :] == numbers[None, :, None])
    ).astype(wide)
    own_table = jnp.einsum(
        "msi,mid->msd", select.astype(narrow), output_rows, preferred_element_type=wide
    ).astype(narrow)
    tables = gather_tables(own_table.reshape(micro * row_queries, width), ring_size, dp_size)
    tables = tables.reshape(dp_size, micro, row_queries, width)
    everyone = tables.transpose(1, 0, 2, 3).reshape(micro, dp_size * row_queries, width)
    embeddings = lax.dynamic_index_in_dim(tables, dp, 0, keepdims=False)
    query_scores = jnp.einsum("mqd,mpd->mqp", queries_all, everyone, preferred_element_type=wide)
    score_peak = jnp.max(query_scores, axis=2, keepdims=True)
    log_total = score_peak[..., 0] + jnp.log(jnp.sum(jnp.exp(query_scores - score_peak), axis=2))
    target_hot = (
        jnp.arange(query_scores.shape[2], dtype=jnp.int32)[None, None, :]
        == targets_all[:, :, None]
    ).astype(wide)
    losses = log_total - jnp.sum(query_scores * target_hot, axis=2)
    query_loss = lax.dynamic_slice(losses, (0, dp * row_queries), (micro, row_queries))
    dscore_query = jnp.exp(query_scores - log_total[..., None]) - target_hot
    own_dscore = lax.dynamic_slice(
        dscore_query, (0, dp * row_queries, 0), (micro, row_queries, dp_size * row_queries)
    )
    query_grad = jnp.einsum("mqp,mpd->mqd", own_dscore, everyone.astype(wide), precision=PRECISE)
    own_columns = lax.dynamic_slice(
        dscore_query, (0, 0, dp * row_queries), (micro, dp_size * row_queries, row_queries)
    )
    embed_grad = jnp.einsum(
        "mqs,mqd->msd", own_columns, queries_all.astype(wide), precision=PRECISE
    )
    cls_grad = jnp.einsum("msi,msd->mid", select, embed_grad, precision=PRECISE)
    dout = cotangent.reshape(tokens, width).astype(wide) + cls_grad.reshape(tokens, width)
    gain_two_grad = jnp.sum(dout * second_normed, axis=0)
    shift_two_grad = jnp.sum(dout, axis=0)
    dsecond = norm_back(dout, second_normed, second_factor, gain_two)
    douter = dsecond.astype(narrow)
    outer_bias_grad = jnp.sum(douter.astype(wide), axis=0)
    outer_weight_grad = jnp.einsum(
        "nf,nd->fd", active, douter, preferred_element_type=wide
    ).astype(narrow)
    dactive = jnp.einsum("nd,fd->nf", douter, w_outer, preferred_element_type=wide)
    dinner = (dactive * gelu_slope(inner_pre)).astype(narrow)
    inner_bias_grad = jnp.sum(dinner.astype(wide), axis=0)
    inner_weight_grad = jnp.einsum(
        "nd,nf->df", first_low, dinner, preferred_element_type=wide
    ).astype(narrow)
    dfirst = dsecond + jnp.einsum("nf,df->nd", dinner, w_inner, preferred_element_type=wide)
    gain_one_grad = jnp.sum(dfirst * first_normed, axis=0)
    shift_one_grad = jnp.sum(dfirst, axis=0)
    dresidual = norm_back(dfirst, first_normed, first_factor, gain_one)
    dattended = dresidual.astype(narrow)
    output_bias_grad = jnp.sum(dattended.astype(wide), axis=0)
    datt_rows = dattended.reshape(micro, block_tokens, width)
    output_weight_grad = jnp.einsum(
        "met,mtd->ed", context_t, datt_rows, preferred_element_type=wide
    ).astype(narrow)
    dcontext_t = jnp.einsum(
        "mtd,ed->met", datt_rows, wo_full, preferred_element_type=wide
    ).astype(narrow)
    dcontext = to_heads((dcontext_t,), ring_size, 5).reshape(
        micro, own_heads, head_dim, length
    )
    dparts = attend_back(qkv, seg_col, seg_row, context, stats, dcontext, score_scale)
    dwindow = jnp.stack(dparts, axis=1)
    dwindow = lax.dynamic_update_slice(
        jnp.zeros((micro, 3, window_heads, head_dim, length), narrow), dwindow, (0, 0, head_at, 0, 0)
    ).reshape(micro, 3 * window, length)
    dhidden_parts = jnp.einsum(
        "met,de->mtd", dwindow, w_window, preferred_element_type=wide
    ).astype(narrow)
    dhidden = dresidual.reshape(micro, block_tokens, width) + scatter_line(
        dhidden_parts.reshape(micro, ring_size, block_tokens, width), ring_size, 6
    )
    window_grad = jnp.einsum(
        "mtd,met->de", hidden_all, dwindow, preferred_element_type=wide
    ).astype(narrow)
    bias_grads = jnp.sum(dwindow.astype(wide), axis=(0, 2))
    query_bias_grad, value_bias_grad = (
        lax.dynamic_update_slice(
            jnp.zeros((width,), wide), bias_grads[at : at + window], (window_at,)
        )
        for at in (0, 2 * window)
    )
    vector_grads = jnp.stack(
        (
            query_bias_grad,
            value_bias_grad,
            output_bias_grad,
            gain_one_grad,
            shift_one_grad,
            outer_bias_grad,
            gain_two_grad,
            shift_two_grad,
        )
    ).astype(narrow)
    grad_pack = jnp.pad(
        jnp.concatenate(
            (
                jnp.pad(
                    vector_grads.reshape(8, dp_size, piece).transpose(1, 0, 2),
                    ((0, 0), (0, 0), (0, inner_piece - piece)),
                ),
                inner_bias_grad.astype(narrow).reshape(dp_size, 1, inner_piece),
            ),
            axis=1,
        ),
        ((0, 0), (0, 7), (0, 0)),
    ).reshape(dp_size * 16, inner_piece)
    grads = (outer_weight_grad, inner_weight_grad, output_weight_grad, window_grad, grad_pack)
    sums = []

    def add_sum(source, row=0, rows=None, column=0, columns=None, gathered=False):
        shape = grads[source].shape
        sums.append(
            {
                "source": source,
                "row": row,
                "rows": rows or shape[0] // dp_size,
                "stride": shape[0] // dp_size,
                "column": column,
                "columns": columns or shape[1],
                "gathered": gathered,
                "route": ways[len(sums) % 2],
            }
        )

    for part in range(4):
        add_sum(0, row=part * piece, rows=piece)
        add_sum(1, column=part * width, columns=width)
    add_sum(2)
    add_sum(3, gathered=True)
    add_sum(4)
    d_outer, d_inner, d_wo, d_window, d_pack = reduce_all(grads, sums, dp_size, ring_size, 7)
    d_outer, d_inner, d_wo, d_pack = (
        part.astype(wide) for part in (d_outer, d_inner, d_wo, d_pack)
    )
    weight_grads = []
    for index in range(3):
        pieces = []
        for member in range(ring_size):
            start = member * group - (member * group) // 128 * 128 + index * window
            pieces.append(d_window[member, :, start : start + group])
        weight_grads.append(jnp.concatenate(pieces, axis=1).astype(wide))
    d_wq, d_wk, d_wv = weight_grads
    d_bq, d_bv, d_bo, d_g1, d_s1, d_bu, d_g2, d_s2 = (d_pack[i, :piece] for i in range(8))
    d_bi = d_pack[8]
    shape = (micro, row_count, block_tokens, width)
    return (
        output_low.reshape(shape),
        embeddings,
        query_loss,
        query_grad,
        dhidden.astype(narrow).reshape(shape),
        d_wq,
        d_wk,
        d_wv,
        d_wo,
        d_bq,
        d_bv,
        d_bo,
        d_g1,
        d_s1,
        d_inner,
        d_bi,
        d_outer,
        d_bu,
        d_g2,
        d_s2,
    )


def solution(mesh):
    in_specs = (
        P(None, "dp", "blk", None),
        P(None, "dp", "blk"),
        P(None, "dp", None),
        P(None, "dp"),
        P(None, "dp", "blk", None),
        P("dp", None),
        P("dp", None),
        P("dp", None),
        P("dp", None),
        P("dp"),
        P("dp"),
        P("dp"),
        P("dp"),
        P("dp"),
        P("dp", None),
        P("dp"),
        P("dp", None),
        P("dp"),
        P("dp"),
        P("dp"),
    )
    out_specs = (
        P(None, "dp", "blk", None),
        P(None, "dp", None),
        P(None, "dp"),
        P(None, "dp", None),
        P(None, "dp", "blk", None),
        P("dp", None),
        P("dp", None),
        P("dp", None),
        P("dp", None),
        P("dp"),
        P("dp"),
        P("dp"),
        P("dp"),
        P("dp"),
        P("dp", None),
        P("dp"),
        P("dp", None),
        P("dp"),
        P("dp"),
        P("dp"),
    )
    fast = mesh.shape["dp"] == 8 and mesh.shape["blk"] == 4
    body = fast_body if fast else ring_body
    return jax.shard_map(body, mesh=mesh, in_specs=in_specs, out_specs=out_specs, check_vma=False)
```

```python
import functools
import math

import jax
import jax.numpy as jnp
from jax import lax
from jax.experimental import pallas as pl
from jax.experimental.pallas import tpu as pltpu
from jax.sharding import PartitionSpec as P

HEADS = 12


EPSILON = 1e-12
NEGATIVE = -1000000000.0
PRECISE = lax.Precision.HIGHEST


def passed_along(x, axis, by):
    size = lax.axis_size(axis)
    return lax.ppermute(x, axis, [(i, (i + by) % size) for i in range(size)])


def as_sent(x):
    return jax.tree.map(lambda a: a.astype(jnp.bfloat16) if a.dtype == jnp.float32 else a, x)


def layer_norm(values, norm_gain, norm_shift):
    center = values - jnp.mean(values, axis=-1, keepdims=True)
    factor = lax.rsqrt(jnp.mean(center * center, axis=-1, keepdims=True) + EPSILON)
    normed = center * factor
    return (normed * norm_gain + norm_shift, normed, factor)


def norm_back(gradient, normed, factor, norm_gain):
    scaled = gradient * norm_gain
    inner_term = (
        scaled
        - jnp.mean(scaled, axis=-1, keepdims=True)
        - normed * jnp.mean(scaled * normed, axis=-1, keepdims=True)
    )
    return inner_term * factor


def gelu_slope(values):
    normal_cdf = 0.5 * (1.0 + lax.erf(values * (1.0 / math.sqrt(2.0))))
    return normal_cdf + values * jnp.exp(-0.5 * values * values) * (1.0 / math.sqrt(2.0 * math.pi))


def scores_of(query_rows, key_rows, query_segment, key_segment, score_scale):
    raw_scores = jnp.einsum(
        "rqhd,rkhd->rhqk", query_rows, key_rows, preferred_element_type=jnp.float32
    )
    same_doc = (query_segment[:, :, None] == key_segment[:, None, :])[:, None]
    return jnp.where(same_doc, score_scale * raw_scores, NEGATIVE)


def contribute(
    query_rows,
    push_grad,
    delta_term,
    peak_term,
    query_segment,
    key_rows,
    value_rows,
    key_segment,
    score_scale,
):
    scores = scores_of(query_rows, key_rows, query_segment, key_segment, score_scale)
    weights = jnp.exp(scores - peak_term[..., None])
    pushed = jnp.einsum(
        "rqhd,rkhd->rhqk", push_grad, value_rows, preferred_element_type=jnp.float32
    )
    dscore = (weights * (pushed - delta_term[..., None]) * score_scale).astype(jnp.bfloat16)
    query_part = jnp.einsum("rhqk,rkhd->rqhd", dscore, key_rows, preferred_element_type=jnp.float32)
    key_part = jnp.einsum("rhqk,rqhd->rkhd", dscore, query_rows, preferred_element_type=jnp.float32)
    value_part = jnp.einsum(
        "rhqk,rqhd->rkhd",
        weights.astype(jnp.bfloat16),
        push_grad,
        preferred_element_type=jnp.float32,
    )
    return (query_part, key_part, value_part)


def ring_body(
    hidden_in,
    segment_ids,
    queries,
    targets,
    cotangent,
    query_weight,
    key_weight,
    value_weight,
    output_weight,
    query_bias,
    value_bias,
    output_bias,
    first_gain,
    first_shift,
    inner_weight,
    inner_bias,
    outer_weight,
    outer_bias,
    second_gain,
    second_shift,
):
    shards = (
        query_weight,
        key_weight,
        value_weight,
        output_weight,
        query_bias,
        value_bias,
        output_bias,
        first_gain,
        first_shift,
        inner_weight,
        inner_bias,
        outer_weight,
        outer_bias,
        second_gain,
        second_shift,
    )
    cycle_size = lax.axis_size("blk")
    cycle_place = lax.axis_index("blk")
    micro_count, row_count, block_tokens, model_width = hidden_in.shape
    segment_count = queries.shape[1] // row_count
    head_count = HEADS
    head_dim = model_width // head_count
    score_scale = 1.0 / math.sqrt(head_dim)
    token_count = row_count * block_tokens
    head_shape = (row_count, block_tokens, head_count, head_dim)
    grad_totals = tuple((jnp.zeros(shard_piece.shape, jnp.float32) for shard_piece in shards))
    local_sum = None
    gathered = None
    out_list, embed_list, loss_list, qgrad_list, hgrad_list = ([], [], [], [], [])
    for micro_index in range(micro_count):
        gathered = (
            lax.all_gather(shards[0], "dp", axis=0, tiled=True),
            lax.all_gather(shards[1], "dp", axis=0, tiled=True),
            lax.all_gather(shards[2], "dp", axis=0, tiled=True),
            lax.all_gather(shards[3], "dp", axis=0, tiled=True),
            lax.all_gather(shards[4], "dp", axis=0, tiled=True),
            lax.all_gather(shards[5], "dp", axis=0, tiled=True),
            lax.all_gather(shards[6], "dp", axis=0, tiled=True),
            lax.all_gather(shards[7], "dp", axis=0, tiled=True),
            lax.all_gather(shards[8], "dp", axis=0, tiled=True),
            lax.all_gather(shards[9], "dp", axis=0, tiled=True),
            lax.all_gather(shards[10], "dp", axis=0, tiled=True),
            lax.all_gather(shards[11], "dp", axis=0, tiled=True),
            lax.all_gather(shards[12], "dp", axis=0, tiled=True),
            lax.all_gather(shards[13], "dp", axis=0, tiled=True),
            lax.all_gather(shards[14], "dp", axis=0, tiled=True),
        )
        (
            wq_full,
            wk_full,
            wv_full,
            wo_full,
            bq_full,
            bv_full,
            bo_full,
            gain_one,
            shift_one,
            w_inner,
            b_inner,
            w_outer,
            b_outer,
            gain_two,
            shift_two,
        ) = gathered
        gain_one = gain_one.astype(jnp.float32)
        gain_two = gain_two.astype(jnp.float32)
        segment = segment_ids[micro_index]
        flat_rows = hidden_in[micro_index].reshape(token_count, model_width)
        query_rows = (
            (
                jnp.dot(flat_rows, wq_full, preferred_element_type=jnp.float32)
                + bq_full.astype(jnp.float32)
            )
            .astype(jnp.bfloat16)
            .reshape(head_shape)
        )
        key_rows = (
            jnp.dot(flat_rows, wk_full, preferred_element_type=jnp.float32)
            .astype(jnp.bfloat16)
            .reshape(head_shape)
        )
        value_rows = (
            (
                jnp.dot(flat_rows, wv_full, preferred_element_type=jnp.float32)
                + bv_full.astype(jnp.float32)
            )
            .astype(jnp.bfloat16)
            .reshape(head_shape)
        )

        def absorb(softmax_state, visit_keys, visit_values, visit_segment):
            running_peak, running_total, running_sum = softmax_state
            scores = scores_of(query_rows, visit_keys, segment, visit_segment, score_scale)
            new_peak = jnp.maximum(running_peak, jnp.max(scores, axis=-1))
            decay_factor = jnp.exp(running_peak - new_peak)
            weights = jnp.exp(scores - new_peak[..., None])
            running_total = running_total * decay_factor + jnp.sum(weights, axis=-1)
            update = jnp.einsum(
                "rhqk,rkhd->rqhd",
                weights.astype(jnp.bfloat16),
                visit_values,
                preferred_element_type=jnp.float32,
            )
            running_sum = running_sum * jnp.transpose(decay_factor, (0, 2, 1))[..., None] + update
            return (new_peak, running_total, running_sum)

        start_state = (
            jnp.full((row_count, head_count, block_tokens), -1e30, jnp.float32),
            jnp.zeros((row_count, head_count, block_tokens), jnp.float32),
            jnp.zeros(head_shape, jnp.float32),
        )
        first_state = absorb(start_state, key_rows, value_rows, segment)

        def forward_step(cycle_step, cycle_carry):
            visit_keys, visit_values, visit_segment, prior_segment, softmax_state = cycle_carry
            visit_keys, visit_values, visit_segment = passed_along(
                (visit_keys, visit_values, visit_segment), "blk", 1
            )
            prior_segment = jnp.where(cycle_step == 1, visit_segment[:, -1], prior_segment)
            return (
                visit_keys,
                visit_values,
                visit_segment,
                prior_segment,
                absorb(softmax_state, visit_keys, visit_values, visit_segment),
            )

        cycle_carry = lax.fori_loop(
            1, cycle_size, forward_step, (key_rows, value_rows, segment, segment[:, 0], first_state)
        )
        prior_segment = cycle_carry[3]
        row_peak, row_total, running_sum = cycle_carry[4]
        total_heads = jnp.transpose(row_total, (0, 2, 1))[..., None]
        context = running_sum / total_heads
        context_low = context.reshape(token_count, model_width).astype(jnp.bfloat16)
        attended = jnp.dot(
            context_low, wo_full, preferred_element_type=jnp.float32
        ) + bo_full.astype(jnp.float32)
        first_out, first_normed, first_factor = layer_norm(
            flat_rows.astype(jnp.float32) + attended, gain_one, shift_one.astype(jnp.float32)
        )
        first_low = first_out.astype(jnp.bfloat16)
        inner_pre = jnp.dot(
            first_low, w_inner, preferred_element_type=jnp.float32
        ) + b_inner.astype(jnp.float32)
        active = jax.nn.gelu(inner_pre, approximate=False).astype(jnp.bfloat16)
        outer_out = jnp.dot(active, w_outer, preferred_element_type=jnp.float32) + b_outer.astype(
            jnp.float32
        )
        output, second_normed, second_factor = layer_norm(
            first_out + outer_out, gain_two, shift_two.astype(jnp.float32)
        )
        output_low = output.astype(jnp.bfloat16)
        out_list.append(output_low.reshape(row_count, block_tokens, model_width))
        position = cycle_place * block_tokens + jnp.arange(block_tokens, dtype=jnp.int32)
        before = jnp.concatenate([prior_segment[:, None], segment[:, :-1]], axis=1)
        leading = (position[None, :] == 0) | (segment != before)
        numbers = jnp.arange(segment_count, dtype=jnp.int32)
        select = (leading[:, None, :] & (segment[:, None, :] == numbers[None, :, None])).astype(
            jnp.float32
        )
        cls_table = jnp.einsum(
            "rsi,rid->rsd",
            select.astype(jnp.bfloat16),
            output_low.reshape(row_count, block_tokens, model_width),
            preferred_element_type=jnp.float32,
        )
        own_table = lax.psum(cls_table.astype(jnp.bfloat16), "blk").reshape(
            row_count * segment_count, model_width
        )
        embed_list.append(own_table)
        everyone = lax.all_gather(own_table, "dp", axis=0, tiled=True)
        query_vectors = queries[micro_index]
        query_scores = jnp.dot(query_vectors, everyone.T, preferred_element_type=jnp.float32)
        score_peak = jnp.max(query_scores, axis=1, keepdims=True)
        log_total = score_peak[:, 0] + jnp.log(jnp.sum(jnp.exp(query_scores - score_peak), axis=1))
        target_hot = (
            jnp.arange(query_scores.shape[1], dtype=jnp.int32)[None, :]
            == targets[micro_index][:, None]
        ).astype(jnp.float32)
        loss_list.append(log_total - jnp.sum(query_scores * target_hot, axis=1))
        dscore_query = jnp.exp(query_scores - log_total[:, None]) - target_hot
        qgrad_list.append(jnp.dot(dscore_query, everyone.astype(jnp.float32), precision=PRECISE))
        embed_part = jnp.dot(dscore_query.T, query_vectors.astype(jnp.float32), precision=PRECISE)
        embed_grad = (
            lax.psum_scatter(embed_part.astype(jnp.bfloat16), "dp", scatter_dimension=0, tiled=True)
            .astype(jnp.float32)
            .reshape(row_count, segment_count, model_width)
        )
        cls_grad = jnp.einsum("rsi,rsd->rid", select, embed_grad, precision=PRECISE)
        dout = cotangent[micro_index].reshape(token_count, model_width).astype(
            jnp.float32
        ) + cls_grad.reshape(token_count, model_width)
        gain_two_grad = jnp.sum(dout * second_normed, axis=0)
        shift_two_grad = jnp.sum(dout, axis=0)
        dsecond = norm_back(dout, second_normed, second_factor, gain_two)
        douter = dsecond.astype(jnp.bfloat16)
        outer_bias_grad = jnp.sum(douter.astype(jnp.float32), axis=0)
        outer_weight_grad = jnp.einsum(
            "nf,nd->fd", active, douter, preferred_element_type=jnp.float32
        )
        dactive = jnp.einsum("nd,fd->nf", douter, w_outer, preferred_element_type=jnp.float32)
        dinner = (dactive * gelu_slope(inner_pre)).astype(jnp.bfloat16)
        inner_bias_grad = jnp.sum(dinner.astype(jnp.float32), axis=0)
        inner_weight_grad = jnp.einsum(
            "nd,nf->df", first_low, dinner, preferred_element_type=jnp.float32
        )
        dfirst = dsecond + jnp.einsum(
            "nf,df->nd", dinner, w_inner, preferred_element_type=jnp.float32
        )
        gain_one_grad = jnp.sum(dfirst * first_normed, axis=0)
        shift_one_grad = jnp.sum(dfirst, axis=0)
        dresidual = norm_back(dfirst, first_normed, first_factor, gain_one)
        dattended = dresidual.astype(jnp.bfloat16)
        output_bias_grad = jnp.sum(dattended.astype(jnp.float32), axis=0)
        output_weight_grad = jnp.einsum(
            "nd,ne->de", context_low, dattended, preferred_element_type=jnp.float32
        )
        dcontext = jnp.einsum(
            "ne,de->nd", dattended, wo_full, preferred_element_type=jnp.float32
        ).astype(jnp.bfloat16)
        dcontext_wide = dcontext.astype(jnp.float32).reshape(head_shape)
        push_grad = (dcontext_wide / total_heads).astype(jnp.bfloat16)
        delta_term = jnp.transpose(
            jnp.sum(dcontext_wide * context, axis=-1) / total_heads[..., 0], (0, 2, 1)
        )
        own_query, own_key, own_value = contribute(
            query_rows,
            push_grad,
            delta_term,
            row_peak,
            segment,
            key_rows,
            value_rows,
            segment,
            score_scale,
        )

        def key_step(cycle_step, cycle_carry):
            visit_keys, visit_values, visit_segment, query_sum, key_sum, value_sum = cycle_carry
            visit_keys, visit_values, visit_segment = passed_along(
                (visit_keys, visit_values, visit_segment), "blk", 1
            )
            key_sum, value_sum = (
                passed_along(key_sum.astype(jnp.bfloat16), "blk", 1).astype(key_sum.dtype),
                passed_along(value_sum.astype(jnp.bfloat16), "blk", 1).astype(value_sum.dtype),
            )
            query_part, key_part, value_part = contribute(
                query_rows,
                push_grad,
                delta_term,
                row_peak,
                segment,
                visit_keys,
                visit_values,
                visit_segment,
                score_scale,
            )
            return (
                visit_keys,
                visit_values,
                visit_segment,
                query_sum + query_part,
                key_sum + key_part,
                value_sum + value_part,
            )

        back_carry = lax.fori_loop(
            1, cycle_size, key_step, (key_rows, value_rows, segment, own_query, own_key, own_value)
        )
        query_sum = back_carry[3]
        key_sum, value_sum = (
            passed_along(back_carry[4].astype(jnp.bfloat16), "blk", 1).astype(jnp.float32),
            passed_along(back_carry[5].astype(jnp.bfloat16), "blk", 1).astype(jnp.float32),
        )
        dquery = query_sum.astype(jnp.bfloat16).reshape(token_count, model_width)
        dkey = key_sum.astype(jnp.bfloat16).reshape(token_count, model_width)
        dvalue = value_sum.astype(jnp.bfloat16).reshape(token_count, model_width)
        dhidden = dresidual + jnp.einsum(
            "ne,de->nd", dquery, wq_full, preferred_element_type=jnp.float32
        )
        dhidden = dhidden + jnp.einsum(
            "ne,de->nd", dkey, wk_full, preferred_element_type=jnp.float32
        )
        dhidden = dhidden + jnp.einsum(
            "ne,de->nd", dvalue, wv_full, preferred_element_type=jnp.float32
        )
        hgrad_list.append(
            dhidden.astype(jnp.bfloat16).reshape(row_count, block_tokens, model_width)
        )
        local_grads = (
            jnp.einsum("nd,ne->de", flat_rows, dquery, preferred_element_type=jnp.float32),
            jnp.einsum("nd,ne->de", flat_rows, dkey, preferred_element_type=jnp.float32),
            jnp.einsum("nd,ne->de", flat_rows, dvalue, preferred_element_type=jnp.float32),
            output_weight_grad,
            jnp.sum(dquery.astype(jnp.float32), axis=0),
            jnp.sum(dvalue.astype(jnp.float32), axis=0),
            output_bias_grad,
            gain_one_grad,
            shift_one_grad,
            inner_weight_grad,
            inner_bias_grad,
            outer_weight_grad,
            outer_bias_grad,
            gain_two_grad,
            shift_two_grad,
        )
        local_sum = local_grads
        reduced = jax.tree.map(
            lambda part: part.astype(jnp.float32),
            lax.psum_scatter(as_sent(local_sum), "dp", scatter_dimension=0, tiled=True),
        )
        reduced = jax.tree.map(
            lambda part: part.astype(jnp.float32), lax.psum(as_sent(reduced), "blk")
        )
        grad_totals = tuple(
            (total_piece + new_piece for total_piece, new_piece in zip(grad_totals, reduced))
        )
        local_sum = None
    return (
        jnp.stack(out_list),
        jnp.stack(embed_list),
        jnp.stack(loss_list),
        jnp.stack(qgrad_list),
        jnp.stack(hgrad_list),
        grad_totals[0],
        grad_totals[1],
        grad_totals[2],
        grad_totals[3],
        grad_totals[4],
        grad_totals[5],
        grad_totals[6],
        grad_totals[7],
        grad_totals[8],
        grad_totals[9],
        grad_totals[10],
        grad_totals[11],
        grad_totals[12],
        grad_totals[13],
        grad_totals[14],
    )


MESH = pl.DeviceIdType.MESH
VMEM_LIMIT = 60 * 1024 * 1024
SIDE = {"c": 1, "x": 2, "y": 4}


def place():
    dp, blk = lax.axis_index("dp"), lax.axis_index("blk")
    bits = {"c": lax.rem(dp, 2), "x": lax.rem(dp // 2, 2), "y": dp // 4}
    return dp, blk, bits


def across(dp, blk, bits, *axes):
    other = dp
    for axis in axes:
        other = other + SIDE[axis] * (1 - 2 * bits[axis])
    return (other, blk)


def greet(peers):
    barrier = pltpu.get_barrier_semaphore()
    for peer in peers:
        pl.semaphore_signal(barrier, inc=1, device_id=peer, device_id_type=MESH)
    pl.semaphore_wait(barrier, len(peers))


def remote(source, target, send_sem, recv_sem, peer):
    return pltpu.make_async_remote_copy(
        src_ref=source,
        dst_ref=target,
        send_sem=send_sem,
        recv_sem=recv_sem,
        device_id=peer,
        device_id_type=MESH,
    )


def comm_params(collective):
    return pltpu.CompilerParams(
        collective_id=collective, has_side_effects=True, vmem_limit_bytes=VMEM_LIMIT
    )


ANY = pl.BlockSpec(memory_space=pl.ANY)
IN_VMEM = pl.BlockSpec(memory_space=pltpu.VMEM)


def forward_kernel(items, ring_size, depth, sources, places, *refs):
    shards, seg_shard, hidden = refs[:sources], refs[sources], refs[sources + 1]
    outs = refs[sources + 2 :]
    fulls = outs[:places]
    seg_full, hidden_row, qkv, context, stats, context_t = outs[places : places + 6]
    (
        hidden_full,
        low,
        seg_line,
        seg_col,
        send_sem,
        recv_sem,
        seg_send,
        seg_recv,
        line_send,
        line_recv,
        head_send,
        head_recv,
        local_sem,
        row_sem,
    ) = outs[places + 6 :]
    w_window, pack_full = fulls[0], fulls[1]
    dp, blk, bits = place()
    sibling = across(dp, blk, bits, "c")
    ring = [(dp, lax.rem(blk + step, ring_size)) for step in range(1, ring_size)]
    greet([sibling, across(dp, blk, bits, "x"), across(dp, blk, bits, "y")] + ring)
    seg_rows = seg_shard.shape[0]
    micro, tokens, width = hidden.shape
    spread = ring_size // micro
    row_at, group_at = blk // spread, lax.rem(blk, spread)
    group, length = context.shape
    heads = group // depth
    score_scale = 1.0 / math.sqrt(depth)
    waiting = []
    mine = pl.ds(pl.multiple_of(blk * tokens, tokens), tokens)

    def line_view(m, side, distance):
        owner = blk + (1 - 2 * side) * distance
        return hidden_full.at[m, pl.ds(pl.multiple_of(owner * tokens, tokens), tokens)]

    def line_copy(m, side, distance):
        view = line_view(m, side, distance)
        return remote(
            hidden.at[m] if distance == 0 else view,
            view,
            line_send.at[m, side, distance],
            line_recv.at[m, side, distance + 1],
            (dp, blk - 1 + 2 * side),
        )

    def arrival(m, side, distance):
        view = line_view(m, side, distance)
        return remote(
            view,
            view,
            line_send.at[m, side, distance],
            line_recv.at[m, side, distance],
            (dp, blk - 1 + 2 * side),
        )

    def passes_on(m, side):
        return blk > m * spread if side == 0 else blk < m * spread + spread - 1

    def comes(m, side, distance):
        if side == 0:
            return (blk >= m * spread) & (blk + distance < ring_size)
        return (blk < m * spread + spread) & (blk >= distance)

    def line_step(m, distance):
        for side in range(2):

            @pl.when(comes(m, side, distance))
            def _():
                arrival(m, side, distance).wait_recv()

            if distance < ring_size - 1:

                @pl.when(comes(m, side, distance) & passes_on(m, side))
                def _():
                    line_copy(m, side, distance).start()

    for m in range(micro):
        for side in range(2):

            @pl.when(passes_on(m, side))
            def _():
                line_copy(m, side, 0).start()

    def own_part(item):
        spec = items[item]
        column = spec["from_column"]
        if column is None:
            column = pl.multiple_of(group_at * group, group)
        return shards[spec["source"]].at[
            pl.ds(spec["row"], spec["rows"]), pl.ds(column, spec["columns"])
        ]

    def block(item, owner):
        spec = items[item]
        first = owner * spec["stride"] + spec["row"]
        return fulls[spec["target"]].at[
            pl.ds(first, spec["rows"]), pl.ds(spec["to_column"], spec["columns"])
        ]

    inbound = {}

    def start_item(item):
        first, second = items[item]["route"]
        for slot, peer in enumerate(
            (across(dp, blk, bits, first), across(dp, blk, bits, second), sibling)
        ):
            copy = remote(
                own_part(item),
                block(item, dp),
                send_sem.at[item, slot],
                recv_sem.at[item, slot],
                peer,
            )
            copy.start()
            inbound[item, slot] = copy
        copy = pltpu.make_async_copy(own_part(item), block(item, dp), local_sem.at[item])
        copy.start()
        inbound[item, "own"] = copy

    def pass_on(item, held, slot, peer):
        copy = remote(held, held, send_sem.at[item, slot], recv_sem.at[item, slot], peer)
        copy.start()
        inbound[item, slot] = copy

    def relay_first(item):
        first, second = items[item]["route"]
        inbound[item, 0].wait_recv()
        held = block(item, across(dp, blk, bits, first)[0])
        pass_on(item, held, 3, across(dp, blk, bits, second))
        pass_on(item, held, 4, sibling)
        inbound[item, 1].wait_recv()
        pass_on(item, block(item, across(dp, blk, bits, second)[0]), 5, sibling)

    def relay_third(item):
        first, second = items[item]["route"]
        inbound[item, 3].wait_recv()
        pass_on(item, block(item, across(dp, blk, bits, first, second)[0]), 6, sibling)

    def all_here(item):
        for slot in (2, 4, 5, 6):
            inbound[item, slot].wait_recv()
        inbound[item, "own"].wait()

    early = [i for i, spec in enumerate(items) if spec["target"] < 2]
    late = [i for i, spec in enumerate(items) if spec["target"] >= 2]
    for item in early:
        start_item(item)
    for step, peer in enumerate(ring):
        copy = remote(
            seg_shard,
            seg_full.at[pl.ds(blk * seg_rows, seg_rows)],
            seg_send.at[step],
            seg_recv.at[step],
            peer,
        )
        copy.start()
        waiting.append(copy)
    for item in late:
        start_item(item)
    seg_full[pl.ds(blk * seg_rows, seg_rows)] = seg_shard[...]
    for m in range(micro):
        hidden_full[m, mine] = hidden[m]

    for item in early:
        relay_first(item)
    for m in range(micro):
        line_step(m, 1)
    for item in early:
        relay_third(item)
    for copy in waiting:
        copy.wait()
    for member in range(ring_size):
        seg_line[:, member * tokens : (member + 1) * tokens] = seg_full[
            pl.ds(member * seg_rows + row_at, 1)
        ].astype(jnp.float32)
    seg_col[...] = jnp.broadcast_to(seg_line[...], (128, length)).T
    for item in early:
        all_here(item)
    pack_turned = pack_full[...].astype(jnp.float32).T
    piece = width // (pack_full.shape[0] // 16)
    lane = lax.broadcasted_iota(jnp.int32, (piece, pack_full.shape[0]), 1)

    def bias_column(vector):
        pieces = []
        for part in range(group // piece):
            at = (group_at * (group // piece) + part) * 16 + vector
            pieces.append(
                jnp.sum(
                    jnp.where(lane == at, pack_turned[:piece], 0.0), axis=1, keepdims=True
                )
            )
        return jnp.concatenate(pieces, axis=0)

    biases = (bias_column(0), None, bias_column(1))
    for m in range(micro):
        line_step(m, 2)
    for m in range(micro):
        for distance in range(3, ring_size):
            line_step(m, distance)
    row_copy = pltpu.make_async_copy(hidden_full.at[row_at], hidden_row, row_sem.at[0])
    row_copy.start()
    row_copy.wait()
    for part in range(3):
        turned = w_window[:, part * group : (part + 1) * group].T
        for start in range(0, length, tokens):
            values = contract(turned, hidden_row[start : start + tokens, :], 1, 1)
            if biases[part] is not None:
                values = values + biases[part]
            qkv[part * group : (part + 1) * group, start : start + tokens] = values.astype(
                jnp.bfloat16
            )

    copies = []

    def one_head(head):
        def rows(part):
            first = part * group + head * depth
            return slice(first, first + depth)

        keys = qkv[rows(1), :].T
        values_t = qkv[rows(2), :]
        for start in range(0, length, tokens):
            span = slice(start, start + tokens)
            raw = contract(keys, qkv[rows(0), span], 1, 0)
            same = seg_col[:, :1] == seg_line[:, span]
            scores = jnp.where(same, raw * score_scale, NEGATIVE)
            peak = jnp.max(scores, axis=0, keepdims=True)
            weights = jnp.exp(scores - peak)
            total = jnp.sum(weights, axis=0, keepdims=True)
            ctx = contract(values_t, weights.astype(jnp.bfloat16), 1, 0) / total
            context[rows(0), span] = ctx
            low[rows(0), span] = ctx.astype(jnp.bfloat16)
            stats[2 * head : 2 * head + 1, span] = peak
            stats[2 * head + 1 : 2 * head + 2, span] = total
        target = context_t.at[row_at, pl.ds(group_at * group + head * depth, depth)]
        for step in range(1, ring_size):
            owner = lax.rem(blk + step, ring_size)
            copy = remote(
                low.at[rows(0), pl.ds(pl.multiple_of(owner * tokens, tokens), tokens)],
                target,
                head_send.at[head, step],
                head_recv.at[head, step],
                (dp, owner),
            )
            copy.start()
            copies.append(copy)
        target[...] = low[rows(0), mine]

    todo = list(late)
    for head in range(heads):
        one_head(head)
        count = -(-len(todo) // (heads - head))
        for item in todo[:count]:
            relay_first(item)
        todo = todo[count:]
    for item in late:
        relay_third(item)
    for item in late:
        all_here(item)
    for item in range(len(items)):
        for slot in range(7):
            inbound[item, slot].wait_send()
    for copy in copies:
        copy.wait()
    for m in range(micro):
        for side in range(2):
            for distance in range(ring_size - 1):
                ready = passes_on(m, side)
                if distance:
                    ready = ready & comes(m, side, distance)

                @pl.when(ready)
                def _():
                    line_copy(m, side, distance).wait_send()


def forward(shards, items, targets, segments, hidden, ring_size, depth):
    micro, tokens, width = hidden.shape
    count = len(shards)
    length = ring_size * tokens
    group = width * micro // ring_size
    heads = group // depth
    shape = jax.ShapeDtypeStruct
    return pl.pallas_call(
        functools.partial(forward_kernel, items, ring_size, depth, count, len(targets)),
        out_shape=tuple(targets)
        + (
            shape((ring_size * segments.shape[0], tokens), jnp.int32),
            shape((length, width), jnp.bfloat16),
            shape((3 * group, length), jnp.bfloat16),
            shape((group, length), jnp.float32),
            shape((2 * heads, length), jnp.float32),
            shape((micro, width, tokens), jnp.bfloat16),
        ),
        in_specs=[IN_VMEM] * (count + 2),
        out_specs=(IN_VMEM, IN_VMEM) + (ANY,) * (len(targets) - 2) + (IN_VMEM,) * 6,
        scratch_shapes=[
            pltpu.VMEM((micro, length, width), jnp.bfloat16),
            pltpu.VMEM((group, length), jnp.bfloat16),
            pltpu.VMEM((1, length), jnp.float32),
            pltpu.VMEM((length, 128), jnp.float32),
            pltpu.SemaphoreType.DMA((len(items), 7)),
            pltpu.SemaphoreType.DMA((len(items), 7)),
            pltpu.SemaphoreType.DMA((ring_size,)),
            pltpu.SemaphoreType.DMA((ring_size,)),
            pltpu.SemaphoreType.DMA((micro, 2, ring_size)),
            pltpu.SemaphoreType.DMA((micro, 2, ring_size)),
            pltpu.SemaphoreType.DMA((heads, ring_size)),
            pltpu.SemaphoreType.DMA((heads, ring_size)),
            pltpu.SemaphoreType.DMA((len(items),)),
            pltpu.SemaphoreType.DMA((1,)),
        ],
        compiler_params=comm_params(1),
    )(*shards, segments, hidden)


def to_heads_kernel(ring_size, part, out, send_sem, recv_sem):
    dp, blk, _ = place()
    greet([(dp, lax.rem(blk + step, ring_size)) for step in range(1, ring_size)])
    micro, rows, tokens = part.shape
    spread = ring_size // micro
    group = rows // spread
    mine = pl.ds(pl.multiple_of(blk * tokens, tokens), tokens)
    copies = []
    for step in range(1, ring_size):
        owner = lax.rem(blk + step, ring_size)
        copy = remote(
            part.at[owner // spread, pl.ds(lax.rem(owner, spread) * group, group)],
            out.at[:, mine],
            send_sem.at[step],
            recv_sem.at[step],
            (dp, owner),
        )
        copy.start()
        copies.append(copy)
    out[:, mine] = part[blk // spread, pl.ds(lax.rem(blk, spread) * group, group)]
    for copy in copies:
        copy.wait()


def to_heads(part, ring_size, collective):
    micro, rows, tokens = part.shape
    return pl.pallas_call(
        functools.partial(to_heads_kernel, ring_size),
        out_shape=jax.ShapeDtypeStruct((rows * micro // ring_size, tokens * ring_size), part.dtype),
        in_specs=[IN_VMEM],
        out_specs=IN_VMEM,
        scratch_shapes=[
            pltpu.SemaphoreType.DMA((ring_size,)),
            pltpu.SemaphoreType.DMA((ring_size,)),
        ],
        compiler_params=comm_params(collective),
    )(part)


def tables_kernel(ring_size, dp_size, own, out, arrived, send_sem, recv_sem, ring_send, ring_recv):
    dp, blk, _ = place()
    ring = [(dp, lax.rem(blk + step, ring_size)) for step in range(1, ring_size)]
    group = [(lax.rem(dp + step, dp_size), blk) for step in range(1, dp_size)]
    greet(ring + group)
    copies = []
    for step, peer in enumerate(ring):
        copy = remote(own, arrived.at[step], ring_send.at[step], ring_recv.at[step], peer)
        copy.start()
        copies.append(copy)
    for copy in copies:
        copy.wait()
    total = own[...].astype(jnp.float32)
    for step in range(ring_size - 1):
        total = total + arrived[step].astype(jnp.float32)
    out[dp] = total.astype(out.dtype)
    copies = []
    for step, peer in enumerate(group):
        copy = remote(out.at[dp], out.at[dp], send_sem.at[step], recv_sem.at[step], peer)
        copy.start()
        copies.append(copy)
    for copy in copies:
        copy.wait()


def gather_tables(own, ring_size, dp_size):
    return pl.pallas_call(
        functools.partial(tables_kernel, ring_size, dp_size),
        out_shape=jax.ShapeDtypeStruct((dp_size,) + own.shape, own.dtype),
        in_specs=[IN_VMEM],
        out_specs=IN_VMEM,
        scratch_shapes=[
            pltpu.VMEM((ring_size - 1,) + own.shape, own.dtype),
            pltpu.SemaphoreType.DMA((dp_size,)),
            pltpu.SemaphoreType.DMA((dp_size,)),
            pltpu.SemaphoreType.DMA((ring_size,)),
            pltpu.SemaphoreType.DMA((ring_size,)),
        ],
        compiler_params=comm_params(4),
    )(own)


def added(left, right):
    return (left.astype(jnp.float32) + right.astype(jnp.float32)).astype(jnp.bfloat16)


def reduce_kernel(items, ring_size, *refs):
    count = len(items)
    inputs = 1 + max(item["source"] for item in items)
    grads, outs = refs[:inputs], refs[inputs : 2 * inputs]
    own, from_core, from_first, from_second, ring_one, ring_two, ring_three = refs[
        2 * inputs : 2 * inputs + 7
    ]
    send_sem, recv_sem, local_sem = refs[2 * inputs + 7 :]
    dp, blk, bits = place()
    sibling = across(dp, blk, bits, "c")
    is_end = (blk == 0) | (blk == 3)
    is_middle = (blk == 1) | (blk == 2)
    partner = (dp, blk + 1 - 2 * lax.rem(blk, 2))
    facing = (dp, 3 - blk)
    ring = [(dp, lax.rem(blk + step, ring_size)) for step in range(1, ring_size)]
    greet([sibling, across(dp, blk, bits, "x"), across(dp, blk, bits, "y")] + ring)

    def owner(core, axes, first_bit, second_bit):
        return core + SIDE[axes[0]] * first_bit + SIDE[axes[1]] * second_bit

    def block(item, which):
        spec = items[item]
        return grads[spec["source"]].at[
            pl.ds(which * spec["stride"] + spec["row"], spec["rows"]),
            pl.ds(spec["column"], spec["columns"]),
        ]

    def cut(buffer, item, *index):
        spec = items[item]
        return buffer.at[(item,) + index + (pl.ds(0, spec["rows"]), pl.ds(0, spec["columns"]))]

    def wide_cut(buffer, item, *index):
        spec = items[item]
        columns = spec["columns"] * spec["widened"]
        return buffer.at[(item,) + index + (pl.ds(0, spec["rows"]), pl.ds(0, columns))]

    def result(item):
        spec = items[item]
        many = spec["widened"]
        return outs[spec["source"]].at[
            pl.ds(spec["row"], spec["rows"]),
            pl.ds(spec["column"] * many, spec["columns"] * many),
        ]

    def copier(source, target, item, slot, peer):
        return remote(source, target, send_sem.at[item, slot], recv_sem.at[item, slot], peer)

    def go(source, target, item, slot, peer):
        copy = copier(source, target, item, slot, peer)
        copy.start()
        return copy

    flying = {}

    def start_core(item):
        axes = items[item]["route"]
        for f in range(2):
            for s in range(2):
                slot = 2 * f + s
                flying[item, slot] = go(
                    block(item, owner(1 - bits["c"], axes, f, s)),
                    cut(from_core, item, f, s),
                    item,
                    slot,
                    sibling,
                )
                mine = pltpu.make_async_copy(
                    block(item, owner(bits["c"], axes, f, s)),
                    cut(own, item, f, s),
                    local_sem.at[item, slot],
                )
                mine.start()
                flying[item, "own", slot] = mine

    def after_core(item):
        axes = items[item]["route"]
        mine = bits[axes[0]]
        for slot in range(4):
            flying[item, slot].wait_recv()
            flying[item, "own", slot].wait()
        for f in (1 - mine, mine):
            for s in range(2):
                part = cut(own, item, f, s)
                part[...] = added(part[...], cut(from_core, item, f, s)[...])
                if f is not mine:
                    flying[item, 4 + s] = go(
                        part,
                        cut(from_first, item, s),
                        item,
                        4 + s,
                        across(dp, blk, bits, axes[0]),
                    )

    def after_first(item):
        axes = items[item]["route"]
        f, mine = bits[axes[0]], bits[axes[1]]
        for s in range(2):
            flying[item, 4 + s].wait_recv()
        part = cut(own, item, f, 1 - mine)
        part[...] = added(part[...], cut(from_first, item, 1 - mine)[...])
        flying[item, 6] = go(
            part, cut(from_second, item), item, 6, across(dp, blk, bits, axes[1])
        )
        part = cut(own, item, f, mine)
        part[...] = added(part[...], cut(from_first, item, mine)[...])

    def after_second(item):
        axes = items[item]["route"]
        f, s = bits[axes[0]], bits[axes[1]]
        flying[item, 6].wait_recv()
        total = added(cut(own, item, f, s)[...], cut(from_second, item)[...])
        spec = items[item]
        if spec["widened"] > 1:
            wide_cut(ring_one, item, 0)[...] = jnp.zeros(
                (spec["rows"], spec["columns"] * spec["widened"]), jnp.bfloat16
            )
            at = pl.multiple_of(lax.rem(blk, spec["widened"]) * spec["columns"], 128)
            ring_one[item, 0, pl.ds(0, spec["rows"]), pl.ds(at, spec["columns"])] = total
        else:
            wide_cut(ring_one, item, 0)[...] = total
        flying[item, 7] = copier(
            wide_cut(ring_one, item, 0), wide_cut(ring_one, item, 1), item, 7, partner
        )
        flying[item, 8] = copier(wide_cut(ring_two, item, 0), wide_cut(ring_two, item, 1), item, 8, facing)
        flying[item, 9] = copier(result(item), result(item), item, 9, partner)

        @pl.when(is_end)
        def _():
            flying[item, 7].start()

    def at_middle(item):
        @pl.when(is_middle)
        def _():
            flying[item, 7].wait_recv()
            part = wide_cut(ring_two, item, 0)
            part[...] = added(wide_cut(ring_one, item, 0)[...], wide_cut(ring_one, item, 1)[...])
            flying[item, 8].start()

    def across_middle(item):
        @pl.when(is_middle)
        def _():
            flying[item, 8].wait_recv()
            result(item)[...] = added(wide_cut(ring_two, item, 0)[...], wide_cut(ring_two, item, 1)[...])
            flying[item, 9].start()

    def at_end(item):
        @pl.when(is_end)
        def _():
            flying[item, 9].wait_recv()

    stages = (after_core, after_first, after_second, at_middle, across_middle, at_end)
    for item in range(count):
        start_core(item)
    for tick in range(count + len(stages) - 1):
        for depth in reversed(range(len(stages))):
            item = tick - depth
            if 0 <= item < count:
                stages[depth](item)
    for item in range(count):
        for slot in range(7):
            flying[item, slot].wait_send()

    @pl.when(is_end)
    def _():
        for item in range(count):
            flying[item, 7].wait_send()

    @pl.when(is_middle)
    def _():
        for item in range(count):
            flying[item, 8].wait_send()
            flying[item, 9].wait_send()


def reduce_all(grads, items, dp_size, ring_size, collective):
    count = len(items)
    inputs = len(grads)
    rows = max(item["rows"] for item in items)
    columns = max(item["columns"] * item["widened"] for item in items)
    piece = (rows, columns)
    outs = []
    for index, grad in enumerate(grads):
        widened = max(item["widened"] for item in items if item["source"] == index)
        shard = (grad.shape[0] // dp_size, grad.shape[1] * widened)
        outs.append(jax.ShapeDtypeStruct(shard, jnp.bfloat16))
    scratch = [
        pltpu.VMEM((count,) + lead + piece, jnp.bfloat16)
        for lead in ((2, 2), (2, 2), (2,), (), (2,), (2,), (2,))
    ]
    return pl.pallas_call(
        functools.partial(reduce_kernel, items, ring_size),
        out_shape=tuple(outs),
        in_specs=[ANY] * inputs,
        out_specs=(IN_VMEM,) * inputs,
        scratch_shapes=scratch
        + [
            pltpu.SemaphoreType.DMA((count, 10)),
            pltpu.SemaphoreType.DMA((count, 10)),
            pltpu.SemaphoreType.DMA((count, 4)),
        ],
        compiler_params=comm_params(collective),
    )(*grads)


def scatter_line_kernel(micro, ring_size, parts, out, passed, arrived, send_sem, recv_sem):
    dp, blk, _ = place()
    greet_line(dp, blk, ring_size)
    spread = ring_size // micro
    low = [m * spread for m in range(micro)]
    high = [m * spread + spread - 1 for m in range(micro)]

    def owns(m):
        return (blk >= low[m]) & (blk <= high[m])

    def receives(m, side):
        return blk + 1 <= high[m] if side == 0 else blk - 1 >= low[m]

    def has_target(side, distance):
        return blk >= distance if side == 0 else blk + distance < ring_size

    def hop(source, m, side, distance):
        return remote(
            source,
            arrived.at[m, side, distance - 1],
            send_sem.at[m, side, distance],
            recv_sem.at[m, side, distance - 1],
            (dp, blk - 1 + 2 * side),
        )

    def arrival(m, side, distance):
        view = arrived.at[m, side, distance]
        return remote(
            view,
            view,
            send_sem.at[m, side, distance],
            recv_sem.at[m, side, distance],
            (dp, blk - 1 + 2 * side),
        )

    for distance in reversed(range(1, ring_size)):
        for m in range(micro):
            for side in range(2):
                target = blk - distance * (1 - 2 * side)
                comes, goes = receives(m, side), has_target(side, distance)
                if distance < ring_size - 1:

                    @pl.when(goes & comes & owns(m))
                    def _():
                        arrival(m, side, distance).wait_recv()
                        passed[m, side, distance] = added(
                            parts[target], arrived[m, side, distance]
                        )
                        hop(passed.at[m, side, distance], m, side, distance).start()

                    @pl.when(goes & comes & jnp.logical_not(owns(m)))
                    def _():
                        arrival(m, side, distance).wait_recv()
                        hop(arrived.at[m, side, distance], m, side, distance).start()

                @pl.when(goes & jnp.logical_not(comes) & owns(m))
                def _():
                    hop(parts.at[target], m, side, distance).start()

    for m in range(micro):

        @pl.when(owns(m))
        def _():
            out[m] = parts[blk].astype(jnp.float32)

        @pl.when(jnp.logical_not(owns(m)))
        def _():
            out[m] = jnp.zeros(out.shape[1:], jnp.float32)

        for side in range(2):
            inside = blk < ring_size - 1 if side == 0 else blk > 0

            @pl.when(receives(m, side) & inside)
            def _():
                arrival(m, side, 0).wait_recv()
                out[m] += arrived[m, side, 0].astype(jnp.float32)

    for distance in range(1, ring_size):
        for m in range(micro):
            for side in range(2):

                @pl.when(has_target(side, distance) & (receives(m, side) | owns(m)))
                def _():
                    hop(passed.at[m, side, distance], m, side, distance).wait_send()


def greet_line(dp, blk, ring_size):
    barrier = pltpu.get_barrier_semaphore()

    @pl.when(blk > 0)
    def _():
        pl.semaphore_signal(barrier, inc=1, device_id=(dp, blk - 1), device_id_type=MESH)

    @pl.when(blk < ring_size - 1)
    def _():
        pl.semaphore_signal(barrier, inc=1, device_id=(dp, blk + 1), device_id_type=MESH)

    @pl.when((blk > 0) & (blk < ring_size - 1))
    def _():
        pl.semaphore_wait(barrier, 2)

    @pl.when((blk == 0) | (blk == ring_size - 1))
    def _():
        pl.semaphore_wait(barrier, 1)


def scatter_line(parts, micro, ring_size, collective):
    _, tokens, width = parts.shape
    return pl.pallas_call(
        functools.partial(scatter_line_kernel, micro, ring_size),
        out_shape=jax.ShapeDtypeStruct((micro, tokens, width), jnp.float32),
        in_specs=[IN_VMEM],
        out_specs=IN_VMEM,
        scratch_shapes=[
            pltpu.VMEM((micro, 2, ring_size, tokens, width), jnp.bfloat16),
            pltpu.VMEM((micro, 2, ring_size, tokens, width), jnp.bfloat16),
            pltpu.SemaphoreType.DMA((micro, 2, ring_size)),
            pltpu.SemaphoreType.DMA((micro, 2, ring_size)),
        ],
        compiler_params=comm_params(collective),
    )(parts)


def contract(left, right, left_dim, right_dim):
    return lax.dot_general(
        left, right, (((left_dim,), (right_dim,)), ((), ())), preferred_element_type=jnp.float32
    )


def columns_of(row):
    return jnp.broadcast_to(row, (128, row.shape[1])).T[:, :1]


def attend_back_kernel(
    score_scale, depth, block, qkv, seg_row, context, stats, dcontext, dwindow
):
    group, length = context.shape
    seg_line = seg_row[...].astype(jnp.float32)
    seg_col = columns_of(seg_line)

    def one_head(head):
        def rows(part):
            return pl.ds(part * group + head * depth, depth)

        queries_t, keys_t, values_t = qkv[rows(0)], qkv[rows(1)], qkv[rows(2)]
        keys, values = keys_t.T, values_t.T
        dkey_sum = jnp.zeros((depth, length), jnp.float32)
        dvalue_sum = jnp.zeros((depth, length), jnp.float32)
        for start in range(0, length, block):
            span = slice(start, start + block)
            peak, total = stats[2 * head : 2 * head + 1, span], stats[2 * head + 1 : 2 * head + 2, span]
            dctx = dcontext[rows(0), span].astype(jnp.float32)
            push = (dctx / total).astype(jnp.bfloat16)
            delta = jnp.sum(dctx * context[rows(0), span], axis=0, keepdims=True) / total
            raw = contract(keys, queries_t[:, span], 1, 0)
            same = seg_col == seg_line[:, span]
            weights = jnp.exp(jnp.where(same, raw * score_scale, NEGATIVE) - peak)
            pushed = contract(values, push, 1, 0)
            dscore = (weights * (pushed - delta) * score_scale).astype(jnp.bfloat16)
            dwindow[rows(0), span] = contract(keys_t, dscore, 1, 0).astype(jnp.bfloat16)
            dkey_sum = dkey_sum + contract(queries_t[:, span], dscore, 1, 1)
            dvalue_sum = dvalue_sum + contract(push, weights.astype(jnp.bfloat16), 1, 1)
        dwindow[rows(1)] = dkey_sum.astype(jnp.bfloat16)
        dwindow[rows(2)] = dvalue_sum.astype(jnp.bfloat16)

    for head in range(group // depth):
        one_head(head)


def attend_back(qkv, seg_row, context, stats, dcontext, score_scale, depth):
    length = qkv.shape[1]
    return pl.pallas_call(
        functools.partial(attend_back_kernel, score_scale, depth, min(256, length)),
        out_shape=jax.ShapeDtypeStruct(qkv.shape, jnp.bfloat16),
        in_specs=[IN_VMEM] * 5,
        out_specs=IN_VMEM,
        compiler_params=pltpu.CompilerParams(vmem_limit_bytes=VMEM_LIMIT),
    )(qkv, seg_row, context, stats, dcontext)


def fast_body(
    hidden_in,
    segment_ids,
    queries,
    targets,
    cotangent,
    query_weight,
    key_weight,
    value_weight,
    output_weight,
    query_bias,
    value_bias,
    output_bias,
    first_gain,
    first_shift,
    inner_weight,
    inner_bias,
    outer_weight,
    outer_bias,
    second_gain,
    second_shift,
):
    dp_size, ring_size = lax.axis_size("dp"), lax.axis_size("blk")
    dp, blk = lax.axis_index("dp"), lax.axis_index("blk")
    micro, row_count, block_tokens, width = hidden_in.shape
    row_queries = queries.shape[1]
    length = block_tokens * ring_size
    head_dim = width // HEADS
    spread = ring_size // micro
    own_heads = HEADS // spread
    score_scale = 1.0 / math.sqrt(head_dim)
    tokens = micro * block_tokens
    wide = jnp.float32
    narrow = jnp.bfloat16

    vectors = (
        query_bias,
        value_bias,
        output_bias,
        first_gain,
        first_shift,
        outer_bias,
        second_gain,
        second_shift,
        inner_bias,
    )
    piece = vectors[0].shape[0]
    inner_piece = inner_bias.shape[0]
    group = own_heads * head_dim
    row_at, group_at = blk // spread, lax.rem(blk, spread) * group
    hidden_rows = hidden_in.reshape(micro, block_tokens, width)
    pack = jnp.concatenate(
        (
            jnp.pad(jnp.stack(vectors[:8]), ((0, 0), (0, inner_piece - piece))),
            jnp.pad(inner_bias[None], ((0, 7), (0, 0))),
        )
    )
    target_pack = jnp.pad(targets, ((0, 8 - micro), (0, 128 - row_queries)))
    seg_pack = jnp.pad(segment_ids.reshape(micro, block_tokens), ((0, 8 - micro), (0, 0)))
    shards = (
        query_weight,
        key_weight,
        value_weight,
        pack,
        target_pack,
        queries.reshape(micro * row_queries, width),
        output_weight,
        inner_weight,
        outer_weight,
    )
    ways = (("x", "y"), ("y", "x"))
    items = []

    def add_item(source, target, row=0, rows=None, from_column=0, columns=None, to_column=0):
        shape = shards[source].shape
        items.append(
            {
                "source": source,
                "target": target,
                "row": row,
                "rows": rows or shape[0],
                "stride": shape[0],
                "from_column": from_column,
                "columns": columns or shape[1],
                "to_column": to_column,
                "route": ways[len(items) % 2],
            }
        )

    for index in range(3):
        add_item(index, 0, from_column=None, columns=group, to_column=index * group)
    for index in range(3, 7):
        add_item(index, index - 2)
    for part in range(4):
        add_item(
            7, 5, from_column=part * width, columns=width, to_column=part * width
        )
        add_item(8, 6, row=part * piece, rows=piece)
    targets_out = [jax.ShapeDtypeStruct((width, 3 * group), narrow)] + [
        jax.ShapeDtypeStruct((dp_size * s.shape[0], s.shape[1]), s.dtype) for s in shards[3:]
    ]
    (
        w_window,
        pack_all,
        targets_all,
        queries_all,
        wo_full,
        w_inner,
        w_outer,
        seg_all,
        hidden_row,
        qkv,
        context,
        stats,
        context_t,
    ) = forward(shards, items, targets_out, seg_pack, hidden_rows, ring_size, head_dim)
    pack_rows = pack_all.reshape(dp_size, 16, inner_piece)
    eight = pack_rows[:, :8, :piece].transpose(1, 0, 2).reshape(8, width).astype(wide)
    bq_full, bv_full, bo_full, gain_one, shift_one, b_outer, gain_two, shift_two = eight
    b_inner = pack_rows[:, 8].reshape(-1).astype(wide)
    targets_all = (
        targets_all.reshape(dp_size, 8, 128)[:, :micro, :row_queries]
        .transpose(1, 0, 2)
        .reshape(micro, dp_size * row_queries)
    )
    queries_all = (
        queries_all.reshape(dp_size, micro, row_queries, width)
        .transpose(1, 0, 2, 3)
        .reshape(micro, dp_size * row_queries, width)
    )
    seg_row = (
        seg_all.reshape(ring_size, 8, block_tokens)[:, :micro]
        .transpose(1, 0, 2)
        .reshape(micro, 1, length)
    )
    seg_mine = lax.dynamic_slice(seg_row, (row_at, 0, 0), (1, 1, length)).reshape(1, length)

    flat_rows = hidden_in.reshape(tokens, width)
    attended = (
        jnp.einsum("met,ed->mtd", context_t, wo_full, preferred_element_type=wide).reshape(
            tokens, width
        )
        + bo_full
    )
    first_out, first_normed, first_factor = layer_norm(
        flat_rows.astype(wide) + attended, gain_one, shift_one
    )
    first_low = first_out.astype(narrow)
    inner_pre = jnp.dot(first_low, w_inner, preferred_element_type=wide) + b_inner
    active = jax.nn.gelu(inner_pre, approximate=False).astype(narrow)
    outer_out = jnp.dot(active, w_outer, preferred_element_type=wide) + b_outer
    output, second_normed, second_factor = layer_norm(first_out + outer_out, gain_two, shift_two)
    output_low = output.astype(narrow)
    output_rows = output_low.reshape(micro, block_tokens, width)

    segment = segment_ids.reshape(micro, block_tokens)
    padded = jnp.pad(seg_row.reshape(micro, length), ((0, 0), (1, 0)), constant_values=-1)
    before = lax.dynamic_slice(padded, (0, blk * block_tokens), (micro, block_tokens))
    numbers = jnp.arange(row_queries, dtype=jnp.int32)
    select = (
        (segment != before)[:, None, :] & (segment[:, None, :] == numbers[None, :, None])
    ).astype(wide)
    own_table = jnp.einsum(
        "msi,mid->msd", select.astype(narrow), output_rows, preferred_element_type=wide
    ).astype(narrow)
    tables = gather_tables(own_table.reshape(micro * row_queries, width), ring_size, dp_size)
    tables = tables.reshape(dp_size, micro, row_queries, width)
    everyone = tables.transpose(1, 0, 2, 3).reshape(micro, dp_size * row_queries, width)
    embeddings = lax.dynamic_index_in_dim(tables, dp, 0, keepdims=False)
    query_scores = jnp.einsum("mqd,mpd->mqp", queries_all, everyone, preferred_element_type=wide)
    score_peak = jnp.max(query_scores, axis=2, keepdims=True)
    log_total = score_peak[..., 0] + jnp.log(jnp.sum(jnp.exp(query_scores - score_peak), axis=2))
    target_hot = (
        jnp.arange(query_scores.shape[2], dtype=jnp.int32)[None, None, :]
        == targets_all[:, :, None]
    ).astype(wide)
    losses = log_total - jnp.sum(query_scores * target_hot, axis=2)
    query_loss = lax.dynamic_slice(losses, (0, dp * row_queries), (micro, row_queries))
    dscore_query = jnp.exp(query_scores - log_total[..., None]) - target_hot
    own_dscore = lax.dynamic_slice(
        dscore_query, (0, dp * row_queries, 0), (micro, row_queries, dp_size * row_queries)
    )
    query_grad = jnp.einsum("mqp,mpd->mqd", own_dscore, everyone.astype(wide), precision=PRECISE)
    own_columns = lax.dynamic_slice(
        dscore_query, (0, 0, dp * row_queries), (micro, dp_size * row_queries, row_queries)
    )
    embed_grad = jnp.einsum(
        "mqs,mqd->msd", own_columns, queries_all.astype(wide), precision=PRECISE
    )
    cls_grad = jnp.einsum("msi,msd->mid", select, embed_grad, precision=PRECISE)
    dout = cotangent.reshape(tokens, width).astype(wide) + cls_grad.reshape(tokens, width)
    gain_two_grad = jnp.sum(dout * second_normed, axis=0)
    shift_two_grad = jnp.sum(dout, axis=0)
    dsecond = norm_back(dout, second_normed, second_factor, gain_two)
    douter = dsecond.astype(narrow)
    outer_bias_grad = jnp.sum(douter.astype(wide), axis=0)
    outer_weight_grad = jnp.einsum(
        "nf,nd->fd", active, douter, preferred_element_type=wide
    ).astype(narrow)
    dactive = jnp.einsum("nd,fd->nf", douter, w_outer, preferred_element_type=wide)
    dinner = (dactive * gelu_slope(inner_pre)).astype(narrow)
    inner_bias_grad = jnp.sum(dinner.astype(wide), axis=0)
    inner_weight_grad = jnp.einsum(
        "nd,nf->df", first_low, dinner, preferred_element_type=wide
    ).astype(narrow)
    dfirst = dsecond + jnp.einsum("nf,df->nd", dinner, w_inner, preferred_element_type=wide)
    gain_one_grad = jnp.sum(dfirst * first_normed, axis=0)
    shift_one_grad = jnp.sum(dfirst, axis=0)
    dresidual = norm_back(dfirst, first_normed, first_factor, gain_one)
    dattended = dresidual.astype(narrow)
    output_bias_grad = jnp.sum(dattended.astype(wide), axis=0)
    datt_rows = dattended.reshape(micro, block_tokens, width)
    output_weight_grad = jnp.einsum(
        "met,mtd->ed", context_t, datt_rows, preferred_element_type=wide
    ).astype(narrow)
    dcontext_t = jnp.einsum(
        "mtd,ed->met", datt_rows, wo_full, preferred_element_type=wide
    ).astype(narrow)
    dcontext = to_heads(dcontext_t, ring_size, 5)
    dwindow = attend_back(qkv, seg_mine, context, stats, dcontext, score_scale, head_dim)
    dhidden_parts = jnp.einsum(
        "et,de->td", dwindow, w_window, preferred_element_type=wide
    ).astype(narrow)
    dhidden = dresidual.reshape(micro, block_tokens, width) + scatter_line(
        dhidden_parts.reshape(ring_size, block_tokens, width), micro, ring_size, 6
    )
    window_grad = jnp.einsum(
        "td,et->de", hidden_row, dwindow, preferred_element_type=wide
    ).astype(narrow)
    bias_grads = jnp.sum(dwindow.astype(wide), axis=1)
    query_bias_grad, value_bias_grad = (
        lax.dynamic_update_slice(
            jnp.zeros((width,), wide), bias_grads[at : at + group], (group_at,)
        )
        for at in (0, 2 * group)
    )
    vector_grads = jnp.stack(
        (
            query_bias_grad,
            value_bias_grad,
            output_bias_grad,
            gain_one_grad,
            shift_one_grad,
            outer_bias_grad,
            gain_two_grad,
            shift_two_grad,
        )
    ).astype(narrow)
    grad_pack = jnp.pad(
        jnp.concatenate(
            (
                jnp.pad(
                    vector_grads.reshape(8, dp_size, piece).transpose(1, 0, 2),
                    ((0, 0), (0, 0), (0, inner_piece - piece)),
                ),
                inner_bias_grad.astype(narrow).reshape(dp_size, 1, inner_piece),
            ),
            axis=1,
        ),
        ((0, 0), (0, 7), (0, 0)),
    ).reshape(dp_size * 16, inner_piece)
    grads = (outer_weight_grad, inner_weight_grad, output_weight_grad, window_grad, grad_pack)
    sums = []

    def add_sum(source, row=0, rows=None, column=0, columns=None, widened=1):
        shape = grads[source].shape
        sums.append(
            {
                "source": source,
                "row": row,
                "rows": rows or shape[0] // dp_size,
                "stride": shape[0] // dp_size,
                "column": column,
                "columns": columns or shape[1],
                "widened": widened,
                "route": ways[len(sums) % 2],
            }
        )

    for part in range(4):
        add_sum(0, row=part * piece, rows=piece)
        add_sum(1, column=part * width, columns=width)
    add_sum(2)
    for index in range(3):
        add_sum(3, column=index * group, columns=group, widened=spread)
    add_sum(4)
    d_outer, d_inner, d_wo, d_window, d_pack = reduce_all(grads, sums, dp_size, ring_size, 7)
    d_outer, d_inner, d_wo, d_window, d_pack = (
        part.astype(wide) for part in (d_outer, d_inner, d_wo, d_window, d_pack)
    )
    d_wq, d_wk, d_wv = (d_window[:, i * width : (i + 1) * width] for i in range(3))
    d_bq, d_bv, d_bo, d_g1, d_s1, d_bu, d_g2, d_s2 = (d_pack[i, :piece] for i in range(8))
    d_bi = d_pack[8]
    shape = (micro, row_count, block_tokens, width)
    return (
        output_low.reshape(shape),
        embeddings,
        query_loss,
        query_grad,
        dhidden.astype(narrow).reshape(shape),
        d_wq,
        d_wk,
        d_wv,
        d_wo,
        d_bq,
        d_bv,
        d_bo,
        d_g1,
        d_s1,
        d_inner,
        d_bi,
        d_outer,
        d_bu,
        d_g2,
        d_s2,
    )


def solution(mesh):
    in_specs = (
        P(None, "dp", "blk", None),
        P(None, "dp", "blk"),
        P(None, "dp", None),
        P(None, "dp"),
        P(None, "dp", "blk", None),
        P("dp", None),
        P("dp", None),
        P("dp", None),
        P("dp", None),
        P("dp"),
        P("dp"),
        P("dp"),
        P("dp"),
        P("dp"),
        P("dp", None),
        P("dp"),
        P("dp", None),
        P("dp"),
        P("dp"),
        P("dp"),
    )
    out_specs = (
        P(None, "dp", "blk", None),
        P(None, "dp", None),
        P(None, "dp"),
        P(None, "dp", None),
        P(None, "dp", "blk", None),
        P("dp", None),
        P("dp", None),
        P("dp", None),
        P("dp", None),
        P("dp"),
        P("dp"),
        P("dp"),
        P("dp"),
        P("dp"),
        P("dp", None),
        P("dp"),
        P("dp", None),
        P("dp"),
        P("dp"),
        P("dp"),
    )
    fast = mesh.shape["dp"] == 8 and mesh.shape["blk"] == 4
    body = fast_body if fast else ring_body
    return jax.shard_map(body, mesh=mesh, in_specs=in_specs, out_specs=out_specs, check_vma=False)
```

```python
import functools
import math

import jax
import jax.numpy as jnp
from jax import lax
from jax.experimental import pallas as pl
from jax.experimental.pallas import tpu as pltpu
from jax.sharding import PartitionSpec as P

HEADS = 12


EPSILON = 1e-12
NEGATIVE = -1000000000.0
PRECISE = lax.Precision.HIGHEST


def passed_along(x, axis, by):
    size = lax.axis_size(axis)
    return lax.ppermute(x, axis, [(i, (i + by) % size) for i in range(size)])


def as_sent(x):
    return jax.tree.map(lambda a: a.astype(jnp.bfloat16) if a.dtype == jnp.float32 else a, x)


def layer_norm(values, norm_gain, norm_shift):
    center = values - jnp.mean(values, axis=-1, keepdims=True)
    factor = lax.rsqrt(jnp.mean(center * center, axis=-1, keepdims=True) + EPSILON)
    normed = center * factor
    return (normed * norm_gain + norm_shift, normed, factor)


def norm_back(gradient, normed, factor, norm_gain):
    scaled = gradient * norm_gain
    inner_term = (
        scaled
        - jnp.mean(scaled, axis=-1, keepdims=True)
        - normed * jnp.mean(scaled * normed, axis=-1, keepdims=True)
    )
    return inner_term * factor


def gelu_slope(values):
    normal_cdf = 0.5 * (1.0 + lax.erf(values * (1.0 / math.sqrt(2.0))))
    return normal_cdf + values * jnp.exp(-0.5 * values * values) * (1.0 / math.sqrt(2.0 * math.pi))


def scores_of(query_rows, key_rows, query_segment, key_segment, score_scale):
    raw_scores = jnp.einsum(
        "rqhd,rkhd->rhqk", query_rows, key_rows, preferred_element_type=jnp.float32
    )
    same_doc = (query_segment[:, :, None] == key_segment[:, None, :])[:, None]
    return jnp.where(same_doc, score_scale * raw_scores, NEGATIVE)


def contribute(
    query_rows,
    push_grad,
    delta_term,
    peak_term,
    query_segment,
    key_rows,
    value_rows,
    key_segment,
    score_scale,
):
    scores = scores_of(query_rows, key_rows, query_segment, key_segment, score_scale)
    weights = jnp.exp(scores - peak_term[..., None])
    pushed = jnp.einsum(
        "rqhd,rkhd->rhqk", push_grad, value_rows, preferred_element_type=jnp.float32
    )
    dscore = (weights * (pushed - delta_term[..., None]) * score_scale).astype(jnp.bfloat16)
    query_part = jnp.einsum("rhqk,rkhd->rqhd", dscore, key_rows, preferred_element_type=jnp.float32)
    key_part = jnp.einsum("rhqk,rqhd->rkhd", dscore, query_rows, preferred_element_type=jnp.float32)
    value_part = jnp.einsum(
        "rhqk,rqhd->rkhd",
        weights.astype(jnp.bfloat16),
        push_grad,
        preferred_element_type=jnp.float32,
    )
    return (query_part, key_part, value_part)


def ring_body(
    hidden_in,
    segment_ids,
    queries,
    targets,
    cotangent,
    query_weight,
    key_weight,
    value_weight,
    output_weight,
    query_bias,
    value_bias,
    output_bias,
    first_gain,
    first_shift,
    inner_weight,
    inner_bias,
    outer_weight,
    outer_bias,
    second_gain,
    second_shift,
):
    shards = (
        query_weight,
        key_weight,
        value_weight,
        output_weight,
        query_bias,
        value_bias,
        output_bias,
        first_gain,
        first_shift,
        inner_weight,
        inner_bias,
        outer_weight,
        outer_bias,
        second_gain,
        second_shift,
    )
    cycle_size = lax.axis_size("blk")
    cycle_place = lax.axis_index("blk")
    micro_count, row_count, block_tokens, model_width = hidden_in.shape
    segment_count = queries.shape[1] // row_count
    head_count = HEADS
    head_dim = model_width // head_count
    score_scale = 1.0 / math.sqrt(head_dim)
    token_count = row_count * block_tokens
    head_shape = (row_count, block_tokens, head_count, head_dim)
    grad_totals = tuple((jnp.zeros(shard_piece.shape, jnp.float32) for shard_piece in shards))
    local_sum = None
    gathered = None
    out_list, embed_list, loss_list, qgrad_list, hgrad_list = ([], [], [], [], [])
    for micro_index in range(micro_count):
        gathered = (
            lax.all_gather(shards[0], "dp", axis=0, tiled=True),
            lax.all_gather(shards[1], "dp", axis=0, tiled=True),
            lax.all_gather(shards[2], "dp", axis=0, tiled=True),
            lax.all_gather(shards[3], "dp", axis=0, tiled=True),
            lax.all_gather(shards[4], "dp", axis=0, tiled=True),
            lax.all_gather(shards[5], "dp", axis=0, tiled=True),
            lax.all_gather(shards[6], "dp", axis=0, tiled=True),
            lax.all_gather(shards[7], "dp", axis=0, tiled=True),
            lax.all_gather(shards[8], "dp", axis=0, tiled=True),
            lax.all_gather(shards[9], "dp", axis=0, tiled=True),
            lax.all_gather(shards[10], "dp", axis=0, tiled=True),
            lax.all_gather(shards[11], "dp", axis=0, tiled=True),
            lax.all_gather(shards[12], "dp", axis=0, tiled=True),
            lax.all_gather(shards[13], "dp", axis=0, tiled=True),
            lax.all_gather(shards[14], "dp", axis=0, tiled=True),
        )
        (
            wq_full,
            wk_full,
            wv_full,
            wo_full,
            bq_full,
            bv_full,
            bo_full,
            gain_one,
            shift_one,
            w_inner,
            b_inner,
            w_outer,
            b_outer,
            gain_two,
            shift_two,
        ) = gathered
        gain_one = gain_one.astype(jnp.float32)
        gain_two = gain_two.astype(jnp.float32)
        segment = segment_ids[micro_index]
        flat_rows = hidden_in[micro_index].reshape(token_count, model_width)
        query_rows = (
            (
                jnp.dot(flat_rows, wq_full, preferred_element_type=jnp.float32)
                + bq_full.astype(jnp.float32)
            )
            .astype(jnp.bfloat16)
            .reshape(head_shape)
        )
        key_rows = (
            jnp.dot(flat_rows, wk_full, preferred_element_type=jnp.float32)
            .astype(jnp.bfloat16)
            .reshape(head_shape)
        )
        value_rows = (
            (
                jnp.dot(flat_rows, wv_full, preferred_element_type=jnp.float32)
                + bv_full.astype(jnp.float32)
            )
            .astype(jnp.bfloat16)
            .reshape(head_shape)
        )

        def absorb(softmax_state, visit_keys, visit_values, visit_segment):
            running_peak, running_total, running_sum = softmax_state
            scores = scores_of(query_rows, visit_keys, segment, visit_segment, score_scale)
            new_peak = jnp.maximum(running_peak, jnp.max(scores, axis=-1))
            decay_factor = jnp.exp(running_peak - new_peak)
            weights = jnp.exp(scores - new_peak[..., None])
            running_total = running_total * decay_factor + jnp.sum(weights, axis=-1)
            update = jnp.einsum(
                "rhqk,rkhd->rqhd",
                weights.astype(jnp.bfloat16),
                visit_values,
                preferred_element_type=jnp.float32,
            )
            running_sum = running_sum * jnp.transpose(decay_factor, (0, 2, 1))[..., None] + update
            return (new_peak, running_total, running_sum)

        start_state = (
            jnp.full((row_count, head_count, block_tokens), -1e30, jnp.float32),
            jnp.zeros((row_count, head_count, block_tokens), jnp.float32),
            jnp.zeros(head_shape, jnp.float32),
        )
        first_state = absorb(start_state, key_rows, value_rows, segment)

        def forward_step(cycle_step, cycle_carry):
            visit_keys, visit_values, visit_segment, prior_segment, softmax_state = cycle_carry
            visit_keys, visit_values, visit_segment = passed_along(
                (visit_keys, visit_values, visit_segment), "blk", 1
            )
            prior_segment = jnp.where(cycle_step == 1, visit_segment[:, -1], prior_segment)
            return (
                visit_keys,
                visit_values,
                visit_segment,
                prior_segment,
                absorb(softmax_state, visit_keys, visit_values, visit_segment),
            )

        cycle_carry = lax.fori_loop(
            1, cycle_size, forward_step, (key_rows, value_rows, segment, segment[:, 0], first_state)
        )
        prior_segment = cycle_carry[3]
        row_peak, row_total, running_sum = cycle_carry[4]
        total_heads = jnp.transpose(row_total, (0, 2, 1))[..., None]
        context = running_sum / total_heads
        context_low = context.reshape(token_count, model_width).astype(jnp.bfloat16)
        attended = jnp.dot(
            context_low, wo_full, preferred_element_type=jnp.float32
        ) + bo_full.astype(jnp.float32)
        first_out, first_normed, first_factor = layer_norm(
            flat_rows.astype(jnp.float32) + attended, gain_one, shift_one.astype(jnp.float32)
        )
        first_low = first_out.astype(jnp.bfloat16)
        inner_pre = jnp.dot(
            first_low, w_inner, preferred_element_type=jnp.float32
        ) + b_inner.astype(jnp.float32)
        active = jax.nn.gelu(inner_pre, approximate=False).astype(jnp.bfloat16)
        outer_out = jnp.dot(active, w_outer, preferred_element_type=jnp.float32) + b_outer.astype(
            jnp.float32
        )
        output, second_normed, second_factor = layer_norm(
            first_out + outer_out, gain_two, shift_two.astype(jnp.float32)
        )
        output_low = output.astype(jnp.bfloat16)
        out_list.append(output_low.reshape(row_count, block_tokens, model_width))
        position = cycle_place * block_tokens + jnp.arange(block_tokens, dtype=jnp.int32)
        before = jnp.concatenate([prior_segment[:, None], segment[:, :-1]], axis=1)
        leading = (position[None, :] == 0) | (segment != before)
        numbers = jnp.arange(segment_count, dtype=jnp.int32)
        select = (leading[:, None, :] & (segment[:, None, :] == numbers[None, :, None])).astype(
            jnp.float32
        )
        cls_table = jnp.einsum(
            "rsi,rid->rsd",
            select.astype(jnp.bfloat16),
            output_low.reshape(row_count, block_tokens, model_width),
            preferred_element_type=jnp.float32,
        )
        own_table = lax.psum(cls_table.astype(jnp.bfloat16), "blk").reshape(
            row_count * segment_count, model_width
        )
        embed_list.append(own_table)
        everyone = lax.all_gather(own_table, "dp", axis=0, tiled=True)
        query_vectors = queries[micro_index]
        query_scores = jnp.dot(query_vectors, everyone.T, preferred_element_type=jnp.float32)
        score_peak = jnp.max(query_scores, axis=1, keepdims=True)
        log_total = score_peak[:, 0] + jnp.log(jnp.sum(jnp.exp(query_scores - score_peak), axis=1))
        target_hot = (
            jnp.arange(query_scores.shape[1], dtype=jnp.int32)[None, :]
            == targets[micro_index][:, None]
        ).astype(jnp.float32)
        loss_list.append(log_total - jnp.sum(query_scores * target_hot, axis=1))
        dscore_query = jnp.exp(query_scores - log_total[:, None]) - target_hot
        qgrad_list.append(jnp.dot(dscore_query, everyone.astype(jnp.float32), precision=PRECISE))
        embed_part = jnp.dot(dscore_query.T, query_vectors.astype(jnp.float32), precision=PRECISE)
        embed_grad = (
            lax.psum_scatter(embed_part.astype(jnp.bfloat16), "dp", scatter_dimension=0, tiled=True)
            .astype(jnp.float32)
            .reshape(row_count, segment_count, model_width)
        )
        cls_grad = jnp.einsum("rsi,rsd->rid", select, embed_grad, precision=PRECISE)
        dout = cotangent[micro_index].reshape(token_count, model_width).astype(
            jnp.float32
        ) + cls_grad.reshape(token_count, model_width)
        gain_two_grad = jnp.sum(dout * second_normed, axis=0)
        shift_two_grad = jnp.sum(dout, axis=0)
        dsecond = norm_back(dout, second_normed, second_factor, gain_two)
        douter = dsecond.astype(jnp.bfloat16)
        outer_bias_grad = jnp.sum(douter.astype(jnp.float32), axis=0)
        outer_weight_grad = jnp.einsum(
            "nf,nd->fd", active, douter, preferred_element_type=jnp.float32
        )
        dactive = jnp.einsum("nd,fd->nf", douter, w_outer, preferred_element_type=jnp.float32)
        dinner = (dactive * gelu_slope(inner_pre)).astype(jnp.bfloat16)
        inner_bias_grad = jnp.sum(dinner.astype(jnp.float32), axis=0)
        inner_weight_grad = jnp.einsum(
            "nd,nf->df", first_low, dinner, preferred_element_type=jnp.float32
        )
        dfirst = dsecond + jnp.einsum(
            "nf,df->nd", dinner, w_inner, preferred_element_type=jnp.float32
        )
        gain_one_grad = jnp.sum(dfirst * first_normed, axis=0)
        shift_one_grad = jnp.sum(dfirst, axis=0)
        dresidual = norm_back(dfirst, first_normed, first_factor, gain_one)
        dattended = dresidual.astype(jnp.bfloat16)
        output_bias_grad = jnp.sum(dattended.astype(jnp.float32), axis=0)
        output_weight_grad = jnp.einsum(
            "nd,ne->de", context_low, dattended, preferred_element_type=jnp.float32
        )
        dcontext = jnp.einsum(
            "ne,de->nd", dattended, wo_full, preferred_element_type=jnp.float32
        ).astype(jnp.bfloat16)
        dcontext_wide = dcontext.astype(jnp.float32).reshape(head_shape)
        push_grad = (dcontext_wide / total_heads).astype(jnp.bfloat16)
        delta_term = jnp.transpose(
            jnp.sum(dcontext_wide * context, axis=-1) / total_heads[..., 0], (0, 2, 1)
        )
        own_query, own_key, own_value = contribute(
            query_rows,
            push_grad,
            delta_term,
            row_peak,
            segment,
            key_rows,
            value_rows,
            segment,
            score_scale,
        )

        def key_step(cycle_step, cycle_carry):
            visit_keys, visit_values, visit_segment, query_sum, key_sum, value_sum = cycle_carry
            visit_keys, visit_values, visit_segment = passed_along(
                (visit_keys, visit_values, visit_segment), "blk", 1
            )
            key_sum, value_sum = (
                passed_along(key_sum.astype(jnp.bfloat16), "blk", 1).astype(key_sum.dtype),
                passed_along(value_sum.astype(jnp.bfloat16), "blk", 1).astype(value_sum.dtype),
            )
            query_part, key_part, value_part = contribute(
                query_rows,
                push_grad,
                delta_term,
                row_peak,
                segment,
                visit_keys,
                visit_values,
                visit_segment,
                score_scale,
            )
            return (
                visit_keys,
                visit_values,
                visit_segment,
                query_sum + query_part,
                key_sum + key_part,
                value_sum + value_part,
            )

        back_carry = lax.fori_loop(
            1, cycle_size, key_step, (key_rows, value_rows, segment, own_query, own_key, own_value)
        )
        query_sum = back_carry[3]
        key_sum, value_sum = (
            passed_along(back_carry[4].astype(jnp.bfloat16), "blk", 1).astype(jnp.float32),
            passed_along(back_carry[5].astype(jnp.bfloat16), "blk", 1).astype(jnp.float32),
        )
        dquery = query_sum.astype(jnp.bfloat16).reshape(token_count, model_width)
        dkey = key_sum.astype(jnp.bfloat16).reshape(token_count, model_width)
        dvalue = value_sum.astype(jnp.bfloat16).reshape(token_count, model_width)
        dhidden = dresidual + jnp.einsum(
            "ne,de->nd", dquery, wq_full, preferred_element_type=jnp.float32
        )
        dhidden = dhidden + jnp.einsum(
            "ne,de->nd", dkey, wk_full, preferred_element_type=jnp.float32
        )
        dhidden = dhidden + jnp.einsum(
            "ne,de->nd", dvalue, wv_full, preferred_element_type=jnp.float32
        )
        hgrad_list.append(
            dhidden.astype(jnp.bfloat16).reshape(row_count, block_tokens, model_width)
        )
        local_grads = (
            jnp.einsum("nd,ne->de", flat_rows, dquery, preferred_element_type=jnp.float32),
            jnp.einsum("nd,ne->de", flat_rows, dkey, preferred_element_type=jnp.float32),
            jnp.einsum("nd,ne->de", flat_rows, dvalue, preferred_element_type=jnp.float32),
            output_weight_grad,
            jnp.sum(dquery.astype(jnp.float32), axis=0),
            jnp.sum(dvalue.astype(jnp.float32), axis=0),
            output_bias_grad,
            gain_one_grad,
            shift_one_grad,
            inner_weight_grad,
            inner_bias_grad,
            outer_weight_grad,
            outer_bias_grad,
            gain_two_grad,
            shift_two_grad,
        )
        local_sum = local_grads
        reduced = jax.tree.map(
            lambda part: part.astype(jnp.float32),
            lax.psum_scatter(as_sent(local_sum), "dp", scatter_dimension=0, tiled=True),
        )
        reduced = jax.tree.map(
            lambda part: part.astype(jnp.float32), lax.psum(as_sent(reduced), "blk")
        )
        grad_totals = tuple(
            (total_piece + new_piece for total_piece, new_piece in zip(grad_totals, reduced))
        )
        local_sum = None
    return (
        jnp.stack(out_list),
        jnp.stack(embed_list),
        jnp.stack(loss_list),
        jnp.stack(qgrad_list),
        jnp.stack(hgrad_list),
        grad_totals[0],
        grad_totals[1],
        grad_totals[2],
        grad_totals[3],
        grad_totals[4],
        grad_totals[5],
        grad_totals[6],
        grad_totals[7],
        grad_totals[8],
        grad_totals[9],
        grad_totals[10],
        grad_totals[11],
        grad_totals[12],
        grad_totals[13],
        grad_totals[14],
    )


MESH = pl.DeviceIdType.MESH
VMEM_LIMIT = 60 * 1024 * 1024
SIDE = {"c": 1, "x": 2, "y": 4}


def place():
    dp, blk = lax.axis_index("dp"), lax.axis_index("blk")
    bits = {"c": lax.rem(dp, 2), "x": lax.rem(dp // 2, 2), "y": dp // 4}
    return dp, blk, bits


def across(dp, blk, bits, *axes):
    other = dp
    for axis in axes:
        other = other + SIDE[axis] * (1 - 2 * bits[axis])
    return (other, blk)


def greet(peers):
    barrier = pltpu.get_barrier_semaphore()
    for peer in peers:
        pl.semaphore_signal(barrier, inc=1, device_id=peer, device_id_type=MESH)
    pl.semaphore_wait(barrier, len(peers))


def remote(source, target, send_sem, recv_sem, peer):
    return pltpu.make_async_remote_copy(
        src_ref=source,
        dst_ref=target,
        send_sem=send_sem,
        recv_sem=recv_sem,
        device_id=peer,
        device_id_type=MESH,
    )


def comm_params(collective):
    return pltpu.CompilerParams(
        collective_id=collective, has_side_effects=True, vmem_limit_bytes=VMEM_LIMIT
    )


ANY = pl.BlockSpec(memory_space=pl.ANY)
IN_VMEM = pl.BlockSpec(memory_space=pltpu.VMEM)


def forward_kernel(items, ring_size, depth, sources, places, *refs):
    shards, seg_shard, hidden = refs[:sources], refs[sources], refs[sources + 1]
    outs = refs[sources + 2 :]
    fulls = outs[:places]
    seg_full, hidden_row, qkv, context, stats, context_t = outs[places : places + 6]
    (
        hidden_full,
        low,
        seg_line,
        seg_col,
        send_sem,
        recv_sem,
        seg_send,
        seg_recv,
        line_send,
        line_recv,
        head_send,
        head_recv,
        local_sem,
        row_sem,
    ) = outs[places + 6 :]
    w_window, pack_full = fulls[0], fulls[1]
    dp, blk, bits = place()
    sibling = across(dp, blk, bits, "c")
    ring = [(dp, lax.rem(blk + step, ring_size)) for step in range(1, ring_size)]
    greet([sibling, across(dp, blk, bits, "x"), across(dp, blk, bits, "y")] + ring)
    seg_rows = seg_shard.shape[0]
    micro, tokens, width = hidden.shape
    spread = ring_size // micro
    row_at, group_at = blk // spread, lax.rem(blk, spread)
    group, length = context.shape
    heads = group // depth
    score_scale = 1.0 / math.sqrt(depth)
    waiting = []
    mine = pl.ds(pl.multiple_of(blk * tokens, tokens), tokens)

    def line_view(m, side, distance):
        owner = blk + (1 - 2 * side) * distance
        return hidden_full.at[m, pl.ds(pl.multiple_of(owner * tokens, tokens), tokens)]

    def line_copy(m, side, distance):
        view = line_view(m, side, distance)
        return remote(
            hidden.at[m] if distance == 0 else view,
            view,
            line_send.at[m, side, distance],
            line_recv.at[m, side, distance + 1],
            (dp, blk - 1 + 2 * side),
        )

    def arrival(m, side, distance):
        view = line_view(m, side, distance)
        return remote(
            view,
            view,
            line_send.at[m, side, distance],
            line_recv.at[m, side, distance],
            (dp, blk - 1 + 2 * side),
        )

    def passes_on(m, side):
        return blk > m * spread if side == 0 else blk < m * spread + spread - 1

    def comes(m, side, distance):
        if side == 0:
            return (blk >= m * spread) & (blk + distance < ring_size)
        return (blk < m * spread + spread) & (blk >= distance)

    def line_step(m, distance):
        for side in range(2):

            @pl.when(comes(m, side, distance))
            def _():
                arrival(m, side, distance).wait_recv()

            if distance < ring_size - 1:

                @pl.when(comes(m, side, distance) & passes_on(m, side))
                def _():
                    line_copy(m, side, distance).start()

    for m in range(micro):
        for side in range(2):

            @pl.when(passes_on(m, side))
            def _():
                line_copy(m, side, 0).start()

    def own_part(item):
        spec = items[item]
        column = spec["from_column"]
        if column is None:
            column = pl.multiple_of(group_at * group, group)
        return shards[spec["source"]].at[
            pl.ds(spec["row"], spec["rows"]), pl.ds(column, spec["columns"])
        ]

    def block(item, owner):
        spec = items[item]
        first = owner * spec["stride"] + spec["row"]
        return fulls[spec["target"]].at[
            pl.ds(first, spec["rows"]), pl.ds(spec["to_column"], spec["columns"])
        ]

    inbound = {}

    def start_item(item):
        first, second = items[item]["route"]
        for slot, peer in enumerate(
            (across(dp, blk, bits, first), across(dp, blk, bits, second), sibling)
        ):
            copy = remote(
                own_part(item),
                block(item, dp),
                send_sem.at[item, slot],
                recv_sem.at[item, slot],
                peer,
            )
            copy.start()
            inbound[item, slot] = copy
        copy = pltpu.make_async_copy(own_part(item), block(item, dp), local_sem.at[item])
        copy.start()
        inbound[item, "own"] = copy

    def pass_on(item, held, slot, peer):
        copy = remote(held, held, send_sem.at[item, slot], recv_sem.at[item, slot], peer)
        copy.start()
        inbound[item, slot] = copy

    def relay_first(item):
        first, second = items[item]["route"]
        inbound[item, 0].wait_recv()
        held = block(item, across(dp, blk, bits, first)[0])
        pass_on(item, held, 3, across(dp, blk, bits, second))
        pass_on(item, held, 4, sibling)
        inbound[item, 1].wait_recv()
        pass_on(item, block(item, across(dp, blk, bits, second)[0]), 5, sibling)

    def relay_third(item):
        first, second = items[item]["route"]
        inbound[item, 3].wait_recv()
        pass_on(item, block(item, across(dp, blk, bits, first, second)[0]), 6, sibling)

    def all_here(item):
        for slot in (2, 4, 5, 6):
            inbound[item, slot].wait_recv()
        inbound[item, "own"].wait()

    early = [i for i, spec in enumerate(items) if spec["target"] < 2]
    late = [i for i, spec in enumerate(items) if spec["target"] >= 2]
    for item in early:
        start_item(item)
    for step, peer in enumerate(ring):
        copy = remote(
            seg_shard,
            seg_full.at[pl.ds(blk * seg_rows, seg_rows)],
            seg_send.at[step],
            seg_recv.at[step],
            peer,
        )
        copy.start()
        waiting.append(copy)
    for item in late:
        start_item(item)
    seg_full[pl.ds(blk * seg_rows, seg_rows)] = seg_shard[...]
    for m in range(micro):
        hidden_full[m, mine] = hidden[m]

    for item in early:
        relay_first(item)
    for m in range(micro):
        line_step(m, 1)
    for item in early:
        relay_third(item)
    for copy in waiting:
        copy.wait()
    for member in range(ring_size):
        seg_line[:, member * tokens : (member + 1) * tokens] = seg_full[
            pl.ds(member * seg_rows + row_at, 1)
        ].astype(jnp.float32)
    seg_col[...] = jnp.broadcast_to(seg_line[...], (128, length)).T
    for item in early:
        all_here(item)
    pack_turned = pack_full[...].astype(jnp.float32).T
    piece = width // (pack_full.shape[0] // 16)
    lane = lax.broadcasted_iota(jnp.int32, (piece, pack_full.shape[0]), 1)

    def bias_column(vector):
        pieces = []
        for part in range(group // piece):
            at = (group_at * (group // piece) + part) * 16 + vector
            pieces.append(
                jnp.sum(
                    jnp.where(lane == at, pack_turned[:piece], 0.0), axis=1, keepdims=True
                )
            )
        return jnp.concatenate(pieces, axis=0)

    biases = (bias_column(0), None, bias_column(1))
    for m in range(micro):
        line_step(m, 2)
    for m in range(micro):
        for distance in range(3, ring_size):
            line_step(m, distance)
    row_copy = pltpu.make_async_copy(hidden_full.at[row_at], hidden_row, row_sem.at[0])
    row_copy.start()
    row_copy.wait()
    for part in range(3):
        turned = w_window[:, part * group : (part + 1) * group].T
        for start in range(0, length, tokens):
            values = contract(turned, hidden_row[start : start + tokens, :], 1, 1)
            if biases[part] is not None:
                values = values + biases[part]
            qkv[part * group : (part + 1) * group, start : start + tokens] = values.astype(
                jnp.bfloat16
            )

    copies = []

    def one_head(head):
        def rows(part):
            first = part * group + head * depth
            return slice(first, first + depth)

        keys = qkv[rows(1), :].T
        values_t = qkv[rows(2), :]
        for start in range(0, length, tokens):
            span = slice(start, start + tokens)
            raw = contract(keys, qkv[rows(0), span], 1, 0)
            same = seg_col[:, :1] == seg_line[:, span]
            scores = jnp.where(same, raw * score_scale, NEGATIVE)
            peak = jnp.max(scores, axis=0, keepdims=True)
            weights = jnp.exp(scores - peak)
            total = jnp.sum(weights, axis=0, keepdims=True)
            ctx = contract(values_t, weights.astype(jnp.bfloat16), 1, 0) / total
            context[rows(0), span] = ctx
            low[rows(0), span] = ctx.astype(jnp.bfloat16)
            stats[2 * head : 2 * head + 1, span] = peak
            stats[2 * head + 1 : 2 * head + 2, span] = total
        target = context_t.at[row_at, pl.ds(group_at * group + head * depth, depth)]
        for step in range(1, ring_size):
            owner = lax.rem(blk + step, ring_size)
            copy = remote(
                low.at[rows(0), pl.ds(pl.multiple_of(owner * tokens, tokens), tokens)],
                target,
                head_send.at[head, step],
                head_recv.at[head, step],
                (dp, owner),
            )
            copy.start()
            copies.append(copy)
        target[...] = low[rows(0), mine]

    todo = list(late)
    for head in range(heads):
        one_head(head)
        count = -(-len(todo) // (heads - head))
        for item in todo[:count]:
            relay_first(item)
        todo = todo[count:]
    for item in late:
        relay_third(item)
    for item in late:
        all_here(item)
    for item in range(len(items)):
        for slot in range(7):
            inbound[item, slot].wait_send()
    for copy in copies:
        copy.wait()
    for m in range(micro):
        for side in range(2):
            for distance in range(ring_size - 1):
                ready = passes_on(m, side)
                if distance:
                    ready = ready & comes(m, side, distance)

                @pl.when(ready)
                def _():
                    line_copy(m, side, distance).wait_send()


def forward(shards, items, targets, segments, hidden, ring_size, depth):
    micro, tokens, width = hidden.shape
    count = len(shards)
    length = ring_size * tokens
    group = width * micro // ring_size
    heads = group // depth
    shape = jax.ShapeDtypeStruct
    return pl.pallas_call(
        functools.partial(forward_kernel, items, ring_size, depth, count, len(targets)),
        out_shape=tuple(targets)
        + (
            shape((ring_size * segments.shape[0], tokens), jnp.int32),
            shape((length, width), jnp.bfloat16),
            shape((3 * group, length), jnp.bfloat16),
            shape((group, length), jnp.float32),
            shape((2 * heads, length), jnp.float32),
            shape((micro, width, tokens), jnp.bfloat16),
        ),
        in_specs=[IN_VMEM] * (count + 2),
        out_specs=(IN_VMEM, IN_VMEM) + (ANY,) * (len(targets) - 2) + (IN_VMEM,) * 6,
        scratch_shapes=[
            pltpu.VMEM((micro, length, width), jnp.bfloat16),
            pltpu.VMEM((group, length), jnp.bfloat16),
            pltpu.VMEM((1, length), jnp.float32),
            pltpu.VMEM((length, 128), jnp.float32),
            pltpu.SemaphoreType.DMA((len(items), 7)),
            pltpu.SemaphoreType.DMA((len(items), 7)),
            pltpu.SemaphoreType.DMA((ring_size,)),
            pltpu.SemaphoreType.DMA((ring_size,)),
            pltpu.SemaphoreType.DMA((micro, 2, ring_size)),
            pltpu.SemaphoreType.DMA((micro, 2, ring_size)),
            pltpu.SemaphoreType.DMA((heads, ring_size)),
            pltpu.SemaphoreType.DMA((heads, ring_size)),
            pltpu.SemaphoreType.DMA((len(items),)),
            pltpu.SemaphoreType.DMA((1,)),
        ],
        compiler_params=comm_params(1),
    )(*shards, segments, hidden)


def tables_kernel(ring_size, dp_size, own, out, arrived, send_sem, recv_sem, ring_send, ring_recv):
    dp, blk, _ = place()
    ring = [(dp, lax.rem(blk + step, ring_size)) for step in range(1, ring_size)]
    group = [(lax.rem(dp + step, dp_size), blk) for step in range(1, dp_size)]
    greet(ring + group)
    copies = []
    for step, peer in enumerate(ring):
        copy = remote(own, arrived.at[step], ring_send.at[step], ring_recv.at[step], peer)
        copy.start()
        copies.append(copy)
    for copy in copies:
        copy.wait()
    total = own[...].astype(jnp.float32)
    for step in range(ring_size - 1):
        total = total + arrived[step].astype(jnp.float32)
    out[dp] = total.astype(out.dtype)
    copies = []
    for step, peer in enumerate(group):
        copy = remote(out.at[dp], out.at[dp], send_sem.at[step], recv_sem.at[step], peer)
        copy.start()
        copies.append(copy)
    for copy in copies:
        copy.wait()


def gather_tables(own, ring_size, dp_size):
    return pl.pallas_call(
        functools.partial(tables_kernel, ring_size, dp_size),
        out_shape=jax.ShapeDtypeStruct((dp_size,) + own.shape, own.dtype),
        in_specs=[IN_VMEM],
        out_specs=IN_VMEM,
        scratch_shapes=[
            pltpu.VMEM((ring_size - 1,) + own.shape, own.dtype),
            pltpu.SemaphoreType.DMA((dp_size,)),
            pltpu.SemaphoreType.DMA((dp_size,)),
            pltpu.SemaphoreType.DMA((ring_size,)),
            pltpu.SemaphoreType.DMA((ring_size,)),
        ],
        compiler_params=comm_params(4),
    )(own)


def contract(left, right, left_dim, right_dim):
    return lax.dot_general(
        left, right, (((left_dim,), (right_dim,)), ((), ())), preferred_element_type=jnp.float32
    )


def columns_of(row):
    return jnp.broadcast_to(row, (128, row.shape[1])).T[:, :1]


def added(left, right):
    return (left.astype(jnp.float32) + right.astype(jnp.float32)).astype(jnp.bfloat16)


def backward_kernel(items, ring_size, depth, *refs):
    (
        dcontext_part,
        seg_row,
        pack_part,
        qkv_out,
        context_out,
        stats,
        w_window_out,
        hidden_row_out,
        dresidual_out,
        outer_grad,
        inner_grad,
        output_grad,
    ) = refs[:12]
    dhidden, d_outer, d_inner, d_output, d_window, d_pack = refs[12:18]
    (
        qkv,
        context,
        w_window,
        hidden_row,
        dresidual,
        dcontext,
        dwindow,
        parts,
        passed,
        arrived,
        window_grad,
        pack_sum,
        pack_low,
        own,
        from_core,
        from_first,
        from_second,
        ring_one,
        ring_two,
        load_sem,
        head_send,
        head_recv,
        hop_send,
        hop_recv,
        send_sem,
        recv_sem,
        local_sem,
    ) = refs[18:]
    grads = (outer_grad, inner_grad, output_grad, window_grad, pack_low)
    outs = (d_outer, d_inner, d_output, d_window, d_pack)
    count = len(items)
    dp, blk, bits = place()
    sibling = across(dp, blk, bits, "c")
    is_end = (blk == 0) | (blk == ring_size - 1)
    is_middle = jnp.logical_not(is_end)
    partner = (dp, blk + 1 - 2 * lax.rem(blk, 2))
    facing = (dp, ring_size - 1 - blk)
    ring = [(dp, lax.rem(blk + step, ring_size)) for step in range(1, ring_size)]
    greet([sibling, across(dp, blk, bits, "x"), across(dp, blk, bits, "y")] + ring)

    micro, width, tokens = dcontext_part.shape
    spread = ring_size // micro
    row_at, group_at = blk // spread, lax.rem(blk, spread)
    group, length = context.shape
    heads = group // depth
    score_scale = 1.0 / math.sqrt(depth)
    mine = pl.ds(pl.multiple_of(blk * tokens, tokens), tokens)

    loads = []
    for index, (source, target) in enumerate(
        (
            (qkv_out, qkv),
            (context_out, context),
            (w_window_out, w_window),
            (hidden_row_out, hidden_row),
            (dresidual_out, dresidual),
        )
    ):
        copy = pltpu.make_async_copy(source, target, load_sem.at[index])
        copy.start()
        loads.append(copy)

    head_copies = []
    for head in range(heads):
        for step in range(1, ring_size):
            owner = lax.rem(blk + step, ring_size)
            first = lax.rem(owner, spread) * group + head * depth
            copy = remote(
                dcontext_part.at[owner // spread, pl.ds(first, depth)],
                dcontext.at[pl.ds(head * depth, depth), mine],
                head_send.at[head, step],
                head_recv.at[head, step],
                (dp, owner),
            )
            copy.start()
            head_copies.append(copy)
    dcontext[:, mine] = dcontext_part[row_at, pl.ds(group_at * group, group)]

    def owner_of(core, axes, first_bit, second_bit):
        return core + SIDE[axes[0]] * first_bit + SIDE[axes[1]] * second_bit

    def block(item, which):
        spec = items[item]
        return grads[spec["source"]].at[
            pl.ds(which * spec["stride"] + spec["row"], spec["rows"]),
            pl.ds(spec["column"], spec["columns"]),
        ]

    def cut(buffer, item, *index):
        spec = items[item]
        return buffer.at[(item,) + index + (pl.ds(0, spec["rows"]), pl.ds(0, spec["columns"]))]

    def wide_cut(buffer, item, *index):
        spec = items[item]
        columns = spec["columns"] * spec["widened"]
        return buffer.at[(item,) + index + (pl.ds(0, spec["rows"]), pl.ds(0, columns))]

    def result(item):
        spec = items[item]
        many = spec["widened"]
        return outs[spec["source"]].at[
            pl.ds(spec["row"], spec["rows"]),
            pl.ds(spec["column"] * many, spec["columns"] * many),
        ]

    def copier(source, target, item, slot, peer):
        return remote(source, target, send_sem.at[item, slot], recv_sem.at[item, slot], peer)

    flying = {}

    def go(source, target, item, slot, peer):
        copy = copier(source, target, item, slot, peer)
        copy.start()
        flying[item, slot] = copy

    def start_core(item):
        axes = items[item]["route"]
        for f in range(2):
            for s in range(2):
                slot = 2 * f + s
                go(
                    block(item, owner_of(1 - bits["c"], axes, f, s)),
                    cut(from_core, item, f, s),
                    item,
                    slot,
                    sibling,
                )
                copy = pltpu.make_async_copy(
                    block(item, owner_of(bits["c"], axes, f, s)),
                    cut(own, item, f, s),
                    local_sem.at[item, slot],
                )
                copy.start()
                flying[item, "own", slot] = copy

    def after_core(item):
        axes = items[item]["route"]
        kept = bits[axes[0]]
        for slot in range(4):
            flying[item, slot].wait_recv()
            flying[item, "own", slot].wait()
        for stays, f in ((False, 1 - kept), (True, kept)):
            for s in range(2):
                part = cut(own, item, f, s)
                part[...] = added(part[...], cut(from_core, item, f, s)[...])
                if not stays:
                    peer = across(dp, blk, bits, axes[0])
                    go(part, cut(from_first, item, s), item, 4 + s, peer)

    def after_first(item):
        axes = items[item]["route"]
        f, kept = bits[axes[0]], bits[axes[1]]
        for s in range(2):
            flying[item, 4 + s].wait_recv()
        part = cut(own, item, f, 1 - kept)
        part[...] = added(part[...], cut(from_first, item, 1 - kept)[...])
        go(part, cut(from_second, item), item, 6, across(dp, blk, bits, axes[1]))
        part = cut(own, item, f, kept)
        part[...] = added(part[...], cut(from_first, item, kept)[...])

    def after_second(item):
        spec = items[item]
        axes = spec["route"]
        f, s = bits[axes[0]], bits[axes[1]]
        flying[item, 6].wait_recv()
        total = added(cut(own, item, f, s)[...], cut(from_second, item)[...])
        if spec["widened"] > 1:
            wide_cut(ring_one, item, 0)[...] = jnp.zeros(
                (spec["rows"], spec["columns"] * spec["widened"]), jnp.bfloat16
            )
            at = pl.multiple_of(group_at * spec["columns"], 128)
            ring_one[item, 0, pl.ds(0, spec["rows"]), pl.ds(at, spec["columns"])] = total
        else:
            wide_cut(ring_one, item, 0)[...] = total
        flying[item, 7] = copier(
            wide_cut(ring_one, item, 0), wide_cut(ring_one, item, 1), item, 7, partner
        )
        flying[item, 8] = copier(
            wide_cut(ring_two, item, 0), wide_cut(ring_two, item, 1), item, 8, facing
        )
        flying[item, 9] = copier(result(item), result(item), item, 9, partner)

        @pl.when(is_end)
        def _():
            flying[item, 7].start()

    def at_middle(item):
        @pl.when(is_middle)
        def _():
            flying[item, 7].wait_recv()
            part = wide_cut(ring_two, item, 0)
            part[...] = added(wide_cut(ring_one, item, 0)[...], wide_cut(ring_one, item, 1)[...])
            flying[item, 8].start()

    def across_middle(item):
        @pl.when(is_middle)
        def _():
            flying[item, 8].wait_recv()
            result(item)[...] = added(
                wide_cut(ring_two, item, 0)[...], wide_cut(ring_two, item, 1)[...]
            )
            flying[item, 9].start()

    def at_end(item):
        @pl.when(is_end)
        def _():
            flying[item, 9].wait_recv()

    stages = (after_core, after_first, after_second, at_middle, across_middle, at_end)
    ticks = iter(range(count + len(stages) - 1))

    def advance(times=1):
        for _ in range(times):
            tick = next(ticks, None)
            if tick is None:
                return
            for stage in reversed(range(len(stages))):
                item = tick - stage
                if 0 <= item < count:
                    stages[stage](item)

    early = [i for i, spec in enumerate(items) if spec["source"] < 3]
    late = [i for i, spec in enumerate(items) if spec["source"] >= 3]
    for item in early:
        start_core(item)

    seg_line = seg_row[...].astype(jnp.float32)
    seg_col = columns_of(seg_line)

    def one_head(head):
        def rows(part):
            first = part * group + head * depth
            return slice(first, first + depth)

        for step in range(ring_size - 1):
            head_copies[head * (ring_size - 1) + step].wait_recv()
        keys, values = qkv[rows(1), :].T, qkv[rows(2), :].T
        keys_t = qkv[rows(1), :]
        dkey_sum = jnp.zeros((depth, length), jnp.float32)
        dvalue_sum = jnp.zeros((depth, length), jnp.float32)
        for start in range(0, length, tokens):
            span = slice(start, start + tokens)
            peak = stats[2 * head : 2 * head + 1, span]
            total = stats[2 * head + 1 : 2 * head + 2, span]
            dctx = dcontext[rows(0), span].astype(jnp.float32)
            push = (dctx / total).astype(jnp.bfloat16)
            delta = jnp.sum(dctx * context[rows(0), span], axis=0, keepdims=True) / total
            queries_t = qkv[rows(0), span]
            raw = contract(keys, queries_t, 1, 0)
            same = seg_col == seg_line[:, span]
            weights = jnp.exp(jnp.where(same, raw * score_scale, NEGATIVE) - peak)
            pushed = contract(values, push, 1, 0)
            dscore = (weights * (pushed - delta) * score_scale).astype(jnp.bfloat16)
            dwindow[rows(0), span] = contract(keys_t, dscore, 1, 0).astype(jnp.bfloat16)
            dkey_sum = dkey_sum + contract(queries_t, dscore, 1, 1)
            dvalue_sum = dvalue_sum + contract(push, weights.astype(jnp.bfloat16), 1, 1)
        dwindow[rows(1), :] = dkey_sum.astype(jnp.bfloat16)
        dwindow[rows(2), :] = dvalue_sum.astype(jnp.bfloat16)

    loads[0].wait()
    loads[1].wait()
    for head in range(heads):
        one_head(head)
        advance()
    loads[2].wait()
    loads[3].wait()
    loads[4].wait()

    low = [m * spread for m in range(micro)]
    high = [m * spread + spread - 1 for m in range(micro)]

    def owns(m):
        return (blk >= low[m]) & (blk <= high[m])

    def receives(m, side):
        return blk + 1 <= high[m] if side == 0 else blk - 1 >= low[m]

    def has_target(side, distance):
        return blk >= distance if side == 0 else blk + distance < ring_size

    def hop(source, m, side, distance):
        return remote(
            source,
            arrived.at[m, side, distance - 1],
            hop_send.at[m, side, distance],
            hop_recv.at[m, side, distance - 1],
            (dp, blk - 1 + 2 * side),
        )

    def arrival(m, side, distance):
        view = arrived.at[m, side, distance]
        return remote(
            view,
            view,
            hop_send.at[m, side, distance],
            hop_recv.at[m, side, distance],
            (dp, blk - 1 + 2 * side),
        )

    def send_fresh(distance):
        for m in range(micro):
            for side in range(2):
                target = blk - distance * (1 - 2 * side)
                goes = has_target(side, distance) & owns(m)

                @pl.when(goes & jnp.logical_not(receives(m, side)))
                def _():
                    hop(parts.at[target], m, side, distance).start()

    def send_on(distance):
        for m in range(micro):
            for side in range(2):
                target = blk - distance * (1 - 2 * side)
                goes = has_target(side, distance) & receives(m, side)

                @pl.when(goes & owns(m))
                def _():
                    arrival(m, side, distance).wait_recv()
                    passed[side, distance - 1] = added(parts[target], arrived[m, side, distance])
                    hop(passed.at[side, distance - 1], m, side, distance).start()

                @pl.when(goes & jnp.logical_not(owns(m)))
                def _():
                    arrival(m, side, distance).wait_recv()
                    hop(arrived.at[m, side, distance], m, side, distance).start()

    end = (ring_size - 1) * (1 - row_at)
    inward = 2 * row_at - 1
    order = (end, end + inward, blk + 1 - 2 * lax.rem(blk, 2), blk)

    def make_part(target):
        at = pl.ds(pl.multiple_of(target * tokens, tokens), tokens)
        parts[target] = contract(dwindow[:, at].T, w_window[...], 1, 1).astype(jnp.bfloat16)

    for index, target in enumerate(order):
        make_part(target)
        if index < ring_size - 1:
            send_fresh(ring_size - 1 - index)
    advance()

    ones = jnp.ones((8, length), jnp.bfloat16)
    line = lax.broadcasted_iota(jnp.int32, (8, 128), 0)
    lane = lax.broadcasted_iota(jnp.int32, (8, 128), 1)
    piece = width // (pack_part.shape[0] // 16)
    pack_sum[...] = pack_part[...]
    for part in range(3):
        rows = slice(part * group, (part + 1) * group)
        window_grad[:, rows] = contract(hidden_row[...].T, dwindow[rows, :], 1, 1).astype(
            jnp.bfloat16
        )
        if part != 1:
            sums = contract(ones, dwindow[rows, :], 1, 1)
            sums = jnp.concatenate((sums, jnp.zeros((8, 128), jnp.float32)), axis=1)
            for step in range(group // piece):
                first = pl.multiple_of((group_at * (group // piece) + step) * 16, 16)
                pack_sum[pl.ds(first, 8), 0:128] += jnp.where(
                    (line == part // 2) & (lane < piece),
                    sums[:, step * piece : step * piece + 128],
                    0.0,
                )
        start_core(late[part])
    pack_low[...] = pack_sum[...].astype(jnp.bfloat16)
    start_core(late[3])

    for distance in reversed(range(1, ring_size - 1)):
        advance()
        send_on(distance)
    advance()

    for m in range(micro):
        total = dresidual[m]
        own_part = jnp.where(owns(m), 1.0, 0.0)
        dhidden[m] = (total + own_part * parts[blk].astype(jnp.float32)).astype(jnp.bfloat16)
        for side in range(2):
            inside = blk < ring_size - 1 if side == 0 else blk > 0

            @pl.when(receives(m, side) & inside)
            def _():
                arrival(m, side, 0).wait_recv()

        @pl.when(receives(m, 0) & (blk < ring_size - 1) & jnp.logical_not(owns(m)))
        def _():
            dhidden[m] = (dresidual[m] + arrived[m, 0, 0].astype(jnp.float32)).astype(jnp.bfloat16)

        @pl.when(receives(m, 1) & (blk > 0) & jnp.logical_not(owns(m)))
        def _():
            dhidden[m] = (dresidual[m] + arrived[m, 1, 0].astype(jnp.float32)).astype(jnp.bfloat16)

        @pl.when(receives(m, 0) & (blk < ring_size - 1) & owns(m))
        def _():
            dhidden[m] = (
                dresidual[m]
                + parts[blk].astype(jnp.float32)
                + arrived[m, 0, 0].astype(jnp.float32)
            ).astype(jnp.bfloat16)

        @pl.when(receives(m, 1) & (blk > 0) & owns(m))
        def _():
            dhidden[m] = (
                dresidual[m]
                + parts[blk].astype(jnp.float32)
                + arrived[m, 1, 0].astype(jnp.float32)
            ).astype(jnp.bfloat16)

    advance(count + len(stages))

    for copy in head_copies:
        copy.wait_send()
    for item in range(count):
        for slot in range(7):
            flying[item, slot].wait_send()
    for distance in range(1, ring_size):
        for m in range(micro):
            for side in range(2):

                @pl.when(has_target(side, distance) & (receives(m, side) | owns(m)))
                def _():
                    hop(parts.at[0], m, side, distance).wait_send()

    @pl.when(is_end)
    def _():
        for item in range(count):
            flying[item, 7].wait_send()

    @pl.when(is_middle)
    def _():
        for item in range(count):
            flying[item, 8].wait_send()
            flying[item, 9].wait_send()


def backward(
    dcontext_part,
    seg_row,
    pack_part,
    saved,
    w_window,
    hidden_row,
    dresidual,
    grads,
    items,
    ring_size,
    dp_size,
    depth,
    collective,
):
    qkv, context, stats = saved
    micro, width, tokens = dcontext_part.shape
    group, length = context.shape
    heads = group // depth
    spread = ring_size // micro
    count = len(items)
    rows = max(item["rows"] for item in items)
    columns = max(item["columns"] * item["widened"] for item in items)
    piece = (rows, columns)
    narrow = jnp.bfloat16
    shape = jax.ShapeDtypeStruct
    outs = [shape((grad.shape[0] // dp_size, grad.shape[1]), narrow) for grad in grads]
    outs.append(shape((width // dp_size, 3 * width), narrow))
    outs.append(shape((pack_part.shape[0] // dp_size, pack_part.shape[1]), narrow))
    scratch = [
        pltpu.VMEM(qkv.shape, narrow),
        pltpu.VMEM(context.shape, jnp.float32),
        pltpu.VMEM(w_window.shape, narrow),
        pltpu.VMEM(hidden_row.shape, narrow),
        pltpu.VMEM(dresidual.shape, jnp.float32),
        pltpu.VMEM((group, length), narrow),
        pltpu.VMEM(qkv.shape, narrow),
        pltpu.VMEM((ring_size, tokens, width), narrow),
        pltpu.VMEM((2, ring_size - 2, tokens, width), narrow),
        pltpu.VMEM((micro, 2, ring_size - 1, tokens, width), narrow),
        pltpu.VMEM((width, 3 * group), narrow),
        pltpu.VMEM(pack_part.shape, jnp.float32),
        pltpu.VMEM(pack_part.shape, narrow),
    ]
    scratch += [
        pltpu.VMEM((count,) + lead + piece, narrow)
        for lead in ((2, 2), (2, 2), (2,), (), (2,), (2,))
    ]
    scratch += [
        pltpu.SemaphoreType.DMA((5,)),
        pltpu.SemaphoreType.DMA((heads, ring_size)),
        pltpu.SemaphoreType.DMA((heads, ring_size)),
        pltpu.SemaphoreType.DMA((micro, 2, ring_size)),
        pltpu.SemaphoreType.DMA((micro, 2, ring_size)),
        pltpu.SemaphoreType.DMA((count, 10)),
        pltpu.SemaphoreType.DMA((count, 10)),
        pltpu.SemaphoreType.DMA((count, 4)),
    ]
    return pl.pallas_call(
        functools.partial(backward_kernel, items, ring_size, depth),
        out_shape=(shape((micro, tokens, width), narrow),) + tuple(outs),
        in_specs=[IN_VMEM] * 3 + [ANY, ANY, IN_VMEM, ANY, ANY, ANY] + [ANY] * 3,
        out_specs=(IN_VMEM,) * 6,
        scratch_shapes=scratch,
        compiler_params=comm_params(collective),
    )(
        dcontext_part,
        seg_row,
        pack_part,
        qkv,
        context,
        stats,
        w_window,
        hidden_row,
        dresidual,
        *grads,
    )


def fast_body(
    hidden_in,
    segment_ids,
    queries,
    targets,
    cotangent,
    query_weight,
    key_weight,
    value_weight,
    output_weight,
    query_bias,
    value_bias,
    output_bias,
    first_gain,
    first_shift,
    inner_weight,
    inner_bias,
    outer_weight,
    outer_bias,
    second_gain,
    second_shift,
):
    dp_size, ring_size = lax.axis_size("dp"), lax.axis_size("blk")
    dp, blk = lax.axis_index("dp"), lax.axis_index("blk")
    micro, row_count, block_tokens, width = hidden_in.shape
    row_queries = queries.shape[1]
    length = block_tokens * ring_size
    head_dim = width // HEADS
    spread = ring_size // micro
    own_heads = HEADS // spread
    tokens = micro * block_tokens
    wide = jnp.float32
    narrow = jnp.bfloat16

    vectors = (
        query_bias,
        value_bias,
        output_bias,
        first_gain,
        first_shift,
        outer_bias,
        second_gain,
        second_shift,
        inner_bias,
    )
    piece = vectors[0].shape[0]
    inner_piece = inner_bias.shape[0]
    group = own_heads * head_dim
    row_at, group_at = blk // spread, lax.rem(blk, spread) * group
    hidden_rows = hidden_in.reshape(micro, block_tokens, width)
    pack = jnp.concatenate(
        (
            jnp.pad(jnp.stack(vectors[:8]), ((0, 0), (0, inner_piece - piece))),
            jnp.pad(inner_bias[None], ((0, 7), (0, 0))),
        )
    )
    target_pack = jnp.pad(targets, ((0, 8 - micro), (0, 128 - row_queries)))
    seg_pack = jnp.pad(segment_ids.reshape(micro, block_tokens), ((0, 8 - micro), (0, 0)))
    shards = (
        query_weight,
        key_weight,
        value_weight,
        pack,
        target_pack,
        queries.reshape(micro * row_queries, width),
        output_weight,
        inner_weight,
        outer_weight,
    )
    ways = (("x", "y"), ("y", "x"))
    items = []

    def add_item(source, target, row=0, rows=None, from_column=0, columns=None, to_column=0):
        shape = shards[source].shape
        items.append(
            {
                "source": source,
                "target": target,
                "row": row,
                "rows": rows or shape[0],
                "stride": shape[0],
                "from_column": from_column,
                "columns": columns or shape[1],
                "to_column": to_column,
                "route": ways[len(items) % 2],
            }
        )

    for index in range(3):
        add_item(index, 0, from_column=None, columns=group, to_column=index * group)
    for index in range(3, 7):
        add_item(index, index - 2)
    for part in range(4):
        add_item(
            7, 5, from_column=part * width, columns=width, to_column=part * width
        )
        add_item(8, 6, row=part * piece, rows=piece)
    targets_out = [jax.ShapeDtypeStruct((width, 3 * group), narrow)] + [
        jax.ShapeDtypeStruct((dp_size * s.shape[0], s.shape[1]), s.dtype) for s in shards[3:]
    ]
    (
        w_window,
        pack_all,
        targets_all,
        queries_all,
        wo_full,
        w_inner,
        w_outer,
        seg_all,
        hidden_row,
        qkv,
        context,
        stats,
        context_t,
    ) = forward(shards, items, targets_out, seg_pack, hidden_rows, ring_size, head_dim)
    pack_rows = pack_all.reshape(dp_size, 16, inner_piece)
    eight = pack_rows[:, :8, :piece].transpose(1, 0, 2).reshape(8, width).astype(wide)
    bq_full, bv_full, bo_full, gain_one, shift_one, b_outer, gain_two, shift_two = eight
    b_inner = pack_rows[:, 8].reshape(-1).astype(wide)
    targets_all = (
        targets_all.reshape(dp_size, 8, 128)[:, :micro, :row_queries]
        .transpose(1, 0, 2)
        .reshape(micro, dp_size * row_queries)
    )
    queries_all = (
        queries_all.reshape(dp_size, micro, row_queries, width)
        .transpose(1, 0, 2, 3)
        .reshape(micro, dp_size * row_queries, width)
    )
    seg_row = (
        seg_all.reshape(ring_size, 8, block_tokens)[:, :micro]
        .transpose(1, 0, 2)
        .reshape(micro, 1, length)
    )
    seg_mine = lax.dynamic_slice(seg_row, (row_at, 0, 0), (1, 1, length)).reshape(1, length)

    flat_rows = hidden_in.reshape(tokens, width)
    attended = (
        jnp.einsum("met,ed->mtd", context_t, wo_full, preferred_element_type=wide).reshape(
            tokens, width
        )
        + bo_full
    )
    first_out, first_normed, first_factor = layer_norm(
        flat_rows.astype(wide) + attended, gain_one, shift_one
    )
    first_low = first_out.astype(narrow)
    inner_pre = jnp.dot(first_low, w_inner, preferred_element_type=wide) + b_inner
    active = jax.nn.gelu(inner_pre, approximate=False).astype(narrow)
    outer_out = jnp.dot(active, w_outer, preferred_element_type=wide) + b_outer
    output, second_normed, second_factor = layer_norm(first_out + outer_out, gain_two, shift_two)
    output_low = output.astype(narrow)
    output_rows = output_low.reshape(micro, block_tokens, width)

    segment = segment_ids.reshape(micro, block_tokens)
    padded = jnp.pad(seg_row.reshape(micro, length), ((0, 0), (1, 0)), constant_values=-1)
    before = lax.dynamic_slice(padded, (0, blk * block_tokens), (micro, block_tokens))
    numbers = jnp.arange(row_queries, dtype=jnp.int32)
    select = (
        (segment != before)[:, None, :] & (segment[:, None, :] == numbers[None, :, None])
    ).astype(wide)
    own_table = jnp.einsum(
        "msi,mid->msd", select.astype(narrow), output_rows, preferred_element_type=wide
    ).astype(narrow)
    tables = gather_tables(own_table.reshape(micro * row_queries, width), ring_size, dp_size)
    tables = tables.reshape(dp_size, micro, row_queries, width)
    everyone = tables.transpose(1, 0, 2, 3).reshape(micro, dp_size * row_queries, width)
    embeddings = lax.dynamic_index_in_dim(tables, dp, 0, keepdims=False)
    query_scores = jnp.einsum("mqd,mpd->mqp", queries_all, everyone, preferred_element_type=wide)
    score_peak = jnp.max(query_scores, axis=2, keepdims=True)
    log_total = score_peak[..., 0] + jnp.log(jnp.sum(jnp.exp(query_scores - score_peak), axis=2))
    target_hot = (
        jnp.arange(query_scores.shape[2], dtype=jnp.int32)[None, None, :]
        == targets_all[:, :, None]
    ).astype(wide)
    losses = log_total - jnp.sum(query_scores * target_hot, axis=2)
    query_loss = lax.dynamic_slice(losses, (0, dp * row_queries), (micro, row_queries))
    dscore_query = jnp.exp(query_scores - log_total[..., None]) - target_hot
    own_dscore = lax.dynamic_slice(
        dscore_query, (0, dp * row_queries, 0), (micro, row_queries, dp_size * row_queries)
    )
    query_grad = jnp.einsum("mqp,mpd->mqd", own_dscore, everyone.astype(wide), precision=PRECISE)
    own_columns = lax.dynamic_slice(
        dscore_query, (0, 0, dp * row_queries), (micro, dp_size * row_queries, row_queries)
    )
    embed_grad = jnp.einsum(
        "mqs,mqd->msd", own_columns, queries_all.astype(wide), precision=PRECISE
    )
    cls_grad = jnp.einsum("msi,msd->mid", select, embed_grad, precision=PRECISE)
    dout = cotangent.reshape(tokens, width).astype(wide) + cls_grad.reshape(tokens, width)
    gain_two_grad = jnp.sum(dout * second_normed, axis=0)
    shift_two_grad = jnp.sum(dout, axis=0)
    dsecond = norm_back(dout, second_normed, second_factor, gain_two)
    douter = dsecond.astype(narrow)
    outer_bias_grad = jnp.sum(douter.astype(wide), axis=0)
    outer_weight_grad = jnp.einsum(
        "nf,nd->fd", active, douter, preferred_element_type=wide
    ).astype(narrow)
    dactive = jnp.einsum("nd,fd->nf", douter, w_outer, preferred_element_type=wide)
    dinner = (dactive * gelu_slope(inner_pre)).astype(narrow)
    inner_bias_grad = jnp.sum(dinner.astype(wide), axis=0)
    inner_weight_grad = jnp.einsum(
        "nd,nf->df", first_low, dinner, preferred_element_type=wide
    ).astype(narrow)
    dfirst = dsecond + jnp.einsum("nf,df->nd", dinner, w_inner, preferred_element_type=wide)
    gain_one_grad = jnp.sum(dfirst * first_normed, axis=0)
    shift_one_grad = jnp.sum(dfirst, axis=0)
    dresidual = norm_back(dfirst, first_normed, first_factor, gain_one)
    dattended = dresidual.astype(narrow)
    output_bias_grad = jnp.sum(dattended.astype(wide), axis=0)
    datt_rows = dattended.reshape(micro, block_tokens, width)
    output_weight_grad = jnp.einsum(
        "met,mtd->ed", context_t, datt_rows, preferred_element_type=wide
    ).astype(narrow)
    dcontext_t = jnp.einsum(
        "mtd,ed->met", datt_rows, wo_full, preferred_element_type=wide
    ).astype(narrow)
    vector_grads = jnp.stack(
        (
            jnp.zeros((width,), wide),
            jnp.zeros((width,), wide),
            output_bias_grad,
            gain_one_grad,
            shift_one_grad,
            outer_bias_grad,
            gain_two_grad,
            shift_two_grad,
        )
    )
    grad_pack = jnp.pad(
        jnp.concatenate(
            (
                jnp.pad(
                    vector_grads.reshape(8, dp_size, piece).transpose(1, 0, 2),
                    ((0, 0), (0, 0), (0, inner_piece - piece)),
                ),
                inner_bias_grad.reshape(dp_size, 1, inner_piece),
            ),
            axis=1,
        ),
        ((0, 0), (0, 7), (0, 0)),
    ).reshape(dp_size * 16, inner_piece)
    grads = (outer_weight_grad, inner_weight_grad, output_weight_grad)
    grad_shapes = [grad.shape for grad in grads] + [(width, 3 * group), grad_pack.shape]
    sums = []

    def add_sum(source, row=0, rows=None, column=0, columns=None, widened=1):
        shape = grad_shapes[source]
        sums.append(
            {
                "source": source,
                "row": row,
                "rows": rows or shape[0] // dp_size,
                "stride": shape[0] // dp_size,
                "column": column,
                "columns": columns or shape[1],
                "widened": widened,
                "route": ways[len(sums) % 2],
            }
        )

    for part in range(4):
        add_sum(0, row=part * piece, rows=piece)
        add_sum(1, column=part * width, columns=width)
    add_sum(2)
    for index in range(3):
        add_sum(3, column=index * group, columns=group, widened=spread)
    add_sum(4)
    dhidden, d_outer, d_inner, d_wo, d_window, d_pack = backward(
        dcontext_t,
        seg_mine,
        grad_pack,
        (qkv, context, stats),
        w_window,
        hidden_row,
        dresidual.reshape(micro, block_tokens, width),
        grads,
        sums,
        ring_size,
        dp_size,
        head_dim,
        5,
    )
    d_outer, d_inner, d_wo, d_window, d_pack = (
        part.astype(wide) for part in (d_outer, d_inner, d_wo, d_window, d_pack)
    )
    d_wq, d_wk, d_wv = (d_window[:, i * width : (i + 1) * width] for i in range(3))
    d_bq, d_bv, d_bo, d_g1, d_s1, d_bu, d_g2, d_s2 = (d_pack[i, :piece] for i in range(8))
    d_bi = d_pack[8]
    shape = (micro, row_count, block_tokens, width)
    return (
        output_low.reshape(shape),
        embeddings,
        query_loss,
        query_grad,
        dhidden.reshape(shape),
        d_wq,
        d_wk,
        d_wv,
        d_wo,
        d_bq,
        d_bv,
        d_bo,
        d_g1,
        d_s1,
        d_inner,
        d_bi,
        d_outer,
        d_bu,
        d_g2,
        d_s2,
    )


def solution(mesh):
    in_specs = (
        P(None, "dp", "blk", None),
        P(None, "dp", "blk"),
        P(None, "dp", None),
        P(None, "dp"),
        P(None, "dp", "blk", None),
        P("dp", None),
        P("dp", None),
        P("dp", None),
        P("dp", None),
        P("dp"),
        P("dp"),
        P("dp"),
        P("dp"),
        P("dp"),
        P("dp", None),
        P("dp"),
        P("dp", None),
        P("dp"),
        P("dp"),
        P("dp"),
    )
    out_specs = (
        P(None, "dp", "blk", None),
        P(None, "dp", None),
        P(None, "dp"),
        P(None, "dp", None),
        P(None, "dp", "blk", None),
        P("dp", None),
        P("dp", None),
        P("dp", None),
        P("dp", None),
        P("dp"),
        P("dp"),
        P("dp"),
        P("dp"),
        P("dp"),
        P("dp", None),
        P("dp"),
        P("dp", None),
        P("dp"),
        P("dp"),
        P("dp"),
    )
    fast = mesh.shape["dp"] == 8 and mesh.shape["blk"] == 4
    body = fast_body if fast else ring_body
    return jax.shard_map(body, mesh=mesh, in_specs=in_specs, out_specs=out_specs, check_vma=False)
```

```python
import functools
import math

import jax
import jax.numpy as jnp
from jax import lax
from jax.experimental import pallas as pl
from jax.experimental.pallas import tpu as pltpu
from jax.sharding import PartitionSpec as P

HEADS = 12


EPSILON = 1e-12
NEGATIVE = -1000000000.0
PRECISE = lax.Precision.HIGHEST


def passed_along(x, axis, by):
    size = lax.axis_size(axis)
    return lax.ppermute(x, axis, [(i, (i + by) % size) for i in range(size)])


def as_sent(x):
    return jax.tree.map(lambda a: a.astype(jnp.bfloat16) if a.dtype == jnp.float32 else a, x)


def layer_norm(values, norm_gain, norm_shift):
    center = values - jnp.mean(values, axis=-1, keepdims=True)
    factor = lax.rsqrt(jnp.mean(center * center, axis=-1, keepdims=True) + EPSILON)
    normed = center * factor
    return (normed * norm_gain + norm_shift, normed, factor)


def norm_back(gradient, normed, factor, norm_gain):
    scaled = gradient * norm_gain
    inner_term = (
        scaled
        - jnp.mean(scaled, axis=-1, keepdims=True)
        - normed * jnp.mean(scaled * normed, axis=-1, keepdims=True)
    )
    return inner_term * factor


def gelu_slope(values):
    normal_cdf = 0.5 * (1.0 + lax.erf(values * (1.0 / math.sqrt(2.0))))
    return normal_cdf + values * jnp.exp(-0.5 * values * values) * (1.0 / math.sqrt(2.0 * math.pi))


def scores_of(query_rows, key_rows, query_segment, key_segment, score_scale):
    raw_scores = jnp.einsum(
        "rqhd,rkhd->rhqk", query_rows, key_rows, preferred_element_type=jnp.float32
    )
    same_doc = (query_segment[:, :, None] == key_segment[:, None, :])[:, None]
    return jnp.where(same_doc, score_scale * raw_scores, NEGATIVE)


def contribute(
    query_rows,
    push_grad,
    delta_term,
    peak_term,
    query_segment,
    key_rows,
    value_rows,
    key_segment,
    score_scale,
):
    scores = scores_of(query_rows, key_rows, query_segment, key_segment, score_scale)
    weights = jnp.exp(scores - peak_term[..., None])
    pushed = jnp.einsum(
        "rqhd,rkhd->rhqk", push_grad, value_rows, preferred_element_type=jnp.float32
    )
    dscore = (weights * (pushed - delta_term[..., None]) * score_scale).astype(jnp.bfloat16)
    query_part = jnp.einsum("rhqk,rkhd->rqhd", dscore, key_rows, preferred_element_type=jnp.float32)
    key_part = jnp.einsum("rhqk,rqhd->rkhd", dscore, query_rows, preferred_element_type=jnp.float32)
    value_part = jnp.einsum(
        "rhqk,rqhd->rkhd",
        weights.astype(jnp.bfloat16),
        push_grad,
        preferred_element_type=jnp.float32,
    )
    return (query_part, key_part, value_part)


def ring_body(
    hidden_in,
    segment_ids,
    queries,
    targets,
    cotangent,
    query_weight,
    key_weight,
    value_weight,
    output_weight,
    query_bias,
    value_bias,
    output_bias,
    first_gain,
    first_shift,
    inner_weight,
    inner_bias,
    outer_weight,
    outer_bias,
    second_gain,
    second_shift,
):
    shards = (
        query_weight,
        key_weight,
        value_weight,
        output_weight,
        query_bias,
        value_bias,
        output_bias,
        first_gain,
        first_shift,
        inner_weight,
        inner_bias,
        outer_weight,
        outer_bias,
        second_gain,
        second_shift,
    )
    cycle_size = lax.axis_size("blk")
    cycle_place = lax.axis_index("blk")
    micro_count, row_count, block_tokens, model_width = hidden_in.shape
    segment_count = queries.shape[1] // row_count
    head_count = HEADS
    head_dim = model_width // head_count
    score_scale = 1.0 / math.sqrt(head_dim)
    token_count = row_count * block_tokens
    head_shape = (row_count, block_tokens, head_count, head_dim)
    grad_totals = tuple((jnp.zeros(shard_piece.shape, jnp.float32) for shard_piece in shards))
    local_sum = None
    gathered = None
    out_list, embed_list, loss_list, qgrad_list, hgrad_list = ([], [], [], [], [])
    for micro_index in range(micro_count):
        gathered = (
            lax.all_gather(shards[0], "dp", axis=0, tiled=True),
            lax.all_gather(shards[1], "dp", axis=0, tiled=True),
            lax.all_gather(shards[2], "dp", axis=0, tiled=True),
            lax.all_gather(shards[3], "dp", axis=0, tiled=True),
            lax.all_gather(shards[4], "dp", axis=0, tiled=True),
            lax.all_gather(shards[5], "dp", axis=0, tiled=True),
            lax.all_gather(shards[6], "dp", axis=0, tiled=True),
            lax.all_gather(shards[7], "dp", axis=0, tiled=True),
            lax.all_gather(shards[8], "dp", axis=0, tiled=True),
            lax.all_gather(shards[9], "dp", axis=0, tiled=True),
            lax.all_gather(shards[10], "dp", axis=0, tiled=True),
            lax.all_gather(shards[11], "dp", axis=0, tiled=True),
            lax.all_gather(shards[12], "dp", axis=0, tiled=True),
            lax.all_gather(shards[13], "dp", axis=0, tiled=True),
            lax.all_gather(shards[14], "dp", axis=0, tiled=True),
        )
        (
            wq_full,
            wk_full,
            wv_full,
            wo_full,
            bq_full,
            bv_full,
            bo_full,
            gain_one,
            shift_one,
            w_inner,
            b_inner,
            w_outer,
            b_outer,
            gain_two,
            shift_two,
        ) = gathered
        gain_one = gain_one.astype(jnp.float32)
        gain_two = gain_two.astype(jnp.float32)
        segment = segment_ids[micro_index]
        flat_rows = hidden_in[micro_index].reshape(token_count, model_width)
        query_rows = (
            (
                jnp.dot(flat_rows, wq_full, preferred_element_type=jnp.float32)
                + bq_full.astype(jnp.float32)
            )
            .astype(jnp.bfloat16)
            .reshape(head_shape)
        )
        key_rows = (
            jnp.dot(flat_rows, wk_full, preferred_element_type=jnp.float32)
            .astype(jnp.bfloat16)
            .reshape(head_shape)
        )
        value_rows = (
            (
                jnp.dot(flat_rows, wv_full, preferred_element_type=jnp.float32)
                + bv_full.astype(jnp.float32)
            )
            .astype(jnp.bfloat16)
            .reshape(head_shape)
        )

        def absorb(softmax_state, visit_keys, visit_values, visit_segment):
            running_peak, running_total, running_sum = softmax_state
            scores = scores_of(query_rows, visit_keys, segment, visit_segment, score_scale)
            new_peak = jnp.maximum(running_peak, jnp.max(scores, axis=-1))
            decay_factor = jnp.exp(running_peak - new_peak)
            weights = jnp.exp(scores - new_peak[..., None])
            running_total = running_total * decay_factor + jnp.sum(weights, axis=-1)
            update = jnp.einsum(
                "rhqk,rkhd->rqhd",
                weights.astype(jnp.bfloat16),
                visit_values,
                preferred_element_type=jnp.float32,
            )
            running_sum = running_sum * jnp.transpose(decay_factor, (0, 2, 1))[..., None] + update
            return (new_peak, running_total, running_sum)

        start_state = (
            jnp.full((row_count, head_count, block_tokens), -1e30, jnp.float32),
            jnp.zeros((row_count, head_count, block_tokens), jnp.float32),
            jnp.zeros(head_shape, jnp.float32),
        )
        first_state = absorb(start_state, key_rows, value_rows, segment)

        def forward_step(cycle_step, cycle_carry):
            visit_keys, visit_values, visit_segment, prior_segment, softmax_state = cycle_carry
            visit_keys, visit_values, visit_segment = passed_along(
                (visit_keys, visit_values, visit_segment), "blk", 1
            )
            prior_segment = jnp.where(cycle_step == 1, visit_segment[:, -1], prior_segment)
            return (
                visit_keys,
                visit_values,
                visit_segment,
                prior_segment,
                absorb(softmax_state, visit_keys, visit_values, visit_segment),
            )

        cycle_carry = lax.fori_loop(
            1, cycle_size, forward_step, (key_rows, value_rows, segment, segment[:, 0], first_state)
        )
        prior_segment = cycle_carry[3]
        row_peak, row_total, running_sum = cycle_carry[4]
        total_heads = jnp.transpose(row_total, (0, 2, 1))[..., None]
        context = running_sum / total_heads
        context_low = context.reshape(token_count, model_width).astype(jnp.bfloat16)
        attended = jnp.dot(
            context_low, wo_full, preferred_element_type=jnp.float32
        ) + bo_full.astype(jnp.float32)
        first_out, first_normed, first_factor = layer_norm(
            flat_rows.astype(jnp.float32) + attended, gain_one, shift_one.astype(jnp.float32)
        )
        first_low = first_out.astype(jnp.bfloat16)
        inner_pre = jnp.dot(
            first_low, w_inner, preferred_element_type=jnp.float32
        ) + b_inner.astype(jnp.float32)
        active = jax.nn.gelu(inner_pre, approximate=False).astype(jnp.bfloat16)
        outer_out = jnp.dot(active, w_outer, preferred_element_type=jnp.float32) + b_outer.astype(
            jnp.float32
        )
        output, second_normed, second_factor = layer_norm(
            first_out + outer_out, gain_two, shift_two.astype(jnp.float32)
        )
        output_low = output.astype(jnp.bfloat16)
        out_list.append(output_low.reshape(row_count, block_tokens, model_width))
        position = cycle_place * block_tokens + jnp.arange(block_tokens, dtype=jnp.int32)
        before = jnp.concatenate([prior_segment[:, None], segment[:, :-1]], axis=1)
        leading = (position[None, :] == 0) | (segment != before)
        numbers = jnp.arange(segment_count, dtype=jnp.int32)
        select = (leading[:, None, :] & (segment[:, None, :] == numbers[None, :, None])).astype(
            jnp.float32
        )
        cls_table = jnp.einsum(
            "rsi,rid->rsd",
            select.astype(jnp.bfloat16),
            output_low.reshape(row_count, block_tokens, model_width),
            preferred_element_type=jnp.float32,
        )
        own_table = lax.psum(cls_table.astype(jnp.bfloat16), "blk").reshape(
            row_count * segment_count, model_width
        )
        embed_list.append(own_table)
        everyone = lax.all_gather(own_table, "dp", axis=0, tiled=True)
        query_vectors = queries[micro_index]
        query_scores = jnp.dot(query_vectors, everyone.T, preferred_element_type=jnp.float32)
        score_peak = jnp.max(query_scores, axis=1, keepdims=True)
        log_total = score_peak[:, 0] + jnp.log(jnp.sum(jnp.exp(query_scores - score_peak), axis=1))
        target_hot = (
            jnp.arange(query_scores.shape[1], dtype=jnp.int32)[None, :]
            == targets[micro_index][:, None]
        ).astype(jnp.float32)
        loss_list.append(log_total - jnp.sum(query_scores * target_hot, axis=1))
        dscore_query = jnp.exp(query_scores - log_total[:, None]) - target_hot
        qgrad_list.append(jnp.dot(dscore_query, everyone.astype(jnp.float32), precision=PRECISE))
        embed_part = jnp.dot(dscore_query.T, query_vectors.astype(jnp.float32), precision=PRECISE)
        embed_grad = (
            lax.psum_scatter(embed_part.astype(jnp.bfloat16), "dp", scatter_dimension=0, tiled=True)
            .astype(jnp.float32)
            .reshape(row_count, segment_count, model_width)
        )
        cls_grad = jnp.einsum("rsi,rsd->rid", select, embed_grad, precision=PRECISE)
        dout = cotangent[micro_index].reshape(token_count, model_width).astype(
            jnp.float32
        ) + cls_grad.reshape(token_count, model_width)
        gain_two_grad = jnp.sum(dout * second_normed, axis=0)
        shift_two_grad = jnp.sum(dout, axis=0)
        dsecond = norm_back(dout, second_normed, second_factor, gain_two)
        douter = dsecond.astype(jnp.bfloat16)
        outer_bias_grad = jnp.sum(douter.astype(jnp.float32), axis=0)
        outer_weight_grad = jnp.einsum(
            "nf,nd->fd", active, douter, preferred_element_type=jnp.float32
        )
        dactive = jnp.einsum("nd,fd->nf", douter, w_outer, preferred_element_type=jnp.float32)
        dinner = (dactive * gelu_slope(inner_pre)).astype(jnp.bfloat16)
        inner_bias_grad = jnp.sum(dinner.astype(jnp.float32), axis=0)
        inner_weight_grad = jnp.einsum(
            "nd,nf->df", first_low, dinner, preferred_element_type=jnp.float32
        )
        dfirst = dsecond + jnp.einsum(
            "nf,df->nd", dinner, w_inner, preferred_element_type=jnp.float32
        )
        gain_one_grad = jnp.sum(dfirst * first_normed, axis=0)
        shift_one_grad = jnp.sum(dfirst, axis=0)
        dresidual = norm_back(dfirst, first_normed, first_factor, gain_one)
        dattended = dresidual.astype(jnp.bfloat16)
        output_bias_grad = jnp.sum(dattended.astype(jnp.float32), axis=0)
        output_weight_grad = jnp.einsum(
            "nd,ne->de", context_low, dattended, preferred_element_type=jnp.float32
        )
        dcontext = jnp.einsum(
            "ne,de->nd", dattended, wo_full, preferred_element_type=jnp.float32
        ).astype(jnp.bfloat16)
        dcontext_wide = dcontext.astype(jnp.float32).reshape(head_shape)
        push_grad = (dcontext_wide / total_heads).astype(jnp.bfloat16)
        delta_term = jnp.transpose(
            jnp.sum(dcontext_wide * context, axis=-1) / total_heads[..., 0], (0, 2, 1)
        )
        own_query, own_key, own_value = contribute(
            query_rows,
            push_grad,
            delta_term,
            row_peak,
            segment,
            key_rows,
            value_rows,
            segment,
            score_scale,
        )

        def key_step(cycle_step, cycle_carry):
            visit_keys, visit_values, visit_segment, query_sum, key_sum, value_sum = cycle_carry
            visit_keys, visit_values, visit_segment = passed_along(
                (visit_keys, visit_values, visit_segment), "blk", 1
            )
            key_sum, value_sum = (
                passed_along(key_sum.astype(jnp.bfloat16), "blk", 1).astype(key_sum.dtype),
                passed_along(value_sum.astype(jnp.bfloat16), "blk", 1).astype(value_sum.dtype),
            )
            query_part, key_part, value_part = contribute(
                query_rows,
                push_grad,
                delta_term,
                row_peak,
                segment,
                visit_keys,
                visit_values,
                visit_segment,
                score_scale,
            )
            return (
                visit_keys,
                visit_values,
                visit_segment,
                query_sum + query_part,
                key_sum + key_part,
                value_sum + value_part,
            )

        back_carry = lax.fori_loop(
            1, cycle_size, key_step, (key_rows, value_rows, segment, own_query, own_key, own_value)
        )
        query_sum = back_carry[3]
        key_sum, value_sum = (
            passed_along(back_carry[4].astype(jnp.bfloat16), "blk", 1).astype(jnp.float32),
            passed_along(back_carry[5].astype(jnp.bfloat16), "blk", 1).astype(jnp.float32),
        )
        dquery = query_sum.astype(jnp.bfloat16).reshape(token_count, model_width)
        dkey = key_sum.astype(jnp.bfloat16).reshape(token_count, model_width)
        dvalue = value_sum.astype(jnp.bfloat16).reshape(token_count, model_width)
        dhidden = dresidual + jnp.einsum(
            "ne,de->nd", dquery, wq_full, preferred_element_type=jnp.float32
        )
        dhidden = dhidden + jnp.einsum(
            "ne,de->nd", dkey, wk_full, preferred_element_type=jnp.float32
        )
        dhidden = dhidden + jnp.einsum(
            "ne,de->nd", dvalue, wv_full, preferred_element_type=jnp.float32
        )
        hgrad_list.append(
            dhidden.astype(jnp.bfloat16).reshape(row_count, block_tokens, model_width)
        )
        local_grads = (
            jnp.einsum("nd,ne->de", flat_rows, dquery, preferred_element_type=jnp.float32),
            jnp.einsum("nd,ne->de", flat_rows, dkey, preferred_element_type=jnp.float32),
            jnp.einsum("nd,ne->de", flat_rows, dvalue, preferred_element_type=jnp.float32),
            output_weight_grad,
            jnp.sum(dquery.astype(jnp.float32), axis=0),
            jnp.sum(dvalue.astype(jnp.float32), axis=0),
            output_bias_grad,
            gain_one_grad,
            shift_one_grad,
            inner_weight_grad,
            inner_bias_grad,
            outer_weight_grad,
            outer_bias_grad,
            gain_two_grad,
            shift_two_grad,
        )
        local_sum = local_grads
        reduced = jax.tree.map(
            lambda part: part.astype(jnp.float32),
            lax.psum_scatter(as_sent(local_sum), "dp", scatter_dimension=0, tiled=True),
        )
        reduced = jax.tree.map(
            lambda part: part.astype(jnp.float32), lax.psum(as_sent(reduced), "blk")
        )
        grad_totals = tuple(
            (total_piece + new_piece for total_piece, new_piece in zip(grad_totals, reduced))
        )
        local_sum = None
    return (
        jnp.stack(out_list),
        jnp.stack(embed_list),
        jnp.stack(loss_list),
        jnp.stack(qgrad_list),
        jnp.stack(hgrad_list),
        grad_totals[0],
        grad_totals[1],
        grad_totals[2],
        grad_totals[3],
        grad_totals[4],
        grad_totals[5],
        grad_totals[6],
        grad_totals[7],
        grad_totals[8],
        grad_totals[9],
        grad_totals[10],
        grad_totals[11],
        grad_totals[12],
        grad_totals[13],
        grad_totals[14],
    )


MESH = pl.DeviceIdType.MESH
VMEM_LIMIT = 60 * 1024 * 1024
SIDE = {"c": 1, "x": 2, "y": 4}


def place():
    dp, blk = lax.axis_index("dp"), lax.axis_index("blk")
    bits = {"c": lax.rem(dp, 2), "x": lax.rem(dp // 2, 2), "y": dp // 4}
    return dp, blk, bits


def across(dp, blk, bits, *axes):
    other = dp
    for axis in axes:
        other = other + SIDE[axis] * (1 - 2 * bits[axis])
    return (other, blk)


def greet(peers):
    barrier = pltpu.get_barrier_semaphore()
    for peer in peers:
        pl.semaphore_signal(barrier, inc=1, device_id=peer, device_id_type=MESH)
    pl.semaphore_wait(barrier, len(peers))


def remote(source, target, send_sem, recv_sem, peer):
    return pltpu.make_async_remote_copy(
        src_ref=source,
        dst_ref=target,
        send_sem=send_sem,
        recv_sem=recv_sem,
        device_id=peer,
        device_id_type=MESH,
    )


def comm_params(collective):
    return pltpu.CompilerParams(
        collective_id=collective, has_side_effects=True, vmem_limit_bytes=VMEM_LIMIT
    )


ANY = pl.BlockSpec(memory_space=pl.ANY)
IN_VMEM = pl.BlockSpec(memory_space=pltpu.VMEM)


SLABS = 2


def forward_kernel(items, ring_size, depth, sources, places, *refs):
    shards, seg_shard, hidden = refs[:sources], refs[sources], refs[sources + 1]
    outs = refs[sources + 2 :]
    fulls = outs[:places]
    seg_full, hidden_row, qkv, context, stats, context_t = outs[places : places + 6]
    (
        hidden_full,
        low,
        seg_line,
        mask,
        turned,
        keys,
        send_sem,
        recv_sem,
        seg_send,
        seg_recv,
        line_send,
        line_recv,
        head_send,
        head_recv,
        local_sem,
    ) = outs[places + 6 :]
    w_window, pack_full = fulls[0], fulls[1]
    dp, blk, bits = place()
    sibling = across(dp, blk, bits, "c")
    ring = [(dp, lax.rem(blk + step, ring_size)) for step in range(1, ring_size)]
    greet([sibling, across(dp, blk, bits, "x"), across(dp, blk, bits, "y")] + ring)
    seg_rows = seg_shard.shape[0]
    micro, tokens, width = hidden.shape
    spread = ring_size // micro
    row_at, group_at = blk // spread, lax.rem(blk, spread)
    group, length = context.shape
    heads = group // depth
    score_scale = 1.0 / math.sqrt(depth)
    waiting = []
    mine = pl.ds(pl.multiple_of(blk * tokens, tokens), tokens)

    slab = tokens // SLABS

    def line_view(m, side, distance, part):
        owner = blk + (1 - 2 * side) * distance
        first = owner * tokens + part * slab
        return hidden_full.at[m, pl.ds(pl.multiple_of(first, slab), slab)]

    def line_copy(m, side, distance, part):
        view = line_view(m, side, distance, part)
        return remote(
            hidden.at[m, pl.ds(part * slab, slab)] if distance == 0 else view,
            view,
            line_send.at[m, side, distance, part],
            line_recv.at[m, side, distance + 1, part],
            (dp, blk - 1 + 2 * side),
        )

    def arrival(m, side, distance, part):
        view = line_view(m, side, distance, part)
        return remote(
            view,
            view,
            line_send.at[m, side, distance, part],
            line_recv.at[m, side, distance, part],
            (dp, blk - 1 + 2 * side),
        )

    def passes_on(m, side):
        return blk > m * spread if side == 0 else blk < m * spread + spread - 1

    def comes(m, side, distance):
        if side == 0:
            return (blk >= m * spread) & (blk + distance < ring_size)
        return (blk < m * spread + spread) & (blk >= distance)

    def line_step(distance, part):
        for m in range(micro):
            for side in range(2):

                @pl.when(comes(m, side, distance))
                def _():
                    arrival(m, side, distance, part).wait_recv()

                if distance < ring_size - 1:

                    @pl.when(comes(m, side, distance) & passes_on(m, side))
                    def _():
                        line_copy(m, side, distance, part).start()

    for part in range(SLABS):
        for m in range(micro):
            for side in range(2):

                @pl.when(passes_on(m, side))
                def _():
                    line_copy(m, side, 0, part).start()

    def own_part(item):
        spec = items[item]
        column = spec["from_column"]
        if column is None:
            column = pl.multiple_of(group_at * group, group)
        return shards[spec["source"]].at[
            pl.ds(spec["row"], spec["rows"]), pl.ds(column, spec["columns"])
        ]

    def block(item, owner):
        spec = items[item]
        first = owner * spec["stride"] + spec["row"]
        return fulls[spec["target"]].at[
            pl.ds(first, spec["rows"]), pl.ds(spec["to_column"], spec["columns"])
        ]

    inbound = {}

    def start_item(item):
        first, second = items[item]["route"]
        for slot, peer in enumerate(
            (across(dp, blk, bits, first), across(dp, blk, bits, second), sibling)
        ):
            copy = remote(
                own_part(item),
                block(item, dp),
                send_sem.at[item, slot],
                recv_sem.at[item, slot],
                peer,
            )
            copy.start()
            inbound[item, slot] = copy
        copy = pltpu.make_async_copy(own_part(item), block(item, dp), local_sem.at[item])
        copy.start()
        inbound[item, "own"] = copy

    def pass_on(item, held, slot, peer):
        copy = remote(held, held, send_sem.at[item, slot], recv_sem.at[item, slot], peer)
        copy.start()
        inbound[item, slot] = copy

    def relay_first(item):
        first, second = items[item]["route"]
        inbound[item, 0].wait_recv()
        held = block(item, across(dp, blk, bits, first)[0])
        pass_on(item, held, 3, across(dp, blk, bits, second))
        pass_on(item, held, 4, sibling)
        inbound[item, 1].wait_recv()
        pass_on(item, block(item, across(dp, blk, bits, second)[0]), 5, sibling)

    def relay_third(item):
        first, second = items[item]["route"]
        inbound[item, 3].wait_recv()
        pass_on(item, block(item, across(dp, blk, bits, first, second)[0]), 6, sibling)

    def all_here(item):
        for slot in (2, 4, 5, 6):
            inbound[item, slot].wait_recv()
        inbound[item, "own"].wait()

    early = [i for i, spec in enumerate(items) if spec["target"] < 2]
    late = [i for i, spec in enumerate(items) if spec["target"] >= 2]
    tick_of = [0]

    def tick(times=1):
        for _ in range(times):
            now = tick_of[0]
            tick_of[0] += 1
            if 0 <= now - 2 * LAG < len(late):
                relay_third(late[now - 2 * LAG])
            if 0 <= now - LAG < len(late):
                relay_first(late[now - LAG])
            if now < len(late):
                start_item(late[now])

    for item in early:
        start_item(item)
    for step, peer in enumerate(ring):
        copy = remote(
            seg_shard,
            seg_full.at[pl.ds(blk * seg_rows, seg_rows)],
            seg_send.at[step],
            seg_recv.at[step],
            peer,
        )
        copy.start()
        waiting.append(copy)
    seg_full[pl.ds(blk * seg_rows, seg_rows)] = seg_shard[...]

    for item in early:
        relay_first(item)
    tick()
    line_step(1, 0)
    tick()
    for part in range(1, SLABS):
        line_step(1, part)
    for item in early:
        relay_third(item)
    tick()
    for copy in waiting:
        copy.wait()
    for member in range(ring_size):
        seg_line[:, member * tokens : (member + 1) * tokens] = seg_full[
            pl.ds(member * seg_rows + row_at, 1)
        ].astype(jnp.float32)
    seg_col = columns_of(seg_line[...])
    for item in early:
        all_here(item)
    pack_turned = pack_full[...].astype(jnp.float32).T
    piece = width // (pack_full.shape[0] // 16)
    lane = lax.broadcasted_iota(jnp.int32, (piece, pack_full.shape[0]), 1)

    def bias_column(vector):
        pieces = []
        for part in range(group // piece):
            at = (group_at * (group // piece) + part) * 16 + vector
            pieces.append(
                jnp.sum(
                    jnp.where(lane == at, pack_turned[:piece], 0.0), axis=1, keepdims=True
                )
            )
        return jnp.concatenate(pieces, axis=0)

    biases = (bias_column(0), None, bias_column(1))
    for part in range(3):
        rows = slice(part * group, (part + 1) * group)
        turned[rows, :] = w_window[:, rows].T

    def project(at, source):
        span = pl.ds(pl.multiple_of(at * tokens, tokens), tokens)
        values = source[...]
        hidden_row[span, :] = values
        for part in range(3):
            rows = slice(part * group, (part + 1) * group)
            result = contract(turned[rows, :], values, 1, 1)
            if biases[part] is not None:
                result = result + biases[part]
            qkv[rows, span] = result.astype(jnp.bfloat16)

    def project_at(distance):
        for side in range(2):
            at = blk + (1 - 2 * side) * distance

            @pl.when((at >= 0) & (at < ring_size))
            def _():
                view = hidden_full.at[row_at, pl.ds(pl.multiple_of(at * tokens, tokens), tokens)]
                project(at, view)

    if ring_size > 2:
        line_step(2, 0)
    project(blk, hidden.at[row_at])
    tick()
    project_at(1)
    for distance in range(2, ring_size):
        for part in range(SLABS):
            if distance > 2 or part > 0:
                line_step(distance, part)
                tick()
        project_at(distance)

    copies = []

    def head_rows(part, head):
        first = part * group + head * depth
        return slice(first, first + depth)

    for head in range(heads):
        keys[head] = qkv[head_rows(1, head), :].T

    def attend(at):
        span = pl.ds(pl.multiple_of(at * tokens, tokens), tokens)
        mask[...] = jnp.where(seg_col == seg_line[:, span], 0.0, NEGATIVE)
        for head in range(heads):
            rows = head_rows(0, head)
            queries = (qkv[rows, span].astype(jnp.float32) * score_scale).astype(jnp.bfloat16)
            scores = contract(keys[head], queries, 1, 0) + mask[...]
            peak = jnp.max(scores, axis=0, keepdims=True)
            weights = jnp.exp(scores - peak)
            total = jnp.sum(weights, axis=0, keepdims=True)
            ctx = contract(qkv[head_rows(2, head), :], weights.astype(jnp.bfloat16), 1, 0) / total
            context[rows, span] = ctx
            low[rows, span] = ctx.astype(jnp.bfloat16)
            stats[2 * head : 2 * head + 1, span] = peak
            stats[2 * head + 1 : 2 * head + 2, span] = total

    end = (ring_size - 1) * (1 - row_at)
    order = (end, end + 2 * row_at - 1, blk + 1 - 2 * lax.rem(blk, 2), blk)
    target = context_t.at[row_at, pl.ds(group_at * group, group)]
    for index, at in enumerate(order):
        attend(at)
        span = pl.ds(pl.multiple_of(at * tokens, tokens), tokens)
        if index < ring_size - 1:
            step = lax.rem(at - blk + ring_size, ring_size)
            copy = remote(low.at[:, span], target, head_send.at[index], head_recv.at[step], (dp, at))
            copy.start()
            copies.append(copy)
        else:
            target[...] = low[:, span]
        tick(2)
    tick(len(late) + 2 * LAG - tick_of[0])
    for item in late:
        all_here(item)
    for item in early + late:
        for slot in range(7):
            inbound[item, slot].wait_send()
    for copy in copies:
        copy.wait_send()
    for step, peer in enumerate(ring):
        remote(target, target, head_send.at[0], head_recv.at[step + 1], peer).wait_recv()
    for m in range(micro):
        for side in range(2):
            for distance in range(ring_size - 1):
                ready = passes_on(m, side)
                if distance:
                    ready = ready & comes(m, side, distance)

                @pl.when(ready)
                def _():
                    for part in range(SLABS):
                        line_copy(m, side, distance, part).wait_send()


def columns_of(row):
    return jnp.broadcast_to(row, (128, row.shape[1])).T[:, :1]


def forward(shards, items, targets, segments, hidden, ring_size, depth):
    micro, tokens, width = hidden.shape
    count = len(shards)
    length = ring_size * tokens
    group = width * micro // ring_size
    heads = group // depth
    shape = jax.ShapeDtypeStruct
    return pl.pallas_call(
        functools.partial(forward_kernel, items, ring_size, depth, count, len(targets)),
        out_shape=tuple(targets)
        + (
            shape((ring_size * segments.shape[0], tokens), jnp.int32),
            shape((length, width), jnp.bfloat16),
            shape((3 * group, length), jnp.bfloat16),
            shape((group, length), jnp.float32),
            shape((2 * heads, length), jnp.float32),
            shape((micro, width, tokens), jnp.bfloat16),
        ),
        in_specs=[IN_VMEM] * (count + 2),
        out_specs=(IN_VMEM, IN_VMEM) + (ANY,) * (len(targets) - 2) + (IN_VMEM,) * 6,
        scratch_shapes=[
            pltpu.VMEM((micro, length, width), jnp.bfloat16),
            pltpu.VMEM((group, length), jnp.bfloat16),
            pltpu.VMEM((1, length), jnp.float32),
            pltpu.VMEM((length, tokens), jnp.float32),
            pltpu.VMEM((3 * group, width), jnp.bfloat16),
            pltpu.VMEM((heads, length, depth), jnp.bfloat16),
            pltpu.SemaphoreType.DMA((len(items), 7)),
            pltpu.SemaphoreType.DMA((len(items), 7)),
            pltpu.SemaphoreType.DMA((ring_size,)),
            pltpu.SemaphoreType.DMA((ring_size,)),
            pltpu.SemaphoreType.DMA((micro, 2, ring_size, SLABS)),
            pltpu.SemaphoreType.DMA((micro, 2, ring_size, SLABS)),
            pltpu.SemaphoreType.DMA((ring_size,)),
            pltpu.SemaphoreType.DMA((ring_size,)),
            pltpu.SemaphoreType.DMA((len(items),)),
        ],
        compiler_params=comm_params(1),
    )(*shards, segments, hidden)


def tables_kernel(ring_size, dp_size, own, out, arrived, send_sem, recv_sem, ring_send, ring_recv):
    dp, blk, _ = place()
    ring = [(dp, lax.rem(blk + step, ring_size)) for step in range(1, ring_size)]
    group = [(lax.rem(dp + step, dp_size), blk) for step in range(1, dp_size)]
    greet(ring + group)
    copies = []
    for step, peer in enumerate(ring):
        copy = remote(own, arrived.at[step], ring_send.at[step], ring_recv.at[step], peer)
        copy.start()
        copies.append(copy)
    for copy in copies:
        copy.wait()
    total = own[...].astype(jnp.float32)
    for step in range(ring_size - 1):
        total = total + arrived[step].astype(jnp.float32)
    out[dp] = total.astype(out.dtype)
    copies = []
    for step, peer in enumerate(group):
        copy = remote(out.at[dp], out.at[dp], send_sem.at[step], recv_sem.at[step], peer)
        copy.start()
        copies.append(copy)
    for copy in copies:
        copy.wait()


def gather_tables(own, ring_size, dp_size):
    return pl.pallas_call(
        functools.partial(tables_kernel, ring_size, dp_size),
        out_shape=jax.ShapeDtypeStruct((dp_size,) + own.shape, own.dtype),
        in_specs=[IN_VMEM],
        out_specs=IN_VMEM,
        scratch_shapes=[
            pltpu.VMEM((ring_size - 1,) + own.shape, own.dtype),
            pltpu.SemaphoreType.DMA((dp_size,)),
            pltpu.SemaphoreType.DMA((dp_size,)),
            pltpu.SemaphoreType.DMA((ring_size,)),
            pltpu.SemaphoreType.DMA((ring_size,)),
        ],
        compiler_params=comm_params(4),
    )(own)


def contract(left, right, left_dim, right_dim):
    return lax.dot_general(
        left, right, (((left_dim,), (right_dim,)), ((), ())), preferred_element_type=jnp.float32
    )


LAG, AHEAD = 2, 3


def added(left, right):
    return (left.astype(jnp.float32) + right.astype(jnp.float32)).astype(jnp.bfloat16)


def backward_kernel(items, ring_size, depth, *refs):
    (
        dcontext_part,
        seg_row,
        pack_part,
        qkv_out,
        context_out,
        stats,
        w_window_out,
        hidden_row_out,
        dresidual_out,
        outer_grad,
        inner_grad,
        output_grad,
    ) = refs[:12]
    dhidden, d_outer, d_inner, d_output, d_window, d_pack = refs[12:18]
    (
        qkv,
        context,
        w_window,
        hidden_row,
        dresidual,
        dcontext,
        dwindow,
        parts,
        passed,
        arrived,
        window_grad,
        pack_sum,
        pack_low,
        own,
        from_core,
        from_first,
        from_second,
        ring_one,
        ring_two,
        load_sem,
        head_send,
        head_recv,
        hop_send,
        hop_recv,
        send_sem,
        recv_sem,
        local_sem,
    ) = refs[18:]
    grads = (outer_grad, inner_grad, output_grad, window_grad, pack_low)
    outs = (d_outer, d_inner, d_output, d_window, d_pack)
    count = len(items)
    dp, blk, bits = place()
    sibling = across(dp, blk, bits, "c")
    is_end = (blk == 0) | (blk == ring_size - 1)
    is_middle = jnp.logical_not(is_end)
    partner = (dp, blk + 1 - 2 * lax.rem(blk, 2))
    facing = (dp, ring_size - 1 - blk)
    ring = [(dp, lax.rem(blk + step, ring_size)) for step in range(1, ring_size)]
    greet([sibling, across(dp, blk, bits, "x"), across(dp, blk, bits, "y")] + ring)

    micro, width, tokens = dcontext_part.shape
    spread = ring_size // micro
    row_at, group_at = blk // spread, lax.rem(blk, spread)
    group, length = context.shape
    heads = group // depth
    score_scale = 1.0 / math.sqrt(depth)
    mine = pl.ds(pl.multiple_of(blk * tokens, tokens), tokens)

    loads = []
    for index, (source, target) in enumerate(
        (
            (qkv_out, qkv),
            (context_out, context),
            (w_window_out, w_window),
            (hidden_row_out, hidden_row),
            (dresidual_out, dresidual),
        )
    ):
        copy = pltpu.make_async_copy(source, target, load_sem.at[index])
        copy.start()
        loads.append(copy)

    head_copies = []
    def send_head(head):
        for step in range(1, ring_size):
            owner = lax.rem(blk + step, ring_size)
            first = lax.rem(owner, spread) * group + head * depth
            copy = remote(
                dcontext_part.at[owner // spread, pl.ds(first, depth)],
                dcontext.at[pl.ds(head * depth, depth), mine],
                head_send.at[head, step],
                head_recv.at[head, step],
                (dp, owner),
            )
            copy.start()
            head_copies.append(copy)
    send_head(0)
    send_head(1)
    dcontext[:, mine] = dcontext_part[row_at, pl.ds(group_at * group, group)]

    def owner_of(core, axes, first_bit, second_bit):
        return core + SIDE[axes[0]] * first_bit + SIDE[axes[1]] * second_bit

    def block(item, which):
        spec = items[item]
        return grads[spec["source"]].at[
            pl.ds(which * spec["stride"] + spec["row"], spec["rows"]),
            pl.ds(spec["column"], spec["columns"]),
        ]

    def cut(buffer, item, *index):
        spec = items[item]
        return buffer.at[(item,) + index + (pl.ds(0, spec["rows"]), pl.ds(0, spec["columns"]))]

    def wide_cut(buffer, item, *index):
        spec = items[item]
        columns = spec["columns"] * spec["widened"]
        return buffer.at[(item,) + index + (pl.ds(0, spec["rows"]), pl.ds(0, columns))]

    def result(item):
        spec = items[item]
        many = spec["widened"]
        return outs[spec["source"]].at[
            pl.ds(spec["row"], spec["rows"]),
            pl.ds(spec["column"] * many, spec["columns"] * many),
        ]

    def copier(source, target, item, slot, peer):
        return remote(source, target, send_sem.at[item, slot], recv_sem.at[item, slot], peer)

    flying = {}

    def go(source, target, item, slot, peer):
        copy = copier(source, target, item, slot, peer)
        copy.start()
        flying[item, slot] = copy

    def start_core(item):
        axes = items[item]["route"]
        for f in range(2):
            for s in range(2):
                slot = 2 * f + s
                go(
                    block(item, owner_of(1 - bits["c"], axes, f, s)),
                    cut(from_core, item, f, s),
                    item,
                    slot,
                    sibling,
                )
                copy = pltpu.make_async_copy(
                    block(item, owner_of(bits["c"], axes, f, s)),
                    cut(own, item, f, s),
                    local_sem.at[item, slot],
                )
                copy.start()
                flying[item, "own", slot] = copy

    def after_core(item):
        axes = items[item]["route"]
        kept = bits[axes[0]]
        for slot in range(4):
            flying[item, slot].wait_recv()
            flying[item, "own", slot].wait()
        for stays, f in ((False, 1 - kept), (True, kept)):
            for s in range(2):
                part = cut(own, item, f, s)
                part[...] = added(part[...], cut(from_core, item, f, s)[...])
                if not stays:
                    peer = across(dp, blk, bits, axes[0])
                    go(part, cut(from_first, item, s), item, 4 + s, peer)

    def after_first(item):
        axes = items[item]["route"]
        f, kept = bits[axes[0]], bits[axes[1]]
        for s in range(2):
            flying[item, 4 + s].wait_recv()
        part = cut(own, item, f, 1 - kept)
        part[...] = added(part[...], cut(from_first, item, 1 - kept)[...])
        go(part, cut(from_second, item), item, 6, across(dp, blk, bits, axes[1]))
        part = cut(own, item, f, kept)
        part[...] = added(part[...], cut(from_first, item, kept)[...])

    def after_second(item):
        spec = items[item]
        axes = spec["route"]
        f, s = bits[axes[0]], bits[axes[1]]
        flying[item, 6].wait_recv()
        total = added(cut(own, item, f, s)[...], cut(from_second, item)[...])
        if spec["widened"] > 1:
            wide_cut(ring_one, item, 0)[...] = jnp.zeros(
                (spec["rows"], spec["columns"] * spec["widened"]), jnp.bfloat16
            )
            at = pl.multiple_of(group_at * spec["columns"], 128)
            ring_one[item, 0, pl.ds(0, spec["rows"]), pl.ds(at, spec["columns"])] = total
        else:
            wide_cut(ring_one, item, 0)[...] = total
        flying[item, 7] = copier(
            wide_cut(ring_one, item, 0), wide_cut(ring_one, item, 1), item, 7, partner
        )
        flying[item, 8] = copier(
            wide_cut(ring_two, item, 0), wide_cut(ring_two, item, 1), item, 8, facing
        )
        flying[item, 9] = copier(result(item), result(item), item, 9, partner)

        @pl.when(is_end)
        def _():
            flying[item, 7].start()

    def at_middle(item):
        @pl.when(is_middle)
        def _():
            flying[item, 7].wait_recv()
            part = wide_cut(ring_two, item, 0)
            part[...] = added(wide_cut(ring_one, item, 0)[...], wide_cut(ring_one, item, 1)[...])
            flying[item, 8].start()

    def across_middle(item):
        @pl.when(is_middle)
        def _():
            flying[item, 8].wait_recv()
            result(item)[...] = added(
                wide_cut(ring_two, item, 0)[...], wide_cut(ring_two, item, 1)[...]
            )
            flying[item, 9].start()

    def at_end(item):
        @pl.when(is_end)
        def _():
            flying[item, 9].wait_recv()

    stages = (after_core, after_first, after_second, at_middle, across_middle, at_end)
    tick_of = [0]

    def tick(times=1):
        for _ in range(times):
            now = tick_of[0]
            tick_of[0] += 1
            for stage in reversed(range(len(stages))):
                item = now - LAG * stage
                if 0 <= item < count:
                    stages[stage](item)
            if now + AHEAD < len(early):
                start_core(early[now + AHEAD])

    early = [i for i, spec in enumerate(items) if spec["source"] < 3]
    late = [i for i, spec in enumerate(items) if spec["source"] >= 3]
    for item in early[:AHEAD]:
        start_core(item)

    seg_line = seg_row[...].astype(jnp.float32)
    seg_col = columns_of(seg_line)

    def one_head(head):
        def rows(part):
            first = part * group + head * depth
            return slice(first, first + depth)

        for step in range(ring_size - 1):
            head_copies[head * (ring_size - 1) + step].wait_recv()
        keys, values = qkv[rows(1), :].T, qkv[rows(2), :].T
        keys_t = qkv[rows(1), :]
        dkey_sum = jnp.zeros((depth, length), jnp.float32)
        dvalue_sum = jnp.zeros((depth, length), jnp.float32)
        for start in range(0, length, tokens):
            span = slice(start, start + tokens)
            peak = stats[2 * head : 2 * head + 1, span]
            total = stats[2 * head + 1 : 2 * head + 2, span]
            dctx = dcontext[rows(0), span].astype(jnp.float32)
            push = (dctx / total).astype(jnp.bfloat16)
            delta = jnp.sum(dctx * context[rows(0), span], axis=0, keepdims=True) / total
            queries_t = qkv[rows(0), span]
            raw = contract(keys, queries_t, 1, 0)
            same = seg_col == seg_line[:, span]
            weights = jnp.exp(jnp.where(same, raw * score_scale, NEGATIVE) - peak)
            pushed = contract(values, push, 1, 0)
            dscore = (weights * (pushed - delta) * score_scale).astype(jnp.bfloat16)
            dwindow[rows(0), span] = contract(keys_t, dscore, 1, 0).astype(jnp.bfloat16)
            dkey_sum = dkey_sum + contract(queries_t, dscore, 1, 1)
            dvalue_sum = dvalue_sum + contract(push, weights.astype(jnp.bfloat16), 1, 1)
        dwindow[rows(1), :] = dkey_sum.astype(jnp.bfloat16)
        dwindow[rows(2), :] = dvalue_sum.astype(jnp.bfloat16)

    loads[0].wait()
    loads[1].wait()
    for head in range(heads):
        if head + 2 < heads:
            send_head(head + 2)
        one_head(head)
        tick()
    loads[2].wait()
    loads[3].wait()
    loads[4].wait()

    low = [m * spread for m in range(micro)]
    high = [m * spread + spread - 1 for m in range(micro)]

    def owns(m):
        return (blk >= low[m]) & (blk <= high[m])

    def receives(m, side):
        return blk + 1 <= high[m] if side == 0 else blk - 1 >= low[m]

    def has_target(side, distance):
        return blk >= distance if side == 0 else blk + distance < ring_size

    def hop(source, m, side, distance):
        return remote(
            source,
            arrived.at[m, side, distance - 1],
            hop_send.at[m, side, distance],
            hop_recv.at[m, side, distance - 1],
            (dp, blk - 1 + 2 * side),
        )

    def arrival(m, side, distance):
        view = arrived.at[m, side, distance]
        return remote(
            view,
            view,
            hop_send.at[m, side, distance],
            hop_recv.at[m, side, distance],
            (dp, blk - 1 + 2 * side),
        )

    def send_fresh(distance):
        for m in range(micro):
            for side in range(2):
                target = blk - distance * (1 - 2 * side)
                goes = has_target(side, distance) & owns(m)

                @pl.when(goes & jnp.logical_not(receives(m, side)))
                def _():
                    hop(parts.at[target], m, side, distance).start()

    def send_on(distance):
        for m in range(micro):
            for side in range(2):
                target = blk - distance * (1 - 2 * side)
                goes = has_target(side, distance) & receives(m, side)

                @pl.when(goes & owns(m))
                def _():
                    arrival(m, side, distance).wait_recv()
                    passed[side, distance - 1] = added(parts[target], arrived[m, side, distance])
                    hop(passed.at[side, distance - 1], m, side, distance).start()

                @pl.when(goes & jnp.logical_not(owns(m)))
                def _():
                    arrival(m, side, distance).wait_recv()
                    hop(arrived.at[m, side, distance], m, side, distance).start()

    def finish_hidden(_):
        for m in range(micro):
            for side in range(2):
                inside = blk < ring_size - 1 if side == 0 else blk > 0
                here = receives(m, side) & inside

                @pl.when(here & owns(m))
                def _():
                    arrival(m, side, 0).wait_recv()
                    dhidden[m] = (
                        dresidual[m]
                        + parts[blk].astype(jnp.float32)
                        + arrived[m, side, 0].astype(jnp.float32)
                    ).astype(jnp.bfloat16)

                @pl.when(here & jnp.logical_not(owns(m)))
                def _():
                    arrival(m, side, 0).wait_recv()
                    dhidden[m] = (
                        dresidual[m] + arrived[m, side, 0].astype(jnp.float32)
                    ).astype(jnp.bfloat16)

    end = (ring_size - 1) * (1 - row_at)
    inward = 2 * row_at - 1
    order = (end, end + inward, blk + 1 - 2 * lax.rem(blk, 2), blk)

    def make_part(target):
        at = pl.ds(pl.multiple_of(target * tokens, tokens), tokens)
        parts[target] = contract(dwindow[:, at].T, w_window[...], 1, 1).astype(jnp.bfloat16)

    ones = jnp.ones((8, length), jnp.bfloat16)
    line = lax.broadcasted_iota(jnp.int32, (8, 128), 0)
    lane = lax.broadcasted_iota(jnp.int32, (8, 128), 1)
    piece = width // (pack_part.shape[0] // 16)
    pack_sum[...] = pack_part[...]

    def make_grad(part):
        rows = slice(part * group, (part + 1) * group)
        window_grad[:, rows] = contract(hidden_row[...].T, dwindow[rows, :], 1, 1).astype(
            jnp.bfloat16
        )
        if part != 1:
            sums = contract(ones, dwindow[rows, :], 1, 1)
            sums = jnp.concatenate((sums, jnp.zeros((8, 128), jnp.float32)), axis=1)
            for step in range(group // piece):
                first = pl.multiple_of((group_at * (group // piece) + step) * 16, 16)
                pack_sum[pl.ds(first, 8), 0:128] += jnp.where(
                    (line == part // 2) & (lane < piece),
                    sums[:, step * piece : step * piece + 128],
                    0.0,
                )
        start_core(late[part])

    for index, target in enumerate(order):
        make_part(target)
        if index < ring_size - 1:
            send_fresh(ring_size - 1 - index)
            make_grad(index)
            tick()
    pack_low[...] = pack_sum[...].astype(jnp.bfloat16)
    start_core(late[3])
    for distance in reversed(range(1, ring_size - 1)):
        send_on(distance)
        tick(2)
    finish_hidden(None)
    tick(count + LAG * (len(stages) - 1) - tick_of[0])

    for copy in head_copies:
        copy.wait_send()
    for item in range(count):
        for slot in range(7):
            flying[item, slot].wait_send()
    for distance in range(1, ring_size):
        for m in range(micro):
            for side in range(2):

                @pl.when(has_target(side, distance) & (receives(m, side) | owns(m)))
                def _():
                    hop(parts.at[0], m, side, distance).wait_send()

    @pl.when(is_end)
    def _():
        for item in range(count):
            flying[item, 7].wait_send()

    @pl.when(is_middle)
    def _():
        for item in range(count):
            flying[item, 8].wait_send()
            flying[item, 9].wait_send()


def backward(
    dcontext_part,
    seg_row,
    pack_part,
    saved,
    w_window,
    hidden_row,
    dresidual,
    grads,
    items,
    ring_size,
    dp_size,
    depth,
    collective,
):
    qkv, context, stats = saved
    micro, width, tokens = dcontext_part.shape
    group, length = context.shape
    heads = group // depth
    spread = ring_size // micro
    count = len(items)
    rows = max(item["rows"] for item in items)
    columns = max(item["columns"] * item["widened"] for item in items)
    piece = (rows, columns)
    narrow = jnp.bfloat16
    shape = jax.ShapeDtypeStruct
    outs = [shape((grad.shape[0] // dp_size, grad.shape[1]), narrow) for grad in grads]
    outs.append(shape((width // dp_size, 3 * width), narrow))
    outs.append(shape((pack_part.shape[0] // dp_size, pack_part.shape[1]), narrow))
    scratch = [
        pltpu.VMEM(qkv.shape, narrow),
        pltpu.VMEM(context.shape, jnp.float32),
        pltpu.VMEM(w_window.shape, narrow),
        pltpu.VMEM(hidden_row.shape, narrow),
        pltpu.VMEM(dresidual.shape, jnp.float32),
        pltpu.VMEM((group, length), narrow),
        pltpu.VMEM(qkv.shape, narrow),
        pltpu.VMEM((ring_size, tokens, width), narrow),
        pltpu.VMEM((2, ring_size - 2, tokens, width), narrow),
        pltpu.VMEM((micro, 2, ring_size - 1, tokens, width), narrow),
        pltpu.VMEM((width, 3 * group), narrow),
        pltpu.VMEM(pack_part.shape, jnp.float32),
        pltpu.VMEM(pack_part.shape, narrow),
    ]
    scratch += [
        pltpu.VMEM((count,) + lead + piece, narrow)
        for lead in ((2, 2), (2, 2), (2,), (), (2,), (2,))
    ]
    scratch += [
        pltpu.SemaphoreType.DMA((5,)),
        pltpu.SemaphoreType.DMA((heads, ring_size)),
        pltpu.SemaphoreType.DMA((heads, ring_size)),
        pltpu.SemaphoreType.DMA((micro, 2, ring_size)),
        pltpu.SemaphoreType.DMA((micro, 2, ring_size)),
        pltpu.SemaphoreType.DMA((count, 10)),
        pltpu.SemaphoreType.DMA((count, 10)),
        pltpu.SemaphoreType.DMA((count, 4)),
    ]
    return pl.pallas_call(
        functools.partial(backward_kernel, items, ring_size, depth),
        out_shape=(shape((micro, tokens, width), narrow),) + tuple(outs),
        in_specs=[IN_VMEM] * 3 + [ANY, ANY, IN_VMEM, ANY, ANY, ANY] + [ANY] * 3,
        out_specs=(IN_VMEM,) * 6,
        scratch_shapes=scratch,
        compiler_params=comm_params(collective),
    )(
        dcontext_part,
        seg_row,
        pack_part,
        qkv,
        context,
        stats,
        w_window,
        hidden_row,
        dresidual,
        *grads,
    )


def fast_body(
    hidden_in,
    segment_ids,
    queries,
    targets,
    cotangent,
    query_weight,
    key_weight,
    value_weight,
    output_weight,
    query_bias,
    value_bias,
    output_bias,
    first_gain,
    first_shift,
    inner_weight,
    inner_bias,
    outer_weight,
    outer_bias,
    second_gain,
    second_shift,
):
    dp_size, ring_size = lax.axis_size("dp"), lax.axis_size("blk")
    dp, blk = lax.axis_index("dp"), lax.axis_index("blk")
    micro, row_count, block_tokens, width = hidden_in.shape
    row_queries = queries.shape[1]
    length = block_tokens * ring_size
    head_dim = width // HEADS
    spread = ring_size // micro
    own_heads = HEADS // spread
    tokens = micro * block_tokens
    wide = jnp.float32
    narrow = jnp.bfloat16

    vectors = (
        query_bias,
        value_bias,
        output_bias,
        first_gain,
        first_shift,
        outer_bias,
        second_gain,
        second_shift,
        inner_bias,
    )
    piece = vectors[0].shape[0]
    inner_piece = inner_bias.shape[0]
    group = own_heads * head_dim
    row_at, group_at = blk // spread, lax.rem(blk, spread) * group
    hidden_rows = hidden_in.reshape(micro, block_tokens, width)
    pack = jnp.concatenate(
        (
            jnp.pad(jnp.stack(vectors[:8]), ((0, 0), (0, inner_piece - piece))),
            jnp.pad(inner_bias[None], ((0, 7), (0, 0))),
        )
    )
    target_pack = jnp.pad(targets, ((0, 8 - micro), (0, 128 - row_queries)))
    seg_pack = jnp.pad(segment_ids.reshape(micro, block_tokens), ((0, 8 - micro), (0, 0)))
    shards = (
        query_weight,
        key_weight,
        value_weight,
        pack,
        target_pack,
        queries.reshape(micro * row_queries, width),
        output_weight,
        inner_weight,
        outer_weight,
    )
    ways = (("x", "y"), ("y", "x"))
    items = []

    def add_item(source, target, row=0, rows=None, from_column=0, columns=None, to_column=0):
        shape = shards[source].shape
        items.append(
            {
                "source": source,
                "target": target,
                "row": row,
                "rows": rows or shape[0],
                "stride": shape[0],
                "from_column": from_column,
                "columns": columns or shape[1],
                "to_column": to_column,
                "route": ways[len(items) % 2],
            }
        )

    for index in range(3):
        add_item(index, 0, from_column=None, columns=group, to_column=index * group)
    add_item(3, 1)
    add_item(6, 4)
    for part in range(4):
        add_item(7, 5, from_column=part * width, columns=width, to_column=part * width)
        add_item(8, 6, row=part * piece, rows=piece)
    add_item(4, 2)
    add_item(5, 3)
    targets_out = [jax.ShapeDtypeStruct((width, 3 * group), narrow)] + [
        jax.ShapeDtypeStruct((dp_size * s.shape[0], s.shape[1]), s.dtype) for s in shards[3:]
    ]
    (
        w_window,
        pack_all,
        targets_all,
        queries_all,
        wo_full,
        w_inner,
        w_outer,
        seg_all,
        hidden_row,
        qkv,
        context,
        stats,
        context_t,
    ) = forward(shards, items, targets_out, seg_pack, hidden_rows, ring_size, head_dim)
    pack_rows = pack_all.reshape(dp_size, 16, inner_piece)
    eight = pack_rows[:, :8, :piece].transpose(1, 0, 2).reshape(8, width).astype(wide)
    bq_full, bv_full, bo_full, gain_one, shift_one, b_outer, gain_two, shift_two = eight
    b_inner = pack_rows[:, 8].reshape(-1).astype(wide)
    targets_all = (
        targets_all.reshape(dp_size, 8, 128)[:, :micro, :row_queries]
        .transpose(1, 0, 2)
        .reshape(micro, dp_size * row_queries)
    )
    queries_all = (
        queries_all.reshape(dp_size, micro, row_queries, width)
        .transpose(1, 0, 2, 3)
        .reshape(micro, dp_size * row_queries, width)
    )
    seg_row = (
        seg_all.reshape(ring_size, 8, block_tokens)[:, :micro]
        .transpose(1, 0, 2)
        .reshape(micro, 1, length)
    )
    seg_mine = lax.dynamic_slice(seg_row, (row_at, 0, 0), (1, 1, length)).reshape(1, length)

    flat_rows = hidden_in.reshape(tokens, width)
    attended = (
        jnp.einsum("met,ed->mtd", context_t, wo_full, preferred_element_type=wide).reshape(
            tokens, width
        )
        + bo_full
    )
    first_out, first_normed, first_factor = layer_norm(
        flat_rows.astype(wide) + attended, gain_one, shift_one
    )
    first_low = first_out.astype(narrow)
    inner_pre = jnp.dot(first_low, w_inner, preferred_element_type=wide) + b_inner
    active = jax.nn.gelu(inner_pre, approximate=False).astype(narrow)
    outer_out = jnp.dot(active, w_outer, preferred_element_type=wide) + b_outer
    output, second_normed, second_factor = layer_norm(first_out + outer_out, gain_two, shift_two)
    output_low = output.astype(narrow)
    output_rows = output_low.reshape(micro, block_tokens, width)

    segment = segment_ids.reshape(micro, block_tokens)
    padded = jnp.pad(seg_row.reshape(micro, length), ((0, 0), (1, 0)), constant_values=-1)
    before = lax.dynamic_slice(padded, (0, blk * block_tokens), (micro, block_tokens))
    numbers = jnp.arange(row_queries, dtype=jnp.int32)
    select = (
        (segment != before)[:, None, :] & (segment[:, None, :] == numbers[None, :, None])
    ).astype(wide)
    own_table = jnp.einsum(
        "msi,mid->msd", select.astype(narrow), output_rows, preferred_element_type=wide
    ).astype(narrow)
    tables = gather_tables(own_table.reshape(micro * row_queries, width), ring_size, dp_size)
    tables = tables.reshape(dp_size, micro, row_queries, width)
    everyone = tables.transpose(1, 0, 2, 3).reshape(micro, dp_size * row_queries, width)
    embeddings = lax.dynamic_index_in_dim(tables, dp, 0, keepdims=False)
    query_scores = jnp.einsum("mqd,mpd->mqp", queries_all, everyone, preferred_element_type=wide)
    score_peak = jnp.max(query_scores, axis=2, keepdims=True)
    log_total = score_peak[..., 0] + jnp.log(jnp.sum(jnp.exp(query_scores - score_peak), axis=2))
    target_hot = (
        jnp.arange(query_scores.shape[2], dtype=jnp.int32)[None, None, :]
        == targets_all[:, :, None]
    ).astype(wide)
    losses = log_total - jnp.sum(query_scores * target_hot, axis=2)
    query_loss = lax.dynamic_slice(losses, (0, dp * row_queries), (micro, row_queries))
    dscore_query = jnp.exp(query_scores - log_total[..., None]) - target_hot
    own_dscore = lax.dynamic_slice(
        dscore_query, (0, dp * row_queries, 0), (micro, row_queries, dp_size * row_queries)
    )
    query_grad = jnp.einsum("mqp,mpd->mqd", own_dscore, everyone.astype(wide), precision=PRECISE)
    own_columns = lax.dynamic_slice(
        dscore_query, (0, 0, dp * row_queries), (micro, dp_size * row_queries, row_queries)
    )
    embed_grad = jnp.einsum(
        "mqs,mqd->msd", own_columns, queries_all.astype(wide), precision=PRECISE
    )
    cls_grad = jnp.einsum("msi,msd->mid", select, embed_grad, precision=PRECISE)
    dout = cotangent.reshape(tokens, width).astype(wide) + cls_grad.reshape(tokens, width)
    gain_two_grad = jnp.sum(dout * second_normed, axis=0)
    shift_two_grad = jnp.sum(dout, axis=0)
    dsecond = norm_back(dout, second_normed, second_factor, gain_two)
    douter = dsecond.astype(narrow)
    outer_bias_grad = jnp.sum(douter.astype(wide), axis=0)
    outer_weight_grad = jnp.einsum(
        "nf,nd->fd", active, douter, preferred_element_type=wide
    ).astype(narrow)
    dactive = jnp.einsum("nd,fd->nf", douter, w_outer, preferred_element_type=wide)
    dinner = (dactive * gelu_slope(inner_pre)).astype(narrow)
    inner_bias_grad = jnp.sum(dinner.astype(wide), axis=0)
    inner_weight_grad = jnp.einsum(
        "nd,nf->df", first_low, dinner, preferred_element_type=wide
    ).astype(narrow)
    dfirst = dsecond + jnp.einsum("nf,df->nd", dinner, w_inner, preferred_element_type=wide)
    gain_one_grad = jnp.sum(dfirst * first_normed, axis=0)
    shift_one_grad = jnp.sum(dfirst, axis=0)
    dresidual = norm_back(dfirst, first_normed, first_factor, gain_one)
    dattended = dresidual.astype(narrow)
    output_bias_grad = jnp.sum(dattended.astype(wide), axis=0)
    datt_rows = dattended.reshape(micro, block_tokens, width)
    output_weight_grad = jnp.einsum(
        "met,mtd->ed", context_t, datt_rows, preferred_element_type=wide
    ).astype(narrow)
    dcontext_t = jnp.einsum(
        "mtd,ed->met", datt_rows, wo_full, preferred_element_type=wide
    ).astype(narrow)
    vector_grads = jnp.stack(
        (
            jnp.zeros((width,), wide),
            jnp.zeros((width,), wide),
            output_bias_grad,
            gain_one_grad,
            shift_one_grad,
            outer_bias_grad,
            gain_two_grad,
            shift_two_grad,
        )
    )
    grad_pack = jnp.pad(
        jnp.concatenate(
            (
                jnp.pad(
                    vector_grads.reshape(8, dp_size, piece).transpose(1, 0, 2),
                    ((0, 0), (0, 0), (0, inner_piece - piece)),
                ),
                inner_bias_grad.reshape(dp_size, 1, inner_piece),
            ),
            axis=1,
        ),
        ((0, 0), (0, 7), (0, 0)),
    ).reshape(dp_size * 16, inner_piece)
    grads = (outer_weight_grad, inner_weight_grad, output_weight_grad)
    grad_shapes = [grad.shape for grad in grads] + [(width, 3 * group), grad_pack.shape]
    sums = []

    def add_sum(source, row=0, rows=None, column=0, columns=None, widened=1):
        shape = grad_shapes[source]
        sums.append(
            {
                "source": source,
                "row": row,
                "rows": rows or shape[0] // dp_size,
                "stride": shape[0] // dp_size,
                "column": column,
                "columns": columns or shape[1],
                "widened": widened,
                "route": ways[len(sums) % 2],
            }
        )

    for part in range(4):
        add_sum(0, row=part * piece, rows=piece)
        add_sum(1, column=part * width, columns=width)
    add_sum(2)
    for index in range(3):
        add_sum(3, column=index * group, columns=group, widened=spread)
    add_sum(4)
    dhidden, d_outer, d_inner, d_wo, d_window, d_pack = backward(
        dcontext_t,
        seg_mine,
        grad_pack,
        (qkv, context, stats),
        w_window,
        hidden_row,
        dresidual.reshape(micro, block_tokens, width),
        grads,
        sums,
        ring_size,
        dp_size,
        head_dim,
        5,
    )
    d_outer, d_inner, d_wo, d_window, d_pack = (
        part.astype(wide) for part in (d_outer, d_inner, d_wo, d_window, d_pack)
    )
    d_wq, d_wk, d_wv = (d_window[:, i * width : (i + 1) * width] for i in range(3))
    d_bq, d_bv, d_bo, d_g1, d_s1, d_bu, d_g2, d_s2 = (d_pack[i, :piece] for i in range(8))
    d_bi = d_pack[8]
    shape = (micro, row_count, block_tokens, width)
    return (
        output_low.reshape(shape),
        embeddings,
        query_loss,
        query_grad,
        dhidden.reshape(shape),
        d_wq,
        d_wk,
        d_wv,
        d_wo,
        d_bq,
        d_bv,
        d_bo,
        d_g1,
        d_s1,
        d_inner,
        d_bi,
        d_outer,
        d_bu,
        d_g2,
        d_s2,
    )


def solution(mesh):
    in_specs = (
        P(None, "dp", "blk", None),
        P(None, "dp", "blk"),
        P(None, "dp", None),
        P(None, "dp"),
        P(None, "dp", "blk", None),
        P("dp", None),
        P("dp", None),
        P("dp", None),
        P("dp", None),
        P("dp"),
        P("dp"),
        P("dp"),
        P("dp"),
        P("dp"),
        P("dp", None),
        P("dp"),
        P("dp", None),
        P("dp"),
        P("dp"),
        P("dp"),
    )
    out_specs = (
        P(None, "dp", "blk", None),
        P(None, "dp", None),
        P(None, "dp"),
        P(None, "dp", None),
        P(None, "dp", "blk", None),
        P("dp", None),
        P("dp", None),
        P("dp", None),
        P("dp", None),
        P("dp"),
        P("dp"),
        P("dp"),
        P("dp"),
        P("dp"),
        P("dp", None),
        P("dp"),
        P("dp", None),
        P("dp"),
        P("dp"),
        P("dp"),
    )
    fast = mesh.shape["dp"] == 8 and mesh.shape["blk"] == 4
    body = fast_body if fast else ring_body
    return jax.shard_map(body, mesh=mesh, in_specs=in_specs, out_specs=out_specs, check_vma=False)
```

```python
import functools
import math

import jax
import jax.numpy as jnp
from jax import lax
from jax.experimental import pallas as pl
from jax.experimental.pallas import tpu as pltpu
from jax.sharding import PartitionSpec as P

HEADS = 12


EPSILON = 1e-12
NEGATIVE = -1000000000.0
PRECISE = lax.Precision.HIGHEST


def passed_along(x, axis, by):
    size = lax.axis_size(axis)
    return lax.ppermute(x, axis, [(i, (i + by) % size) for i in range(size)])


def as_sent(x):
    return jax.tree.map(lambda a: a.astype(jnp.bfloat16) if a.dtype == jnp.float32 else a, x)


def layer_norm(values, norm_gain, norm_shift):
    center = values - jnp.mean(values, axis=-1, keepdims=True)
    factor = lax.rsqrt(jnp.mean(center * center, axis=-1, keepdims=True) + EPSILON)
    normed = center * factor
    return (normed * norm_gain + norm_shift, normed, factor)


def norm_back(gradient, normed, factor, norm_gain):
    scaled = gradient * norm_gain
    inner_term = (
        scaled
        - jnp.mean(scaled, axis=-1, keepdims=True)
        - normed * jnp.mean(scaled * normed, axis=-1, keepdims=True)
    )
    return inner_term * factor


def gelu_slope(values):
    normal_cdf = 0.5 * (1.0 + lax.erf(values * (1.0 / math.sqrt(2.0))))
    return normal_cdf + values * jnp.exp(-0.5 * values * values) * (1.0 / math.sqrt(2.0 * math.pi))


def scores_of(query_rows, key_rows, query_segment, key_segment, score_scale):
    raw_scores = jnp.einsum(
        "rqhd,rkhd->rhqk", query_rows, key_rows, preferred_element_type=jnp.float32
    )
    same_doc = (query_segment[:, :, None] == key_segment[:, None, :])[:, None]
    return jnp.where(same_doc, score_scale * raw_scores, NEGATIVE)


def contribute(
    query_rows,
    push_grad,
    delta_term,
    peak_term,
    query_segment,
    key_rows,
    value_rows,
    key_segment,
    score_scale,
):
    scores = scores_of(query_rows, key_rows, query_segment, key_segment, score_scale)
    weights = jnp.exp(scores - peak_term[..., None])
    pushed = jnp.einsum(
        "rqhd,rkhd->rhqk", push_grad, value_rows, preferred_element_type=jnp.float32
    )
    dscore = (weights * (pushed - delta_term[..., None]) * score_scale).astype(jnp.bfloat16)
    query_part = jnp.einsum("rhqk,rkhd->rqhd", dscore, key_rows, preferred_element_type=jnp.float32)
    key_part = jnp.einsum("rhqk,rqhd->rkhd", dscore, query_rows, preferred_element_type=jnp.float32)
    value_part = jnp.einsum(
        "rhqk,rqhd->rkhd",
        weights.astype(jnp.bfloat16),
        push_grad,
        preferred_element_type=jnp.float32,
    )
    return (query_part, key_part, value_part)


def ring_body(
    hidden_in,
    segment_ids,
    queries,
    targets,
    cotangent,
    query_weight,
    key_weight,
    value_weight,
    output_weight,
    query_bias,
    value_bias,
    output_bias,
    first_gain,
    first_shift,
    inner_weight,
    inner_bias,
    outer_weight,
    outer_bias,
    second_gain,
    second_shift,
):
    shards = (
        query_weight,
        key_weight,
        value_weight,
        output_weight,
        query_bias,
        value_bias,
        output_bias,
        first_gain,
        first_shift,
        inner_weight,
        inner_bias,
        outer_weight,
        outer_bias,
        second_gain,
        second_shift,
    )
    cycle_size = lax.axis_size("blk")
    cycle_place = lax.axis_index("blk")
    micro_count, row_count, block_tokens, model_width = hidden_in.shape
    segment_count = queries.shape[1] // row_count
    head_count = HEADS
    head_dim = model_width // head_count
    score_scale = 1.0 / math.sqrt(head_dim)
    token_count = row_count * block_tokens
    head_shape = (row_count, block_tokens, head_count, head_dim)
    grad_totals = tuple((jnp.zeros(shard_piece.shape, jnp.float32) for shard_piece in shards))
    local_sum = None
    gathered = None
    out_list, embed_list, loss_list, qgrad_list, hgrad_list = ([], [], [], [], [])
    for micro_index in range(micro_count):
        gathered = (
            lax.all_gather(shards[0], "dp", axis=0, tiled=True),
            lax.all_gather(shards[1], "dp", axis=0, tiled=True),
            lax.all_gather(shards[2], "dp", axis=0, tiled=True),
            lax.all_gather(shards[3], "dp", axis=0, tiled=True),
            lax.all_gather(shards[4], "dp", axis=0, tiled=True),
            lax.all_gather(shards[5], "dp", axis=0, tiled=True),
            lax.all_gather(shards[6], "dp", axis=0, tiled=True),
            lax.all_gather(shards[7], "dp", axis=0, tiled=True),
            lax.all_gather(shards[8], "dp", axis=0, tiled=True),
            lax.all_gather(shards[9], "dp", axis=0, tiled=True),
            lax.all_gather(shards[10], "dp", axis=0, tiled=True),
            lax.all_gather(shards[11], "dp", axis=0, tiled=True),
            lax.all_gather(shards[12], "dp", axis=0, tiled=True),
            lax.all_gather(shards[13], "dp", axis=0, tiled=True),
            lax.all_gather(shards[14], "dp", axis=0, tiled=True),
        )
        (
            wq_full,
            wk_full,
            wv_full,
            wo_full,
            bq_full,
            bv_full,
            bo_full,
            gain_one,
            shift_one,
            w_inner,
            b_inner,
            w_outer,
            b_outer,
            gain_two,
            shift_two,
        ) = gathered
        gain_one = gain_one.astype(jnp.float32)
        gain_two = gain_two.astype(jnp.float32)
        segment = segment_ids[micro_index]
        flat_rows = hidden_in[micro_index].reshape(token_count, model_width)
        query_rows = (
            (
                jnp.dot(flat_rows, wq_full, preferred_element_type=jnp.float32)
                + bq_full.astype(jnp.float32)
            )
            .astype(jnp.bfloat16)
            .reshape(head_shape)
        )
        key_rows = (
            jnp.dot(flat_rows, wk_full, preferred_element_type=jnp.float32)
            .astype(jnp.bfloat16)
            .reshape(head_shape)
        )
        value_rows = (
            (
                jnp.dot(flat_rows, wv_full, preferred_element_type=jnp.float32)
                + bv_full.astype(jnp.float32)
            )
            .astype(jnp.bfloat16)
            .reshape(head_shape)
        )

        def absorb(softmax_state, visit_keys, visit_values, visit_segment):
            running_peak, running_total, running_sum = softmax_state
            scores = scores_of(query_rows, visit_keys, segment, visit_segment, score_scale)
            new_peak = jnp.maximum(running_peak, jnp.max(scores, axis=-1))
            decay_factor = jnp.exp(running_peak - new_peak)
            weights = jnp.exp(scores - new_peak[..., None])
            running_total = running_total * decay_factor + jnp.sum(weights, axis=-1)
            update = jnp.einsum(
                "rhqk,rkhd->rqhd",
                weights.astype(jnp.bfloat16),
                visit_values,
                preferred_element_type=jnp.float32,
            )
            running_sum = running_sum * jnp.transpose(decay_factor, (0, 2, 1))[..., None] + update
            return (new_peak, running_total, running_sum)

        start_state = (
            jnp.full((row_count, head_count, block_tokens), -1e30, jnp.float32),
            jnp.zeros((row_count, head_count, block_tokens), jnp.float32),
            jnp.zeros(head_shape, jnp.float32),
        )
        first_state = absorb(start_state, key_rows, value_rows, segment)

        def forward_step(cycle_step, cycle_carry):
            visit_keys, visit_values, visit_segment, prior_segment, softmax_state = cycle_carry
            visit_keys, visit_values, visit_segment = passed_along(
                (visit_keys, visit_values, visit_segment), "blk", 1
            )
            prior_segment = jnp.where(cycle_step == 1, visit_segment[:, -1], prior_segment)
            return (
                visit_keys,
                visit_values,
                visit_segment,
                prior_segment,
                absorb(softmax_state, visit_keys, visit_values, visit_segment),
            )

        cycle_carry = lax.fori_loop(
            1, cycle_size, forward_step, (key_rows, value_rows, segment, segment[:, 0], first_state)
        )
        prior_segment = cycle_carry[3]
        row_peak, row_total, running_sum = cycle_carry[4]
        total_heads = jnp.transpose(row_total, (0, 2, 1))[..., None]
        context = running_sum / total_heads
        context_low = context.reshape(token_count, model_width).astype(jnp.bfloat16)
        attended = jnp.dot(
            context_low, wo_full, preferred_element_type=jnp.float32
        ) + bo_full.astype(jnp.float32)
        first_out, first_normed, first_factor = layer_norm(
            flat_rows.astype(jnp.float32) + attended, gain_one, shift_one.astype(jnp.float32)
        )
        first_low = first_out.astype(jnp.bfloat16)
        inner_pre = jnp.dot(
            first_low, w_inner, preferred_element_type=jnp.float32
        ) + b_inner.astype(jnp.float32)
        active = jax.nn.gelu(inner_pre, approximate=False).astype(jnp.bfloat16)
        outer_out = jnp.dot(active, w_outer, preferred_element_type=jnp.float32) + b_outer.astype(
            jnp.float32
        )
        output, second_normed, second_factor = layer_norm(
            first_out + outer_out, gain_two, shift_two.astype(jnp.float32)
        )
        output_low = output.astype(jnp.bfloat16)
        out_list.append(output_low.reshape(row_count, block_tokens, model_width))
        position = cycle_place * block_tokens + jnp.arange(block_tokens, dtype=jnp.int32)
        before = jnp.concatenate([prior_segment[:, None], segment[:, :-1]], axis=1)
        leading = (position[None, :] == 0) | (segment != before)
        numbers = jnp.arange(segment_count, dtype=jnp.int32)
        select = (leading[:, None, :] & (segment[:, None, :] == numbers[None, :, None])).astype(
            jnp.float32
        )
        cls_table = jnp.einsum(
            "rsi,rid->rsd",
            select.astype(jnp.bfloat16),
            output_low.reshape(row_count, block_tokens, model_width),
            preferred_element_type=jnp.float32,
        )
        own_table = lax.psum(cls_table.astype(jnp.bfloat16), "blk").reshape(
            row_count * segment_count, model_width
        )
        embed_list.append(own_table)
        everyone = lax.all_gather(own_table, "dp", axis=0, tiled=True)
        query_vectors = queries[micro_index]
        query_scores = jnp.dot(query_vectors, everyone.T, preferred_element_type=jnp.float32)
        score_peak = jnp.max(query_scores, axis=1, keepdims=True)
        log_total = score_peak[:, 0] + jnp.log(jnp.sum(jnp.exp(query_scores - score_peak), axis=1))
        target_hot = (
            jnp.arange(query_scores.shape[1], dtype=jnp.int32)[None, :]
            == targets[micro_index][:, None]
        ).astype(jnp.float32)
        loss_list.append(log_total - jnp.sum(query_scores * target_hot, axis=1))
        dscore_query = jnp.exp(query_scores - log_total[:, None]) - target_hot
        qgrad_list.append(jnp.dot(dscore_query, everyone.astype(jnp.float32), precision=PRECISE))
        embed_part = jnp.dot(dscore_query.T, query_vectors.astype(jnp.float32), precision=PRECISE)
        embed_grad = (
            lax.psum_scatter(embed_part.astype(jnp.bfloat16), "dp", scatter_dimension=0, tiled=True)
            .astype(jnp.float32)
            .reshape(row_count, segment_count, model_width)
        )
        cls_grad = jnp.einsum("rsi,rsd->rid", select, embed_grad, precision=PRECISE)
        dout = cotangent[micro_index].reshape(token_count, model_width).astype(
            jnp.float32
        ) + cls_grad.reshape(token_count, model_width)
        gain_two_grad = jnp.sum(dout * second_normed, axis=0)
        shift_two_grad = jnp.sum(dout, axis=0)
        dsecond = norm_back(dout, second_normed, second_factor, gain_two)
        douter = dsecond.astype(jnp.bfloat16)
        outer_bias_grad = jnp.sum(douter.astype(jnp.float32), axis=0)
        outer_weight_grad = jnp.einsum(
            "nf,nd->fd", active, douter, preferred_element_type=jnp.float32
        )
        dactive = jnp.einsum("nd,fd->nf", douter, w_outer, preferred_element_type=jnp.float32)
        dinner = (dactive * gelu_slope(inner_pre)).astype(jnp.bfloat16)
        inner_bias_grad = jnp.sum(dinner.astype(jnp.float32), axis=0)
        inner_weight_grad = jnp.einsum(
            "nd,nf->df", first_low, dinner, preferred_element_type=jnp.float32
        )
        dfirst = dsecond + jnp.einsum(
            "nf,df->nd", dinner, w_inner, preferred_element_type=jnp.float32
        )
        gain_one_grad = jnp.sum(dfirst * first_normed, axis=0)
        shift_one_grad = jnp.sum(dfirst, axis=0)
        dresidual = norm_back(dfirst, first_normed, first_factor, gain_one)
        dattended = dresidual.astype(jnp.bfloat16)
        output_bias_grad = jnp.sum(dattended.astype(jnp.float32), axis=0)
        output_weight_grad = jnp.einsum(
            "nd,ne->de", context_low, dattended, preferred_element_type=jnp.float32
        )
        dcontext = jnp.einsum(
            "ne,de->nd", dattended, wo_full, preferred_element_type=jnp.float32
        ).astype(jnp.bfloat16)
        dcontext_wide = dcontext.astype(jnp.float32).reshape(head_shape)
        push_grad = (dcontext_wide / total_heads).astype(jnp.bfloat16)
        delta_term = jnp.transpose(
            jnp.sum(dcontext_wide * context, axis=-1) / total_heads[..., 0], (0, 2, 1)
        )
        own_query, own_key, own_value = contribute(
            query_rows,
            push_grad,
            delta_term,
            row_peak,
            segment,
            key_rows,
            value_rows,
            segment,
            score_scale,
        )

        def key_step(cycle_step, cycle_carry):
            visit_keys, visit_values, visit_segment, query_sum, key_sum, value_sum = cycle_carry
            visit_keys, visit_values, visit_segment = passed_along(
                (visit_keys, visit_values, visit_segment), "blk", 1
            )
            key_sum, value_sum = (
                passed_along(key_sum.astype(jnp.bfloat16), "blk", 1).astype(key_sum.dtype),
                passed_along(value_sum.astype(jnp.bfloat16), "blk", 1).astype(value_sum.dtype),
            )
            query_part, key_part, value_part = contribute(
                query_rows,
                push_grad,
                delta_term,
                row_peak,
                segment,
                visit_keys,
                visit_values,
                visit_segment,
                score_scale,
            )
            return (
                visit_keys,
                visit_values,
                visit_segment,
                query_sum + query_part,
                key_sum + key_part,
                value_sum + value_part,
            )

        back_carry = lax.fori_loop(
            1, cycle_size, key_step, (key_rows, value_rows, segment, own_query, own_key, own_value)
        )
        query_sum = back_carry[3]
        key_sum, value_sum = (
            passed_along(back_carry[4].astype(jnp.bfloat16), "blk", 1).astype(jnp.float32),
            passed_along(back_carry[5].astype(jnp.bfloat16), "blk", 1).astype(jnp.float32),
        )
        dquery = query_sum.astype(jnp.bfloat16).reshape(token_count, model_width)
        dkey = key_sum.astype(jnp.bfloat16).reshape(token_count, model_width)
        dvalue = value_sum.astype(jnp.bfloat16).reshape(token_count, model_width)
        dhidden = dresidual + jnp.einsum(
            "ne,de->nd", dquery, wq_full, preferred_element_type=jnp.float32
        )
        dhidden = dhidden + jnp.einsum(
            "ne,de->nd", dkey, wk_full, preferred_element_type=jnp.float32
        )
        dhidden = dhidden + jnp.einsum(
            "ne,de->nd", dvalue, wv_full, preferred_element_type=jnp.float32
        )
        hgrad_list.append(
            dhidden.astype(jnp.bfloat16).reshape(row_count, block_tokens, model_width)
        )
        local_grads = (
            jnp.einsum("nd,ne->de", flat_rows, dquery, preferred_element_type=jnp.float32),
            jnp.einsum("nd,ne->de", flat_rows, dkey, preferred_element_type=jnp.float32),
            jnp.einsum("nd,ne->de", flat_rows, dvalue, preferred_element_type=jnp.float32),
            output_weight_grad,
            jnp.sum(dquery.astype(jnp.float32), axis=0),
            jnp.sum(dvalue.astype(jnp.float32), axis=0),
            output_bias_grad,
            gain_one_grad,
            shift_one_grad,
            inner_weight_grad,
            inner_bias_grad,
            outer_weight_grad,
            outer_bias_grad,
            gain_two_grad,
            shift_two_grad,
        )
        local_sum = local_grads
        reduced = jax.tree.map(
            lambda part: part.astype(jnp.float32),
            lax.psum_scatter(as_sent(local_sum), "dp", scatter_dimension=0, tiled=True),
        )
        reduced = jax.tree.map(
            lambda part: part.astype(jnp.float32), lax.psum(as_sent(reduced), "blk")
        )
        grad_totals = tuple(
            (total_piece + new_piece for total_piece, new_piece in zip(grad_totals, reduced))
        )
        local_sum = None
    return (
        jnp.stack(out_list),
        jnp.stack(embed_list),
        jnp.stack(loss_list),
        jnp.stack(qgrad_list),
        jnp.stack(hgrad_list),
        grad_totals[0],
        grad_totals[1],
        grad_totals[2],
        grad_totals[3],
        grad_totals[4],
        grad_totals[5],
        grad_totals[6],
        grad_totals[7],
        grad_totals[8],
        grad_totals[9],
        grad_totals[10],
        grad_totals[11],
        grad_totals[12],
        grad_totals[13],
        grad_totals[14],
    )


MESH = pl.DeviceIdType.MESH
VMEM_LIMIT = 60 * 1024 * 1024
SIDE = {"c": 1, "x": 2, "y": 4}


def place():
    dp, blk = lax.axis_index("dp"), lax.axis_index("blk")
    bits = {"c": lax.rem(dp, 2), "x": lax.rem(dp // 2, 2), "y": dp // 4}
    return dp, blk, bits


def across(dp, blk, bits, *axes):
    other = dp
    for axis in axes:
        other = other + SIDE[axis] * (1 - 2 * bits[axis])
    return (other, blk)


def greet(peers):
    barrier = pltpu.get_barrier_semaphore()
    for peer in peers:
        pl.semaphore_signal(barrier, inc=1, device_id=peer, device_id_type=MESH)
    pl.semaphore_wait(barrier, len(peers))


def remote(source, target, send_sem, recv_sem, peer):
    return pltpu.make_async_remote_copy(
        src_ref=source,
        dst_ref=target,
        send_sem=send_sem,
        recv_sem=recv_sem,
        device_id=peer,
        device_id_type=MESH,
    )


def comm_params(collective):
    return pltpu.CompilerParams(
        collective_id=collective, has_side_effects=True, vmem_limit_bytes=VMEM_LIMIT
    )


ANY = pl.BlockSpec(memory_space=pl.ANY)
IN_VMEM = pl.BlockSpec(memory_space=pltpu.VMEM)


SLABS = 2


def forward_kernel(items, ring_size, depth, sources, places, *refs):
    shards, seg_shard, hidden = refs[:sources], refs[sources], refs[sources + 1]
    outs = refs[sources + 2 :]
    fulls = outs[:places]
    seg_full, hidden_row, qkv, context, stats, context_t = outs[places : places + 6]
    (
        hidden_full,
        low,
        seg_line,
        mask,
        turned,
        keys,
        send_sem,
        recv_sem,
        seg_send,
        seg_recv,
        line_send,
        line_recv,
        head_send,
        head_recv,
        local_sem,
    ) = outs[places + 6 :]
    w_window, pack_full = fulls[0], fulls[1]
    dp, blk, bits = place()
    sibling = across(dp, blk, bits, "c")
    ring = [(dp, lax.rem(blk + step, ring_size)) for step in range(1, ring_size)]
    greet([sibling, across(dp, blk, bits, "x"), across(dp, blk, bits, "y")] + ring)
    seg_rows = seg_shard.shape[0]
    micro, tokens, width = hidden.shape
    spread = ring_size // micro
    row_at, group_at = blk // spread, lax.rem(blk, spread)
    group, length = context.shape
    heads = group // depth
    score_scale = 1.0 / math.sqrt(depth)
    waiting = []
    mine = pl.ds(pl.multiple_of(blk * tokens, tokens), tokens)

    slab = tokens // SLABS

    def line_view(m, side, distance, part):
        owner = blk + (1 - 2 * side) * distance
        first = owner * tokens + part * slab
        return hidden_full.at[m, pl.ds(pl.multiple_of(first, slab), slab)]

    def line_copy(m, side, distance, part):
        view = line_view(m, side, distance, part)
        return remote(
            hidden.at[m, pl.ds(part * slab, slab)] if distance == 0 else view,
            view,
            line_send.at[m, side, distance, part],
            line_recv.at[m, side, distance + 1, part],
            (dp, blk - 1 + 2 * side),
        )

    def arrival(m, side, distance, part):
        view = line_view(m, side, distance, part)
        return remote(
            view,
            view,
            line_send.at[m, side, distance, part],
            line_recv.at[m, side, distance, part],
            (dp, blk - 1 + 2 * side),
        )

    def passes_on(m, side):
        return blk > m * spread if side == 0 else blk < m * spread + spread - 1

    def comes(m, side, distance):
        if side == 0:
            return (blk >= m * spread) & (blk + distance < ring_size)
        return (blk < m * spread + spread) & (blk >= distance)

    def line_step(distance, part):
        for m in range(micro):
            for side in range(2):

                @pl.when(comes(m, side, distance))
                def _():
                    arrival(m, side, distance, part).wait_recv()

                if distance < ring_size - 1:

                    @pl.when(comes(m, side, distance) & passes_on(m, side))
                    def _():
                        line_copy(m, side, distance, part).start()

    for part in range(SLABS):
        for m in range(micro):
            for side in range(2):

                @pl.when(passes_on(m, side))
                def _():
                    line_copy(m, side, 0, part).start()

    def own_part(item):
        spec = items[item]
        column = spec["from_column"]
        if column is None:
            column = pl.multiple_of(group_at * group, group)
        return shards[spec["source"]].at[
            pl.ds(spec["row"], spec["rows"]), pl.ds(column, spec["columns"])
        ]

    def block(item, owner):
        spec = items[item]
        first = owner * spec["stride"] + spec["row"]
        return fulls[spec["target"]].at[
            pl.ds(first, spec["rows"]), pl.ds(spec["to_column"], spec["columns"])
        ]

    inbound = {}

    def start_item(item):
        first, second = items[item]["route"]
        for slot, peer in enumerate(
            (across(dp, blk, bits, first), across(dp, blk, bits, second), sibling)
        ):
            copy = remote(
                own_part(item),
                block(item, dp),
                send_sem.at[item, slot],
                recv_sem.at[item, slot],
                peer,
            )
            copy.start()
            inbound[item, slot] = copy
        copy = pltpu.make_async_copy(own_part(item), block(item, dp), local_sem.at[item])
        copy.start()
        inbound[item, "own"] = copy

    def pass_on(item, held, slot, peer):
        copy = remote(held, held, send_sem.at[item, slot], recv_sem.at[item, slot], peer)
        copy.start()
        inbound[item, slot] = copy

    def relay_first(item):
        first, second = items[item]["route"]
        inbound[item, 0].wait_recv()
        held = block(item, across(dp, blk, bits, first)[0])
        pass_on(item, held, 3, across(dp, blk, bits, second))
        pass_on(item, held, 4, sibling)
        inbound[item, 1].wait_recv()
        pass_on(item, block(item, across(dp, blk, bits, second)[0]), 5, sibling)

    def relay_third(item):
        first, second = items[item]["route"]
        inbound[item, 3].wait_recv()
        pass_on(item, block(item, across(dp, blk, bits, first, second)[0]), 6, sibling)

    def all_here(item):
        for slot in (2, 4, 5, 6):
            inbound[item, slot].wait_recv()
        inbound[item, "own"].wait()

    early = [i for i, spec in enumerate(items) if spec["target"] < 2]
    late = [i for i, spec in enumerate(items) if spec["target"] >= 2]
    tick_of = [0]

    def tick(times=1):
        for _ in range(times):
            now = tick_of[0]
            tick_of[0] += 1
            if 0 <= now - 2 * LAG < len(late):
                relay_third(late[now - 2 * LAG])
            if 0 <= now - LAG < len(late):
                relay_first(late[now - LAG])
            if now < len(late):
                start_item(late[now])

    for item in early:
        start_item(item)
    for step, peer in enumerate(ring):
        copy = remote(
            seg_shard,
            seg_full.at[pl.ds(blk * seg_rows, seg_rows)],
            seg_send.at[step],
            seg_recv.at[step],
            peer,
        )
        copy.start()
        waiting.append(copy)
    seg_full[pl.ds(blk * seg_rows, seg_rows)] = seg_shard[...]

    for item in early:
        relay_first(item)
    tick()
    line_step(1, 0)
    tick()
    for part in range(1, SLABS):
        line_step(1, part)
    for item in early:
        relay_third(item)
    tick()
    for copy in waiting:
        copy.wait()
    for member in range(ring_size):
        seg_line[:, member * tokens : (member + 1) * tokens] = seg_full[
            pl.ds(member * seg_rows + row_at, 1)
        ].astype(jnp.float32)
    seg_col = columns_of(seg_line[...])
    for item in early:
        all_here(item)
    pack_turned = pack_full[...].astype(jnp.float32).T
    piece = width // (pack_full.shape[0] // 16)
    lane = lax.broadcasted_iota(jnp.int32, (piece, pack_full.shape[0]), 1)

    def bias_column(vector):
        pieces = []
        for part in range(group // piece):
            at = (group_at * (group // piece) + part) * 16 + vector
            pieces.append(
                jnp.sum(
                    jnp.where(lane == at, pack_turned[:piece], 0.0), axis=1, keepdims=True
                )
            )
        return jnp.concatenate(pieces, axis=0)

    biases = (bias_column(0), None, bias_column(1))
    for part in range(3):
        rows = slice(part * group, (part + 1) * group)
        turned[rows, :] = w_window[:, rows].T

    def project(at, source):
        span = pl.ds(pl.multiple_of(at * tokens, tokens), tokens)
        values = source[...]
        hidden_row[span, :] = values
        for part in range(3):
            rows = slice(part * group, (part + 1) * group)
            result = contract(turned[rows, :], values, 1, 1)
            if biases[part] is not None:
                result = result + biases[part]
            qkv[rows, span] = result.astype(jnp.bfloat16)

    def project_at(distance):
        for side in range(2):
            at = blk + (1 - 2 * side) * distance

            @pl.when((at >= 0) & (at < ring_size))
            def _():
                view = hidden_full.at[row_at, pl.ds(pl.multiple_of(at * tokens, tokens), tokens)]
                project(at, view)

    if ring_size > 2:
        line_step(2, 0)
    project(blk, hidden.at[row_at])
    tick()
    project_at(1)
    for distance in range(2, ring_size):
        for part in range(SLABS):
            if distance > 2 or part > 0:
                line_step(distance, part)
                tick()
        project_at(distance)

    copies = []

    def head_rows(part, head):
        first = part * group + head * depth
        return slice(first, first + depth)

    for head in range(heads):
        keys[head] = qkv[head_rows(1, head), :].T

    def attend(at):
        span = pl.ds(pl.multiple_of(at * tokens, tokens), tokens)
        mask[...] = jnp.where(seg_col == seg_line[:, span], 0.0, NEGATIVE)
        for head in range(heads):
            rows = head_rows(0, head)
            queries = (qkv[rows, span].astype(jnp.float32) * score_scale).astype(jnp.bfloat16)
            scores = contract(keys[head], queries, 1, 0) + mask[...]
            peak = jnp.max(scores, axis=0, keepdims=True)
            weights = jnp.exp(scores - peak)
            total = jnp.sum(weights, axis=0, keepdims=True)
            ctx = contract(qkv[head_rows(2, head), :], weights.astype(jnp.bfloat16), 1, 0) / total
            context[rows, span] = ctx
            low[rows, span] = ctx.astype(jnp.bfloat16)
            stats[2 * head : 2 * head + 1, span] = peak
            stats[2 * head + 1 : 2 * head + 2, span] = total

    end = (ring_size - 1) * (1 - row_at)
    order = (end, end + 2 * row_at - 1, blk + 1 - 2 * lax.rem(blk, 2), blk)
    target = context_t.at[row_at, pl.ds(group_at * group, group)]
    for index, at in enumerate(order):
        attend(at)
        span = pl.ds(pl.multiple_of(at * tokens, tokens), tokens)
        if index < ring_size - 1:
            step = lax.rem(at - blk + ring_size, ring_size)
            copy = remote(low.at[:, span], target, head_send.at[index], head_recv.at[step], (dp, at))
            copy.start()
            copies.append(copy)
        else:
            target[...] = low[:, span]
        tick(2)
    tick(len(late) + 2 * LAG - tick_of[0])
    for item in late:
        all_here(item)
    for item in early + late:
        for slot in range(7):
            inbound[item, slot].wait_send()
    for copy in copies:
        copy.wait_send()
    for step, peer in enumerate(ring):
        remote(target, target, head_send.at[0], head_recv.at[step + 1], peer).wait_recv()
    for m in range(micro):
        for side in range(2):
            for distance in range(ring_size - 1):
                ready = passes_on(m, side)
                if distance:
                    ready = ready & comes(m, side, distance)

                @pl.when(ready)
                def _():
                    for part in range(SLABS):
                        line_copy(m, side, distance, part).wait_send()


def columns_of(row):
    return jnp.broadcast_to(row, (128, row.shape[1])).T[:, :1]


def forward(shards, items, targets, segments, hidden, ring_size, depth):
    micro, tokens, width = hidden.shape
    count = len(shards)
    length = ring_size * tokens
    group = width * micro // ring_size
    heads = group // depth
    shape = jax.ShapeDtypeStruct
    return pl.pallas_call(
        functools.partial(forward_kernel, items, ring_size, depth, count, len(targets)),
        out_shape=tuple(targets)
        + (
            shape((ring_size * segments.shape[0], tokens), jnp.int32),
            shape((length, width), jnp.bfloat16),
            shape((3 * group, length), jnp.bfloat16),
            shape((group, length), jnp.float32),
            shape((2 * heads, length), jnp.float32),
            shape((micro, width, tokens), jnp.bfloat16),
        ),
        in_specs=[IN_VMEM] * (count + 2),
        out_specs=(IN_VMEM, IN_VMEM) + (ANY,) * (len(targets) - 2) + (IN_VMEM,) * 6,
        scratch_shapes=[
            pltpu.VMEM((micro, length, width), jnp.bfloat16),
            pltpu.VMEM((group, length), jnp.bfloat16),
            pltpu.VMEM((1, length), jnp.float32),
            pltpu.VMEM((length, tokens), jnp.float32),
            pltpu.VMEM((3 * group, width), jnp.bfloat16),
            pltpu.VMEM((heads, length, depth), jnp.bfloat16),
            pltpu.SemaphoreType.DMA((len(items), 7)),
            pltpu.SemaphoreType.DMA((len(items), 7)),
            pltpu.SemaphoreType.DMA((ring_size,)),
            pltpu.SemaphoreType.DMA((ring_size,)),
            pltpu.SemaphoreType.DMA((micro, 2, ring_size, SLABS)),
            pltpu.SemaphoreType.DMA((micro, 2, ring_size, SLABS)),
            pltpu.SemaphoreType.DMA((ring_size,)),
            pltpu.SemaphoreType.DMA((ring_size,)),
            pltpu.SemaphoreType.DMA((len(items),)),
        ],
        compiler_params=comm_params(1),
    )(*shards, segments, hidden)


def contract(left, right, left_dim, right_dim):
    return lax.dot_general(
        left, right, (((left_dim,), (right_dim,)), ((), ())), preferred_element_type=jnp.float32
    )


LAG, AHEAD = 2, 3


def added(left, right):
    return (left.astype(jnp.float32) + right.astype(jnp.float32)).astype(jnp.bfloat16)


def backward_kernel(items, ring_size, depth, *refs):
    (
        dcontext_part,
        seg_row,
        pack_part,
        qkv_out,
        context_out,
        stats,
        w_window_out,
        hidden_row_out,
        dresidual_out,
        outer_grad,
        inner_grad,
        output_grad,
    ) = refs[:12]
    dhidden, d_outer, d_inner, d_output, d_window, d_pack = refs[12:18]
    (
        qkv,
        context,
        w_window,
        hidden_row,
        dresidual,
        dcontext,
        dwindow,
        parts,
        passed,
        arrived,
        window_grad,
        pack_sum,
        pack_low,
        own,
        from_core,
        from_first,
        from_second,
        ring_one,
        ring_two,
        load_sem,
        head_send,
        head_recv,
        hop_send,
        hop_recv,
        send_sem,
        recv_sem,
        local_sem,
    ) = refs[18:]
    grads = (outer_grad, inner_grad, output_grad, window_grad, pack_low)
    outs = (d_outer, d_inner, d_output, d_window, d_pack)
    count = len(items)
    dp, blk, bits = place()
    sibling = across(dp, blk, bits, "c")
    is_end = (blk == 0) | (blk == ring_size - 1)
    is_middle = jnp.logical_not(is_end)
    partner = (dp, blk + 1 - 2 * lax.rem(blk, 2))
    facing = (dp, ring_size - 1 - blk)
    ring = [(dp, lax.rem(blk + step, ring_size)) for step in range(1, ring_size)]
    greet([sibling, across(dp, blk, bits, "x"), across(dp, blk, bits, "y")] + ring)

    micro, width, tokens = dcontext_part.shape
    spread = ring_size // micro
    row_at, group_at = blk // spread, lax.rem(blk, spread)
    group, length = context.shape
    heads = group // depth
    score_scale = 1.0 / math.sqrt(depth)
    mine = pl.ds(pl.multiple_of(blk * tokens, tokens), tokens)

    loads = []
    for index, (source, target) in enumerate(
        (
            (qkv_out, qkv),
            (context_out, context),
            (w_window_out, w_window),
            (hidden_row_out, hidden_row),
            (dresidual_out, dresidual),
        )
    ):
        copy = pltpu.make_async_copy(source, target, load_sem.at[index])
        copy.start()
        loads.append(copy)

    head_copies = []
    def send_head(head):
        for step in range(1, ring_size):
            owner = lax.rem(blk + step, ring_size)
            first = lax.rem(owner, spread) * group + head * depth
            copy = remote(
                dcontext_part.at[owner // spread, pl.ds(first, depth)],
                dcontext.at[pl.ds(head * depth, depth), mine],
                head_send.at[head, step],
                head_recv.at[head, step],
                (dp, owner),
            )
            copy.start()
            head_copies.append(copy)
    send_head(0)
    send_head(1)
    dcontext[:, mine] = dcontext_part[row_at, pl.ds(group_at * group, group)]

    def owner_of(core, axes, first_bit, second_bit):
        return core + SIDE[axes[0]] * first_bit + SIDE[axes[1]] * second_bit

    def block(item, which):
        spec = items[item]
        return grads[spec["source"]].at[
            pl.ds(which * spec["stride"] + spec["row"], spec["rows"]),
            pl.ds(spec["column"], spec["columns"]),
        ]

    def cut(buffer, item, *index):
        spec = items[item]
        return buffer.at[(item,) + index + (pl.ds(0, spec["rows"]), pl.ds(0, spec["columns"]))]

    def wide_cut(buffer, item, *index):
        spec = items[item]
        columns = spec["columns"] * spec["widened"]
        return buffer.at[(item,) + index + (pl.ds(0, spec["rows"]), pl.ds(0, columns))]

    def result(item):
        spec = items[item]
        many = spec["widened"]
        return outs[spec["source"]].at[
            pl.ds(spec["row"], spec["rows"]),
            pl.ds(spec["column"] * many, spec["columns"] * many),
        ]

    def copier(source, target, item, slot, peer):
        return remote(source, target, send_sem.at[item, slot], recv_sem.at[item, slot], peer)

    flying = {}

    def go(source, target, item, slot, peer):
        copy = copier(source, target, item, slot, peer)
        copy.start()
        flying[item, slot] = copy

    def start_core(item):
        axes = items[item]["route"]
        for f in range(2):
            for s in range(2):
                slot = 2 * f + s
                go(
                    block(item, owner_of(1 - bits["c"], axes, f, s)),
                    cut(from_core, item, f, s),
                    item,
                    slot,
                    sibling,
                )
                copy = pltpu.make_async_copy(
                    block(item, owner_of(bits["c"], axes, f, s)),
                    cut(own, item, f, s),
                    local_sem.at[item, slot],
                )
                copy.start()
                flying[item, "own", slot] = copy

    def after_core(item):
        axes = items[item]["route"]
        kept = bits[axes[0]]
        for slot in range(4):
            flying[item, slot].wait_recv()
            flying[item, "own", slot].wait()
        for stays, f in ((False, 1 - kept), (True, kept)):
            for s in range(2):
                part = cut(own, item, f, s)
                part[...] = added(part[...], cut(from_core, item, f, s)[...])
                if not stays:
                    peer = across(dp, blk, bits, axes[0])
                    go(part, cut(from_first, item, s), item, 4 + s, peer)

    def after_first(item):
        axes = items[item]["route"]
        f, kept = bits[axes[0]], bits[axes[1]]
        for s in range(2):
            flying[item, 4 + s].wait_recv()
        part = cut(own, item, f, 1 - kept)
        part[...] = added(part[...], cut(from_first, item, 1 - kept)[...])
        go(part, cut(from_second, item), item, 6, across(dp, blk, bits, axes[1]))
        part = cut(own, item, f, kept)
        part[...] = added(part[...], cut(from_first, item, kept)[...])

    def after_second(item):
        spec = items[item]
        axes = spec["route"]
        f, s = bits[axes[0]], bits[axes[1]]
        flying[item, 6].wait_recv()
        total = added(cut(own, item, f, s)[...], cut(from_second, item)[...])
        if spec["widened"] > 1:
            wide_cut(ring_one, item, 0)[...] = jnp.zeros(
                (spec["rows"], spec["columns"] * spec["widened"]), jnp.bfloat16
            )
            at = pl.multiple_of(group_at * spec["columns"], 128)
            ring_one[item, 0, pl.ds(0, spec["rows"]), pl.ds(at, spec["columns"])] = total
        else:
            wide_cut(ring_one, item, 0)[...] = total
        flying[item, 7] = copier(
            wide_cut(ring_one, item, 0), wide_cut(ring_one, item, 1), item, 7, partner
        )
        flying[item, 8] = copier(
            wide_cut(ring_two, item, 0), wide_cut(ring_two, item, 1), item, 8, facing
        )
        flying[item, 9] = copier(result(item), result(item), item, 9, partner)

        @pl.when(is_end)
        def _():
            flying[item, 7].start()

    def at_middle(item):
        @pl.when(is_middle)
        def _():
            flying[item, 7].wait_recv()
            part = wide_cut(ring_two, item, 0)
            part[...] = added(wide_cut(ring_one, item, 0)[...], wide_cut(ring_one, item, 1)[...])
            flying[item, 8].start()

    def across_middle(item):
        @pl.when(is_middle)
        def _():
            flying[item, 8].wait_recv()
            result(item)[...] = added(
                wide_cut(ring_two, item, 0)[...], wide_cut(ring_two, item, 1)[...]
            )
            flying[item, 9].start()

    def at_end(item):
        @pl.when(is_end)
        def _():
            flying[item, 9].wait_recv()

    stages = (after_core, after_first, after_second, at_middle, across_middle, at_end)
    tick_of = [0]

    def tick(times=1):
        for _ in range(times):
            now = tick_of[0]
            tick_of[0] += 1
            for stage in reversed(range(len(stages))):
                item = now - LAG * stage
                if 0 <= item < count:
                    stages[stage](item)
            if now + AHEAD < len(early):
                start_core(early[now + AHEAD])

    early = [i for i, spec in enumerate(items) if spec["source"] < 3]
    late = [i for i, spec in enumerate(items) if spec["source"] >= 3]
    for item in early[:AHEAD]:
        start_core(item)

    seg_line = seg_row[...].astype(jnp.float32)
    seg_col = columns_of(seg_line)

    def one_head(head):
        def rows(part):
            first = part * group + head * depth
            return slice(first, first + depth)

        for step in range(ring_size - 1):
            head_copies[head * (ring_size - 1) + step].wait_recv()
        keys, values = qkv[rows(1), :].T, qkv[rows(2), :].T
        keys_t = qkv[rows(1), :]
        dkey_sum = jnp.zeros((depth, length), jnp.float32)
        dvalue_sum = jnp.zeros((depth, length), jnp.float32)
        for start in range(0, length, tokens):
            span = slice(start, start + tokens)
            peak = stats[2 * head : 2 * head + 1, span]
            total = stats[2 * head + 1 : 2 * head + 2, span]
            dctx = dcontext[rows(0), span].astype(jnp.float32)
            push = (dctx / total).astype(jnp.bfloat16)
            delta = jnp.sum(dctx * context[rows(0), span], axis=0, keepdims=True) / total
            queries_t = qkv[rows(0), span]
            raw = contract(keys, queries_t, 1, 0)
            same = seg_col == seg_line[:, span]
            weights = jnp.exp(jnp.where(same, raw * score_scale, NEGATIVE) - peak)
            pushed = contract(values, push, 1, 0)
            dscore = (weights * (pushed - delta) * score_scale).astype(jnp.bfloat16)
            dwindow[rows(0), span] = contract(keys_t, dscore, 1, 0).astype(jnp.bfloat16)
            dkey_sum = dkey_sum + contract(queries_t, dscore, 1, 1)
            dvalue_sum = dvalue_sum + contract(push, weights.astype(jnp.bfloat16), 1, 1)
        dwindow[rows(1), :] = dkey_sum.astype(jnp.bfloat16)
        dwindow[rows(2), :] = dvalue_sum.astype(jnp.bfloat16)

    loads[0].wait()
    loads[1].wait()
    for head in range(heads):
        if head + 2 < heads:
            send_head(head + 2)
        one_head(head)
        tick()
    loads[2].wait()
    loads[3].wait()
    loads[4].wait()

    low = [m * spread for m in range(micro)]
    high = [m * spread + spread - 1 for m in range(micro)]

    def owns(m):
        return (blk >= low[m]) & (blk <= high[m])

    def receives(m, side):
        return blk + 1 <= high[m] if side == 0 else blk - 1 >= low[m]

    def has_target(side, distance):
        return blk >= distance if side == 0 else blk + distance < ring_size

    def hop(source, m, side, distance):
        return remote(
            source,
            arrived.at[m, side, distance - 1],
            hop_send.at[m, side, distance],
            hop_recv.at[m, side, distance - 1],
            (dp, blk - 1 + 2 * side),
        )

    def arrival(m, side, distance):
        view = arrived.at[m, side, distance]
        return remote(
            view,
            view,
            hop_send.at[m, side, distance],
            hop_recv.at[m, side, distance],
            (dp, blk - 1 + 2 * side),
        )

    def send_fresh(distance):
        for m in range(micro):
            for side in range(2):
                target = blk - distance * (1 - 2 * side)
                goes = has_target(side, distance) & owns(m)

                @pl.when(goes & jnp.logical_not(receives(m, side)))
                def _():
                    hop(parts.at[target], m, side, distance).start()

    def send_on(distance):
        for m in range(micro):
            for side in range(2):
                target = blk - distance * (1 - 2 * side)
                goes = has_target(side, distance) & receives(m, side)

                @pl.when(goes & owns(m))
                def _():
                    arrival(m, side, distance).wait_recv()
                    passed[side, distance - 1] = added(parts[target], arrived[m, side, distance])
                    hop(passed.at[side, distance - 1], m, side, distance).start()

                @pl.when(goes & jnp.logical_not(owns(m)))
                def _():
                    arrival(m, side, distance).wait_recv()
                    hop(arrived.at[m, side, distance], m, side, distance).start()

    def finish_hidden(_):
        for m in range(micro):
            for side in range(2):
                inside = blk < ring_size - 1 if side == 0 else blk > 0
                here = receives(m, side) & inside

                @pl.when(here & owns(m))
                def _():
                    arrival(m, side, 0).wait_recv()
                    dhidden[m] = (
                        dresidual[m]
                        + parts[blk].astype(jnp.float32)
                        + arrived[m, side, 0].astype(jnp.float32)
                    ).astype(jnp.bfloat16)

                @pl.when(here & jnp.logical_not(owns(m)))
                def _():
                    arrival(m, side, 0).wait_recv()
                    dhidden[m] = (
                        dresidual[m] + arrived[m, side, 0].astype(jnp.float32)
                    ).astype(jnp.bfloat16)

    end = (ring_size - 1) * (1 - row_at)
    inward = 2 * row_at - 1
    order = (end, end + inward, blk + 1 - 2 * lax.rem(blk, 2), blk)

    def make_part(target):
        at = pl.ds(pl.multiple_of(target * tokens, tokens), tokens)
        parts[target] = contract(dwindow[:, at].T, w_window[...], 1, 1).astype(jnp.bfloat16)

    ones = jnp.ones((8, length), jnp.bfloat16)
    line = lax.broadcasted_iota(jnp.int32, (8, 128), 0)
    lane = lax.broadcasted_iota(jnp.int32, (8, 128), 1)
    piece = width // (pack_part.shape[0] // 16)
    pack_sum[...] = pack_part[...]

    def make_grad(part):
        rows = slice(part * group, (part + 1) * group)
        window_grad[:, rows] = contract(hidden_row[...].T, dwindow[rows, :], 1, 1).astype(
            jnp.bfloat16
        )
        if part != 1:
            sums = contract(ones, dwindow[rows, :], 1, 1)
            sums = jnp.concatenate((sums, jnp.zeros((8, 128), jnp.float32)), axis=1)
            for step in range(group // piece):
                first = pl.multiple_of((group_at * (group // piece) + step) * 16, 16)
                pack_sum[pl.ds(first, 8), 0:128] += jnp.where(
                    (line == part // 2) & (lane < piece),
                    sums[:, step * piece : step * piece + 128],
                    0.0,
                )
        start_core(late[part])

    for index, target in enumerate(order):
        make_part(target)
        if index < ring_size - 1:
            send_fresh(ring_size - 1 - index)
            make_grad(index)
            tick()
    pack_low[...] = pack_sum[...].astype(jnp.bfloat16)
    start_core(late[3])
    for distance in reversed(range(1, ring_size - 1)):
        send_on(distance)
        tick(2)
    finish_hidden(None)
    tick(count + LAG * (len(stages) - 1) - tick_of[0])

    for copy in head_copies:
        copy.wait_send()
    for item in range(count):
        for slot in range(7):
            flying[item, slot].wait_send()
    for distance in range(1, ring_size):
        for m in range(micro):
            for side in range(2):

                @pl.when(has_target(side, distance) & (receives(m, side) | owns(m)))
                def _():
                    hop(parts.at[0], m, side, distance).wait_send()

    @pl.when(is_end)
    def _():
        for item in range(count):
            flying[item, 7].wait_send()

    @pl.when(is_middle)
    def _():
        for item in range(count):
            flying[item, 8].wait_send()
            flying[item, 9].wait_send()


def backward(
    dcontext_part,
    seg_row,
    pack_part,
    saved,
    w_window,
    hidden_row,
    dresidual,
    grads,
    items,
    ring_size,
    dp_size,
    depth,
    collective,
):
    qkv, context, stats = saved
    micro, width, tokens = dcontext_part.shape
    group, length = context.shape
    heads = group // depth
    spread = ring_size // micro
    count = len(items)
    rows = max(item["rows"] for item in items)
    columns = max(item["columns"] * item["widened"] for item in items)
    piece = (rows, columns)
    narrow = jnp.bfloat16
    shape = jax.ShapeDtypeStruct
    outs = [shape((grad.shape[0] // dp_size, grad.shape[1]), narrow) for grad in grads]
    outs.append(shape((width // dp_size, 3 * width), narrow))
    outs.append(shape((pack_part.shape[0] // dp_size, pack_part.shape[1]), narrow))
    scratch = [
        pltpu.VMEM(qkv.shape, narrow),
        pltpu.VMEM(context.shape, jnp.float32),
        pltpu.VMEM(w_window.shape, narrow),
        pltpu.VMEM(hidden_row.shape, narrow),
        pltpu.VMEM(dresidual.shape, jnp.float32),
        pltpu.VMEM((group, length), narrow),
        pltpu.VMEM(qkv.shape, narrow),
        pltpu.VMEM((ring_size, tokens, width), narrow),
        pltpu.VMEM((2, ring_size - 2, tokens, width), narrow),
        pltpu.VMEM((micro, 2, ring_size - 1, tokens, width), narrow),
        pltpu.VMEM((width, 3 * group), narrow),
        pltpu.VMEM(pack_part.shape, jnp.float32),
        pltpu.VMEM(pack_part.shape, narrow),
    ]
    scratch += [
        pltpu.VMEM((count,) + lead + piece, narrow)
        for lead in ((2, 2), (2, 2), (2,), (), (2,), (2,))
    ]
    scratch += [
        pltpu.SemaphoreType.DMA((5,)),
        pltpu.SemaphoreType.DMA((heads, ring_size)),
        pltpu.SemaphoreType.DMA((heads, ring_size)),
        pltpu.SemaphoreType.DMA((micro, 2, ring_size)),
        pltpu.SemaphoreType.DMA((micro, 2, ring_size)),
        pltpu.SemaphoreType.DMA((count, 10)),
        pltpu.SemaphoreType.DMA((count, 10)),
        pltpu.SemaphoreType.DMA((count, 4)),
    ]
    return pl.pallas_call(
        functools.partial(backward_kernel, items, ring_size, depth),
        out_shape=(shape((micro, tokens, width), narrow),) + tuple(outs),
        in_specs=[IN_VMEM] * 3 + [ANY, ANY, IN_VMEM, ANY, ANY, ANY] + [ANY] * 3,
        out_specs=(IN_VMEM,) * 6,
        scratch_shapes=scratch,
        compiler_params=comm_params(collective),
    )(
        dcontext_part,
        seg_row,
        pack_part,
        qkv,
        context,
        stats,
        w_window,
        hidden_row,
        dresidual,
        *grads,
    )


def split_dot(left, right, left_dim, right_dim):
    high = left.astype(jnp.bfloat16)
    rest = (left - high.astype(jnp.float32)).astype(jnp.bfloat16)
    return contract(high, right, left_dim, right_dim) + contract(rest, right, left_dim, right_dim)


def retrieve_kernel(
    ring_size,
    dp_size,
    output,
    cotangent,
    seg_full,
    queries_all,
    hot_all,
    dout,
    embeddings,
    loss,
    query_grad,
    own,
    arrived,
    tables,
    everyone,
    asked,
    hot,
    wide_loss,
    dscore,
    turned,
    send_sem,
    recv_sem,
    ring_send,
    ring_recv,
):
    dp, blk, _ = place()
    ring = [(dp, lax.rem(blk + step, ring_size)) for step in range(1, ring_size)]
    members = [(lax.rem(dp + step, dp_size), blk) for step in range(1, dp_size)]
    greet(ring + members)
    micro, tokens, _ = output.shape
    many = own.shape[0] // micro
    seg_rows = seg_full.shape[0] // ring_size
    lane = lax.broadcasted_iota(jnp.int32, (many, tokens), 1)
    number = lax.broadcasted_iota(jnp.int32, (many, tokens), 0)
    selects = []
    for m in range(micro):
        here = seg_full[pl.ds(blk * seg_rows + m, 1)]
        there = seg_full[pl.ds(jnp.maximum(blk - 1, 0) * seg_rows + m, 1)]
        here = jnp.broadcast_to(here, (many, tokens))
        there = jnp.broadcast_to(there, (many, tokens))
        there = jnp.where(blk == 0, -1, there)
        before = jnp.where(lane == 0, pltpu.roll(there, 1, 1), pltpu.roll(here, 1, 1))
        chosen = (here != before) & (here == number)
        selects.append(jnp.where(chosen, 1.0, 0.0).astype(jnp.bfloat16))
        own[m * many : (m + 1) * many] = contract(selects[m], output[m], 1, 0).astype(jnp.bfloat16)
    copies = []
    for step, peer in enumerate(ring):
        copy = remote(own, arrived.at[step], ring_send.at[step], ring_recv.at[step], peer)
        copy.start()
        copies.append(copy)
    for d in range(dp_size):
        for m in range(micro):
            rows = slice((d * micro + m) * many, (d * micro + m + 1) * many)
            at = slice(d * many, (d + 1) * many)
            asked[m, at] = queries_all[rows]
            hot[m, at] = hot_all[rows]
    for copy in copies:
        copy.wait()
    total = own[...].astype(jnp.float32)
    for step in range(ring_size - 1):
        total = total + arrived[step].astype(jnp.float32)
    tables[dp] = total.astype(jnp.bfloat16)
    copies = []
    for step, peer in enumerate(members):
        copy = remote(tables.at[dp], tables.at[dp], send_sem.at[step], recv_sem.at[step], peer)
        copy.start()
        copies.append(copy)
    for m in range(micro):
        embeddings[m] = total[m * many : (m + 1) * many].astype(jnp.bfloat16)
    for copy in copies:
        copy.wait()
    for m in range(micro):
        for d in range(dp_size):
            everyone[m, d * many : (d + 1) * many] = tables[d, m * many : (m + 1) * many]
    mine = pl.ds(pl.multiple_of(dp * many, many), many)
    for m in range(micro):
        scores = contract(asked[m], everyone[m], 1, 1)
        peak = jnp.max(scores, axis=1, keepdims=True)
        log_total = peak + jnp.log(jnp.sum(jnp.exp(scores - peak), axis=1, keepdims=True))
        target = hot[m].astype(jnp.float32)
        value = log_total - jnp.sum(scores * target, axis=1, keepdims=True)
        wide_loss[...] = jnp.broadcast_to(value, wide_loss.shape)
        loss[m] = wide_loss[mine]
        slope = jnp.exp(scores - log_total) - target
        dscore[...] = slope
        turned[...] = slope.T
        query_grad[m] = split_dot(dscore[mine], everyone[m], 1, 0)
        embed_grad = split_dot(turned[mine], asked[m], 1, 0)
        high = embed_grad.astype(jnp.bfloat16)
        rest = (embed_grad - high.astype(jnp.float32)).astype(jnp.bfloat16)
        dout[m] = (
            cotangent[m].astype(jnp.float32)
            + contract(selects[m], high, 0, 0)
            + contract(selects[m], rest, 0, 0)
        )


def retrieve(output, cotangent, seg_full, queries_all, hot_all, ring_size, dp_size):
    micro, tokens, width = output.shape
    many = queries_all.shape[0] // (dp_size * micro)
    total = dp_size * many
    narrow, wide = jnp.bfloat16, jnp.float32
    shape = jax.ShapeDtypeStruct
    return pl.pallas_call(
        functools.partial(retrieve_kernel, ring_size, dp_size),
        out_shape=(
            shape((micro, tokens, width), wide),
            shape((micro, many, width), narrow),
            shape((micro, many, 128), wide),
            shape((micro, many, width), wide),
        ),
        in_specs=[IN_VMEM] * 5,
        out_specs=(IN_VMEM,) * 4,
        scratch_shapes=[
            pltpu.VMEM((micro * many, width), narrow),
            pltpu.VMEM((ring_size - 1, micro * many, width), narrow),
            pltpu.VMEM((dp_size, micro * many, width), narrow),
            pltpu.VMEM((micro, total, width), narrow),
            pltpu.VMEM((micro, total, width), narrow),
            pltpu.VMEM((micro, total, total), narrow),
            pltpu.VMEM((total, 128), wide),
            pltpu.VMEM((total, total), wide),
            pltpu.VMEM((total, total), wide),
            pltpu.SemaphoreType.DMA((dp_size,)),
            pltpu.SemaphoreType.DMA((dp_size,)),
            pltpu.SemaphoreType.DMA((ring_size,)),
            pltpu.SemaphoreType.DMA((ring_size,)),
        ],
        compiler_params=comm_params(4),
    )(output, cotangent, seg_full, queries_all, hot_all)


def gelu_and_slope(values):
    size = jnp.abs(values)
    step = 1.0 / (1.0 + (0.3275911 / math.sqrt(2.0)) * size)
    series = 0.5 * 1.061405429
    for factor in (-1.453152027, 1.421413741, -0.284496736, 0.254829592):
        series = series * step + 0.5 * factor
    bell = jnp.exp(-0.5 * values * values)
    tail = series * step * bell
    normal_cdf = jnp.where(values >= 0.0, 1.0 - tail, tail)
    slope = normal_cdf + values * bell * (1.0 / math.sqrt(2.0 * math.pi))
    return values * normal_cdf, slope


def fast_body(
    hidden_in,
    segment_ids,
    queries,
    targets,
    cotangent,
    query_weight,
    key_weight,
    value_weight,
    output_weight,
    query_bias,
    value_bias,
    output_bias,
    first_gain,
    first_shift,
    inner_weight,
    inner_bias,
    outer_weight,
    outer_bias,
    second_gain,
    second_shift,
):
    dp_size, ring_size = lax.axis_size("dp"), lax.axis_size("blk")
    dp, blk = lax.axis_index("dp"), lax.axis_index("blk")
    micro, row_count, block_tokens, width = hidden_in.shape
    row_queries = queries.shape[1]
    length = block_tokens * ring_size
    head_dim = width // HEADS
    spread = ring_size // micro
    own_heads = HEADS // spread
    tokens = micro * block_tokens
    wide = jnp.float32
    narrow = jnp.bfloat16

    vectors = (
        query_bias,
        value_bias,
        output_bias,
        first_gain,
        first_shift,
        outer_bias,
        second_gain,
        second_shift,
        inner_bias,
    )
    piece = vectors[0].shape[0]
    inner_piece = inner_bias.shape[0]
    group = own_heads * head_dim
    row_at, group_at = blk // spread, lax.rem(blk, spread) * group
    hidden_rows = hidden_in.reshape(micro, block_tokens, width)
    pack = jnp.concatenate(
        (
            jnp.pad(jnp.stack(vectors[:8]), ((0, 0), (0, inner_piece - piece))),
            jnp.pad(inner_bias[None], ((0, 7), (0, 0))),
        )
    )
    passages = dp_size * row_queries
    hot = (
        targets[:, :, None] == jnp.arange(passages, dtype=jnp.int32)[None, None, :]
    ).astype(narrow)
    seg_pack = jnp.pad(segment_ids.reshape(micro, block_tokens), ((0, 8 - micro), (0, 0)))
    shards = (
        query_weight,
        key_weight,
        value_weight,
        pack,
        hot.reshape(micro * row_queries, passages),
        queries.reshape(micro * row_queries, width),
        output_weight,
        inner_weight,
        outer_weight,
    )
    ways = (("x", "y"), ("y", "x"))
    items = []

    def add_item(source, target, row=0, rows=None, from_column=0, columns=None, to_column=0):
        shape = shards[source].shape
        items.append(
            {
                "source": source,
                "target": target,
                "row": row,
                "rows": rows or shape[0],
                "stride": shape[0],
                "from_column": from_column,
                "columns": columns or shape[1],
                "to_column": to_column,
                "route": ways[len(items) % 2],
            }
        )

    for index in range(3):
        add_item(index, 0, from_column=None, columns=group, to_column=index * group)
    add_item(3, 1)
    add_item(6, 4)
    for part in range(4):
        add_item(7, 5, from_column=part * width, columns=width, to_column=part * width)
        add_item(8, 6, row=part * piece, rows=piece)
    add_item(4, 2)
    add_item(5, 3)
    targets_out = [jax.ShapeDtypeStruct((width, 3 * group), narrow)] + [
        jax.ShapeDtypeStruct((dp_size * s.shape[0], s.shape[1]), s.dtype) for s in shards[3:]
    ]
    (
        w_window,
        pack_all,
        hot_all,
        queries_all,
        wo_full,
        w_inner,
        w_outer,
        seg_all,
        hidden_row,
        qkv,
        context,
        stats,
        context_t,
    ) = forward(shards, items, targets_out, seg_pack, hidden_rows, ring_size, head_dim)
    pack_rows = pack_all.reshape(dp_size, 16, inner_piece)
    eight = pack_rows[:, :8, :piece].transpose(1, 0, 2).reshape(8, width).astype(wide)
    bq_full, bv_full, bo_full, gain_one, shift_one, b_outer, gain_two, shift_two = eight
    b_inner = pack_rows[:, 8].reshape(-1).astype(wide)
    seg_row = (
        seg_all.reshape(ring_size, 8, block_tokens)[:, :micro]
        .transpose(1, 0, 2)
        .reshape(micro, 1, length)
    )
    seg_mine = lax.dynamic_slice(seg_row, (row_at, 0, 0), (1, 1, length)).reshape(1, length)

    flat_rows = hidden_in.reshape(tokens, width)
    attended = (
        jnp.einsum("met,ed->mtd", context_t, wo_full, preferred_element_type=wide).reshape(
            tokens, width
        )
        + bo_full
    )
    first_out, first_normed, first_factor = layer_norm(
        flat_rows.astype(wide) + attended, gain_one, shift_one
    )
    first_low = first_out.astype(narrow)
    inner_pre = jnp.dot(first_low, w_inner, preferred_element_type=wide) + b_inner
    active, slope = gelu_and_slope(inner_pre)
    active, slope = lax.optimization_barrier((active.astype(narrow), slope.astype(narrow)))
    outer_out = jnp.dot(active, w_outer, preferred_element_type=wide) + b_outer
    output, second_normed, second_factor = layer_norm(first_out + outer_out, gain_two, shift_two)
    output_low = output.astype(narrow)
    output_rows = output_low.reshape(micro, block_tokens, width)

    dout, embeddings, query_loss, query_grad = retrieve(
        output_rows,
        cotangent.reshape(micro, block_tokens, width),
        seg_all,
        queries_all,
        hot_all,
        ring_size,
        dp_size,
    )
    query_loss = query_loss[:, :, 0]
    dout = dout.reshape(tokens, width)
    gain_two_grad = jnp.sum(dout * second_normed, axis=0)
    shift_two_grad = jnp.sum(dout, axis=0)
    dsecond = norm_back(dout, second_normed, second_factor, gain_two)
    douter = dsecond.astype(narrow)
    outer_bias_grad = jnp.sum(douter.astype(wide), axis=0)
    outer_weight_grad = jnp.einsum(
        "nf,nd->fd", active, douter, preferred_element_type=wide
    ).astype(narrow)
    dactive = jnp.einsum("nd,fd->nf", douter, w_outer, preferred_element_type=wide)
    dinner = (dactive * slope.astype(wide)).astype(narrow)
    inner_bias_grad = jnp.sum(dinner.astype(wide), axis=0)
    inner_weight_grad = jnp.einsum(
        "nd,nf->df", first_low, dinner, preferred_element_type=wide
    ).astype(narrow)
    dfirst = dsecond + jnp.einsum("nf,df->nd", dinner, w_inner, preferred_element_type=wide)
    gain_one_grad = jnp.sum(dfirst * first_normed, axis=0)
    shift_one_grad = jnp.sum(dfirst, axis=0)
    dresidual = norm_back(dfirst, first_normed, first_factor, gain_one)
    dattended = dresidual.astype(narrow)
    output_bias_grad = jnp.sum(dattended.astype(wide), axis=0)
    datt_rows = dattended.reshape(micro, block_tokens, width)
    output_weight_grad = jnp.einsum(
        "met,mtd->ed", context_t, datt_rows, preferred_element_type=wide
    ).astype(narrow)
    dcontext_t = jnp.einsum(
        "mtd,ed->met", datt_rows, wo_full, preferred_element_type=wide
    ).astype(narrow)
    vector_grads = jnp.stack(
        (
            jnp.zeros((width,), wide),
            jnp.zeros((width,), wide),
            output_bias_grad,
            gain_one_grad,
            shift_one_grad,
            outer_bias_grad,
            gain_two_grad,
            shift_two_grad,
        )
    )
    grad_pack = jnp.pad(
        jnp.concatenate(
            (
                jnp.pad(
                    vector_grads.reshape(8, dp_size, piece).transpose(1, 0, 2),
                    ((0, 0), (0, 0), (0, inner_piece - piece)),
                ),
                inner_bias_grad.reshape(dp_size, 1, inner_piece),
            ),
            axis=1,
        ),
        ((0, 0), (0, 7), (0, 0)),
    ).reshape(dp_size * 16, inner_piece)
    grads = (outer_weight_grad, inner_weight_grad, output_weight_grad)
    grad_shapes = [grad.shape for grad in grads] + [(width, 3 * group), grad_pack.shape]
    sums = []

    def add_sum(source, row=0, rows=None, column=0, columns=None, widened=1):
        shape = grad_shapes[source]
        sums.append(
            {
                "source": source,
                "row": row,
                "rows": rows or shape[0] // dp_size,
                "stride": shape[0] // dp_size,
                "column": column,
                "columns": columns or shape[1],
                "widened": widened,
                "route": ways[len(sums) % 2],
            }
        )

    for part in range(4):
        add_sum(0, row=part * piece, rows=piece)
        add_sum(1, column=part * width, columns=width)
    add_sum(2)
    for index in range(3):
        add_sum(3, column=index * group, columns=group, widened=spread)
    add_sum(4)
    dhidden, d_outer, d_inner, d_wo, d_window, d_pack = backward(
        dcontext_t,
        seg_mine,
        grad_pack,
        (qkv, context, stats),
        w_window,
        hidden_row,
        dresidual.reshape(micro, block_tokens, width),
        grads,
        sums,
        ring_size,
        dp_size,
        head_dim,
        5,
    )
    d_outer, d_inner, d_wo, d_window, d_pack = (
        part.astype(wide) for part in (d_outer, d_inner, d_wo, d_window, d_pack)
    )
    d_wq, d_wk, d_wv = (d_window[:, i * width : (i + 1) * width] for i in range(3))
    d_bq, d_bv, d_bo, d_g1, d_s1, d_bu, d_g2, d_s2 = (d_pack[i, :piece] for i in range(8))
    d_bi = d_pack[8]
    shape = (micro, row_count, block_tokens, width)
    return (
        output_low.reshape(shape),
        embeddings,
        query_loss,
        query_grad,
        dhidden.reshape(shape),
        d_wq,
        d_wk,
        d_wv,
        d_wo,
        d_bq,
        d_bv,
        d_bo,
        d_g1,
        d_s1,
        d_inner,
        d_bi,
        d_outer,
        d_bu,
        d_g2,
        d_s2,
    )


def solution(mesh):
    in_specs = (
        P(None, "dp", "blk", None),
        P(None, "dp", "blk"),
        P(None, "dp", None),
        P(None, "dp"),
        P(None, "dp", "blk", None),
        P("dp", None),
        P("dp", None),
        P("dp", None),
        P("dp", None),
        P("dp"),
        P("dp"),
        P("dp"),
        P("dp"),
        P("dp"),
        P("dp", None),
        P("dp"),
        P("dp", None),
        P("dp"),
        P("dp"),
        P("dp"),
    )
    out_specs = (
        P(None, "dp", "blk", None),
        P(None, "dp", None),
        P(None, "dp"),
        P(None, "dp", None),
        P(None, "dp", "blk", None),
        P("dp", None),
        P("dp", None),
        P("dp", None),
        P("dp", None),
        P("dp"),
        P("dp"),
        P("dp"),
        P("dp"),
        P("dp"),
        P("dp", None),
        P("dp"),
        P("dp", None),
        P("dp"),
        P("dp"),
        P("dp"),
    )
    fast = mesh.shape["dp"] == 8 and mesh.shape["blk"] == 4
    body = fast_body if fast else ring_body
    return jax.shard_map(body, mesh=mesh, in_specs=in_specs, out_specs=out_specs, check_vma=False)
```

```python
import functools
import math

import jax
import jax.numpy as jnp
from jax import lax
from jax.experimental import pallas as pl
from jax.experimental.pallas import tpu as pltpu
from jax.sharding import PartitionSpec as P

HEADS = 12


EPSILON = 1e-12
NEGATIVE = -1000000000.0
PRECISE = lax.Precision.HIGHEST


def passed_along(x, axis, by):
    size = lax.axis_size(axis)
    return lax.ppermute(x, axis, [(i, (i + by) % size) for i in range(size)])


def as_sent(x):
    return jax.tree.map(lambda a: a.astype(jnp.bfloat16) if a.dtype == jnp.float32 else a, x)


def layer_norm(values, norm_gain, norm_shift):
    center = values - jnp.mean(values, axis=-1, keepdims=True)
    factor = lax.rsqrt(jnp.mean(center * center, axis=-1, keepdims=True) + EPSILON)
    normed = center * factor
    return (normed * norm_gain + norm_shift, normed, factor)


def norm_back(gradient, normed, factor, norm_gain):
    scaled = gradient * norm_gain
    inner_term = (
        scaled
        - jnp.mean(scaled, axis=-1, keepdims=True)
        - normed * jnp.mean(scaled * normed, axis=-1, keepdims=True)
    )
    return inner_term * factor


def gelu_slope(values):
    normal_cdf = 0.5 * (1.0 + lax.erf(values * (1.0 / math.sqrt(2.0))))
    return normal_cdf + values * jnp.exp(-0.5 * values * values) * (1.0 / math.sqrt(2.0 * math.pi))


def scores_of(query_rows, key_rows, query_segment, key_segment, score_scale):
    raw_scores = jnp.einsum(
        "rqhd,rkhd->rhqk", query_rows, key_rows, preferred_element_type=jnp.float32
    )
    same_doc = (query_segment[:, :, None] == key_segment[:, None, :])[:, None]
    return jnp.where(same_doc, score_scale * raw_scores, NEGATIVE)


def contribute(
    query_rows,
    push_grad,
    delta_term,
    peak_term,
    query_segment,
    key_rows,
    value_rows,
    key_segment,
    score_scale,
):
    scores = scores_of(query_rows, key_rows, query_segment, key_segment, score_scale)
    weights = jnp.exp(scores - peak_term[..., None])
    pushed = jnp.einsum(
        "rqhd,rkhd->rhqk", push_grad, value_rows, preferred_element_type=jnp.float32
    )
    dscore = (weights * (pushed - delta_term[..., None]) * score_scale).astype(jnp.bfloat16)
    query_part = jnp.einsum("rhqk,rkhd->rqhd", dscore, key_rows, preferred_element_type=jnp.float32)
    key_part = jnp.einsum("rhqk,rqhd->rkhd", dscore, query_rows, preferred_element_type=jnp.float32)
    value_part = jnp.einsum(
        "rhqk,rqhd->rkhd",
        weights.astype(jnp.bfloat16),
        push_grad,
        preferred_element_type=jnp.float32,
    )
    return (query_part, key_part, value_part)


def ring_body(
    hidden_in,
    segment_ids,
    queries,
    targets,
    cotangent,
    query_weight,
    key_weight,
    value_weight,
    output_weight,
    query_bias,
    value_bias,
    output_bias,
    first_gain,
    first_shift,
    inner_weight,
    inner_bias,
    outer_weight,
    outer_bias,
    second_gain,
    second_shift,
):
    shards = (
        query_weight,
        key_weight,
        value_weight,
        output_weight,
        query_bias,
        value_bias,
        output_bias,
        first_gain,
        first_shift,
        inner_weight,
        inner_bias,
        outer_weight,
        outer_bias,
        second_gain,
        second_shift,
    )
    cycle_size = lax.axis_size("blk")
    cycle_place = lax.axis_index("blk")
    micro_count, row_count, block_tokens, model_width = hidden_in.shape
    segment_count = queries.shape[1] // row_count
    head_count = HEADS
    head_dim = model_width // head_count
    score_scale = 1.0 / math.sqrt(head_dim)
    token_count = row_count * block_tokens
    head_shape = (row_count, block_tokens, head_count, head_dim)
    grad_totals = tuple((jnp.zeros(shard_piece.shape, jnp.float32) for shard_piece in shards))
    local_sum = None
    gathered = None
    out_list, embed_list, loss_list, qgrad_list, hgrad_list = ([], [], [], [], [])
    for micro_index in range(micro_count):
        gathered = (
            lax.all_gather(shards[0], "dp", axis=0, tiled=True),
            lax.all_gather(shards[1], "dp", axis=0, tiled=True),
            lax.all_gather(shards[2], "dp", axis=0, tiled=True),
            lax.all_gather(shards[3], "dp", axis=0, tiled=True),
            lax.all_gather(shards[4], "dp", axis=0, tiled=True),
            lax.all_gather(shards[5], "dp", axis=0, tiled=True),
            lax.all_gather(shards[6], "dp", axis=0, tiled=True),
            lax.all_gather(shards[7], "dp", axis=0, tiled=True),
            lax.all_gather(shards[8], "dp", axis=0, tiled=True),
            lax.all_gather(shards[9], "dp", axis=0, tiled=True),
            lax.all_gather(shards[10], "dp", axis=0, tiled=True),
            lax.all_gather(shards[11], "dp", axis=0, tiled=True),
            lax.all_gather(shards[12], "dp", axis=0, tiled=True),
            lax.all_gather(shards[13], "dp", axis=0, tiled=True),
            lax.all_gather(shards[14], "dp", axis=0, tiled=True),
        )
        (
            wq_full,
            wk_full,
            wv_full,
            wo_full,
            bq_full,
            bv_full,
            bo_full,
            gain_one,
            shift_one,
            w_inner,
            b_inner,
            w_outer,
            b_outer,
            gain_two,
            shift_two,
        ) = gathered
        gain_one = gain_one.astype(jnp.float32)
        gain_two = gain_two.astype(jnp.float32)
        segment = segment_ids[micro_index]
        flat_rows = hidden_in[micro_index].reshape(token_count, model_width)
        query_rows = (
            (
                jnp.dot(flat_rows, wq_full, preferred_element_type=jnp.float32)
                + bq_full.astype(jnp.float32)
            )
            .astype(jnp.bfloat16)
            .reshape(head_shape)
        )
        key_rows = (
            jnp.dot(flat_rows, wk_full, preferred_element_type=jnp.float32)
            .astype(jnp.bfloat16)
            .reshape(head_shape)
        )
        value_rows = (
            (
                jnp.dot(flat_rows, wv_full, preferred_element_type=jnp.float32)
                + bv_full.astype(jnp.float32)
            )
            .astype(jnp.bfloat16)
            .reshape(head_shape)
        )

        def absorb(softmax_state, visit_keys, visit_values, visit_segment):
            running_peak, running_total, running_sum = softmax_state
            scores = scores_of(query_rows, visit_keys, segment, visit_segment, score_scale)
            new_peak = jnp.maximum(running_peak, jnp.max(scores, axis=-1))
            decay_factor = jnp.exp(running_peak - new_peak)
            weights = jnp.exp(scores - new_peak[..., None])
            running_total = running_total * decay_factor + jnp.sum(weights, axis=-1)
            update = jnp.einsum(
                "rhqk,rkhd->rqhd",
                weights.astype(jnp.bfloat16),
                visit_values,
                preferred_element_type=jnp.float32,
            )
            running_sum = running_sum * jnp.transpose(decay_factor, (0, 2, 1))[..., None] + update
            return (new_peak, running_total, running_sum)

        start_state = (
            jnp.full((row_count, head_count, block_tokens), -1e30, jnp.float32),
            jnp.zeros((row_count, head_count, block_tokens), jnp.float32),
            jnp.zeros(head_shape, jnp.float32),
        )
        first_state = absorb(start_state, key_rows, value_rows, segment)

        def forward_step(cycle_step, cycle_carry):
            visit_keys, visit_values, visit_segment, prior_segment, softmax_state = cycle_carry
            visit_keys, visit_values, visit_segment = passed_along(
                (visit_keys, visit_values, visit_segment), "blk", 1
            )
            prior_segment = jnp.where(cycle_step == 1, visit_segment[:, -1], prior_segment)
            return (
                visit_keys,
                visit_values,
                visit_segment,
                prior_segment,
                absorb(softmax_state, visit_keys, visit_values, visit_segment),
            )

        cycle_carry = lax.fori_loop(
            1, cycle_size, forward_step, (key_rows, value_rows, segment, segment[:, 0], first_state)
        )
        prior_segment = cycle_carry[3]
        row_peak, row_total, running_sum = cycle_carry[4]
        total_heads = jnp.transpose(row_total, (0, 2, 1))[..., None]
        context = running_sum / total_heads
        context_low = context.reshape(token_count, model_width).astype(jnp.bfloat16)
        attended = jnp.dot(
            context_low, wo_full, preferred_element_type=jnp.float32
        ) + bo_full.astype(jnp.float32)
        first_out, first_normed, first_factor = layer_norm(
            flat_rows.astype(jnp.float32) + attended, gain_one, shift_one.astype(jnp.float32)
        )
        first_low = first_out.astype(jnp.bfloat16)
        inner_pre = jnp.dot(
            first_low, w_inner, preferred_element_type=jnp.float32
        ) + b_inner.astype(jnp.float32)
        active = jax.nn.gelu(inner_pre, approximate=False).astype(jnp.bfloat16)
        outer_out = jnp.dot(active, w_outer, preferred_element_type=jnp.float32) + b_outer.astype(
            jnp.float32
        )
        output, second_normed, second_factor = layer_norm(
            first_out + outer_out, gain_two, shift_two.astype(jnp.float32)
        )
        output_low = output.astype(jnp.bfloat16)
        out_list.append(output_low.reshape(row_count, block_tokens, model_width))
        position = cycle_place * block_tokens + jnp.arange(block_tokens, dtype=jnp.int32)
        before = jnp.concatenate([prior_segment[:, None], segment[:, :-1]], axis=1)
        leading = (position[None, :] == 0) | (segment != before)
        numbers = jnp.arange(segment_count, dtype=jnp.int32)
        select = (leading[:, None, :] & (segment[:, None, :] == numbers[None, :, None])).astype(
            jnp.float32
        )
        cls_table = jnp.einsum(
            "rsi,rid->rsd",
            select.astype(jnp.bfloat16),
            output_low.reshape(row_count, block_tokens, model_width),
            preferred_element_type=jnp.float32,
        )
        own_table = lax.psum(cls_table.astype(jnp.bfloat16), "blk").reshape(
            row_count * segment_count, model_width
        )
        embed_list.append(own_table)
        everyone = lax.all_gather(own_table, "dp", axis=0, tiled=True)
        query_vectors = queries[micro_index]
        query_scores = jnp.dot(query_vectors, everyone.T, preferred_element_type=jnp.float32)
        score_peak = jnp.max(query_scores, axis=1, keepdims=True)
        log_total = score_peak[:, 0] + jnp.log(jnp.sum(jnp.exp(query_scores - score_peak), axis=1))
        target_hot = (
            jnp.arange(query_scores.shape[1], dtype=jnp.int32)[None, :]
            == targets[micro_index][:, None]
        ).astype(jnp.float32)
        loss_list.append(log_total - jnp.sum(query_scores * target_hot, axis=1))
        dscore_query = jnp.exp(query_scores - log_total[:, None]) - target_hot
        qgrad_list.append(jnp.dot(dscore_query, everyone.astype(jnp.float32), precision=PRECISE))
        embed_part = jnp.dot(dscore_query.T, query_vectors.astype(jnp.float32), precision=PRECISE)
        embed_grad = (
            lax.psum_scatter(embed_part.astype(jnp.bfloat16), "dp", scatter_dimension=0, tiled=True)
            .astype(jnp.float32)
            .reshape(row_count, segment_count, model_width)
        )
        cls_grad = jnp.einsum("rsi,rsd->rid", select, embed_grad, precision=PRECISE)
        dout = cotangent[micro_index].reshape(token_count, model_width).astype(
            jnp.float32
        ) + cls_grad.reshape(token_count, model_width)
        gain_two_grad = jnp.sum(dout * second_normed, axis=0)
        shift_two_grad = jnp.sum(dout, axis=0)
        dsecond = norm_back(dout, second_normed, second_factor, gain_two)
        douter = dsecond.astype(jnp.bfloat16)
        outer_bias_grad = jnp.sum(douter.astype(jnp.float32), axis=0)
        outer_weight_grad = jnp.einsum(
            "nf,nd->fd", active, douter, preferred_element_type=jnp.float32
        )
        dactive = jnp.einsum("nd,fd->nf", douter, w_outer, preferred_element_type=jnp.float32)
        dinner = (dactive * gelu_slope(inner_pre)).astype(jnp.bfloat16)
        inner_bias_grad = jnp.sum(dinner.astype(jnp.float32), axis=0)
        inner_weight_grad = jnp.einsum(
            "nd,nf->df", first_low, dinner, preferred_element_type=jnp.float32
        )
        dfirst = dsecond + jnp.einsum(
            "nf,df->nd", dinner, w_inner, preferred_element_type=jnp.float32
        )
        gain_one_grad = jnp.sum(dfirst * first_normed, axis=0)
        shift_one_grad = jnp.sum(dfirst, axis=0)
        dresidual = norm_back(dfirst, first_normed, first_factor, gain_one)
        dattended = dresidual.astype(jnp.bfloat16)
        output_bias_grad = jnp.sum(dattended.astype(jnp.float32), axis=0)
        output_weight_grad = jnp.einsum(
            "nd,ne->de", context_low, dattended, preferred_element_type=jnp.float32
        )
        dcontext = jnp.einsum(
            "ne,de->nd", dattended, wo_full, preferred_element_type=jnp.float32
        ).astype(jnp.bfloat16)
        dcontext_wide = dcontext.astype(jnp.float32).reshape(head_shape)
        push_grad = (dcontext_wide / total_heads).astype(jnp.bfloat16)
        delta_term = jnp.transpose(
            jnp.sum(dcontext_wide * context, axis=-1) / total_heads[..., 0], (0, 2, 1)
        )
        own_query, own_key, own_value = contribute(
            query_rows,
            push_grad,
            delta_term,
            row_peak,
            segment,
            key_rows,
            value_rows,
            segment,
            score_scale,
        )

        def key_step(cycle_step, cycle_carry):
            visit_keys, visit_values, visit_segment, query_sum, key_sum, value_sum = cycle_carry
            visit_keys, visit_values, visit_segment = passed_along(
                (visit_keys, visit_values, visit_segment), "blk", 1
            )
            key_sum, value_sum = (
                passed_along(key_sum.astype(jnp.bfloat16), "blk", 1).astype(key_sum.dtype),
                passed_along(value_sum.astype(jnp.bfloat16), "blk", 1).astype(value_sum.dtype),
            )
            query_part, key_part, value_part = contribute(
                query_rows,
                push_grad,
                delta_term,
                row_peak,
                segment,
                visit_keys,
                visit_values,
                visit_segment,
                score_scale,
            )
            return (
                visit_keys,
                visit_values,
                visit_segment,
                query_sum + query_part,
                key_sum + key_part,
                value_sum + value_part,
            )

        back_carry = lax.fori_loop(
            1, cycle_size, key_step, (key_rows, value_rows, segment, own_query, own_key, own_value)
        )
        query_sum = back_carry[3]
        key_sum, value_sum = (
            passed_along(back_carry[4].astype(jnp.bfloat16), "blk", 1).astype(jnp.float32),
            passed_along(back_carry[5].astype(jnp.bfloat16), "blk", 1).astype(jnp.float32),
        )
        dquery = query_sum.astype(jnp.bfloat16).reshape(token_count, model_width)
        dkey = key_sum.astype(jnp.bfloat16).reshape(token_count, model_width)
        dvalue = value_sum.astype(jnp.bfloat16).reshape(token_count, model_width)
        dhidden = dresidual + jnp.einsum(
            "ne,de->nd", dquery, wq_full, preferred_element_type=jnp.float32
        )
        dhidden = dhidden + jnp.einsum(
            "ne,de->nd", dkey, wk_full, preferred_element_type=jnp.float32
        )
        dhidden = dhidden + jnp.einsum(
            "ne,de->nd", dvalue, wv_full, preferred_element_type=jnp.float32
        )
        hgrad_list.append(
            dhidden.astype(jnp.bfloat16).reshape(row_count, block_tokens, model_width)
        )
        local_grads = (
            jnp.einsum("nd,ne->de", flat_rows, dquery, preferred_element_type=jnp.float32),
            jnp.einsum("nd,ne->de", flat_rows, dkey, preferred_element_type=jnp.float32),
            jnp.einsum("nd,ne->de", flat_rows, dvalue, preferred_element_type=jnp.float32),
            output_weight_grad,
            jnp.sum(dquery.astype(jnp.float32), axis=0),
            jnp.sum(dvalue.astype(jnp.float32), axis=0),
            output_bias_grad,
            gain_one_grad,
            shift_one_grad,
            inner_weight_grad,
            inner_bias_grad,
            outer_weight_grad,
            outer_bias_grad,
            gain_two_grad,
            shift_two_grad,
        )
        local_sum = local_grads
        reduced = jax.tree.map(
            lambda part: part.astype(jnp.float32),
            lax.psum_scatter(as_sent(local_sum), "dp", scatter_dimension=0, tiled=True),
        )
        reduced = jax.tree.map(
            lambda part: part.astype(jnp.float32), lax.psum(as_sent(reduced), "blk")
        )
        grad_totals = tuple(
            (total_piece + new_piece for total_piece, new_piece in zip(grad_totals, reduced))
        )
        local_sum = None
    return (
        jnp.stack(out_list),
        jnp.stack(embed_list),
        jnp.stack(loss_list),
        jnp.stack(qgrad_list),
        jnp.stack(hgrad_list),
        grad_totals[0],
        grad_totals[1],
        grad_totals[2],
        grad_totals[3],
        grad_totals[4],
        grad_totals[5],
        grad_totals[6],
        grad_totals[7],
        grad_totals[8],
        grad_totals[9],
        grad_totals[10],
        grad_totals[11],
        grad_totals[12],
        grad_totals[13],
        grad_totals[14],
    )


MESH = pl.DeviceIdType.MESH
VMEM_LIMIT = 60 * 1024 * 1024
SIDE = {"c": 1, "x": 2, "y": 4}


def place():
    dp, blk = lax.axis_index("dp"), lax.axis_index("blk")
    bits = {"c": lax.rem(dp, 2), "x": lax.rem(dp // 2, 2), "y": dp // 4}
    return dp, blk, bits


def across(dp, blk, bits, *axes):
    other = dp
    for axis in axes:
        other = other + SIDE[axis] * (1 - 2 * bits[axis])
    return (other, blk)


def greet(peers):
    barrier = pltpu.get_barrier_semaphore()
    for peer in peers:
        pl.semaphore_signal(barrier, inc=1, device_id=peer, device_id_type=MESH)
    pl.semaphore_wait(barrier, len(peers))


def remote(source, target, send_sem, recv_sem, peer):
    return pltpu.make_async_remote_copy(
        src_ref=source,
        dst_ref=target,
        send_sem=send_sem,
        recv_sem=recv_sem,
        device_id=peer,
        device_id_type=MESH,
    )


def comm_params(collective):
    return pltpu.CompilerParams(
        collective_id=collective, has_side_effects=True, vmem_limit_bytes=VMEM_LIMIT
    )


ANY = pl.BlockSpec(memory_space=pl.ANY)
IN_VMEM = pl.BlockSpec(memory_space=pltpu.VMEM)


SLABS = 2


def forward_kernel(items, ring_size, depth, sources, places, *refs):
    shards, seg_shard, hidden = refs[:sources], refs[sources], refs[sources + 1]
    outs = refs[sources + 2 :]
    w_window_out, hidden_row_out, qkv_out, context_out = (
        outs[0],
        outs[places + 1],
        outs[places + 2],
        outs[places + 3],
    )
    seg_full, stats, context_t = outs[places], outs[places + 4], outs[places + 5]
    (
        w_window,
        hidden_row,
        qkv,
        context,
        hidden_full,
        low,
        seg_line,
        mask,
        turned,
        keys,
        send_sem,
        recv_sem,
        seg_send,
        seg_recv,
        line_send,
        line_recv,
        head_send,
        head_recv,
        local_sem,
        store_sem,
    ) = outs[places + 6 :]
    fulls = (w_window,) + tuple(outs[1:places])
    pack_full = fulls[1]
    stores = []

    def store(source, target):
        copy = pltpu.make_async_copy(source, target, store_sem.at[len(stores)])
        copy.start()
        stores.append(copy)

    dp, blk, bits = place()
    sibling = across(dp, blk, bits, "c")
    ring = [(dp, lax.rem(blk + step, ring_size)) for step in range(1, ring_size)]
    greet([sibling, across(dp, blk, bits, "x"), across(dp, blk, bits, "y")] + ring)
    seg_rows = seg_shard.shape[0]
    micro, tokens, width = hidden.shape
    spread = ring_size // micro
    row_at, group_at = blk // spread, lax.rem(blk, spread)
    group, length = context.shape
    heads = group // depth
    score_scale = 1.0 / math.sqrt(depth)
    waiting = []
    mine = pl.ds(pl.multiple_of(blk * tokens, tokens), tokens)

    slab = tokens // SLABS

    def line_view(m, side, distance, part):
        owner = blk + (1 - 2 * side) * distance
        first = owner * tokens + part * slab
        return hidden_full.at[m, pl.ds(pl.multiple_of(first, slab), slab)]

    def line_copy(m, side, distance, part):
        view = line_view(m, side, distance, part)
        return remote(
            hidden.at[m, pl.ds(part * slab, slab)] if distance == 0 else view,
            view,
            line_send.at[m, side, distance, part],
            line_recv.at[m, side, distance + 1, part],
            (dp, blk - 1 + 2 * side),
        )

    def arrival(m, side, distance, part):
        view = line_view(m, side, distance, part)
        return remote(
            view,
            view,
            line_send.at[m, side, distance, part],
            line_recv.at[m, side, distance, part],
            (dp, blk - 1 + 2 * side),
        )

    def passes_on(m, side):
        return blk > m * spread if side == 0 else blk < m * spread + spread - 1

    def comes(m, side, distance):
        if side == 0:
            return (blk >= m * spread) & (blk + distance < ring_size)
        return (blk < m * spread + spread) & (blk >= distance)

    def line_step(distance, part):
        for m in range(micro):
            for side in range(2):

                @pl.when(comes(m, side, distance))
                def _():
                    arrival(m, side, distance, part).wait_recv()

                if distance < ring_size - 1:

                    @pl.when(comes(m, side, distance) & passes_on(m, side))
                    def _():
                        line_copy(m, side, distance, part).start()

    for part in range(SLABS):
        for m in range(micro):
            for side in range(2):

                @pl.when(passes_on(m, side))
                def _():
                    line_copy(m, side, 0, part).start()

    def own_part(item):
        spec = items[item]
        column = spec["from_column"]
        if column is None:
            column = pl.multiple_of(group_at * group, group)
        return shards[spec["source"]].at[
            pl.ds(spec["row"], spec["rows"]), pl.ds(column, spec["columns"])
        ]

    def block(item, owner):
        spec = items[item]
        first = owner * spec["stride"] + spec["row"]
        return fulls[spec["target"]].at[
            pl.ds(first, spec["rows"]), pl.ds(spec["to_column"], spec["columns"])
        ]

    inbound = {}

    def start_item(item):
        first, second = items[item]["route"]
        for slot, peer in enumerate(
            (across(dp, blk, bits, first), across(dp, blk, bits, second), sibling)
        ):
            copy = remote(
                own_part(item),
                block(item, dp),
                send_sem.at[item, slot],
                recv_sem.at[item, slot],
                peer,
            )
            copy.start()
            inbound[item, slot] = copy
        copy = pltpu.make_async_copy(own_part(item), block(item, dp), local_sem.at[item])
        copy.start()
        inbound[item, "own"] = copy

    def pass_on(item, held, slot, peer):
        copy = remote(held, held, send_sem.at[item, slot], recv_sem.at[item, slot], peer)
        copy.start()
        inbound[item, slot] = copy

    def relay_first(item):
        first, second = items[item]["route"]
        inbound[item, 0].wait_recv()
        held = block(item, across(dp, blk, bits, first)[0])
        pass_on(item, held, 3, across(dp, blk, bits, second))
        pass_on(item, held, 4, sibling)
        inbound[item, 1].wait_recv()
        pass_on(item, block(item, across(dp, blk, bits, second)[0]), 5, sibling)

    def relay_third(item):
        first, second = items[item]["route"]
        inbound[item, 3].wait_recv()
        pass_on(item, block(item, across(dp, blk, bits, first, second)[0]), 6, sibling)

    def all_here(item):
        for slot in (2, 4, 5, 6):
            inbound[item, slot].wait_recv()
        inbound[item, "own"].wait()

    early = [i for i, spec in enumerate(items) if spec["target"] < 2]
    late = [i for i, spec in enumerate(items) if spec["target"] >= 2]
    tick_of = [0]

    def tick(times=1):
        for _ in range(times):
            now = tick_of[0]
            tick_of[0] += 1
            if 0 <= now - 2 * LAG < len(late):
                relay_third(late[now - 2 * LAG])
            if 0 <= now - LAG < len(late):
                relay_first(late[now - LAG])
            if now < len(late):
                start_item(late[now])

    for item in early:
        start_item(item)
    for step, peer in enumerate(ring):
        copy = remote(
            seg_shard,
            seg_full.at[pl.ds(blk * seg_rows, seg_rows)],
            seg_send.at[step],
            seg_recv.at[step],
            peer,
        )
        copy.start()
        waiting.append(copy)
    seg_full[pl.ds(blk * seg_rows, seg_rows)] = seg_shard[...]

    for item in early:
        relay_first(item)
    tick()
    line_step(1, 0)
    tick()
    for part in range(1, SLABS):
        line_step(1, part)
    for item in early:
        relay_third(item)
    tick()
    for copy in waiting:
        copy.wait()
    for member in range(ring_size):
        seg_line[:, member * tokens : (member + 1) * tokens] = seg_full[
            pl.ds(member * seg_rows + row_at, 1)
        ].astype(jnp.float32)
    seg_col = columns_of(seg_line[...])
    for item in early:
        all_here(item)
    store(w_window, w_window_out)
    pack_turned = pack_full[...].astype(jnp.float32).T
    piece = width // (pack_full.shape[0] // 16)
    lane = lax.broadcasted_iota(jnp.int32, (piece, pack_full.shape[0]), 1)

    def bias_column(vector):
        pieces = []
        for part in range(group // piece):
            at = (group_at * (group // piece) + part) * 16 + vector
            pieces.append(
                jnp.sum(
                    jnp.where(lane == at, pack_turned[:piece], 0.0), axis=1, keepdims=True
                )
            )
        return jnp.concatenate(pieces, axis=0)

    biases = (bias_column(0), None, bias_column(1))
    for part in range(3):
        rows = slice(part * group, (part + 1) * group)
        turned[rows, :] = w_window[:, rows].T

    def project(at, source):
        span = pl.ds(pl.multiple_of(at * tokens, tokens), tokens)
        values = source[...]
        hidden_row[span, :] = values
        for part in range(3):
            rows = slice(part * group, (part + 1) * group)
            result = contract(turned[rows, :], values, 1, 1)
            if biases[part] is not None:
                result = result + biases[part]
            qkv[rows, span] = result.astype(jnp.bfloat16)

    def project_at(distance):
        for side in range(2):
            at = blk + (1 - 2 * side) * distance

            @pl.when((at >= 0) & (at < ring_size))
            def _():
                view = hidden_full.at[row_at, pl.ds(pl.multiple_of(at * tokens, tokens), tokens)]
                project(at, view)

    if ring_size > 2:
        line_step(2, 0)
    project(blk, hidden.at[row_at])
    tick()
    project_at(1)
    for distance in range(2, ring_size):
        for part in range(SLABS):
            if distance > 2 or part > 0:
                line_step(distance, part)
                tick()
        project_at(distance)

    store(hidden_row, hidden_row_out)
    store(qkv, qkv_out)
    copies = []

    def head_rows(part, head):
        first = part * group + head * depth
        return slice(first, first + depth)

    for head in range(heads):
        keys[head] = qkv[head_rows(1, head), :].T

    def attend(at):
        span = pl.ds(pl.multiple_of(at * tokens, tokens), tokens)
        mask[...] = jnp.where(seg_col == seg_line[:, span], 0.0, NEGATIVE)
        for head in range(heads):
            rows = head_rows(0, head)
            queries = (qkv[rows, span].astype(jnp.float32) * score_scale).astype(jnp.bfloat16)
            scores = contract(keys[head], queries, 1, 0) + mask[...]
            peak = jnp.max(scores, axis=0, keepdims=True)
            weights = jnp.exp(scores - peak)
            total = jnp.sum(weights, axis=0, keepdims=True)
            ctx = contract(qkv[head_rows(2, head), :], weights.astype(jnp.bfloat16), 1, 0) / total
            context[rows, span] = ctx
            low[rows, span] = ctx.astype(jnp.bfloat16)
            stats[2 * head : 2 * head + 1, span] = peak
            stats[2 * head + 1 : 2 * head + 2, span] = total

    end = (ring_size - 1) * (1 - row_at)
    order = (end, end + 2 * row_at - 1, blk + 1 - 2 * lax.rem(blk, 2), blk)
    target = context_t.at[row_at, pl.ds(group_at * group, group)]
    for index, at in enumerate(order):
        attend(at)
        span = pl.ds(pl.multiple_of(at * tokens, tokens), tokens)
        if index < ring_size - 1:
            step = lax.rem(at - blk + ring_size, ring_size)
            copy = remote(low.at[:, span], target, head_send.at[index], head_recv.at[step], (dp, at))
            copy.start()
            copies.append(copy)
        else:
            target[...] = low[:, span]
        tick(2)
    store(context, context_out)
    tick(len(late) + 2 * LAG - tick_of[0])
    for item in late:
        all_here(item)
    for item in early + late:
        for slot in range(7):
            inbound[item, slot].wait_send()
    for copy in copies:
        copy.wait_send()
    for copy in stores:
        copy.wait()
    for step, peer in enumerate(ring):
        remote(target, target, head_send.at[0], head_recv.at[step + 1], peer).wait_recv()
    for m in range(micro):
        for side in range(2):
            for distance in range(ring_size - 1):
                ready = passes_on(m, side)
                if distance:
                    ready = ready & comes(m, side, distance)

                @pl.when(ready)
                def _():
                    for part in range(SLABS):
                        line_copy(m, side, distance, part).wait_send()


def columns_of(row):
    return jnp.broadcast_to(row, (128, row.shape[1])).T[:, :1]


def forward(shards, items, targets, segments, hidden, ring_size, depth):
    micro, tokens, width = hidden.shape
    count = len(shards)
    length = ring_size * tokens
    group = width * micro // ring_size
    heads = group // depth
    shape = jax.ShapeDtypeStruct
    return pl.pallas_call(
        functools.partial(forward_kernel, items, ring_size, depth, count, len(targets)),
        out_shape=tuple(targets)
        + (
            shape((ring_size * segments.shape[0], tokens), jnp.int32),
            shape((length, width), jnp.bfloat16),
            shape((3 * group, length), jnp.bfloat16),
            shape((group, length), jnp.float32),
            shape((2 * heads, length), jnp.float32),
            shape((micro, width, tokens), jnp.bfloat16),
        ),
        in_specs=[IN_VMEM] * (count + 2),
        out_specs=(ANY, IN_VMEM)
        + (ANY,) * (len(targets) - 2)
        + (IN_VMEM, ANY, ANY, ANY, IN_VMEM, IN_VMEM),
        scratch_shapes=[
            pltpu.VMEM((width, 3 * group), jnp.bfloat16),
            pltpu.VMEM((length, width), jnp.bfloat16),
            pltpu.VMEM((3 * group, length), jnp.bfloat16),
            pltpu.VMEM((group, length), jnp.float32),
            pltpu.VMEM((micro, length, width), jnp.bfloat16),
            pltpu.VMEM((group, length), jnp.bfloat16),
            pltpu.VMEM((1, length), jnp.float32),
            pltpu.VMEM((length, tokens), jnp.float32),
            pltpu.VMEM((3 * group, width), jnp.bfloat16),
            pltpu.VMEM((heads, length, depth), jnp.bfloat16),
            pltpu.SemaphoreType.DMA((len(items), 7)),
            pltpu.SemaphoreType.DMA((len(items), 7)),
            pltpu.SemaphoreType.DMA((ring_size,)),
            pltpu.SemaphoreType.DMA((ring_size,)),
            pltpu.SemaphoreType.DMA((micro, 2, ring_size, SLABS)),
            pltpu.SemaphoreType.DMA((micro, 2, ring_size, SLABS)),
            pltpu.SemaphoreType.DMA((ring_size,)),
            pltpu.SemaphoreType.DMA((ring_size,)),
            pltpu.SemaphoreType.DMA((len(items),)),
            pltpu.SemaphoreType.DMA((4,)),
        ],
        compiler_params=comm_params(1),
    )(*shards, segments, hidden)


def contract(left, right, left_dim, right_dim):
    return lax.dot_general(
        left, right, (((left_dim,), (right_dim,)), ((), ())), preferred_element_type=jnp.float32
    )


LAG, AHEAD = 3, 3


def added(left, right):
    return (left.astype(jnp.float32) + right.astype(jnp.float32)).astype(jnp.bfloat16)


def backward_kernel(items, ring_size, depth, *refs):
    (
        dcontext_part,
        seg_row,
        pack_part,
        qkv_out,
        context_out,
        stats,
        w_window_out,
        hidden_row_out,
        dresidual_out,
        active_out,
        douter,
        inner_grad,
        output_grad,
    ) = refs[:13]
    dhidden, d_outer, d_inner, d_output, d_window, d_pack = refs[13:19]
    (
        qkv,
        context,
        w_window,
        hidden_row,
        dresidual,
        dcontext,
        dwindow,
        pool,
        arrived,
        window_grad,
        pack_sum,
        pack_low,
        outer_parts,
        own_big,
        own_small,
        core_big,
        core_small,
        first_big,
        first_small,
        second_big,
        second_small,
        ring_one,
        ring_two,
        load_sem,
        head_send,
        head_recv,
        hop_send,
        hop_recv,
        send_sem,
        recv_sem,
        local_sem,
    ) = refs[19:]
    own, from_core = (own_big, own_small), (core_big, core_small)
    from_first, from_second = (first_big, first_small), (second_big, second_small)
    big = own_big.shape[0]
    parts, passed_at = pool, ring_size
    grads = (None, inner_grad, output_grad, window_grad, pack_low)
    outs = (d_outer, d_inner, d_output, d_window, d_pack)
    count = len(items)
    dp, blk, bits = place()
    sibling = across(dp, blk, bits, "c")
    is_end = (blk == 0) | (blk == ring_size - 1)
    is_middle = jnp.logical_not(is_end)
    partner = (dp, blk + 1 - 2 * lax.rem(blk, 2))
    facing = (dp, ring_size - 1 - blk)
    ring = [(dp, lax.rem(blk + step, ring_size)) for step in range(1, ring_size)]
    greet([sibling, across(dp, blk, bits, "x"), across(dp, blk, bits, "y")] + ring)

    micro, width, tokens = dcontext_part.shape
    spread = ring_size // micro
    row_at, group_at = blk // spread, lax.rem(blk, spread)
    group, length = context.shape
    heads = group // depth
    score_scale = 1.0 / math.sqrt(depth)
    mine = pl.ds(pl.multiple_of(blk * tokens, tokens), tokens)

    loads = []
    for index, (source, target) in enumerate(
        (
            (qkv_out, qkv),
            (context_out, context),
            (w_window_out, w_window),
            (hidden_row_out, hidden_row),
            (dresidual_out, dresidual),
        )
    ):
        copy = pltpu.make_async_copy(source, target, load_sem.at[index])
        copy.start()
        loads.append(copy)

    for half in range(micro):
        for part in range(ring_size):
            copy = pltpu.make_async_copy(
                active_out.at[pl.ds(half * tokens, tokens), pl.ds(part * width, width)],
                pool.at[part * micro + half],
                load_sem.at[len(loads)],
            )
            copy.start()
            loads.append(copy)

    head_copies = []
    def send_head(head):
        for step in range(1, ring_size):
            owner = lax.rem(blk + step, ring_size)
            first = lax.rem(owner, spread) * group + head * depth
            copy = remote(
                dcontext_part.at[owner // spread, pl.ds(first, depth)],
                dcontext.at[pl.ds(head * depth, depth), mine],
                head_send.at[head, step],
                head_recv.at[head, step],
                (dp, owner),
            )
            copy.start()
            head_copies.append(copy)
    send_head(0)
    send_head(1)
    dcontext[:, mine] = dcontext_part[row_at, pl.ds(group_at * group, group)]

    def owner_of(core, axes, first_bit, second_bit):
        return core + SIDE[axes[0]] * first_bit + SIDE[axes[1]] * second_bit

    def block(item, which):
        spec = items[item]
        return grads[spec["source"]].at[
            pl.ds(which * spec["stride"] + spec["row"], spec["rows"]),
            pl.ds(spec["column"], spec["columns"]),
        ]

    def cut(buffers, item, *index):
        spec = items[item]
        buffer, at = (buffers[0], item) if item < big else (buffers[1], item - big)
        return buffer.at[(at,) + index + (pl.ds(0, spec["rows"]), pl.ds(0, spec["columns"]))]

    def wide_cut(buffer, item, *index):
        spec = items[item]
        columns = spec["columns"] * spec["widened"]
        return buffer.at[(item,) + index + (pl.ds(0, spec["rows"]), pl.ds(0, columns))]

    def result(item):
        spec = items[item]
        many = spec["widened"]
        return outs[spec["source"]].at[
            pl.ds(spec["row"], spec["rows"]),
            pl.ds(spec["column"] * many, spec["columns"] * many),
        ]

    def copier(source, target, item, slot, peer):
        return remote(source, target, send_sem.at[item, slot], recv_sem.at[item, slot], peer)

    flying = {}

    def go(source, target, item, slot, peer):
        copy = copier(source, target, item, slot, peer)
        copy.start()
        flying[item, slot] = copy

    def start_core(item):
        axes = items[item]["route"]
        for f in range(2):
            for s in range(2):
                slot = 2 * f + s
                if items[item]["source"] == 0:
                    rows = pl.ds(items[item]["row"], items[item]["rows"])
                    ahead, behind = (f, s) if axes[0] == "x" else (s, f)
                    part = outer_parts.at[ahead, behind, rows]
                    go(part, cut(from_core, item, f, s), item, slot, sibling)
                    continue
                go(
                    block(item, owner_of(1 - bits["c"], axes, f, s)),
                    cut(from_core, item, f, s),
                    item,
                    slot,
                    sibling,
                )
                copy = pltpu.make_async_copy(
                    block(item, owner_of(bits["c"], axes, f, s)),
                    cut(own, item, f, s),
                    local_sem.at[item, slot],
                )
                copy.start()
                flying[item, "own", slot] = copy

    def after_core(item):
        axes = items[item]["route"]
        kept = bits[axes[0]]
        for slot in range(4):
            flying[item, slot].wait_recv()
            if items[item]["source"] != 0:
                flying[item, "own", slot].wait()
        for stays, f in ((False, 1 - kept), (True, kept)):
            for s in range(2):
                part = cut(own, item, f, s)
                part[...] = added(part[...], cut(from_core, item, f, s)[...])
                if not stays:
                    peer = across(dp, blk, bits, axes[0])
                    go(part, cut(from_first, item, s), item, 4 + s, peer)

    def after_first(item):
        axes = items[item]["route"]
        f, kept = bits[axes[0]], bits[axes[1]]
        for s in range(2):
            flying[item, 4 + s].wait_recv()
        part = cut(own, item, f, 1 - kept)
        part[...] = added(part[...], cut(from_first, item, 1 - kept)[...])
        go(part, cut(from_second, item), item, 6, across(dp, blk, bits, axes[1]))
        part = cut(own, item, f, kept)
        part[...] = added(part[...], cut(from_first, item, kept)[...])

    def after_second(item):
        spec = items[item]
        axes = spec["route"]
        f, s = bits[axes[0]], bits[axes[1]]
        flying[item, 6].wait_recv()
        total = added(cut(own, item, f, s)[...], cut(from_second, item)[...])
        if spec["widened"] > 1:
            at = pl.multiple_of(group_at * spec["columns"], 128)
            part = ring_two.at[item, 0, pl.ds(0, spec["rows"]), pl.ds(at, spec["columns"])]
            part[...] = total
            flying[item, 7] = copier(part, part, item, 7, partner)
        else:
            wide_cut(ring_one, item, 0)[...] = total
            flying[item, 7] = copier(
                wide_cut(ring_one, item, 0), wide_cut(ring_one, item, 1), item, 7, partner
            )
        flying[item, 8] = copier(
            wide_cut(ring_two, item, 0), wide_cut(ring_two, item, 1), item, 8, facing
        )
        flying[item, 9] = copier(result(item), result(item), item, 9, partner)

        @pl.when(is_end)
        def _():
            flying[item, 7].start()

    def at_middle(item):
        @pl.when(is_middle)
        def _():
            flying[item, 7].wait_recv()
            if items[item]["widened"] == 1:
                part = wide_cut(ring_two, item, 0)
                part[...] = added(
                    wide_cut(ring_one, item, 0)[...], wide_cut(ring_one, item, 1)[...]
                )
            flying[item, 8].start()

    def across_middle(item):
        @pl.when(is_middle)
        def _():
            flying[item, 8].wait_recv()
            result(item)[...] = added(
                wide_cut(ring_two, item, 0)[...], wide_cut(ring_two, item, 1)[...]
            )
            flying[item, 9].start()

    def at_end(item):
        @pl.when(is_end)
        def _():
            flying[item, 9].wait_recv()

    stages = (after_core, after_first, after_second, at_middle, across_middle, at_end)
    tick_of = [0]

    def tick(times=1):
        for _ in range(times):
            now = tick_of[0]
            tick_of[0] += 1
            for stage in reversed(range(len(stages))):
                item = now - LAG * stage
                if 0 <= item < count:
                    stages[stage](item)
            if now + AHEAD < len(early):
                start_core(early[now + AHEAD])

    early = [i for i, spec in enumerate(items) if spec["source"] < 3]
    late = [i for i, spec in enumerate(items) if spec["source"] >= 3]
    for item in early[:AHEAD]:
        start_core(item)

    seg_line = seg_row[...].astype(jnp.float32)
    seg_col = columns_of(seg_line)

    def one_head(head):
        def rows(part):
            first = part * group + head * depth
            return slice(first, first + depth)

        for step in range(ring_size - 1):
            head_copies[head * (ring_size - 1) + step].wait_recv()
        keys, values = qkv[rows(1), :].T, qkv[rows(2), :].T
        keys_t = qkv[rows(1), :]
        dkey_sum = jnp.zeros((depth, length), jnp.float32)
        dvalue_sum = jnp.zeros((depth, length), jnp.float32)
        for start in range(0, length, tokens):
            span = slice(start, start + tokens)
            peak = stats[2 * head : 2 * head + 1, span]
            total = stats[2 * head + 1 : 2 * head + 2, span]
            dctx = dcontext[rows(0), span].astype(jnp.float32)
            push = (dctx / total).astype(jnp.bfloat16)
            delta = jnp.sum(dctx * context[rows(0), span], axis=0, keepdims=True) / total
            queries_t = qkv[rows(0), span]
            raw = contract(keys, queries_t, 1, 0)
            same = seg_col == seg_line[:, span]
            weights = jnp.exp(jnp.where(same, raw * score_scale, NEGATIVE) - peak)
            pushed = contract(values, push, 1, 0)
            dscore = (weights * (pushed - delta) * score_scale).astype(jnp.bfloat16)
            dwindow[rows(0), span] = contract(keys_t, dscore, 1, 0).astype(jnp.bfloat16)
            dkey_sum = dkey_sum + contract(queries_t, dscore, 1, 1)
            dvalue_sum = dvalue_sum + contract(push, weights.astype(jnp.bfloat16), 1, 1)
        dwindow[rows(1), :] = dkey_sum.astype(jnp.bfloat16)
        dwindow[rows(2), :] = dvalue_sum.astype(jnp.bfloat16)

    def outer_block(core, x_bit, y_bit):
        stride = width // 2
        rows = pl.ds(pl.multiple_of(core * stride, 128), stride)
        part = x_bit + 2 * y_bit
        total = sum(
            contract(
                pool[part * micro + half, :, rows],
                douter[half * tokens : (half + 1) * tokens, :],
                0,
                0,
            )
            for half in range(micro)
        )
        return total.astype(jnp.bfloat16)

    def outer_work(step):
        x_bit, y_bit = step % 4 // 2, step % 2
        if step < 4:
            outer_parts[x_bit, y_bit] = outer_block(1 - bits["c"], x_bit, y_bit)
            return
        values = outer_block(bits["c"], x_bit, y_bit)
        for item, spec in enumerate(items):
            if spec["source"] == 0:
                f, s = (x_bit, y_bit) if spec["route"][0] == "x" else (y_bit, x_bit)
                cut(own, item, f, s)[...] = values[spec["row"] : spec["row"] + spec["rows"]]

    loads[0].wait()
    loads[1].wait()
    for head in range(heads):
        if head + 2 < heads:
            send_head(head + 2)
        one_head(head)
        if head == 0:
            for copy in loads[5:]:
                copy.wait()
        if head < 4:
            outer_work(2 * head)
            outer_work(2 * head + 1)
        tick()
    loads[2].wait()
    loads[3].wait()
    loads[4].wait()

    low = [m * spread for m in range(micro)]
    high = [m * spread + spread - 1 for m in range(micro)]

    def owns(m):
        return (blk >= low[m]) & (blk <= high[m])

    def receives(m, side):
        return blk + 1 <= high[m] if side == 0 else blk - 1 >= low[m]

    def has_target(side, distance):
        return blk >= distance if side == 0 else blk + distance < ring_size

    def hop(source, m, side, distance):
        return remote(
            source,
            arrived.at[m, side, distance - 1],
            hop_send.at[m, side, distance],
            hop_recv.at[m, side, distance - 1],
            (dp, blk - 1 + 2 * side),
        )

    def arrival(m, side, distance):
        view = arrived.at[m, side, distance]
        return remote(
            view,
            view,
            hop_send.at[m, side, distance],
            hop_recv.at[m, side, distance],
            (dp, blk - 1 + 2 * side),
        )

    def send_fresh(distance):
        for m in range(micro):
            for side in range(2):
                target = blk - distance * (1 - 2 * side)
                goes = has_target(side, distance) & owns(m)

                @pl.when(goes & jnp.logical_not(receives(m, side)))
                def _():
                    hop(parts.at[target], m, side, distance).start()

    def send_on(distance):
        for m in range(micro):
            for side in range(2):
                target = blk - distance * (1 - 2 * side)
                goes = has_target(side, distance) & receives(m, side)

                @pl.when(goes & owns(m))
                def _():
                    arrival(m, side, distance).wait_recv()
                    pool[passed_at + 2 * side + distance - 1] = added(parts[target], arrived[m, side, distance])
                    hop(pool.at[passed_at + 2 * side + distance - 1], m, side, distance).start()

                @pl.when(goes & jnp.logical_not(owns(m)))
                def _():
                    arrival(m, side, distance).wait_recv()
                    hop(arrived.at[m, side, distance], m, side, distance).start()

    def finish_hidden(_):
        for m in range(micro):
            for side in range(2):
                inside = blk < ring_size - 1 if side == 0 else blk > 0
                here = receives(m, side) & inside

                @pl.when(here & owns(m))
                def _():
                    arrival(m, side, 0).wait_recv()
                    dhidden[m] = (
                        dresidual[m]
                        + parts[blk].astype(jnp.float32)
                        + arrived[m, side, 0].astype(jnp.float32)
                    ).astype(jnp.bfloat16)

                @pl.when(here & jnp.logical_not(owns(m)))
                def _():
                    arrival(m, side, 0).wait_recv()
                    dhidden[m] = (
                        dresidual[m] + arrived[m, side, 0].astype(jnp.float32)
                    ).astype(jnp.bfloat16)

    end = (ring_size - 1) * (1 - row_at)
    inward = 2 * row_at - 1
    order = (end, end + inward, blk + 1 - 2 * lax.rem(blk, 2), blk)

    def make_part(target):
        at = pl.ds(pl.multiple_of(target * tokens, tokens), tokens)
        parts[target] = contract(dwindow[:, at].T, w_window[...], 1, 1).astype(jnp.bfloat16)

    ones = jnp.ones((8, length), jnp.bfloat16)
    line = lax.broadcasted_iota(jnp.int32, (8, 128), 0)
    lane = lax.broadcasted_iota(jnp.int32, (8, 128), 1)
    piece = width // (pack_part.shape[0] // 16)
    pack_sum[...] = pack_part[...]

    def make_grad(part):
        rows = slice(part * group, (part + 1) * group)
        window_grad[:, rows] = contract(hidden_row[...].T, dwindow[rows, :], 1, 1).astype(
            jnp.bfloat16
        )
        if part != 1:
            sums = contract(ones, dwindow[rows, :], 1, 1)
            sums = jnp.concatenate((sums, jnp.zeros((8, 128), jnp.float32)), axis=1)
            for step in range(group // piece):
                first = pl.multiple_of((group_at * (group // piece) + step) * 16, 16)
                pack_sum[pl.ds(first, 8), 0:128] += jnp.where(
                    (line == part // 2) & (lane < piece),
                    sums[:, step * piece : step * piece + 128],
                    0.0,
                )
        start_core(late[part])

    for index, target in enumerate(order):
        make_part(target)
        if index < ring_size - 1:
            send_fresh(ring_size - 1 - index)
            make_grad(index)
            tick()
    pack_low[...] = pack_sum[...].astype(jnp.bfloat16)
    start_core(late[3])
    for distance in reversed(range(1, ring_size - 1)):
        send_on(distance)
        tick(2)
    finish_hidden(None)
    tick(count + LAG * (len(stages) - 1) - tick_of[0])

    for copy in head_copies:
        copy.wait_send()
    for item in range(count):
        for slot in range(7):
            flying[item, slot].wait_send()
    for distance in range(1, ring_size):
        for m in range(micro):
            for side in range(2):

                @pl.when(has_target(side, distance) & (receives(m, side) | owns(m)))
                def _():
                    hop(parts.at[0], m, side, distance).wait_send()

    @pl.when(is_end)
    def _():
        for item in range(count):
            flying[item, 7].wait_send()

    @pl.when(is_middle)
    def _():
        for item in range(count):
            flying[item, 8].wait_send()
            flying[item, 9].wait_send()


def backward(
    dcontext_part,
    seg_row,
    pack_part,
    saved,
    w_window,
    hidden_row,
    dresidual,
    active,
    douter,
    grads,
    items,
    ring_size,
    dp_size,
    depth,
    collective,
):
    qkv, context, stats = saved
    micro, width, tokens = dcontext_part.shape
    group, length = context.shape
    heads = group // depth
    spread = ring_size // micro
    count = len(items)
    rows = max(item["rows"] for item in items)
    columns = max(item["columns"] * item["widened"] for item in items)
    piece = (rows, columns)
    narrow = jnp.bfloat16
    shape = jax.ShapeDtypeStruct
    outs = [shape((active.shape[1] // dp_size, width), narrow)]
    outs += [shape((grad.shape[0] // dp_size, grad.shape[1]), narrow) for grad in grads]
    outs.append(shape((width // dp_size, 3 * width), narrow))
    outs.append(shape((pack_part.shape[0] // dp_size, pack_part.shape[1]), narrow))
    scratch = [
        pltpu.VMEM(qkv.shape, narrow),
        pltpu.VMEM(context.shape, jnp.float32),
        pltpu.VMEM(w_window.shape, narrow),
        pltpu.VMEM(hidden_row.shape, narrow),
        pltpu.VMEM(dresidual.shape, jnp.float32),
        pltpu.VMEM((group, length), narrow),
        pltpu.VMEM(qkv.shape, narrow),
        pltpu.VMEM((2 * ring_size, tokens, width), narrow),
        pltpu.VMEM((micro, 2, ring_size - 1, tokens, width), narrow),
        pltpu.VMEM((width, 3 * group), narrow),
        pltpu.VMEM(pack_part.shape, jnp.float32),
        pltpu.VMEM(pack_part.shape, narrow),
    ]
    big = sum(item["source"] < 3 for item in items)
    scratch += [
        pltpu.VMEM((2, 2, active.shape[1] // dp_size, width), narrow),
    ]
    for lead in ((2, 2), (2, 2), (2,), ()):
        scratch += [
            pltpu.VMEM((big,) + lead + (rows, width), narrow),
            pltpu.VMEM((count - big,) + lead + (rows, group), narrow),
        ]
    scratch += [pltpu.VMEM((count, 2) + piece, narrow)] * 2
    scratch += [
        pltpu.SemaphoreType.DMA((5 + 2 * ring_size,)),
        pltpu.SemaphoreType.DMA((heads, ring_size)),
        pltpu.SemaphoreType.DMA((heads, ring_size)),
        pltpu.SemaphoreType.DMA((micro, 2, ring_size)),
        pltpu.SemaphoreType.DMA((micro, 2, ring_size)),
        pltpu.SemaphoreType.DMA((count, 10)),
        pltpu.SemaphoreType.DMA((count, 10)),
        pltpu.SemaphoreType.DMA((count, 4)),
    ]
    return pl.pallas_call(
        functools.partial(backward_kernel, items, ring_size, depth),
        out_shape=(shape((micro, tokens, width), narrow),) + tuple(outs),
        in_specs=[IN_VMEM] * 3 + [ANY, ANY, IN_VMEM, ANY, ANY, ANY, ANY, IN_VMEM, ANY, ANY],
        out_specs=(IN_VMEM,) * 6,
        scratch_shapes=scratch,
        compiler_params=comm_params(collective),
    )(
        dcontext_part,
        seg_row,
        pack_part,
        qkv,
        context,
        stats,
        w_window,
        hidden_row,
        dresidual,
        active,
        douter,
        *grads,
    )


def split_dot(left, right, left_dim, right_dim):
    high = left.astype(jnp.bfloat16)
    rest = (left - high.astype(jnp.float32)).astype(jnp.bfloat16)
    return contract(high, right, left_dim, right_dim) + contract(rest, right, left_dim, right_dim)


def retrieve_kernel(
    ring_size,
    dp_size,
    output,
    cotangent,
    seg_full,
    queries_all,
    hot_all,
    normed,
    factor,
    gain,
    dsecond,
    douter,
    sums,
    embeddings,
    loss,
    query_grad,
    own,
    arrived,
    tables,
    everyone,
    asked,
    hot,
    wide_loss,
    dscore,
    turned,
    send_sem,
    recv_sem,
    ring_send,
    ring_recv,
):
    dp, blk, _ = place()
    ring = [(dp, lax.rem(blk + step, ring_size)) for step in range(1, ring_size)]
    members = [(lax.rem(dp + step, dp_size), blk) for step in range(1, dp_size)]
    greet(ring + members)
    micro, tokens, _ = output.shape
    many = own.shape[0] // micro
    seg_rows = seg_full.shape[0] // ring_size
    lane = lax.broadcasted_iota(jnp.int32, (many, tokens), 1)
    number = lax.broadcasted_iota(jnp.int32, (many, tokens), 0)
    selects = []
    for m in range(micro):
        here = seg_full[pl.ds(blk * seg_rows + m, 1)]
        there = seg_full[pl.ds(jnp.maximum(blk - 1, 0) * seg_rows + m, 1)]
        here = jnp.broadcast_to(here, (many, tokens))
        there = jnp.broadcast_to(there, (many, tokens))
        there = jnp.where(blk == 0, -1, there)
        before = jnp.where(lane == 0, pltpu.roll(there, 1, 1), pltpu.roll(here, 1, 1))
        chosen = (here != before) & (here == number)
        selects.append(jnp.where(chosen, 1.0, 0.0).astype(jnp.bfloat16))
        own[m * many : (m + 1) * many] = contract(selects[m], output[m], 1, 0).astype(jnp.bfloat16)
    copies = []
    for step, peer in enumerate(ring):
        copy = remote(own, arrived.at[step], ring_send.at[step], ring_recv.at[step], peer)
        copy.start()
        copies.append(copy)
    for d in range(dp_size):
        for m in range(micro):
            rows = slice((d * micro + m) * many, (d * micro + m + 1) * many)
            at = slice(d * many, (d + 1) * many)
            asked[m, at] = queries_all[rows]
            hot[m, at] = hot_all[rows]
    for copy in copies:
        copy.wait()
    total = own[...].astype(jnp.float32)
    for step in range(ring_size - 1):
        total = total + arrived[step].astype(jnp.float32)
    tables[dp] = total.astype(jnp.bfloat16)
    copies = []
    for step, peer in enumerate(members):
        copy = remote(tables.at[dp], tables.at[dp], send_sem.at[step], recv_sem.at[step], peer)
        copy.start()
        copies.append(copy)
    for m in range(micro):
        embeddings[m] = total[m * many : (m + 1) * many].astype(jnp.bfloat16)
    for copy in copies:
        copy.wait()
    for m in range(micro):
        for d in range(dp_size):
            everyone[m, d * many : (d + 1) * many] = tables[d, m * many : (m + 1) * many]
    mine = pl.ds(pl.multiple_of(dp * many, many), many)
    for m in range(micro):
        scores = contract(asked[m], everyone[m], 1, 1)
        peak = jnp.max(scores, axis=1, keepdims=True)
        log_total = peak + jnp.log(jnp.sum(jnp.exp(scores - peak), axis=1, keepdims=True))
        target = hot[m].astype(jnp.float32)
        value = log_total - jnp.sum(scores * target, axis=1, keepdims=True)
        wide_loss[...] = jnp.broadcast_to(value, wide_loss.shape)
        loss[m] = wide_loss[mine]
        slope = jnp.exp(scores - log_total) - target
        dscore[...] = slope
        turned[...] = slope.T
        query_grad[m] = split_dot(dscore[mine], everyone[m], 1, 0)
        embed_grad = split_dot(turned[mine], asked[m], 1, 0)
        high = embed_grad.astype(jnp.bfloat16)
        rest = (embed_grad - high.astype(jnp.float32)).astype(jnp.bfloat16)
        dout = (
            cotangent[m].astype(jnp.float32)
            + contract(selects[m], high, 0, 0)
            + contract(selects[m], rest, 0, 0)
        )
        scaled = dout * gain[...]
        product = dout * normed[m]
        inner_term = (
            scaled
            - jnp.mean(scaled, axis=1, keepdims=True)
            - normed[m] * jnp.mean(scaled * normed[m], axis=1, keepdims=True)
        ) * factor[m]
        dsecond[m] = inner_term
        rounded = inner_term.astype(jnp.bfloat16)
        douter[m] = rounded
        for row, values in enumerate((product, dout, rounded.astype(jnp.float32))):
            line = jnp.sum(values, axis=0, keepdims=True)
            if m == 0:
                sums[row : row + 1] = line
            else:
                sums[row : row + 1] += line


def retrieve(
    output, cotangent, seg_full, queries_all, hot_all, normed, factor, gain, ring_size, dp_size
):
    micro, tokens, width = output.shape
    many = queries_all.shape[0] // (dp_size * micro)
    total = dp_size * many
    narrow, wide = jnp.bfloat16, jnp.float32
    shape = jax.ShapeDtypeStruct
    return pl.pallas_call(
        functools.partial(retrieve_kernel, ring_size, dp_size),
        out_shape=(
            shape((micro, tokens, width), wide),
            shape((micro, tokens, width), narrow),
            shape((8, width), wide),
            shape((micro, many, width), narrow),
            shape((micro, many, 128), wide),
            shape((micro, many, width), wide),
        ),
        in_specs=[IN_VMEM] * 8,
        out_specs=(IN_VMEM,) * 6,
        scratch_shapes=[
            pltpu.VMEM((micro * many, width), narrow),
            pltpu.VMEM((ring_size - 1, micro * many, width), narrow),
            pltpu.VMEM((dp_size, micro * many, width), narrow),
            pltpu.VMEM((micro, total, width), narrow),
            pltpu.VMEM((micro, total, width), narrow),
            pltpu.VMEM((micro, total, total), narrow),
            pltpu.VMEM((total, 128), wide),
            pltpu.VMEM((total, total), wide),
            pltpu.VMEM((total, total), wide),
            pltpu.SemaphoreType.DMA((dp_size,)),
            pltpu.SemaphoreType.DMA((dp_size,)),
            pltpu.SemaphoreType.DMA((ring_size,)),
            pltpu.SemaphoreType.DMA((ring_size,)),
        ],
        compiler_params=comm_params(4),
    )(output, cotangent, seg_full, queries_all, hot_all, normed, factor, gain)


def gelu_and_slope(values):
    size = jnp.abs(values)
    step = 1.0 / (1.0 + (0.3275911 / math.sqrt(2.0)) * size)
    series = 0.5 * 1.061405429
    for factor in (-1.453152027, 1.421413741, -0.284496736, 0.254829592):
        series = series * step + 0.5 * factor
    bell = jnp.exp(-0.5 * values * values)
    tail = series * step * bell
    normal_cdf = jnp.where(values >= 0.0, 1.0 - tail, tail)
    slope = normal_cdf + values * bell * (1.0 / math.sqrt(2.0 * math.pi))
    return values * normal_cdf, slope


def fast_body(
    hidden_in,
    segment_ids,
    queries,
    targets,
    cotangent,
    query_weight,
    key_weight,
    value_weight,
    output_weight,
    query_bias,
    value_bias,
    output_bias,
    first_gain,
    first_shift,
    inner_weight,
    inner_bias,
    outer_weight,
    outer_bias,
    second_gain,
    second_shift,
):
    dp_size, ring_size = lax.axis_size("dp"), lax.axis_size("blk")
    dp, blk = lax.axis_index("dp"), lax.axis_index("blk")
    micro, row_count, block_tokens, width = hidden_in.shape
    row_queries = queries.shape[1]
    length = block_tokens * ring_size
    head_dim = width // HEADS
    spread = ring_size // micro
    own_heads = HEADS // spread
    tokens = micro * block_tokens
    wide = jnp.float32
    narrow = jnp.bfloat16

    vectors = (
        query_bias,
        value_bias,
        output_bias,
        first_gain,
        first_shift,
        outer_bias,
        second_gain,
        second_shift,
        inner_bias,
    )
    piece = vectors[0].shape[0]
    inner_piece = inner_bias.shape[0]
    group = own_heads * head_dim
    row_at, group_at = blk // spread, lax.rem(blk, spread) * group
    hidden_rows = hidden_in.reshape(micro, block_tokens, width)
    pack = jnp.concatenate(
        (
            jnp.pad(jnp.stack(vectors[:8]), ((0, 0), (0, inner_piece - piece))),
            jnp.pad(inner_bias[None], ((0, 7), (0, 0))),
        )
    )
    passages = dp_size * row_queries
    hot = (
        targets[:, :, None] == jnp.arange(passages, dtype=jnp.int32)[None, None, :]
    ).astype(narrow)
    seg_pack = jnp.pad(segment_ids.reshape(micro, block_tokens), ((0, 8 - micro), (0, 0)))
    shards = (
        query_weight,
        key_weight,
        value_weight,
        pack,
        hot.reshape(micro * row_queries, passages),
        queries.reshape(micro * row_queries, width),
        output_weight,
        inner_weight,
        outer_weight,
    )
    ways = (("x", "y"), ("y", "x"))
    items = []

    def add_item(source, target, row=0, rows=None, from_column=0, columns=None, to_column=0):
        shape = shards[source].shape
        items.append(
            {
                "source": source,
                "target": target,
                "row": row,
                "rows": rows or shape[0],
                "stride": shape[0],
                "from_column": from_column,
                "columns": columns or shape[1],
                "to_column": to_column,
                "route": ways[len(items) % 2],
            }
        )

    for index in range(3):
        add_item(index, 0, from_column=None, columns=group, to_column=index * group)
    add_item(3, 1)
    add_item(6, 4)
    for part in range(4):
        add_item(7, 5, from_column=part * width, columns=width, to_column=part * width)
        add_item(8, 6, row=part * piece, rows=piece)
    add_item(4, 2)
    add_item(5, 3)
    targets_out = [jax.ShapeDtypeStruct((width, 3 * group), narrow)] + [
        jax.ShapeDtypeStruct((dp_size * s.shape[0], s.shape[1]), s.dtype) for s in shards[3:]
    ]
    (
        w_window,
        pack_all,
        hot_all,
        queries_all,
        wo_full,
        w_inner,
        w_outer,
        seg_all,
        hidden_row,
        qkv,
        context,
        stats,
        context_t,
    ) = forward(shards, items, targets_out, seg_pack, hidden_rows, ring_size, head_dim)
    pack_rows = pack_all.reshape(dp_size, 16, inner_piece)
    eight = pack_rows[:, :8, :piece].transpose(1, 0, 2).reshape(8, width).astype(wide)
    bq_full, bv_full, bo_full, gain_one, shift_one, b_outer, gain_two, shift_two = eight
    b_inner = pack_rows[:, 8].reshape(-1).astype(wide)
    seg_row = (
        seg_all.reshape(ring_size, 8, block_tokens)[:, :micro]
        .transpose(1, 0, 2)
        .reshape(micro, 1, length)
    )
    seg_mine = lax.dynamic_slice(seg_row, (row_at, 0, 0), (1, 1, length)).reshape(1, length)

    flat_rows = hidden_in.reshape(tokens, width)
    attended = (
        jnp.einsum("met,ed->mtd", context_t, wo_full, preferred_element_type=wide).reshape(
            tokens, width
        )
        + bo_full
    )
    first_out, first_normed, first_factor = layer_norm(
        flat_rows.astype(wide) + attended, gain_one, shift_one
    )
    first_low = first_out.astype(narrow)
    inner_pre = jnp.dot(first_low, w_inner, preferred_element_type=wide) + b_inner
    active, slope = gelu_and_slope(inner_pre)
    active, slope = lax.optimization_barrier((active.astype(narrow), slope.astype(narrow)))
    outer_out = jnp.dot(active, w_outer, preferred_element_type=wide) + b_outer
    output, second_normed, second_factor = layer_norm(first_out + outer_out, gain_two, shift_two)
    output_low = output.astype(narrow)
    output_rows = output_low.reshape(micro, block_tokens, width)

    dsecond, douter, second_sums, embeddings, query_loss, query_grad = retrieve(
        output_rows,
        cotangent.reshape(micro, block_tokens, width),
        seg_all,
        queries_all,
        hot_all,
        second_normed.reshape(micro, block_tokens, width),
        second_factor.reshape(micro, block_tokens, 1),
        gain_two.reshape(1, width),
        ring_size,
        dp_size,
    )
    query_loss = query_loss[:, :, 0]
    dsecond = dsecond.reshape(tokens, width)
    douter = douter.reshape(tokens, width)
    gain_two_grad, shift_two_grad, outer_bias_grad = second_sums[:3]
    dactive = jnp.einsum("nd,fd->nf", douter, w_outer, preferred_element_type=wide)
    dinner = (dactive * slope.astype(wide)).astype(narrow)
    inner_bias_grad = jnp.sum(dinner.astype(wide), axis=0)
    inner_weight_grad = jnp.einsum(
        "nd,nf->df", first_low, dinner, preferred_element_type=wide
    ).astype(narrow)
    dfirst = dsecond + jnp.einsum("nf,df->nd", dinner, w_inner, preferred_element_type=wide)
    gain_one_grad = jnp.sum(dfirst * first_normed, axis=0)
    shift_one_grad = jnp.sum(dfirst, axis=0)
    dresidual = norm_back(dfirst, first_normed, first_factor, gain_one)
    dattended = dresidual.astype(narrow)
    output_bias_grad = jnp.sum(dattended.astype(wide), axis=0)
    datt_rows = dattended.reshape(micro, block_tokens, width)
    output_weight_grad = jnp.einsum(
        "met,mtd->ed", context_t, datt_rows, preferred_element_type=wide
    ).astype(narrow)
    dcontext_t = jnp.einsum(
        "mtd,ed->met", datt_rows, wo_full, preferred_element_type=wide
    ).astype(narrow)
    vector_grads = jnp.stack(
        (
            jnp.zeros((width,), wide),
            jnp.zeros((width,), wide),
            output_bias_grad,
            gain_one_grad,
            shift_one_grad,
            outer_bias_grad,
            gain_two_grad,
            shift_two_grad,
        )
    )
    grad_pack = jnp.pad(
        jnp.concatenate(
            (
                jnp.pad(
                    vector_grads.reshape(8, dp_size, piece).transpose(1, 0, 2),
                    ((0, 0), (0, 0), (0, inner_piece - piece)),
                ),
                inner_bias_grad.reshape(dp_size, 1, inner_piece),
            ),
            axis=1,
        ),
        ((0, 0), (0, 7), (0, 0)),
    ).reshape(dp_size * 16, inner_piece)
    grads = (inner_weight_grad, output_weight_grad)
    grad_shapes = [(inner_bias.shape[0] * dp_size, width)]
    grad_shapes += [grad.shape for grad in grads] + [(width, 3 * group), grad_pack.shape]
    sums = []

    def add_sum(source, row=0, rows=None, column=0, columns=None, widened=1):
        shape = grad_shapes[source]
        sums.append(
            {
                "source": source,
                "row": row,
                "rows": rows or shape[0] // dp_size,
                "stride": shape[0] // dp_size,
                "column": column,
                "columns": columns or shape[1],
                "widened": widened,
                "route": ways[len(sums) % 2],
            }
        )

    for part in range(4):
        add_sum(1, column=part * width, columns=width)
    add_sum(2)
    for part in range(4):
        add_sum(0, row=part * piece, rows=piece)
    for index in range(3):
        add_sum(3, column=index * group, columns=group, widened=spread)
    add_sum(4)
    dhidden, d_outer, d_inner, d_wo, d_window, d_pack = backward(
        dcontext_t,
        seg_mine,
        grad_pack,
        (qkv, context, stats),
        w_window,
        hidden_row,
        dresidual.reshape(micro, block_tokens, width),
        active,
        douter,
        grads,
        sums,
        ring_size,
        dp_size,
        head_dim,
        5,
    )
    d_outer, d_inner, d_wo, d_window, d_pack = (
        part.astype(wide) for part in (d_outer, d_inner, d_wo, d_window, d_pack)
    )
    d_wq, d_wk, d_wv = (d_window[:, i * width : (i + 1) * width] for i in range(3))
    d_bq, d_bv, d_bo, d_g1, d_s1, d_bu, d_g2, d_s2 = (d_pack[i, :piece] for i in range(8))
    d_bi = d_pack[8]
    shape = (micro, row_count, block_tokens, width)
    return (
        output_low.reshape(shape),
        embeddings,
        query_loss,
        query_grad,
        dhidden.reshape(shape),
        d_wq,
        d_wk,
        d_wv,
        d_wo,
        d_bq,
        d_bv,
        d_bo,
        d_g1,
        d_s1,
        d_inner,
        d_bi,
        d_outer,
        d_bu,
        d_g2,
        d_s2,
    )


def solution(mesh):
    in_specs = (
        P(None, "dp", "blk", None),
        P(None, "dp", "blk"),
        P(None, "dp", None),
        P(None, "dp"),
        P(None, "dp", "blk", None),
        P("dp", None),
        P("dp", None),
        P("dp", None),
        P("dp", None),
        P("dp"),
        P("dp"),
        P("dp"),
        P("dp"),
        P("dp"),
        P("dp", None),
        P("dp"),
        P("dp", None),
        P("dp"),
        P("dp"),
        P("dp"),
    )
    out_specs = (
        P(None, "dp", "blk", None),
        P(None, "dp", None),
        P(None, "dp"),
        P(None, "dp", None),
        P(None, "dp", "blk", None),
        P("dp", None),
        P("dp", None),
        P("dp", None),
        P("dp", None),
        P("dp"),
        P("dp"),
        P("dp"),
        P("dp"),
        P("dp"),
        P("dp", None),
        P("dp"),
        P("dp", None),
        P("dp"),
        P("dp"),
        P("dp"),
    )
    fast = mesh.shape["dp"] == 8 and mesh.shape["blk"] == 4
    body = fast_body if fast else ring_body
    return jax.shard_map(body, mesh=mesh, in_specs=in_specs, out_specs=out_specs, check_vma=False)
```

```python
import functools
import math

import jax
import jax.numpy as jnp
from jax import lax
from jax.experimental import pallas as pl
from jax.experimental.pallas import tpu as pltpu
from jax.sharding import PartitionSpec as P

HEADS = 12


EPSILON = 1e-12
NEGATIVE = -1000000000.0
PRECISE = lax.Precision.HIGHEST


def passed_along(x, axis, by):
    size = lax.axis_size(axis)
    return lax.ppermute(x, axis, [(i, (i + by) % size) for i in range(size)])


def as_sent(x):
    return jax.tree.map(lambda a: a.astype(jnp.bfloat16) if a.dtype == jnp.float32 else a, x)


def layer_norm(values, norm_gain, norm_shift):
    center = values - jnp.mean(values, axis=-1, keepdims=True)
    factor = lax.rsqrt(jnp.mean(center * center, axis=-1, keepdims=True) + EPSILON)
    normed = center * factor
    return (normed * norm_gain + norm_shift, normed, factor)


def norm_back(gradient, normed, factor, norm_gain):
    scaled = gradient * norm_gain
    inner_term = (
        scaled
        - jnp.mean(scaled, axis=-1, keepdims=True)
        - normed * jnp.mean(scaled * normed, axis=-1, keepdims=True)
    )
    return inner_term * factor


def gelu_slope(values):
    normal_cdf = 0.5 * (1.0 + lax.erf(values * (1.0 / math.sqrt(2.0))))
    return normal_cdf + values * jnp.exp(-0.5 * values * values) * (1.0 / math.sqrt(2.0 * math.pi))


def scores_of(query_rows, key_rows, query_segment, key_segment, score_scale):
    raw_scores = jnp.einsum(
        "rqhd,rkhd->rhqk", query_rows, key_rows, preferred_element_type=jnp.float32
    )
    same_doc = (query_segment[:, :, None] == key_segment[:, None, :])[:, None]
    return jnp.where(same_doc, score_scale * raw_scores, NEGATIVE)


def contribute(
    query_rows,
    push_grad,
    delta_term,
    peak_term,
    query_segment,
    key_rows,
    value_rows,
    key_segment,
    score_scale,
):
    scores = scores_of(query_rows, key_rows, query_segment, key_segment, score_scale)
    weights = jnp.exp(scores - peak_term[..., None])
    pushed = jnp.einsum(
        "rqhd,rkhd->rhqk", push_grad, value_rows, preferred_element_type=jnp.float32
    )
    dscore = (weights * (pushed - delta_term[..., None]) * score_scale).astype(jnp.bfloat16)
    query_part = jnp.einsum("rhqk,rkhd->rqhd", dscore, key_rows, preferred_element_type=jnp.float32)
    key_part = jnp.einsum("rhqk,rqhd->rkhd", dscore, query_rows, preferred_element_type=jnp.float32)
    value_part = jnp.einsum(
        "rhqk,rqhd->rkhd",
        weights.astype(jnp.bfloat16),
        push_grad,
        preferred_element_type=jnp.float32,
    )
    return (query_part, key_part, value_part)


def ring_body(
    hidden_in,
    segment_ids,
    queries,
    targets,
    cotangent,
    query_weight,
    key_weight,
    value_weight,
    output_weight,
    query_bias,
    value_bias,
    output_bias,
    first_gain,
    first_shift,
    inner_weight,
    inner_bias,
    outer_weight,
    outer_bias,
    second_gain,
    second_shift,
):
    shards = (
        query_weight,
        key_weight,
        value_weight,
        output_weight,
        query_bias,
        value_bias,
        output_bias,
        first_gain,
        first_shift,
        inner_weight,
        inner_bias,
        outer_weight,
        outer_bias,
        second_gain,
        second_shift,
    )
    cycle_size = lax.axis_size("blk")
    cycle_place = lax.axis_index("blk")
    micro_count, row_count, block_tokens, model_width = hidden_in.shape
    segment_count = queries.shape[1] // row_count
    head_count = HEADS
    head_dim = model_width // head_count
    score_scale = 1.0 / math.sqrt(head_dim)
    token_count = row_count * block_tokens
    head_shape = (row_count, block_tokens, head_count, head_dim)
    grad_totals = tuple((jnp.zeros(shard_piece.shape, jnp.float32) for shard_piece in shards))
    local_sum = None
    gathered = None
    out_list, embed_list, loss_list, qgrad_list, hgrad_list = ([], [], [], [], [])
    for micro_index in range(micro_count):
        gathered = (
            lax.all_gather(shards[0], "dp", axis=0, tiled=True),
            lax.all_gather(shards[1], "dp", axis=0, tiled=True),
            lax.all_gather(shards[2], "dp", axis=0, tiled=True),
            lax.all_gather(shards[3], "dp", axis=0, tiled=True),
            lax.all_gather(shards[4], "dp", axis=0, tiled=True),
            lax.all_gather(shards[5], "dp", axis=0, tiled=True),
            lax.all_gather(shards[6], "dp", axis=0, tiled=True),
            lax.all_gather(shards[7], "dp", axis=0, tiled=True),
            lax.all_gather(shards[8], "dp", axis=0, tiled=True),
            lax.all_gather(shards[9], "dp", axis=0, tiled=True),
            lax.all_gather(shards[10], "dp", axis=0, tiled=True),
            lax.all_gather(shards[11], "dp", axis=0, tiled=True),
            lax.all_gather(shards[12], "dp", axis=0, tiled=True),
            lax.all_gather(shards[13], "dp", axis=0, tiled=True),
            lax.all_gather(shards[14], "dp", axis=0, tiled=True),
        )
        (
            wq_full,
            wk_full,
            wv_full,
            wo_full,
            bq_full,
            bv_full,
            bo_full,
            gain_one,
            shift_one,
            w_inner,
            b_inner,
            w_outer,
            b_outer,
            gain_two,
            shift_two,
        ) = gathered
        gain_one = gain_one.astype(jnp.float32)
        gain_two = gain_two.astype(jnp.float32)
        segment = segment_ids[micro_index]
        flat_rows = hidden_in[micro_index].reshape(token_count, model_width)
        query_rows = (
            (
                jnp.dot(flat_rows, wq_full, preferred_element_type=jnp.float32)
                + bq_full.astype(jnp.float32)
            )
            .astype(jnp.bfloat16)
            .reshape(head_shape)
        )
        key_rows = (
            jnp.dot(flat_rows, wk_full, preferred_element_type=jnp.float32)
            .astype(jnp.bfloat16)
            .reshape(head_shape)
        )
        value_rows = (
            (
                jnp.dot(flat_rows, wv_full, preferred_element_type=jnp.float32)
                + bv_full.astype(jnp.float32)
            )
            .astype(jnp.bfloat16)
            .reshape(head_shape)
        )

        def absorb(softmax_state, visit_keys, visit_values, visit_segment):
            running_peak, running_total, running_sum = softmax_state
            scores = scores_of(query_rows, visit_keys, segment, visit_segment, score_scale)
            new_peak = jnp.maximum(running_peak, jnp.max(scores, axis=-1))
            decay_factor = jnp.exp(running_peak - new_peak)
            weights = jnp.exp(scores - new_peak[..., None])
            running_total = running_total * decay_factor + jnp.sum(weights, axis=-1)
            update = jnp.einsum(
                "rhqk,rkhd->rqhd",
                weights.astype(jnp.bfloat16),
                visit_values,
                preferred_element_type=jnp.float32,
            )
            running_sum = running_sum * jnp.transpose(decay_factor, (0, 2, 1))[..., None] + update
            return (new_peak, running_total, running_sum)

        start_state = (
            jnp.full((row_count, head_count, block_tokens), -1e30, jnp.float32),
            jnp.zeros((row_count, head_count, block_tokens), jnp.float32),
            jnp.zeros(head_shape, jnp.float32),
        )
        first_state = absorb(start_state, key_rows, value_rows, segment)

        def forward_step(cycle_step, cycle_carry):
            visit_keys, visit_values, visit_segment, prior_segment, softmax_state = cycle_carry
            visit_keys, visit_values, visit_segment = passed_along(
                (visit_keys, visit_values, visit_segment), "blk", 1
            )
            prior_segment = jnp.where(cycle_step == 1, visit_segment[:, -1], prior_segment)
            return (
                visit_keys,
                visit_values,
                visit_segment,
                prior_segment,
                absorb(softmax_state, visit_keys, visit_values, visit_segment),
            )

        cycle_carry = lax.fori_loop(
            1, cycle_size, forward_step, (key_rows, value_rows, segment, segment[:, 0], first_state)
        )
        prior_segment = cycle_carry[3]
        row_peak, row_total, running_sum = cycle_carry[4]
        total_heads = jnp.transpose(row_total, (0, 2, 1))[..., None]
        context = running_sum / total_heads
        context_low = context.reshape(token_count, model_width).astype(jnp.bfloat16)
        attended = jnp.dot(
            context_low, wo_full, preferred_element_type=jnp.float32
        ) + bo_full.astype(jnp.float32)
        first_out, first_normed, first_factor = layer_norm(
            flat_rows.astype(jnp.float32) + attended, gain_one, shift_one.astype(jnp.float32)
        )
        first_low = first_out.astype(jnp.bfloat16)
        inner_pre = jnp.dot(
            first_low, w_inner, preferred_element_type=jnp.float32
        ) + b_inner.astype(jnp.float32)
        active = jax.nn.gelu(inner_pre, approximate=False).astype(jnp.bfloat16)
        outer_out = jnp.dot(active, w_outer, preferred_element_type=jnp.float32) + b_outer.astype(
            jnp.float32
        )
        output, second_normed, second_factor = layer_norm(
            first_out + outer_out, gain_two, shift_two.astype(jnp.float32)
        )
        output_low = output.astype(jnp.bfloat16)
        out_list.append(output_low.reshape(row_count, block_tokens, model_width))
        position = cycle_place * block_tokens + jnp.arange(block_tokens, dtype=jnp.int32)
        before = jnp.concatenate([prior_segment[:, None], segment[:, :-1]], axis=1)
        leading = (position[None, :] == 0) | (segment != before)
        numbers = jnp.arange(segment_count, dtype=jnp.int32)
        select = (leading[:, None, :] & (segment[:, None, :] == numbers[None, :, None])).astype(
            jnp.float32
        )
        cls_table = jnp.einsum(
            "rsi,rid->rsd",
            select.astype(jnp.bfloat16),
            output_low.reshape(row_count, block_tokens, model_width),
            preferred_element_type=jnp.float32,
        )
        own_table = lax.psum(cls_table.astype(jnp.bfloat16), "blk").reshape(
            row_count * segment_count, model_width
        )
        embed_list.append(own_table)
        everyone = lax.all_gather(own_table, "dp", axis=0, tiled=True)
        query_vectors = queries[micro_index]
        query_scores = jnp.dot(query_vectors, everyone.T, preferred_element_type=jnp.float32)
        score_peak = jnp.max(query_scores, axis=1, keepdims=True)
        log_total = score_peak[:, 0] + jnp.log(jnp.sum(jnp.exp(query_scores - score_peak), axis=1))
        target_hot = (
            jnp.arange(query_scores.shape[1], dtype=jnp.int32)[None, :]
            == targets[micro_index][:, None]
        ).astype(jnp.float32)
        loss_list.append(log_total - jnp.sum(query_scores * target_hot, axis=1))
        dscore_query = jnp.exp(query_scores - log_total[:, None]) - target_hot
        qgrad_list.append(jnp.dot(dscore_query, everyone.astype(jnp.float32), precision=PRECISE))
        embed_part = jnp.dot(dscore_query.T, query_vectors.astype(jnp.float32), precision=PRECISE)
        embed_grad = (
            lax.psum_scatter(embed_part.astype(jnp.bfloat16), "dp", scatter_dimension=0, tiled=True)
            .astype(jnp.float32)
            .reshape(row_count, segment_count, model_width)
        )
        cls_grad = jnp.einsum("rsi,rsd->rid", select, embed_grad, precision=PRECISE)
        dout = cotangent[micro_index].reshape(token_count, model_width).astype(
            jnp.float32
        ) + cls_grad.reshape(token_count, model_width)
        gain_two_grad = jnp.sum(dout * second_normed, axis=0)
        shift_two_grad = jnp.sum(dout, axis=0)
        dsecond = norm_back(dout, second_normed, second_factor, gain_two)
        douter = dsecond.astype(jnp.bfloat16)
        outer_bias_grad = jnp.sum(douter.astype(jnp.float32), axis=0)
        outer_weight_grad = jnp.einsum(
            "nf,nd->fd", active, douter, preferred_element_type=jnp.float32
        )
        dactive = jnp.einsum("nd,fd->nf", douter, w_outer, preferred_element_type=jnp.float32)
        dinner = (dactive * gelu_slope(inner_pre)).astype(jnp.bfloat16)
        inner_bias_grad = jnp.sum(dinner.astype(jnp.float32), axis=0)
        inner_weight_grad = jnp.einsum(
            "nd,nf->df", first_low, dinner, preferred_element_type=jnp.float32
        )
        dfirst = dsecond + jnp.einsum(
            "nf,df->nd", dinner, w_inner, preferred_element_type=jnp.float32
        )
        gain_one_grad = jnp.sum(dfirst * first_normed, axis=0)
        shift_one_grad = jnp.sum(dfirst, axis=0)
        dresidual = norm_back(dfirst, first_normed, first_factor, gain_one)
        dattended = dresidual.astype(jnp.bfloat16)
        output_bias_grad = jnp.sum(dattended.astype(jnp.float32), axis=0)
        output_weight_grad = jnp.einsum(
            "nd,ne->de", context_low, dattended, preferred_element_type=jnp.float32
        )
        dcontext = jnp.einsum(
            "ne,de->nd", dattended, wo_full, preferred_element_type=jnp.float32
        ).astype(jnp.bfloat16)
        dcontext_wide = dcontext.astype(jnp.float32).reshape(head_shape)
        push_grad = (dcontext_wide / total_heads).astype(jnp.bfloat16)
        delta_term = jnp.transpose(
            jnp.sum(dcontext_wide * context, axis=-1) / total_heads[..., 0], (0, 2, 1)
        )
        own_query, own_key, own_value = contribute(
            query_rows,
            push_grad,
            delta_term,
            row_peak,
            segment,
            key_rows,
            value_rows,
            segment,
            score_scale,
        )

        def key_step(cycle_step, cycle_carry):
            visit_keys, visit_values, visit_segment, query_sum, key_sum, value_sum = cycle_carry
            visit_keys, visit_values, visit_segment = passed_along(
                (visit_keys, visit_values, visit_segment), "blk", 1
            )
            key_sum, value_sum = (
                passed_along(key_sum.astype(jnp.bfloat16), "blk", 1).astype(key_sum.dtype),
                passed_along(value_sum.astype(jnp.bfloat16), "blk", 1).astype(value_sum.dtype),
            )
            query_part, key_part, value_part = contribute(
                query_rows,
                push_grad,
                delta_term,
                row_peak,
                segment,
                visit_keys,
                visit_values,
                visit_segment,
                score_scale,
            )
            return (
                visit_keys,
                visit_values,
                visit_segment,
                query_sum + query_part,
                key_sum + key_part,
                value_sum + value_part,
            )

        back_carry = lax.fori_loop(
            1, cycle_size, key_step, (key_rows, value_rows, segment, own_query, own_key, own_value)
        )
        query_sum = back_carry[3]
        key_sum, value_sum = (
            passed_along(back_carry[4].astype(jnp.bfloat16), "blk", 1).astype(jnp.float32),
            passed_along(back_carry[5].astype(jnp.bfloat16), "blk", 1).astype(jnp.float32),
        )
        dquery = query_sum.astype(jnp.bfloat16).reshape(token_count, model_width)
        dkey = key_sum.astype(jnp.bfloat16).reshape(token_count, model_width)
        dvalue = value_sum.astype(jnp.bfloat16).reshape(token_count, model_width)
        dhidden = dresidual + jnp.einsum(
            "ne,de->nd", dquery, wq_full, preferred_element_type=jnp.float32
        )
        dhidden = dhidden + jnp.einsum(
            "ne,de->nd", dkey, wk_full, preferred_element_type=jnp.float32
        )
        dhidden = dhidden + jnp.einsum(
            "ne,de->nd", dvalue, wv_full, preferred_element_type=jnp.float32
        )
        hgrad_list.append(
            dhidden.astype(jnp.bfloat16).reshape(row_count, block_tokens, model_width)
        )
        local_grads = (
            jnp.einsum("nd,ne->de", flat_rows, dquery, preferred_element_type=jnp.float32),
            jnp.einsum("nd,ne->de", flat_rows, dkey, preferred_element_type=jnp.float32),
            jnp.einsum("nd,ne->de", flat_rows, dvalue, preferred_element_type=jnp.float32),
            output_weight_grad,
            jnp.sum(dquery.astype(jnp.float32), axis=0),
            jnp.sum(dvalue.astype(jnp.float32), axis=0),
            output_bias_grad,
            gain_one_grad,
            shift_one_grad,
            inner_weight_grad,
            inner_bias_grad,
            outer_weight_grad,
            outer_bias_grad,
            gain_two_grad,
            shift_two_grad,
        )
        local_sum = local_grads
        reduced = jax.tree.map(
            lambda part: part.astype(jnp.float32),
            lax.psum_scatter(as_sent(local_sum), "dp", scatter_dimension=0, tiled=True),
        )
        reduced = jax.tree.map(
            lambda part: part.astype(jnp.float32), lax.psum(as_sent(reduced), "blk")
        )
        grad_totals = tuple(
            (total_piece + new_piece for total_piece, new_piece in zip(grad_totals, reduced))
        )
        local_sum = None
    return (
        jnp.stack(out_list),
        jnp.stack(embed_list),
        jnp.stack(loss_list),
        jnp.stack(qgrad_list),
        jnp.stack(hgrad_list),
        grad_totals[0],
        grad_totals[1],
        grad_totals[2],
        grad_totals[3],
        grad_totals[4],
        grad_totals[5],
        grad_totals[6],
        grad_totals[7],
        grad_totals[8],
        grad_totals[9],
        grad_totals[10],
        grad_totals[11],
        grad_totals[12],
        grad_totals[13],
        grad_totals[14],
    )


MESH = pl.DeviceIdType.MESH
VMEM_LIMIT = 60 * 1024 * 1024
SIDE = {"c": 1, "x": 2, "y": 4}


def place():
    dp, blk = lax.axis_index("dp"), lax.axis_index("blk")
    bits = {"c": lax.rem(dp, 2), "x": lax.rem(dp // 2, 2), "y": dp // 4}
    return dp, blk, bits


def across(dp, blk, bits, *axes):
    other = dp
    for axis in axes:
        other = other + SIDE[axis] * (1 - 2 * bits[axis])
    return (other, blk)


def greet(peers):
    barrier = pltpu.get_barrier_semaphore()
    for peer in peers:
        pl.semaphore_signal(barrier, inc=1, device_id=peer, device_id_type=MESH)
    pl.semaphore_wait(barrier, len(peers))


def remote(source, target, send_sem, recv_sem, peer):
    return pltpu.make_async_remote_copy(
        src_ref=source,
        dst_ref=target,
        send_sem=send_sem,
        recv_sem=recv_sem,
        device_id=peer,
        device_id_type=MESH,
    )


def comm_params(collective):
    return pltpu.CompilerParams(
        collective_id=collective, has_side_effects=True, vmem_limit_bytes=VMEM_LIMIT
    )


ANY = pl.BlockSpec(memory_space=pl.ANY)
IN_VMEM = pl.BlockSpec(memory_space=pltpu.VMEM)


SLABS = 2


def forward_kernel(items, ring_size, depth, sources, places, *refs):
    shards, seg_shard, hidden = refs[:sources], refs[sources], refs[sources + 1]
    outs = refs[sources + 2 :]
    w_window_out, hidden_row_out, qkv_out, context_out = (
        outs[0],
        outs[places + 1],
        outs[places + 2],
        outs[places + 3],
    )
    seg_full, stats, context_t = outs[places], outs[places + 4], outs[places + 5]
    (
        w_window,
        hidden_row,
        qkv,
        context,
        hidden_full,
        low,
        seg_line,
        mask,
        turned,
        keys,
        send_sem,
        recv_sem,
        seg_send,
        seg_recv,
        line_send,
        line_recv,
        head_send,
        head_recv,
        local_sem,
        store_sem,
    ) = outs[places + 6 :]
    fulls = (w_window,) + tuple(outs[1:places])
    pack_full = fulls[1]
    stores = []

    def store(source, target):
        copy = pltpu.make_async_copy(source, target, store_sem.at[len(stores)])
        copy.start()
        stores.append(copy)

    dp, blk, bits = place()
    sibling = across(dp, blk, bits, "c")
    ring = [(dp, lax.rem(blk + step, ring_size)) for step in range(1, ring_size)]
    greet([sibling, across(dp, blk, bits, "x"), across(dp, blk, bits, "y")] + ring)
    seg_rows = seg_shard.shape[0]
    micro, tokens, width = hidden.shape
    spread = ring_size // micro
    row_at, group_at = blk // spread, lax.rem(blk, spread)
    group, length = context.shape
    heads = group // depth
    score_scale = 1.0 / math.sqrt(depth)
    waiting = []
    mine = pl.ds(pl.multiple_of(blk * tokens, tokens), tokens)

    slab = tokens // SLABS

    def line_view(m, side, distance, part):
        owner = blk + (1 - 2 * side) * distance
        first = owner * tokens + part * slab
        return hidden_full.at[m, pl.ds(pl.multiple_of(first, slab), slab)]

    def line_copy(m, side, distance, part):
        view = line_view(m, side, distance, part)
        return remote(
            hidden.at[m, pl.ds(part * slab, slab)] if distance == 0 else view,
            view,
            line_send.at[m, side, distance, part],
            line_recv.at[m, side, distance + 1, part],
            (dp, blk - 1 + 2 * side),
        )

    def arrival(m, side, distance, part):
        view = line_view(m, side, distance, part)
        return remote(
            view,
            view,
            line_send.at[m, side, distance, part],
            line_recv.at[m, side, distance, part],
            (dp, blk - 1 + 2 * side),
        )

    def passes_on(m, side):
        return blk > m * spread if side == 0 else blk < m * spread + spread - 1

    def comes(m, side, distance):
        if side == 0:
            return (blk >= m * spread) & (blk + distance < ring_size)
        return (blk < m * spread + spread) & (blk >= distance)

    def line_step(distance, part):
        for m in range(micro):
            for side in range(2):

                @pl.when(comes(m, side, distance))
                def _():
                    arrival(m, side, distance, part).wait_recv()

                if distance < ring_size - 1:

                    @pl.when(comes(m, side, distance) & passes_on(m, side))
                    def _():
                        line_copy(m, side, distance, part).start()

    for part in range(SLABS):
        for m in range(micro):
            for side in range(2):

                @pl.when(passes_on(m, side))
                def _():
                    line_copy(m, side, 0, part).start()

    def own_part(item):
        spec = items[item]
        column = spec["from_column"]
        if column is None:
            column = pl.multiple_of(group_at * group, group)
        return shards[spec["source"]].at[
            pl.ds(spec["row"], spec["rows"]), pl.ds(column, spec["columns"])
        ]

    def block(item, owner):
        spec = items[item]
        first = owner * spec["stride"] + spec["row"]
        return fulls[spec["target"]].at[
            pl.ds(first, spec["rows"]), pl.ds(spec["to_column"], spec["columns"])
        ]

    inbound = {}

    def start_item(item):
        first, second = items[item]["route"]
        for slot, peer in enumerate(
            (across(dp, blk, bits, first), across(dp, blk, bits, second), sibling)
        ):
            copy = remote(
                own_part(item),
                block(item, dp),
                send_sem.at[item, slot],
                recv_sem.at[item, slot],
                peer,
            )
            copy.start()
            inbound[item, slot] = copy
        copy = pltpu.make_async_copy(own_part(item), block(item, dp), local_sem.at[item])
        copy.start()
        inbound[item, "own"] = copy

    def pass_on(item, held, slot, peer):
        copy = remote(held, held, send_sem.at[item, slot], recv_sem.at[item, slot], peer)
        copy.start()
        inbound[item, slot] = copy

    def relay_first(item):
        first, second = items[item]["route"]
        inbound[item, 0].wait_recv()
        held = block(item, across(dp, blk, bits, first)[0])
        pass_on(item, held, 3, across(dp, blk, bits, second))
        pass_on(item, held, 4, sibling)
        inbound[item, 1].wait_recv()
        pass_on(item, block(item, across(dp, blk, bits, second)[0]), 5, sibling)

    def relay_third(item):
        first, second = items[item]["route"]
        inbound[item, 3].wait_recv()
        pass_on(item, block(item, across(dp, blk, bits, first, second)[0]), 6, sibling)

    def all_here(item):
        for slot in (2, 4, 5, 6):
            inbound[item, slot].wait_recv()
        inbound[item, "own"].wait()

    early = [i for i, spec in enumerate(items) if spec["target"] < 2]
    late = [i for i, spec in enumerate(items) if spec["target"] >= 2]
    tick_of = [0]

    def tick(times=1):
        for _ in range(times):
            now = tick_of[0]
            tick_of[0] += 1
            if 0 <= now - 2 * LAG < len(late):
                relay_third(late[now - 2 * LAG])
            if 0 <= now - LAG < len(late):
                relay_first(late[now - LAG])
            if now < len(late):
                start_item(late[now])

    for item in early:
        start_item(item)
    for step, peer in enumerate(ring):
        copy = remote(
            seg_shard,
            seg_full.at[pl.ds(blk * seg_rows, seg_rows)],
            seg_send.at[step],
            seg_recv.at[step],
            peer,
        )
        copy.start()
        waiting.append(copy)
    seg_full[pl.ds(blk * seg_rows, seg_rows)] = seg_shard[...]

    for item in early:
        relay_first(item)
    tick()
    line_step(1, 0)
    tick()
    for part in range(1, SLABS):
        line_step(1, part)
    for item in early:
        relay_third(item)
    tick()
    for copy in waiting:
        copy.wait()
    for member in range(ring_size):
        seg_line[:, member * tokens : (member + 1) * tokens] = seg_full[
            pl.ds(member * seg_rows + row_at, 1)
        ].astype(jnp.float32)
    seg_col = columns_of(seg_line[...])
    for item in early:
        all_here(item)
    store(w_window, w_window_out)
    pack_turned = pack_full[...].astype(jnp.float32).T
    piece = width // (pack_full.shape[0] // 16)
    lane = lax.broadcasted_iota(jnp.int32, (piece, pack_full.shape[0]), 1)

    def bias_column(vector):
        pieces = []
        for part in range(group // piece):
            at = (group_at * (group // piece) + part) * 16 + vector
            pieces.append(
                jnp.sum(
                    jnp.where(lane == at, pack_turned[:piece], 0.0), axis=1, keepdims=True
                )
            )
        return jnp.concatenate(pieces, axis=0)

    biases = (bias_column(0), None, bias_column(1))
    for part in range(3):
        rows = slice(part * group, (part + 1) * group)
        turned[rows, :] = w_window[:, rows].T

    def project(at, source):
        span = pl.ds(pl.multiple_of(at * tokens, tokens), tokens)
        values = source[...]
        hidden_row[span, :] = values
        for part in range(3):
            rows = slice(part * group, (part + 1) * group)
            result = contract(turned[rows, :], values, 1, 1)
            if biases[part] is not None:
                result = result + biases[part]
            qkv[rows, span] = result.astype(jnp.bfloat16)

    def project_at(distance):
        for side in range(2):
            at = blk + (1 - 2 * side) * distance

            @pl.when((at >= 0) & (at < ring_size))
            def _():
                view = hidden_full.at[row_at, pl.ds(pl.multiple_of(at * tokens, tokens), tokens)]
                project(at, view)

    if ring_size > 2:
        line_step(2, 0)
    project(blk, hidden.at[row_at])
    tick()
    project_at(1)
    for distance in range(2, ring_size):
        for part in range(SLABS):
            if distance > 2 or part > 0:
                line_step(distance, part)
                tick()
        project_at(distance)

    store(hidden_row, hidden_row_out)
    store(qkv, qkv_out)
    copies = []

    def head_rows(part, head):
        first = part * group + head * depth
        return slice(first, first + depth)

    for head in range(heads):
        keys[head] = qkv[head_rows(1, head), :].T

    def attend(at):
        span = pl.ds(pl.multiple_of(at * tokens, tokens), tokens)
        mask[...] = jnp.where(seg_col == seg_line[:, span], 0.0, NEGATIVE)
        for head in range(heads):
            rows = head_rows(0, head)
            queries = (qkv[rows, span].astype(jnp.float32) * score_scale).astype(jnp.bfloat16)
            scores = contract(keys[head], queries, 1, 0) + mask[...]
            peak = jnp.max(scores, axis=0, keepdims=True)
            weights = jnp.exp(scores - peak)
            total = jnp.sum(weights, axis=0, keepdims=True)
            ctx = contract(qkv[head_rows(2, head), :], weights.astype(jnp.bfloat16), 1, 0) / total
            context[rows, span] = ctx
            low[rows, span] = ctx.astype(jnp.bfloat16)
            stats[2 * head : 2 * head + 1, span] = peak
            stats[2 * head + 1 : 2 * head + 2, span] = total

    end = (ring_size - 1) * (1 - row_at)
    order = (end, end + 2 * row_at - 1, blk + 1 - 2 * lax.rem(blk, 2), blk)
    target = context_t.at[row_at, pl.ds(group_at * group, group)]
    for index, at in enumerate(order):
        attend(at)
        span = pl.ds(pl.multiple_of(at * tokens, tokens), tokens)
        if index < ring_size - 1:
            step = lax.rem(at - blk + ring_size, ring_size)
            copy = remote(low.at[:, span], target, head_send.at[index], head_recv.at[step], (dp, at))
            copy.start()
            copies.append(copy)
        else:
            target[...] = low[:, span]
        tick(2)
    store(context, context_out)
    tick(len(late) + 2 * LAG - tick_of[0])
    for item in late:
        all_here(item)
    for item in early + late:
        for slot in range(7):
            inbound[item, slot].wait_send()
    for copy in copies:
        copy.wait_send()
    for copy in stores:
        copy.wait()
    for step, peer in enumerate(ring):
        remote(target, target, head_send.at[0], head_recv.at[step + 1], peer).wait_recv()
    for m in range(micro):
        for side in range(2):
            for distance in range(ring_size - 1):
                ready = passes_on(m, side)
                if distance:
                    ready = ready & comes(m, side, distance)

                @pl.when(ready)
                def _():
                    for part in range(SLABS):
                        line_copy(m, side, distance, part).wait_send()


def columns_of(row):
    return jnp.broadcast_to(row, (128, row.shape[1])).T[:, :1]


def forward(shards, items, targets, segments, hidden, ring_size, depth):
    micro, tokens, width = hidden.shape
    count = len(shards)
    length = ring_size * tokens
    group = width * micro // ring_size
    heads = group // depth
    shape = jax.ShapeDtypeStruct
    return pl.pallas_call(
        functools.partial(forward_kernel, items, ring_size, depth, count, len(targets)),
        out_shape=tuple(targets)
        + (
            shape((ring_size * segments.shape[0], tokens), jnp.int32),
            shape((length, width), jnp.bfloat16),
            shape((3 * group, length), jnp.bfloat16),
            shape((group, length), jnp.float32),
            shape((2 * heads, length), jnp.float32),
            shape((micro, width, tokens), jnp.bfloat16),
        ),
        in_specs=[IN_VMEM] * (count + 2),
        out_specs=(ANY, IN_VMEM)
        + (ANY,) * (len(targets) - 2)
        + (IN_VMEM, ANY, ANY, ANY, IN_VMEM, IN_VMEM),
        scratch_shapes=[
            pltpu.VMEM((width, 3 * group), jnp.bfloat16),
            pltpu.VMEM((length, width), jnp.bfloat16),
            pltpu.VMEM((3 * group, length), jnp.bfloat16),
            pltpu.VMEM((group, length), jnp.float32),
            pltpu.VMEM((micro, length, width), jnp.bfloat16),
            pltpu.VMEM((group, length), jnp.bfloat16),
            pltpu.VMEM((1, length), jnp.float32),
            pltpu.VMEM((length, tokens), jnp.float32),
            pltpu.VMEM((3 * group, width), jnp.bfloat16),
            pltpu.VMEM((heads, length, depth), jnp.bfloat16),
            pltpu.SemaphoreType.DMA((len(items), 7)),
            pltpu.SemaphoreType.DMA((len(items), 7)),
            pltpu.SemaphoreType.DMA((ring_size,)),
            pltpu.SemaphoreType.DMA((ring_size,)),
            pltpu.SemaphoreType.DMA((micro, 2, ring_size, SLABS)),
            pltpu.SemaphoreType.DMA((micro, 2, ring_size, SLABS)),
            pltpu.SemaphoreType.DMA((ring_size,)),
            pltpu.SemaphoreType.DMA((ring_size,)),
            pltpu.SemaphoreType.DMA((len(items),)),
            pltpu.SemaphoreType.DMA((4,)),
        ],
        compiler_params=comm_params(1),
    )(*shards, segments, hidden)


def contract(left, right, left_dim, right_dim):
    return lax.dot_general(
        left, right, (((left_dim,), (right_dim,)), ((), ())), preferred_element_type=jnp.float32
    )


LAG, AHEAD = 3, 3


def added(left, right):
    return (left.astype(jnp.float32) + right.astype(jnp.float32)).astype(jnp.bfloat16)


def backward_kernel(items, ring_size, depth, *refs):
    (
        dcontext_part,
        seg_row,
        pack_part,
        qkv_out,
        context_out,
        stats,
        w_window_out,
        hidden_row_out,
        dresidual_out,
        active_out,
        douter,
        inner_grad,
        output_grad,
    ) = refs[:13]
    dhidden, d_outer, d_inner, d_output, d_window, d_pack = refs[13:19]
    (
        qkv,
        context,
        w_window,
        hidden_row,
        dresidual,
        dcontext,
        dwindow,
        pool,
        arrived,
        window_grad,
        pack_sum,
        pack_low,
        outer_parts,
        own_big,
        own_small,
        core_big,
        core_small,
        first_big,
        first_small,
        second_big,
        second_small,
        ring_one,
        ring_two,
        load_sem,
        head_send,
        head_recv,
        hop_send,
        hop_recv,
        send_sem,
        recv_sem,
        local_sem,
    ) = refs[19:]
    own, from_core = (own_big, own_small), (core_big, core_small)
    from_first, from_second = (first_big, first_small), (second_big, second_small)
    big = own_big.shape[0]
    parts, passed_at = pool, ring_size
    grads = (None, inner_grad, output_grad, window_grad, pack_low)
    outs = (d_outer, d_inner, d_output, d_window, d_pack)
    count = len(items)
    dp, blk, bits = place()
    sibling = across(dp, blk, bits, "c")
    is_end = (blk == 0) | (blk == ring_size - 1)
    is_middle = jnp.logical_not(is_end)
    partner = (dp, blk + 1 - 2 * lax.rem(blk, 2))
    facing = (dp, ring_size - 1 - blk)
    ring = [(dp, lax.rem(blk + step, ring_size)) for step in range(1, ring_size)]
    greet([sibling, across(dp, blk, bits, "x"), across(dp, blk, bits, "y")] + ring)

    micro, width, tokens = dcontext_part.shape
    spread = ring_size // micro
    row_at, group_at = blk // spread, lax.rem(blk, spread)
    group, length = context.shape
    heads = group // depth
    score_scale = 1.0 / math.sqrt(depth)
    mine = pl.ds(pl.multiple_of(blk * tokens, tokens), tokens)

    loads = []
    for index, (source, target) in enumerate(
        (
            (qkv_out, qkv),
            (context_out, context),
            (w_window_out, w_window),
            (hidden_row_out, hidden_row),
            (dresidual_out, dresidual),
        )
    ):
        copy = pltpu.make_async_copy(source, target, load_sem.at[index])
        copy.start()
        loads.append(copy)

    for half in range(micro):
        for part in range(ring_size):
            copy = pltpu.make_async_copy(
                active_out.at[pl.ds(half * tokens, tokens), pl.ds(part * width, width)],
                pool.at[part * micro + half],
                load_sem.at[len(loads)],
            )
            copy.start()
            loads.append(copy)

    head_copies = []
    def send_head(head):
        for step in range(1, ring_size):
            owner = lax.rem(blk + step, ring_size)
            first = lax.rem(owner, spread) * group + head * depth
            copy = remote(
                dcontext_part.at[owner // spread, pl.ds(first, depth)],
                dcontext.at[pl.ds(head * depth, depth), mine],
                head_send.at[head, step],
                head_recv.at[head, step],
                (dp, owner),
            )
            copy.start()
            head_copies.append(copy)
    send_head(0)
    send_head(1)
    dcontext[:, mine] = dcontext_part[row_at, pl.ds(group_at * group, group)]

    def owner_of(core, axes, first_bit, second_bit):
        return core + SIDE[axes[0]] * first_bit + SIDE[axes[1]] * second_bit

    def block(item, which):
        spec = items[item]
        return grads[spec["source"]].at[
            pl.ds(which * spec["stride"] + spec["row"], spec["rows"]),
            pl.ds(spec["column"], spec["columns"]),
        ]

    def cut(buffers, item, *index):
        spec = items[item]
        buffer, at = (buffers[0], item) if item < big else (buffers[1], item - big)
        return buffer.at[(at,) + index + (pl.ds(0, spec["rows"]), pl.ds(0, spec["columns"]))]

    def wide_cut(buffer, item, *index):
        spec = items[item]
        columns = spec["columns"] * spec["widened"]
        return buffer.at[(item,) + index + (pl.ds(0, spec["rows"]), pl.ds(0, columns))]

    def result(item):
        spec = items[item]
        many = spec["widened"]
        return outs[spec["source"]].at[
            pl.ds(spec["row"], spec["rows"]),
            pl.ds(spec["column"] * many, spec["columns"] * many),
        ]

    def copier(source, target, item, slot, peer):
        return remote(source, target, send_sem.at[item, slot], recv_sem.at[item, slot], peer)

    flying = {}

    def go(source, target, item, slot, peer):
        copy = copier(source, target, item, slot, peer)
        copy.start()
        flying[item, slot] = copy

    def start_core(item):
        axes = items[item]["route"]
        for f in range(2):
            for s in range(2):
                slot = 2 * f + s
                if items[item]["source"] == 0:
                    rows = pl.ds(items[item]["row"], items[item]["rows"])
                    ahead, behind = (f, s) if axes[0] == "x" else (s, f)
                    part = outer_parts.at[ahead, behind, rows]
                    go(part, cut(from_core, item, f, s), item, slot, sibling)
                    continue
                go(
                    block(item, owner_of(1 - bits["c"], axes, f, s)),
                    cut(from_core, item, f, s),
                    item,
                    slot,
                    sibling,
                )
                copy = pltpu.make_async_copy(
                    block(item, owner_of(bits["c"], axes, f, s)),
                    cut(own, item, f, s),
                    local_sem.at[item, slot],
                )
                copy.start()
                flying[item, "own", slot] = copy

    def after_core(item):
        axes = items[item]["route"]
        kept = bits[axes[0]]
        for slot in range(4):
            flying[item, slot].wait_recv()
            if items[item]["source"] != 0:
                flying[item, "own", slot].wait()
        for stays, f in ((False, 1 - kept), (True, kept)):
            for s in range(2):
                part = cut(own, item, f, s)
                part[...] = added(part[...], cut(from_core, item, f, s)[...])
                if not stays:
                    peer = across(dp, blk, bits, axes[0])
                    go(part, cut(from_first, item, s), item, 4 + s, peer)

    def after_first(item):
        axes = items[item]["route"]
        f, kept = bits[axes[0]], bits[axes[1]]
        for s in range(2):
            flying[item, 4 + s].wait_recv()
        part = cut(own, item, f, 1 - kept)
        part[...] = added(part[...], cut(from_first, item, 1 - kept)[...])
        go(part, cut(from_second, item), item, 6, across(dp, blk, bits, axes[1]))
        part = cut(own, item, f, kept)
        part[...] = added(part[...], cut(from_first, item, kept)[...])

    def after_second(item):
        spec = items[item]
        axes = spec["route"]
        f, s = bits[axes[0]], bits[axes[1]]
        flying[item, 6].wait_recv()
        total = added(cut(own, item, f, s)[...], cut(from_second, item)[...])
        if spec["widened"] > 1:
            at = pl.multiple_of(group_at * spec["columns"], 128)
            part = ring_two.at[item, 0, pl.ds(0, spec["rows"]), pl.ds(at, spec["columns"])]
            part[...] = total
            flying[item, 7] = copier(part, part, item, 7, partner)
        else:
            wide_cut(ring_one, item, 0)[...] = total
            flying[item, 7] = copier(
                wide_cut(ring_one, item, 0), wide_cut(ring_one, item, 1), item, 7, partner
            )
        flying[item, 8] = copier(
            wide_cut(ring_two, item, 0), wide_cut(ring_two, item, 1), item, 8, facing
        )
        flying[item, 9] = copier(result(item), result(item), item, 9, partner)

        @pl.when(is_end)
        def _():
            flying[item, 7].start()

    def at_middle(item):
        @pl.when(is_middle)
        def _():
            flying[item, 7].wait_recv()
            if items[item]["widened"] == 1:
                part = wide_cut(ring_two, item, 0)
                part[...] = added(
                    wide_cut(ring_one, item, 0)[...], wide_cut(ring_one, item, 1)[...]
                )
            flying[item, 8].start()

    def across_middle(item):
        @pl.when(is_middle)
        def _():
            flying[item, 8].wait_recv()
            result(item)[...] = added(
                wide_cut(ring_two, item, 0)[...], wide_cut(ring_two, item, 1)[...]
            )
            flying[item, 9].start()

    def at_end(item):
        @pl.when(is_end)
        def _():
            flying[item, 9].wait_recv()

    stages = (after_core, after_first, after_second, at_middle, across_middle, at_end)
    tick_of = [0]

    def tick(times=1):
        for _ in range(times):
            now = tick_of[0]
            tick_of[0] += 1
            for stage in reversed(range(len(stages))):
                item = now - LAG * stage
                if 0 <= item < count:
                    stages[stage](item)
            if now + AHEAD < len(early):
                start_core(early[now + AHEAD])

    early = [i for i, spec in enumerate(items) if spec["source"] < 3]
    late = [i for i, spec in enumerate(items) if spec["source"] >= 3]
    for item in early[:AHEAD]:
        start_core(item)

    seg_line = seg_row[...].astype(jnp.float32)
    seg_col = columns_of(seg_line)

    def one_head(head):
        def rows(part):
            first = part * group + head * depth
            return slice(first, first + depth)

        for step in range(ring_size - 1):
            head_copies[head * (ring_size - 1) + step].wait_recv()
        keys, values = qkv[rows(1), :].T, qkv[rows(2), :].T
        keys_t = qkv[rows(1), :]
        dkey_sum = jnp.zeros((depth, length), jnp.float32)
        dvalue_sum = jnp.zeros((depth, length), jnp.float32)
        for start in range(0, length, tokens):
            span = slice(start, start + tokens)
            peak = stats[2 * head : 2 * head + 1, span]
            total = stats[2 * head + 1 : 2 * head + 2, span]
            dctx = dcontext[rows(0), span].astype(jnp.float32)
            push = (dctx / total).astype(jnp.bfloat16)
            delta = jnp.sum(dctx * context[rows(0), span], axis=0, keepdims=True) / total
            queries_t = qkv[rows(0), span]
            raw = contract(keys, queries_t, 1, 0)
            same = seg_col == seg_line[:, span]
            weights = jnp.exp(jnp.where(same, raw * score_scale, NEGATIVE) - peak)
            pushed = contract(values, push, 1, 0)
            dscore = (weights * (pushed - delta) * score_scale).astype(jnp.bfloat16)
            dwindow[rows(0), span] = contract(keys_t, dscore, 1, 0).astype(jnp.bfloat16)
            dkey_sum = dkey_sum + contract(queries_t, dscore, 1, 1)
            dvalue_sum = dvalue_sum + contract(push, weights.astype(jnp.bfloat16), 1, 1)
        dwindow[rows(1), :] = dkey_sum.astype(jnp.bfloat16)
        dwindow[rows(2), :] = dvalue_sum.astype(jnp.bfloat16)

    def outer_block(core, x_bit, y_bit):
        stride = width // 2
        rows = pl.ds(pl.multiple_of(core * stride, 128), stride)
        part = x_bit + 2 * y_bit
        total = sum(
            contract(
                pool[part * micro + half, :, rows],
                douter[half * tokens : (half + 1) * tokens, :],
                0,
                0,
            )
            for half in range(micro)
        )
        return total.astype(jnp.bfloat16)

    def outer_work(step):
        x_bit, y_bit = step % 4 // 2, step % 2
        if step < 4:
            outer_parts[x_bit, y_bit] = outer_block(1 - bits["c"], x_bit, y_bit)
            return
        values = outer_block(bits["c"], x_bit, y_bit)
        for item, spec in enumerate(items):
            if spec["source"] == 0:
                f, s = (x_bit, y_bit) if spec["route"][0] == "x" else (y_bit, x_bit)
                cut(own, item, f, s)[...] = values[spec["row"] : spec["row"] + spec["rows"]]

    loads[0].wait()
    loads[1].wait()
    tick(2)
    for head in range(heads):
        if head + 2 < heads:
            send_head(head + 2)
        one_head(head)
        if head == 0:
            for copy in loads[5:]:
                copy.wait()
            for step in range(4):
                outer_work(step)
        if head in (1, 2):
            outer_work(2 * head + 2)
            outer_work(2 * head + 3)
        tick()
    loads[2].wait()
    loads[3].wait()
    loads[4].wait()

    low = [m * spread for m in range(micro)]
    high = [m * spread + spread - 1 for m in range(micro)]

    def owns(m):
        return (blk >= low[m]) & (blk <= high[m])

    def receives(m, side):
        return blk + 1 <= high[m] if side == 0 else blk - 1 >= low[m]

    def has_target(side, distance):
        return blk >= distance if side == 0 else blk + distance < ring_size

    def hop(source, m, side, distance):
        return remote(
            source,
            arrived.at[m, side, distance - 1],
            hop_send.at[m, side, distance],
            hop_recv.at[m, side, distance - 1],
            (dp, blk - 1 + 2 * side),
        )

    def arrival(m, side, distance):
        view = arrived.at[m, side, distance]
        return remote(
            view,
            view,
            hop_send.at[m, side, distance],
            hop_recv.at[m, side, distance],
            (dp, blk - 1 + 2 * side),
        )

    def send_fresh(distance):
        for m in range(micro):
            for side in range(2):
                target = blk - distance * (1 - 2 * side)
                goes = has_target(side, distance) & owns(m)

                @pl.when(goes & jnp.logical_not(receives(m, side)))
                def _():
                    hop(parts.at[target], m, side, distance).start()

    def send_on(distance):
        for m in range(micro):
            for side in range(2):
                target = blk - distance * (1 - 2 * side)
                goes = has_target(side, distance) & receives(m, side)

                @pl.when(goes & owns(m))
                def _():
                    arrival(m, side, distance).wait_recv()
                    pool[passed_at + 2 * side + distance - 1] = added(parts[target], arrived[m, side, distance])
                    hop(pool.at[passed_at + 2 * side + distance - 1], m, side, distance).start()

                @pl.when(goes & jnp.logical_not(owns(m)))
                def _():
                    arrival(m, side, distance).wait_recv()
                    hop(arrived.at[m, side, distance], m, side, distance).start()

    def finish_hidden(_):
        for m in range(micro):
            for side in range(2):
                inside = blk < ring_size - 1 if side == 0 else blk > 0
                here = receives(m, side) & inside

                @pl.when(here & owns(m))
                def _():
                    arrival(m, side, 0).wait_recv()
                    dhidden[m] = (
                        dresidual[m]
                        + parts[blk].astype(jnp.float32)
                        + arrived[m, side, 0].astype(jnp.float32)
                    ).astype(jnp.bfloat16)

                @pl.when(here & jnp.logical_not(owns(m)))
                def _():
                    arrival(m, side, 0).wait_recv()
                    dhidden[m] = (
                        dresidual[m] + arrived[m, side, 0].astype(jnp.float32)
                    ).astype(jnp.bfloat16)

    end = (ring_size - 1) * (1 - row_at)
    inward = 2 * row_at - 1
    order = (end, end + inward, blk + 1 - 2 * lax.rem(blk, 2), blk)

    def make_part(target):
        at = pl.ds(pl.multiple_of(target * tokens, tokens), tokens)
        parts[target] = contract(dwindow[:, at].T, w_window[...], 1, 1).astype(jnp.bfloat16)

    ones = jnp.ones((8, length), jnp.bfloat16)
    line = lax.broadcasted_iota(jnp.int32, (8, 128), 0)
    lane = lax.broadcasted_iota(jnp.int32, (8, 128), 1)
    piece = width // (pack_part.shape[0] // 16)
    pack_sum[...] = pack_part[...]

    def make_grad(part):
        rows = slice(part * group, (part + 1) * group)
        window_grad[:, rows] = contract(hidden_row[...].T, dwindow[rows, :], 1, 1).astype(
            jnp.bfloat16
        )
        if part != 1:
            sums = contract(ones, dwindow[rows, :], 1, 1)
            sums = jnp.concatenate((sums, jnp.zeros((8, 128), jnp.float32)), axis=1)
            for step in range(group // piece):
                first = pl.multiple_of((group_at * (group // piece) + step) * 16, 16)
                pack_sum[pl.ds(first, 8), 0:128] += jnp.where(
                    (line == part // 2) & (lane < piece),
                    sums[:, step * piece : step * piece + 128],
                    0.0,
                )
        start_core(late[part])

    for index, target in enumerate(order):
        make_part(target)
        if index < ring_size - 1:
            send_fresh(ring_size - 1 - index)
            make_grad(index)
            tick()
    pack_low[...] = pack_sum[...].astype(jnp.bfloat16)
    start_core(late[3])
    for distance in reversed(range(1, ring_size - 1)):
        send_on(distance)
        tick(2)
    finish_hidden(None)
    tick(count + LAG * (len(stages) - 1) - tick_of[0])

    for copy in head_copies:
        copy.wait_send()
    for item in range(count):
        for slot in range(7):
            flying[item, slot].wait_send()
    for distance in range(1, ring_size):
        for m in range(micro):
            for side in range(2):

                @pl.when(has_target(side, distance) & (receives(m, side) | owns(m)))
                def _():
                    hop(parts.at[0], m, side, distance).wait_send()

    @pl.when(is_end)
    def _():
        for item in range(count):
            flying[item, 7].wait_send()

    @pl.when(is_middle)
    def _():
        for item in range(count):
            flying[item, 8].wait_send()
            flying[item, 9].wait_send()


def backward(
    dcontext_part,
    seg_row,
    pack_part,
    saved,
    w_window,
    hidden_row,
    dresidual,
    active,
    douter,
    grads,
    items,
    ring_size,
    dp_size,
    depth,
    collective,
):
    qkv, context, stats = saved
    micro, width, tokens = dcontext_part.shape
    group, length = context.shape
    heads = group // depth
    spread = ring_size // micro
    count = len(items)
    rows = max(item["rows"] for item in items)
    columns = max(item["columns"] * item["widened"] for item in items)
    piece = (rows, columns)
    narrow = jnp.bfloat16
    shape = jax.ShapeDtypeStruct
    outs = [shape((active.shape[1] // dp_size, width), narrow)]
    outs += [shape((grad.shape[0] // dp_size, grad.shape[1]), narrow) for grad in grads]
    outs.append(shape((width // dp_size, 3 * width), narrow))
    outs.append(shape((pack_part.shape[0] // dp_size, pack_part.shape[1]), narrow))
    scratch = [
        pltpu.VMEM(qkv.shape, narrow),
        pltpu.VMEM(context.shape, jnp.float32),
        pltpu.VMEM(w_window.shape, narrow),
        pltpu.VMEM(hidden_row.shape, narrow),
        pltpu.VMEM(dresidual.shape, jnp.float32),
        pltpu.VMEM((group, length), narrow),
        pltpu.VMEM(qkv.shape, narrow),
        pltpu.VMEM((2 * ring_size, tokens, width), narrow),
        pltpu.VMEM((micro, 2, ring_size - 1, tokens, width), narrow),
        pltpu.VMEM((width, 3 * group), narrow),
        pltpu.VMEM(pack_part.shape, jnp.float32),
        pltpu.VMEM(pack_part.shape, narrow),
    ]
    big = sum(item["source"] < 3 for item in items)
    scratch += [
        pltpu.VMEM((2, 2, active.shape[1] // dp_size, width), narrow),
    ]
    for lead in ((2, 2), (2, 2), (2,), ()):
        scratch += [
            pltpu.VMEM((big,) + lead + (rows, width), narrow),
            pltpu.VMEM((count - big,) + lead + (rows, group), narrow),
        ]
    scratch += [pltpu.VMEM((count, 2) + piece, narrow)] * 2
    scratch += [
        pltpu.SemaphoreType.DMA((5 + 2 * ring_size,)),
        pltpu.SemaphoreType.DMA((heads, ring_size)),
        pltpu.SemaphoreType.DMA((heads, ring_size)),
        pltpu.SemaphoreType.DMA((micro, 2, ring_size)),
        pltpu.SemaphoreType.DMA((micro, 2, ring_size)),
        pltpu.SemaphoreType.DMA((count, 10)),
        pltpu.SemaphoreType.DMA((count, 10)),
        pltpu.SemaphoreType.DMA((count, 4)),
    ]
    return pl.pallas_call(
        functools.partial(backward_kernel, items, ring_size, depth),
        out_shape=(shape((micro, tokens, width), narrow),) + tuple(outs),
        in_specs=[IN_VMEM] * 3 + [ANY, ANY, IN_VMEM, ANY, ANY, ANY, ANY, IN_VMEM, ANY, ANY],
        out_specs=(IN_VMEM,) * 6,
        scratch_shapes=scratch,
        compiler_params=comm_params(collective),
    )(
        dcontext_part,
        seg_row,
        pack_part,
        qkv,
        context,
        stats,
        w_window,
        hidden_row,
        dresidual,
        active,
        douter,
        *grads,
    )


def split_dot(left, right, left_dim, right_dim):
    high = left.astype(jnp.bfloat16)
    rest = (left - high.astype(jnp.float32)).astype(jnp.bfloat16)
    return contract(high, right, left_dim, right_dim) + contract(rest, right, left_dim, right_dim)


def retrieve_kernel(
    ring_size,
    dp_size,
    output,
    cotangent,
    seg_full,
    queries_all,
    hot_all,
    normed,
    factor,
    gain,
    dsecond,
    douter,
    sums,
    embeddings,
    loss,
    query_grad,
    own,
    arrived,
    tables,
    everyone,
    asked,
    hot,
    wide_loss,
    dscore,
    turned,
    send_sem,
    recv_sem,
    ring_send,
    ring_recv,
):
    dp, blk, _ = place()
    ring = [(dp, lax.rem(blk + step, ring_size)) for step in range(1, ring_size)]
    members = [(lax.rem(dp + step, dp_size), blk) for step in range(1, dp_size)]
    greet(ring + members)
    micro, tokens, _ = output.shape
    many = own.shape[0] // micro
    seg_rows = seg_full.shape[0] // ring_size
    lane = lax.broadcasted_iota(jnp.int32, (many, tokens), 1)
    number = lax.broadcasted_iota(jnp.int32, (many, tokens), 0)
    selects = []
    for m in range(micro):
        here = seg_full[pl.ds(blk * seg_rows + m, 1)]
        there = seg_full[pl.ds(jnp.maximum(blk - 1, 0) * seg_rows + m, 1)]
        here = jnp.broadcast_to(here, (many, tokens))
        there = jnp.broadcast_to(there, (many, tokens))
        there = jnp.where(blk == 0, -1, there)
        before = jnp.where(lane == 0, pltpu.roll(there, 1, 1), pltpu.roll(here, 1, 1))
        chosen = (here != before) & (here == number)
        selects.append(jnp.where(chosen, 1.0, 0.0).astype(jnp.bfloat16))
        own[m * many : (m + 1) * many] = contract(selects[m], output[m], 1, 0).astype(jnp.bfloat16)
    copies = []
    for step, peer in enumerate(ring):
        copy = remote(own, arrived.at[step], ring_send.at[step], ring_recv.at[step], peer)
        copy.start()
        copies.append(copy)
    for d in range(dp_size):
        for m in range(micro):
            rows = slice((d * micro + m) * many, (d * micro + m + 1) * many)
            at = slice(d * many, (d + 1) * many)
            asked[m, at] = queries_all[rows]
            hot[m, at] = hot_all[rows]
    for copy in copies:
        copy.wait()
    total = own[...].astype(jnp.float32)
    for step in range(ring_size - 1):
        total = total + arrived[step].astype(jnp.float32)
    tables[dp] = total.astype(jnp.bfloat16)
    copies = []
    for step, peer in enumerate(members):
        copy = remote(tables.at[dp], tables.at[dp], send_sem.at[step], recv_sem.at[step], peer)
        copy.start()
        copies.append(copy)
    for m in range(micro):
        embeddings[m] = total[m * many : (m + 1) * many].astype(jnp.bfloat16)
    for copy in copies:
        copy.wait()
    for m in range(micro):
        for d in range(dp_size):
            everyone[m, d * many : (d + 1) * many] = tables[d, m * many : (m + 1) * many]
    mine = pl.ds(pl.multiple_of(dp * many, many), many)
    for m in range(micro):
        scores = contract(asked[m], everyone[m], 1, 1)
        peak = jnp.max(scores, axis=1, keepdims=True)
        log_total = peak + jnp.log(jnp.sum(jnp.exp(scores - peak), axis=1, keepdims=True))
        target = hot[m].astype(jnp.float32)
        value = log_total - jnp.sum(scores * target, axis=1, keepdims=True)
        wide_loss[...] = jnp.broadcast_to(value, wide_loss.shape)
        loss[m] = wide_loss[mine]
        slope = jnp.exp(scores - log_total) - target
        dscore[...] = slope
        turned[...] = slope.T
        query_grad[m] = split_dot(dscore[mine], everyone[m], 1, 0)
        embed_grad = split_dot(turned[mine], asked[m], 1, 0)
        high = embed_grad.astype(jnp.bfloat16)
        rest = (embed_grad - high.astype(jnp.float32)).astype(jnp.bfloat16)
        dout = (
            cotangent[m].astype(jnp.float32)
            + contract(selects[m], high, 0, 0)
            + contract(selects[m], rest, 0, 0)
        )
        scaled = dout * gain[...]
        product = dout * normed[m]
        inner_term = (
            scaled
            - jnp.mean(scaled, axis=1, keepdims=True)
            - normed[m] * jnp.mean(scaled * normed[m], axis=1, keepdims=True)
        ) * factor[m]
        dsecond[m] = inner_term
        rounded = inner_term.astype(jnp.bfloat16)
        douter[m] = rounded
        for row, values in enumerate((rounded.astype(jnp.float32), product, dout)):
            line = jnp.sum(values, axis=0, keepdims=True)
            if m == 0:
                sums[row : row + 1] = line
            else:
                sums[row : row + 1] += line


def retrieve(
    output, cotangent, seg_full, queries_all, hot_all, normed, factor, gain, ring_size, dp_size
):
    micro, tokens, width = output.shape
    many = queries_all.shape[0] // (dp_size * micro)
    total = dp_size * many
    narrow, wide = jnp.bfloat16, jnp.float32
    shape = jax.ShapeDtypeStruct
    return pl.pallas_call(
        functools.partial(retrieve_kernel, ring_size, dp_size),
        out_shape=(
            shape((micro, tokens, width), wide),
            shape((micro, tokens, width), narrow),
            shape((8, width), wide),
            shape((micro, many, width), narrow),
            shape((micro, many, 128), wide),
            shape((micro, many, width), wide),
        ),
        in_specs=[IN_VMEM] * 8,
        out_specs=(IN_VMEM,) * 6,
        scratch_shapes=[
            pltpu.VMEM((micro * many, width), narrow),
            pltpu.VMEM((ring_size - 1, micro * many, width), narrow),
            pltpu.VMEM((dp_size, micro * many, width), narrow),
            pltpu.VMEM((micro, total, width), narrow),
            pltpu.VMEM((micro, total, width), narrow),
            pltpu.VMEM((micro, total, total), narrow),
            pltpu.VMEM((total, 128), wide),
            pltpu.VMEM((total, total), wide),
            pltpu.VMEM((total, total), wide),
            pltpu.SemaphoreType.DMA((dp_size,)),
            pltpu.SemaphoreType.DMA((dp_size,)),
            pltpu.SemaphoreType.DMA((ring_size,)),
            pltpu.SemaphoreType.DMA((ring_size,)),
        ],
        compiler_params=comm_params(4),
    )(output, cotangent, seg_full, queries_all, hot_all, normed, factor, gain)


def gelu_and_slope(values):
    size = jnp.abs(values)
    step = 1.0 / (1.0 + (0.3275911 / math.sqrt(2.0)) * size)
    series = 0.5 * 1.061405429
    for factor in (-1.453152027, 1.421413741, -0.284496736, 0.254829592):
        series = series * step + 0.5 * factor
    bell = jnp.exp(-0.5 * values * values)
    tail = series * step * bell
    normal_cdf = jnp.where(values >= 0.0, 1.0 - tail, tail)
    slope = normal_cdf + values * bell * (1.0 / math.sqrt(2.0 * math.pi))
    return values * normal_cdf, slope


def fast_body(
    hidden_in,
    segment_ids,
    queries,
    targets,
    cotangent,
    query_weight,
    key_weight,
    value_weight,
    output_weight,
    query_bias,
    value_bias,
    output_bias,
    first_gain,
    first_shift,
    inner_weight,
    inner_bias,
    outer_weight,
    outer_bias,
    second_gain,
    second_shift,
):
    dp_size, ring_size = lax.axis_size("dp"), lax.axis_size("blk")
    dp, blk = lax.axis_index("dp"), lax.axis_index("blk")
    micro, row_count, block_tokens, width = hidden_in.shape
    row_queries = queries.shape[1]
    length = block_tokens * ring_size
    head_dim = width // HEADS
    spread = ring_size // micro
    own_heads = HEADS // spread
    tokens = micro * block_tokens
    wide = jnp.float32
    narrow = jnp.bfloat16

    vectors = (
        query_bias,
        value_bias,
        output_bias,
        first_gain,
        first_shift,
        outer_bias,
        second_gain,
        second_shift,
        inner_bias,
    )
    piece = vectors[0].shape[0]
    inner_piece = inner_bias.shape[0]
    group = own_heads * head_dim
    row_at, group_at = blk // spread, lax.rem(blk, spread) * group
    hidden_rows = hidden_in.reshape(micro, block_tokens, width)
    pack = jnp.concatenate(
        (
            jnp.pad(jnp.stack(vectors[:8]), ((0, 0), (0, inner_piece - piece))),
            jnp.pad(inner_bias[None], ((0, 7), (0, 0))),
        )
    )
    passages = dp_size * row_queries
    hot = jnp.where(
        targets.reshape(micro * row_queries, 1) == jnp.arange(passages, dtype=jnp.int32)[None],
        1.0,
        0.0,
    ).astype(narrow)
    seg_pack = jnp.pad(segment_ids.reshape(micro, block_tokens), ((0, 8 - micro), (0, 0)))
    shards = (
        query_weight,
        key_weight,
        value_weight,
        pack,
        hot,
        queries.reshape(micro * row_queries, width),
        output_weight,
        inner_weight,
        outer_weight,
    )
    ways = (("x", "y"), ("y", "x"))
    items = []

    def add_item(source, target, row=0, rows=None, from_column=0, columns=None, to_column=0):
        shape = shards[source].shape
        items.append(
            {
                "source": source,
                "target": target,
                "row": row,
                "rows": rows or shape[0],
                "stride": shape[0],
                "from_column": from_column,
                "columns": columns or shape[1],
                "to_column": to_column,
                "route": ways[len(items) % 2],
            }
        )

    for index in range(3):
        add_item(index, 0, from_column=None, columns=group, to_column=index * group)
    add_item(3, 1)
    add_item(6, 4)
    for part in range(4):
        add_item(7, 5, from_column=part * width, columns=width, to_column=part * width)
        add_item(8, 6, row=part * piece, rows=piece)
    add_item(4, 2)
    add_item(5, 3)
    targets_out = [jax.ShapeDtypeStruct((width, 3 * group), narrow)] + [
        jax.ShapeDtypeStruct((dp_size * s.shape[0], s.shape[1]), s.dtype) for s in shards[3:]
    ]
    (
        w_window,
        pack_all,
        hot_all,
        queries_all,
        wo_full,
        w_inner,
        w_outer,
        seg_all,
        hidden_row,
        qkv,
        context,
        stats,
        context_t,
    ) = forward(shards, items, targets_out, seg_pack, hidden_rows, ring_size, head_dim)
    pack_rows = pack_all.reshape(dp_size, 16, inner_piece)
    eight = pack_rows[:, :8, :piece].transpose(1, 0, 2).reshape(8, width).astype(wide)
    bq_full, bv_full, bo_full, gain_one, shift_one, b_outer, gain_two, shift_two = eight
    b_inner = pack_rows[:, 8].reshape(-1).astype(wide)
    seg_row = (
        seg_all.reshape(ring_size, 8, block_tokens)[:, :micro]
        .transpose(1, 0, 2)
        .reshape(micro, 1, length)
    )
    seg_mine = lax.dynamic_slice(seg_row, (row_at, 0, 0), (1, 1, length)).reshape(1, length)

    flat_rows = hidden_in.reshape(tokens, width)
    flat_rows, context_t = lax.optimization_barrier((flat_rows, context_t))
    attended = (
        jnp.einsum("met,ed->mtd", context_t, wo_full, preferred_element_type=wide).reshape(
            tokens, width
        )
        + bo_full
    )
    first_out, first_normed, first_factor = layer_norm(
        flat_rows.astype(wide) + attended, gain_one, shift_one
    )
    first_low = first_out.astype(narrow)
    inner_pre = jnp.dot(first_low, w_inner, preferred_element_type=wide) + b_inner
    active, slope = gelu_and_slope(inner_pre)
    active, slope = lax.optimization_barrier((active.astype(narrow), slope.astype(narrow)))
    outer_out = jnp.dot(active, w_outer, preferred_element_type=wide) + b_outer
    output, second_normed, second_factor = layer_norm(first_out + outer_out, gain_two, shift_two)
    output_low = output.astype(narrow)
    output_rows = output_low.reshape(micro, block_tokens, width)

    dsecond, douter, second_sums, embeddings, query_loss, query_grad = retrieve(
        output_rows,
        cotangent.reshape(micro, block_tokens, width),
        seg_all,
        queries_all,
        hot_all,
        second_normed.reshape(micro, block_tokens, width),
        second_factor.reshape(micro, block_tokens, 1),
        gain_two.reshape(1, width),
        ring_size,
        dp_size,
    )
    query_loss = query_loss[:, :, 0]
    dsecond = dsecond.reshape(tokens, width)
    douter = douter.reshape(tokens, width)
    dactive = jnp.einsum("nd,fd->nf", douter, w_outer, preferred_element_type=wide)
    dinner = (dactive * slope.astype(wide)).astype(narrow)
    inner_bias_grad = jnp.sum(dinner.astype(wide), axis=0)
    inner_weight_grad = jnp.einsum(
        "nd,nf->df", first_low, dinner, preferred_element_type=wide
    ).astype(narrow)
    dfirst = dsecond + jnp.einsum("nf,df->nd", dinner, w_inner, preferred_element_type=wide)
    gain_one_grad = jnp.sum(dfirst * first_normed, axis=0)
    shift_one_grad = jnp.sum(dfirst, axis=0)
    dresidual = norm_back(dfirst, first_normed, first_factor, gain_one)
    dattended = dresidual.astype(narrow)
    output_bias_grad = jnp.sum(dattended.astype(wide), axis=0)
    datt_rows = dattended.reshape(micro, block_tokens, width)
    output_weight_grad = jnp.einsum(
        "met,mtd->ed", context_t, datt_rows, preferred_element_type=wide
    ).astype(narrow)
    dcontext_t = jnp.einsum(
        "mtd,ed->met", datt_rows, wo_full, preferred_element_type=wide
    ).astype(narrow)
    vector_grads = jnp.concatenate(
        (
            jnp.zeros((2, width), wide),
            jnp.stack((output_bias_grad, gain_one_grad, shift_one_grad)),
            second_sums[:3],
        )
    )
    grad_pack = jnp.pad(
        jnp.concatenate(
            (
                jnp.pad(
                    vector_grads.reshape(8, dp_size, piece).transpose(1, 0, 2),
                    ((0, 0), (0, 0), (0, inner_piece - piece)),
                ),
                inner_bias_grad.reshape(dp_size, 1, inner_piece),
            ),
            axis=1,
        ),
        ((0, 0), (0, 7), (0, 0)),
    ).reshape(dp_size * 16, inner_piece)
    grads = (inner_weight_grad, output_weight_grad)
    grad_shapes = [(inner_bias.shape[0] * dp_size, width)]
    grad_shapes += [grad.shape for grad in grads] + [(width, 3 * group), grad_pack.shape]
    sums = []

    def add_sum(source, row=0, rows=None, column=0, columns=None, widened=1):
        shape = grad_shapes[source]
        sums.append(
            {
                "source": source,
                "row": row,
                "rows": rows or shape[0] // dp_size,
                "stride": shape[0] // dp_size,
                "column": column,
                "columns": columns or shape[1],
                "widened": widened,
                "route": ways[len(sums) % 2],
            }
        )

    for part in range(4):
        add_sum(1, column=part * width, columns=width)
    add_sum(2)
    for part in range(4):
        add_sum(0, row=part * piece, rows=piece)
    for index in range(3):
        add_sum(3, column=index * group, columns=group, widened=spread)
    add_sum(4)
    dhidden, d_outer, d_inner, d_wo, d_window, d_pack = backward(
        dcontext_t,
        seg_mine,
        grad_pack,
        (qkv, context, stats),
        w_window,
        hidden_row,
        dresidual.reshape(micro, block_tokens, width),
        active,
        douter,
        grads,
        sums,
        ring_size,
        dp_size,
        head_dim,
        5,
    )
    d_outer, d_inner, d_wo, d_window, d_pack = (
        part.astype(wide) for part in (d_outer, d_inner, d_wo, d_window, d_pack)
    )
    d_wq, d_wk, d_wv = (d_window[:, i * width : (i + 1) * width] for i in range(3))
    d_bq, d_bv, d_bo, d_g1, d_s1, d_bu, d_g2, d_s2 = (d_pack[i, :piece] for i in range(8))
    d_bi = d_pack[8]
    shape = (micro, row_count, block_tokens, width)
    return (
        output_low.reshape(shape),
        embeddings,
        query_loss,
        query_grad,
        dhidden.reshape(shape),
        d_wq,
        d_wk,
        d_wv,
        d_wo,
        d_bq,
        d_bv,
        d_bo,
        d_g1,
        d_s1,
        d_inner,
        d_bi,
        d_outer,
        d_bu,
        d_g2,
        d_s2,
    )


def solution(mesh):
    in_specs = (
        P(None, "dp", "blk", None),
        P(None, "dp", "blk"),
        P(None, "dp", None),
        P(None, "dp"),
        P(None, "dp", "blk", None),
        P("dp", None),
        P("dp", None),
        P("dp", None),
        P("dp", None),
        P("dp"),
        P("dp"),
        P("dp"),
        P("dp"),
        P("dp"),
        P("dp", None),
        P("dp"),
        P("dp", None),
        P("dp"),
        P("dp"),
        P("dp"),
    )
    out_specs = (
        P(None, "dp", "blk", None),
        P(None, "dp", None),
        P(None, "dp"),
        P(None, "dp", None),
        P(None, "dp", "blk", None),
        P("dp", None),
        P("dp", None),
        P("dp", None),
        P("dp", None),
        P("dp"),
        P("dp"),
        P("dp"),
        P("dp"),
        P("dp"),
        P("dp", None),
        P("dp"),
        P("dp", None),
        P("dp"),
        P("dp"),
        P("dp"),
    )
    fast = mesh.shape["dp"] == 8 and mesh.shape["blk"] == 4
    body = fast_body if fast else ring_body
    return jax.shard_map(body, mesh=mesh, in_specs=in_specs, out_specs=out_specs, check_vma=False)
```
